32 devices in a mesh: dp: 4 (over y, x), row: 2 (over core), col: 4 (over z).
Axes of the slice: x: 2, y: 2, z: 4, core: 2. Of those that a mesh axis runs over, the one named last changes fastest.
Arguments:
- tokens: bfloat16 [16384, 1536], P(('dp', 'row', 'col')), may hold values from -6 to 6
- norm_gain: bfloat16 [1536], replicated, may hold values from 0.5 to 1.5
- w_gate: bfloat16 [1536, 3072], P('row', 'col'), may hold values from -0.15625 to 0.15625
- w_value: bfloat16 [1536, 3072], P('row', 'col'), may hold values from -0.15625 to 0.15625
- w_state: bfloat16 [1536, 256], P('row', 'col'), may hold values from -0.15625 to 0.15625
- w_step: bfloat16 [1536, 48], P('row', 'col'), may hold values from -0.15625 to 0.15625
- conv_value: bfloat16 [3072, 4], P('col'), may hold values from -3 to 3
- bias_value: bfloat16 [3072], P('col'), may hold values from -3 to 3
- conv_state: bfloat16 [256, 4], P('col'), may hold values from -3 to 3
- bias_state: bfloat16 [256], P('col'), may hold values from -3 to 3
- a_log: bfloat16 [48], P('col'), may hold values from -4 to 2.765625
- d_skip: bfloat16 [48], P('col'), may hold values from 0.5 to 1.5
- dt_bias: bfloat16 [48], P('col'), may hold values from -5 to -1
- mix_gain: bfloat16 [3072], P('col'), may hold values from 0.5 to 1.5
- w_out: bfloat16 [3072, 1536], P('col', 'row'), may hold values from -0.109375 to 0.109375
- cotangent: bfloat16 [16384, 1536], P(('dp', 'row', 'col')), may hold values from -6 to 6
Outputs:
- block_out: bfloat16 [16384, 1536], P(('dp', 'row', 'col'))
- tokens_grad: float32 [16384, 1536], P(('dp', 'row', 'col'))
- grad_norm_gain: float32 [1536], replicated
- grad_w_gate: float32 [1536, 3072], P('row', 'col')
- grad_w_value: float32 [1536, 3072], P('row', 'col')
- grad_w_state: float32 [1536, 256], P('row', 'col')
- grad_w_step: float32 [1536, 48], P('row', 'col')
- grad_conv_value: float32 [3072, 4], P('col')
- grad_bias_value: float32 [3072], P('col')
- grad_conv_state: float32 [256, 4], P('col')
- grad_bias_state: float32 [256], P('col')
- grad_a_log: float32 [48], P('col')
- grad_d_skip: float32 [48], P('col')
- grad_dt_bias: float32 [48], P('col')
- grad_mix_gain: float32 [3072], P('col')
- grad_w_out: float32 [3072, 1536], P('col', 'row')
The draws below stay inside these ranges and needn't reach their ends.
All inputs are finite; a program needn't handle non-finite values.
Results may differ from the reference program's by a relative error of at most 0.003.
The reference program's roundings to bfloat16 on the way count: a program that leaves them out, or rounds other values in their place, can miss the bound.
Values may be sent and summed in bfloat16 or wider, within the bound.
A program may use at most 256 MiB of HBM per device.

```python
from functools import partial
import jax
import jax.numpy as jnp
from jax import lax

D = 1536
H = 48
N = 128
K = 4
Q = 256
SEQ_LEN = 2048
DI = 3072
TOKENS = 16384


def levels(rng, extent, shards, least, top_value):
    level = 1.0
    for axis_at, shards_of in shards:
        draws = jax.random.uniform(jax.random.fold_in(jax.random.fold_in(rng, 6), axis_at), (shards_of,), jnp.float32, least / len(shards), top_value / len(shards))
        level = level * jnp.repeat(jnp.exp(draws), extent[axis_at] // shards_of).reshape((-1,) + (1,) * (len(extent) - 1 - axis_at))
    return level


def scatter_about(rng, extent, scale, most, pieces=(), held_as=jnp.bfloat16):
    array = scale * jax.random.normal(rng, extent, jnp.float32)
    if pieces:
        array = array * levels(rng, extent, pieces, -0.22, 0.18)
    return jnp.clip(array, -most, most).astype(held_as)


def setup_inputs(seed: int = 0) -> dict:
    splits = jax.random.split(jax.random.key(seed), 17)
    tokens = scatter_about(splits[0], (TOKENS, D), 1.0, 6.0, ((0, 32),))
    norm_gain = jnp.clip(1.0 + 0.1 * jax.random.normal(splits[1], (D,), jnp.float32), 0.5, 1.5).astype(jnp.bfloat16)
    w_gate = scatter_about(splits[2], (D, DI), D ** -0.5, 0.15625, ((0, 2), (1, 4)))
    w_value = scatter_about(splits[3], (D, DI), D ** -0.5, 0.15625, ((0, 2), (1, 4)))
    w_state = scatter_about(splits[4], (D, 2 * N), D ** -0.5, 0.15625, ((0, 2), (1, 4)))
    w_step = scatter_about(splits[5], (D, H), D ** -0.5, 0.15625, ((0, 2), (1, 4)))
    conv_value = scatter_about(splits[6], (DI, K), K ** -0.5, 3.0, ((0, 4),))
    bias_value = scatter_about(splits[7], (DI,), 0.5, 3.0, ((0, 4),))
    conv_state = scatter_about(splits[8], (2 * N, K), K ** -0.5, 3.0, ((0, 4),))
    bias_state = scatter_about(splits[9], (2 * N,), 0.5, 3.0, ((0, 4),))
    a_log = jnp.clip(-4.0 + 6.765625 * jax.random.uniform(splits[10], (H,), jnp.float32) ** levels(splits[10], (H,), ((0, 4),), -0.2, 0.2), -4.0, 2.765625).astype(jnp.bfloat16)
    d_skip = jnp.clip(0.5 + 1.0 * jax.random.uniform(splits[11], (H,), jnp.float32) ** levels(splits[11], (H,), ((0, 4),), -0.2, 0.2), 0.5, 1.5).astype(jnp.bfloat16)
    dt_bias = jnp.clip(-5.0 + 4.0 * jax.random.uniform(splits[12], (H,), jnp.float32) ** levels(splits[12], (H,), ((0, 4),), -0.2, 0.2), -5.0, -1.0).astype(jnp.bfloat16)
    mix_gain = jnp.clip(1.0 + 0.1 * jax.random.normal(splits[13], (DI,), jnp.float32), 0.5, 1.5).astype(jnp.bfloat16)
    w_out = scatter_about(splits[14], (DI, D), DI ** -0.5, 0.109375, ((0, 4), (1, 2)))
    cotangent = scatter_about(splits[15], (TOKENS, D), 1.0, 6.0, ((0, 32),))
    return dict(tokens=tokens, norm_gain=norm_gain, w_gate=w_gate, w_value=w_value, w_state=w_state, w_step=w_step, conv_value=conv_value, bias_value=bias_value, conv_state=conv_state, bias_state=bias_state, a_log=a_log, d_skip=d_skip, dt_bias=dt_bias, mix_gain=mix_gain, w_out=w_out, cotangent=cotangent)


@jax.custom_vjp
def low(v):
    return lax.optimization_barrier(v.astype(jnp.bfloat16)).astype(jnp.float32)

@jax.custom_vjp
def low_back(v):
    return v

def low_keep(v):
    return (low(v), None)

def low_pass(kept, grad):
    return (grad,)

def back_keep(v):
    return (v, None)

def back_low(kept, grad):
    return (low(grad),)
low.defvjp(low_keep, low_pass)
low_back.defvjp(back_keep, back_low)
EPSILON = 1e-05
HIGHEST = lax.Precision.HIGHEST

def matmul(left, right):
    return jnp.dot(left, right, precision=HIGHEST)

def precise(form, *operands):
    return jnp.einsum(form, *operands, precision=HIGHEST)

def causal_conv(inputs, kernel, offsets):
    tap_count = kernel.shape[1]
    length = inputs.shape[0]
    padded = jnp.pad(inputs, ((tap_count - 1, 0), (0, 0)))
    running = jnp.zeros_like(inputs) + offsets
    for offset in range(tap_count):
        running = running + kernel[:, offset] * padded[offset:offset + length]
    return running

def scan_blocks(head_values, step_sizes, decay_rate, b_matrix, c_matrix):
    length, head_count, head_size = head_values.shape
    blocks = length // Q
    x_blocks = head_values.reshape(blocks, Q, head_count, head_size)
    step_blocks = step_sizes.reshape(blocks, Q, head_count)
    b_blocks = b_matrix.reshape(blocks, Q, -1)
    c_blocks = c_matrix.reshape(blocks, Q, -1)
    cumulative = jnp.cumsum(step_blocks * decay_rate, axis=1)
    cum_heads = jnp.transpose(cumulative, (0, 2, 1))
    step_heads = jnp.transpose(step_blocks, (0, 2, 1))
    causal = lax.broadcasted_iota(jnp.int32, (Q, Q), 0) >= lax.broadcasted_iota(jnp.int32, (Q, Q), 1)
    affinity = precise('cin,cjn->cij', c_blocks, b_blocks)
    spread = cum_heads[:, :, :, None] - cum_heads[:, :, None, :]
    weights_decay = jnp.where(causal, jnp.exp(jnp.where(causal, spread, 0.0)), 0.0)
    mixing = affinity[:, None] * weights_decay * step_heads[:, :, None, :]
    tail_weight = jnp.exp(cumulative[:, -1:, :] - cumulative) * step_blocks
    fresh_state = precise('cjn,cjh,cjhp->chnp', b_blocks, tail_weight, x_blocks)
    block_fall = jnp.exp(cumulative[:, -1, :])

    def advance(carried, scan_item):
        fall_rate, added_state = scan_item
        return (fall_rate[:, None, None] * carried + added_state, carried)
    _, before = lax.scan(advance, jnp.zeros(fresh_state.shape[1:], fresh_state.dtype), (block_fall, fresh_state))
    reached = precise('cin,chnp->cihp', c_blocks, before)
    output = precise('chij,cjhp->cihp', mixing, x_blocks) + reached * jnp.exp(cumulative)[..., None]
    return output.reshape(length, head_count, head_size)

def mixer(weights, rows):
    norm_gain, w_gate, w_value, w_state, w_step, conv_value, bias_value, conv_state, bias_state, a_log, d_skip, dt_bias, mix_gain, w_out = weights
    rstd = lax.rsqrt(lax.optimization_barrier(jnp.mean(rows * rows, axis=-1, keepdims=True)) + EPSILON)
    normed = low(rows * rstd * norm_gain)
    gate_raw = low_back(matmul(normed, w_gate))
    value_raw = low_back(matmul(normed, w_value))
    state_raw = low_back(matmul(normed, w_state))
    step_raw = low_back(matmul(normed, w_step))
    value_act = low(jax.nn.silu(causal_conv(value_raw, conv_value, bias_value)))
    state_act = low(jax.nn.silu(causal_conv(state_raw, conv_state, bias_state)))
    step_size = jax.nn.softplus(step_raw + dt_bias)
    decay_rate = -jnp.exp(a_log)
    length = rows.shape[0]
    head_values = value_act.reshape(length, a_log.shape[0], -1)
    scanned = scan_blocks(head_values, step_size, decay_rate, state_act[:, :N], state_act[:, N:])
    y_full = (scanned + d_skip[None, :, None] * head_values).reshape(length, -1)
    gated = y_full * jax.nn.silu(gate_raw)
    inv_gate = lax.rsqrt(lax.optimization_barrier(jnp.mean(gated * gated, axis=-1, keepdims=True)) + EPSILON)
    mixed = low(gated * inv_gate * mix_gain)
    return rows + matmul(mixed, w_out)

def reference(tokens, norm_gain, w_gate, w_value, w_state, w_step, conv_value, bias_value, conv_state, bias_state, a_log, d_skip, dt_bias, mix_gain, w_out, cotangent):
    params = tuple((member.astype(jnp.float32) for member in (norm_gain, w_gate, w_value, w_state, w_step, conv_value, bias_value, conv_state, bias_state, a_log, d_skip, dt_bias, mix_gain, w_out)))
    sequences = tokens.astype(jnp.float32).reshape(TOKENS // SEQ_LEN, SEQ_LEN, D)

    def forward(weights, rows):
        return lax.map(jax.checkpoint(partial(mixer, weights)), rows)
    outputs, pullback = jax.vjp(forward, params, sequences)
    grads, grad_rows = pullback(cotangent.astype(jnp.float32).reshape(sequences.shape))
    g_norm, g_gate, g_value, g_state, g_step, g_conv_value, g_bias_value, g_conv_state, g_bias_state, g_a_log, g_skip, g_dt_bias, g_mix, g_out = grads
    return (outputs.reshape(TOKENS, D).astype(jnp.bfloat16), grad_rows.reshape(TOKENS, D), g_norm, g_gate, g_value, g_state, g_step, g_conv_value, g_bias_value, g_conv_state, g_bias_state, g_a_log, g_skip, g_dt_bias, g_mix, g_out)
```

```python
from functools import partial

import jax
import jax.numpy as jnp
from jax import lax
from jax.experimental import pallas as pl
from jax.experimental.pallas import tpu as pltpu
from jax.sharding import PartitionSpec as P

BF = jnp.bfloat16
F32 = jnp.float32
EPSILON = 1e-05
N = 128
Q = 128
HEAD = 64
HALO = 16
TILE = 256
HIGHEST = lax.Precision.HIGHEST
VMEM_LIMIT = 56 * 2**20


def mm(a, b):
    return lax.dot_general(a, b, (((1,), (0,)), ((), ())), preferred_element_type=F32)


def mm_nt(a, b):
    return lax.dot_general(a, b, (((1,), (1,)), ((), ())), preferred_element_type=F32)


def mm_exact(a, b):
    return lax.dot_general(
        a, b, (((1,), (0,)), ((), ())), precision=HIGHEST, preferred_element_type=F32
    )


def split2(values):
    high = values.astype(BF)
    return high, (values - high.astype(F32)).astype(BF)


def sigmoid(values):
    return 1.0 / (1.0 + jnp.exp(-values))


def iota2(shape, axis):
    return lax.broadcasted_iota(jnp.int32, shape, axis)


def params(*names):
    return pltpu.CompilerParams(
        dimension_semantics=names or ("arbitrary",), vmem_limit_bytes=VMEM_LIMIT
    )


def cost(micros):
    return pl.CostEstimate(flops=0, bytes_accessed=int(micros * 3.0e6), transcendentals=0)


def whole(shape):
    return pl.BlockSpec(shape, lambda *_: (0,) * len(shape))


def columns(rows, width=TILE):
    return pl.BlockSpec((rows, width), lambda j: (0, j))


def sds(shape, dtype=F32):
    return jax.ShapeDtypeStruct(shape, dtype)


def conv_rows(raw_ref, taps, start, size):
    total = taps[4:5, :] + jnp.zeros((size, taps.shape[1]), F32)
    for k in range(4):
        total = total + taps[k : k + 1, :] * raw_ref[pl.ds(HALO - 3 + k + start, size), :]
    return total


def project_kernel(
    normed_ref, w_ref, taps_ref, wstep_ref, head_ref,
    raw_ref, act_ref, stepin_ref, step_ref, cum_ref, grow_ref, offs_ref,
):
    tokens = act_ref.shape[0]
    raw_ref[...] = mm(normed_ref[...], w_ref[...])
    taps = taps_ref[...]
    for at in range(0, tokens, Q):
        pre = conv_rows(raw_ref, taps, at, Q)
        act_ref[at : at + Q, :] = (pre * sigmoid(pre)).astype(BF)

    @pl.when(pl.program_id(0) == 0)
    def _():
        step_in = mm(normed_ref[HALO:, :], wstep_ref[...]) + head_ref[0:1, :]
        small = jnp.exp(-jnp.abs(step_in))
        plus = 1.0 + small
        log_part = jnp.where(plus == 1.0, small, jnp.log(plus) * (small / jnp.where(plus == 1.0, 1.0, plus - 1.0)))
        step = jnp.maximum(step_in, 0.0) + log_part
        stepin_ref[...] = step_in
        step_ref[...] = step
        falls = step * head_ref[1:2, :]
        lower = (iota2((Q, Q), 0) >= iota2((Q, Q), 1)).astype(F32)
        before = jnp.zeros((1, 128), F32)
        offs_ref[...] = jnp.zeros_like(offs_ref)
        for b in range(tokens // Q):
            rows = slice(b * Q, b * Q + Q)
            cum = mm_exact(lower, falls[rows, :])
            cum_ref[rows, :] = cum
            high, low = split2(jnp.exp(cum + before))
            grow_ref[rows, 0:128] = high
            grow_ref[rows, 128:256] = low
            before = before + cum[Q - 1 : Q, :]
            offs_ref[b + 1 : b + 2, :] = before


def project(normed, weights, taps, w_step, head_rows):
    rows, width = normed.shape
    tokens = rows - HALO
    total = weights.shape[1]
    return pl.pallas_call(
        project_kernel,
        grid=(total // TILE,),
        in_specs=[
            whole((rows, width)),
            columns(width),
            columns(8),
            whole((width, 128)),
            whole((8, 128)),
        ],
        out_specs=[
            columns(rows),
            columns(tokens),
            whole((tokens, 128)),
            whole((tokens, 128)),
            whole((tokens, 128)),
            whole((tokens, 256)),
            whole((16, 128)),
        ],
        out_shape=[
            sds((rows, total)),
            sds((tokens, total), BF),
            sds((tokens, 128)),
            sds((tokens, 128)),
            sds((tokens, 128)),
            sds((tokens, 256), BF),
            sds((16, 128)),
        ],
        compiler_params=params(),
        cost_estimate=cost(9),
        name="project",
    )(normed, weights, taps, w_step, head_rows)


def expand(per_head, spread):
    high, low = split2(per_head)
    return mm(jnp.concatenate([high, low], 1), spread)


def transpose_bf(values):
    return values.astype(F32).T.astype(BF)


def states_kernel(x_ref, b_ref, step_ref, cum_ref, spread_ref, states_ref, final_ref, held):
    at = pl.program_id(0)
    last = pl.num_programs(0) - 1

    @pl.when(at == 0)
    def _():
        held[...] = jnp.zeros_like(held)

    states_ref[0] = held[...]

    @pl.when(at == last)
    def _():
        final_ref[...] = held[...]

    @pl.when(at < last)
    def _():
        cum = cum_ref[...]
        end = cum[Q - 1 : Q, :]
        tail = jnp.exp(end - cum) * step_ref[...]
        fall = jnp.broadcast_to(jnp.exp(end), (8, 128))
        b_t = transpose_bf(b_ref[...])
        b_t2 = jnp.concatenate([b_t, b_t], 1)
        for start in range(0, x_ref.shape[1], TILE):
            lanes = slice(start, start + TILE)
            spread = spread_ref[:, lanes]
            scaled = expand(tail, spread) * x_ref[:, lanes].astype(F32)
            high, low = split2(scaled)
            fresh = mm(b_t2, jnp.concatenate([high, low], 0))
            held[:, lanes] = held[:, lanes] * expand(fall, spread)[0:1, :] + fresh


def scan_states(act, step, cum, spread, channels):
    blocks = act.shape[0] // Q
    clamp = lambda i: jnp.minimum(i, blocks - 1)
    return pl.pallas_call(
        states_kernel,
        grid=(blocks + 1,),
        in_specs=[
            pl.BlockSpec((Q, channels), lambda i: (clamp(i), 0)),
            pl.BlockSpec((Q, N), lambda i: (clamp(i), channels // N)),
            pl.BlockSpec((Q, 128), lambda i: (clamp(i), 0)),
            pl.BlockSpec((Q, 128), lambda i: (clamp(i), 0)),
            whole((256, channels)),
        ],
        out_specs=[
            pl.BlockSpec((1, N, channels), lambda i: (i, 0, 0)),
            whole((N, channels)),
        ],
        out_shape=[sds((blocks + 1, N, channels)), sds((N, channels))],
        scratch_shapes=[pltpu.VMEM((N, channels), F32)],
        compiler_params=params(),
        cost_estimate=cost(6),
        name="scan_states",
    )(act, act, step, cum, spread)


def forward_kernel(x_ref, b_ref, c_ref, step_ref, cum_ref, spread_ref, state_ref, y_ref):
    b_blk, c_blk = b_ref[...], c_ref[...]
    affinity = mm_nt(c_blk, b_blk)
    causal = iota2((Q, Q), 0) >= iota2((Q, Q), 1)
    first = iota2((Q, 128), 1) < HEAD
    cum = cum_ref[...]
    cum_t = cum.T
    step_t = step_ref[...].T
    growth = jnp.exp(cum)
    c2 = jnp.concatenate([c_blk, c_blk], 1)
    zero = jnp.zeros((Q, 128), BF)
    for start in range(0, x_ref.shape[1], TILE):
        lanes = slice(start, start + TILE)
        s_high, s_low = split2(state_ref[0, :, lanes])
        reached = mm(c2, jnp.concatenate([s_high, s_low], 0)) * expand(growth, spread_ref[:, lanes])
        for pair in range(2):
            at = start + pair * 128
            x_pair = x_ref[:, at : at + 128]
            x0, x1 = jnp.where(first, x_pair, zero), jnp.where(first, zero, x_pair)
            pieces = []
            for half in range(2):
                h = at // HEAD + half
                spread_h = cum[:, h : h + 1] - cum_t[h : h + 1, :]
                decay = jnp.exp(jnp.where(causal, spread_h, -1e30))
                mixing = affinity * decay * step_t[h : h + 1, :]
                pieces += split2(mixing)
            intra = mm(jnp.concatenate(pieces, 1), jnp.concatenate([x0, x0, x1, x1], 0))
            y_ref[:, at : at + 128] = intra + reached[:, pair * 128 : pair * 128 + 128]


def scan_forward(act, step, cum, spread, states, channels):
    tokens = act.shape[0]
    return pl.pallas_call(
        forward_kernel,
        grid=(tokens // Q,),
        in_specs=[
            pl.BlockSpec((Q, channels), lambda i: (i, 0)),
            pl.BlockSpec((Q, N), lambda i: (i, channels // N)),
            pl.BlockSpec((Q, N), lambda i: (i, channels // N + 1)),
            pl.BlockSpec((Q, 128), lambda i: (i, 0)),
            pl.BlockSpec((Q, 128), lambda i: (i, 0)),
            whole((256, channels)),
            pl.BlockSpec((1, N, channels), lambda i: (i, 0, 0)),
        ],
        out_specs=pl.BlockSpec((Q, channels), lambda i: (i, 0)),
        out_shape=sds((tokens, channels)),
        compiler_params=params(),
        cost_estimate=cost(13),
        name="scan_forward",
    )(act, act, act, step, cum, spread, states)


def grad_states_kernel(dy_ref, c_ref, cum_ref, spread_ref, after_ref, first_ref, held):
    at = pl.program_id(0)

    @pl.when(at == 0)
    def _():
        held[...] = jnp.zeros_like(held)

    after_ref[0] = held[...]
    cum = cum_ref[...]
    growth = jnp.exp(cum)
    fall = jnp.broadcast_to(growth[Q - 1 : Q, :], (8, 128))
    c_t = transpose_bf(c_ref[...])
    c_t2 = jnp.concatenate([c_t, c_t], 1)
    for start in range(0, dy_ref.shape[1], TILE):
        lanes = slice(start, start + TILE)
        spread = spread_ref[:, lanes]
        high, low = split2(dy_ref[:, lanes] * expand(growth, spread))
        direct = mm(c_t2, jnp.concatenate([high, low], 0))
        held[:, lanes] = held[:, lanes] * expand(fall, spread)[0:1, :] + direct
    first_ref[...] = held[...]


def scan_grad_states(dy, act, cum, spread):
    tokens, channels = dy.shape
    blocks = tokens // Q
    return pl.pallas_call(
        grad_states_kernel,
        grid=(blocks,),
        in_specs=[
            pl.BlockSpec((Q, channels), lambda i: (blocks - 1 - i, 0)),
            pl.BlockSpec((Q, N), lambda i: (blocks - 1 - i, channels // N + 1)),
            pl.BlockSpec((Q, 128), lambda i: (blocks - 1 - i, 0)),
            whole((256, channels)),
        ],
        out_specs=[
            pl.BlockSpec((1, N, channels), lambda i: (blocks - 1 - i, 0, 0)),
            whole((N, channels)),
        ],
        out_shape=[sds((blocks, N, channels)), sds((N, channels))],
        scratch_shapes=[pltpu.VMEM((N, channels), F32)],
        compiler_params=params(),
        cost_estimate=cost(6),
        name="scan_grad_states",
    )(dy, act, cum, spread)


def backward_near_kernel(
    dy_ref, x_ref, b_ref, c_ref, step_ref, cum_ref, spread_ref, state_ref, early_ref, offs_ref,
    gx_ref, gbc_ref,
):
    at_block = pl.program_id(0)
    b_blk, c_blk = b_ref[...], c_ref[...]
    affinity_t = mm_nt(b_blk, c_blk)
    causal_t = iota2((Q, Q), 1) >= iota2((Q, Q), 0)
    first = iota2((Q, 128), 1) < HEAD
    cum = cum_ref[...]
    cum_t = cum.T
    step = step_ref[...]
    growth = jnp.exp(cum)
    early_fall = jnp.broadcast_to(jnp.exp(offs_ref[pl.ds(at_block, 1), :]), (8, 128))
    zero = jnp.zeros((Q, 128), BF)
    grad_affinity_t = jnp.zeros((Q, Q), F32)
    grad_c = jnp.zeros((Q, N), F32)
    for start in range(0, x_ref.shape[1], TILE):
        lanes = slice(start, start + TILE)
        spread = spread_ref[:, lanes]
        before = state_ref[0, :, lanes] + expand(early_fall, spread)[0:1, :] * early_ref[:, lanes]
        dy_quad = dy_ref[:, lanes]
        s_high, s_low = split2(before)
        g_high, g_low = split2(dy_quad * expand(growth, spread))
        grad_c = grad_c + mm_nt(
            jnp.concatenate([g_high, g_low, g_high], 1), jnp.concatenate([s_high, s_high, s_low], 1)
        )
        for pair in range(2):
            at = start + pair * 128
            d_high, d_low = split2(dy_quad[:, pair * 128 : pair * 128 + 128])
            x_pair = x_ref[:, at : at + 128]
            x0, x1 = jnp.where(first, x_pair, zero), jnp.where(first, zero, x_pair)
            grad_mixing = mm_nt(
                jnp.concatenate([jnp.concatenate([x0, x0], 1), jnp.concatenate([x1, x1], 1)], 0),
                jnp.concatenate([d_high, d_low], 1),
            )
            left, right = [], []
            for half in range(2):
                h = at // HEAD + half
                spread_h = cum_t[h : h + 1, :] - cum[:, h : h + 1]
                decay = jnp.exp(jnp.where(causal_t, spread_h, -1e30))
                m_high, m_low = split2(affinity_t * decay)
                grad_affinity_t = grad_affinity_t + (
                    grad_mixing[half * Q : half * Q + Q, :] * decay * step[:, h : h + 1]
                )
                keep = first if half == 0 else jnp.logical_not(first)
                dh, dl = jnp.where(keep, d_high, zero), jnp.where(keep, d_low, zero)
                left += [m_high, m_low, m_high]
                right += [dh, dh, dl]
            gx_ref[:, at : at + 128] = mm(jnp.concatenate(left, 1), jnp.concatenate(right, 0))
    a_high, a_low = split2(grad_affinity_t)
    gbc_ref[:, 0:N] = mm(jnp.concatenate([a_high, a_low], 1), jnp.concatenate([c_blk, c_blk], 0))
    t_high, t_low = split2(grad_affinity_t.T)
    gbc_ref[:, N : 2 * N] = grad_c + mm(
        jnp.concatenate([t_high, t_low], 1), jnp.concatenate([b_blk, b_blk], 0)
    )


def scan_backward_near(dy, act, step, cum, spread, states, early, offs):
    tokens, channels = dy.shape
    rows = pl.BlockSpec((Q, channels), lambda i: (i, 0))
    return pl.pallas_call(
        backward_near_kernel,
        grid=(tokens // Q,),
        in_specs=[
            rows,
            rows,
            pl.BlockSpec((Q, N), lambda i: (i, channels // N)),
            pl.BlockSpec((Q, N), lambda i: (i, channels // N + 1)),
            pl.BlockSpec((Q, 128), lambda i: (i, 0)),
            pl.BlockSpec((Q, 128), lambda i: (i, 0)),
            whole((256, channels)),
            pl.BlockSpec((1, N, channels), lambda i: (i, 0, 0)),
            whole((N, channels)),
            whole((16, 128)),
        ],
        out_specs=[rows, pl.BlockSpec((Q, 2 * N), lambda i: (i, 0))],
        out_shape=[sds((tokens, channels)), sds((tokens, 2 * N))],
        compiler_params=params(),
        cost_estimate=cost(20),
        name="scan_backward_near",
    )(dy, act, act, act, step, cum, spread, states, early, offs)


def backward_far_kernel(
    dy_ref, x_ref, y_ref, gx_ref, b_ref, step_ref, cum_ref, stepin_ref, spread_ref, gather_ref,
    after_ref, late_ref, state_ref, early_ref, offs_ref, head_ref, skip_ref, gbc_ref,
    ga_ref, gstep_ref, gbc_out_ref, sums_ref,
):
    blocks = pl.num_programs(0)
    at_block = pl.program_id(0)

    @pl.when(at_block == 0)
    def _():
        sums_ref[...] = jnp.zeros_like(sums_ref)

    b_blk = b_ref[...]
    b2 = jnp.concatenate([b_blk, b_blk], 1)
    cum, step = cum_ref[...], step_ref[...]
    tail = jnp.exp(cum[Q - 1 : Q, :] - cum)
    tail_step = tail * step
    offs_after = offs_ref[pl.ds(at_block + 1, 1), :]
    offs_end = offs_ref[pl.ds(blocks, 1), :]
    late_fall = jnp.broadcast_to(jnp.exp(offs_end - offs_after), (8, 128))
    early_fall = jnp.broadcast_to(jnp.exp(offs_after), (8, 128))
    row_dots = jnp.zeros((Q, 128), F32)
    col_dots = jnp.zeros((Q, 128), F32)
    last_add = jnp.zeros((8, 128), F32)
    grad_b = gbc_ref[:, 0:N]
    for start in range(0, x_ref.shape[1], TILE):
        lanes = slice(start, start + TILE)
        spread = spread_ref[:, lanes]
        gather = gather_ref[lanes, :]
        gather2 = jnp.concatenate([gather, gather], 0)
        x_quad = x_ref[:, lanes].astype(F32)
        dy_quad = dy_ref[:, lanes]
        skip = skip_ref[0:1, lanes]
        d_state = after_ref[0, :, lanes] + expand(late_fall, spread)[0:1, :] * late_ref[:, lanes]
        state = state_ref[0, :, lanes] + expand(early_fall, spread)[0:1, :] * early_ref[:, lanes]
        touch = jnp.broadcast_to(jnp.sum(d_state * state, axis=0, keepdims=True), (8, TILE))
        t_high, t_low = split2(touch)
        last_add = last_add + mm(jnp.concatenate([t_high, t_low], 1), gather2)
        s_high, s_low = split2(d_state)
        gx = gx_ref[:, lanes] + expand(tail, spread) * mm(b2, jnp.concatenate([s_high, s_low], 0))
        w_high, w_low = split2(expand(tail_step, spread) * x_quad)
        grad_b = grad_b + mm_nt(
            jnp.concatenate([w_high, w_low, w_high], 1), jnp.concatenate([s_high, s_high, s_low], 1)
        )
        p_high, p_low = split2(dy_quad * (y_ref[:, lanes] - skip * x_quad))
        row_dots = row_dots + mm(jnp.concatenate([p_high, p_low], 1), gather2)
        r_high, r_low = split2(x_quad * gx)
        col_dots = col_dots + mm(jnp.concatenate([r_high, r_low], 1), gather2)
        ga_ref[:, lanes] = expand(step, spread) * gx + skip * dy_quad
    last_row = iota2((Q, 128), 0) == Q - 1
    grad_cum = row_dots - step * col_dots + jnp.where(last_row, last_add[0:1, :], 0.0)
    upper = (iota2((Q, Q), 1) >= iota2((Q, Q), 0)).astype(F32)
    grad_rate = mm_exact(upper, grad_cum)
    grad_step = col_dots + grad_rate * head_ref[1:2, :]
    grad_raw = grad_step * sigmoid(stepin_ref[...])
    gstep_ref[...] = grad_raw.astype(BF)
    sums_ref[0:1, :] += jnp.sum(grad_rate * step, axis=0, keepdims=True)
    sums_ref[1:2, :] += jnp.sum(grad_raw, axis=0, keepdims=True)
    gbc_out_ref[:, 0:N] = grad_b
    gbc_out_ref[:, N : 2 * N] = gbc_ref[:, N : 2 * N]


def scan_backward_far(
    dy, act, y, gx, step, cum, step_in, spread, gather, after, late, states, early, offs, head_rows, skip, gbc
):
    tokens, channels = dy.shape
    rows = pl.BlockSpec((Q, channels), lambda i: (i, 0))
    heads = pl.BlockSpec((Q, 128), lambda i: (i, 0))
    pairs = pl.BlockSpec((Q, 2 * N), lambda i: (i, 0))
    return pl.pallas_call(
        backward_far_kernel,
        grid=(tokens // Q,),
        in_specs=[
            rows,
            rows,
            rows,
            rows,
            pl.BlockSpec((Q, N), lambda i: (i, channels // N)),
            heads,
            heads,
            heads,
            whole((256, channels)),
            whole((channels, 128)),
            pl.BlockSpec((1, N, channels), lambda i: (i, 0, 0)),
            whole((N, channels)),
            pl.BlockSpec((1, N, channels), lambda i: (i + 1, 0, 0)),
            whole((N, channels)),
            whole((16, 128)),
            whole((8, 128)),
            whole((8, channels)),
            pairs,
        ],
        out_specs=[rows, heads, pairs, whole((8, 128))],
        out_shape=[
            sds((tokens, channels)),
            sds((tokens, 128), BF),
            sds((tokens, 2 * N)),
            sds((8, 128)),
        ],
        compiler_params=params(),
        cost_estimate=cost(14),
        name="scan_backward_far",
    )(dy, act, y, gx, act, step, cum, step_in, spread, gather, after, late, states, early, offs, head_rows, skip, gbc)


def gate_kernel(
    normed_ref, cot_ref, wg_ref, wo_ref, y0_ref, x_ref, early_ref, c_ref, grow_ref, spread_ref, vec_ref,
    graw_ref, y_ref, gm_ref, stats_ref, squares, inners,
):
    at = pl.program_id(0)
    tokens = cot_ref.shape[0]

    @pl.when(at == 0)
    def _():
        squares[...] = jnp.zeros_like(squares)
        inners[...] = jnp.zeros_like(inners)

    graw_ref[...] = mm(normed_ref[HALO:, :], wg_ref[...])
    gm_ref[...] = mm_nt(cot_ref[...], wo_ref[...])
    s_high, s_low = split2(early_ref[...])
    s2 = jnp.concatenate([s_high, s_low], 0)
    spread = spread_ref[...]
    skip, gain = vec_ref[0:1, :], vec_ref[1:2, :]
    for row in range(0, tokens, Q):
        rows = slice(row, row + Q)
        c_blk = c_ref[rows, :]
        carried = mm(jnp.concatenate([c_blk, c_blk], 1), s2) * mm(grow_ref[rows, :], spread)
        y = y0_ref[rows, :] + carried + skip * x_ref[rows, :].astype(F32)
        y_ref[rows, :] = y
        raw = graw_ref[rows, :]
        gated = y * raw * sigmoid(raw)
        square = gated * gated
        inner = gm_ref[rows, :] * gain * gated
        squares[rows, :] += square[:, 0:128] + square[:, 128:256]
        inners[rows, :] += inner[:, 0:128] + inner[:, 128:256]

    @pl.when(at == pl.num_programs(0) - 1)
    def _():
        ones = jnp.ones((8, 128), F32)
        nt = (((1,), (1,)), ((), ()))
        square_row = lax.dot_general(ones, squares[...], nt, precision=HIGHEST, preferred_element_type=F32)
        inner_row = lax.dot_general(ones, inners[...], nt, precision=HIGHEST, preferred_element_type=F32)
        stats_ref[...] = jnp.where(iota2(square_row.shape, 0) == 0, square_row, inner_row)


def gate_forward(normed, cot, w_gate, w_out, y0, act, early, grow, spread, vectors):
    rows, width = normed.shape
    tokens, channels = y0.shape
    return pl.pallas_call(
        gate_kernel,
        grid=(channels // TILE,),
        in_specs=[
            whole((rows, width)),
            whole((tokens, width)),
            columns(width),
            pl.BlockSpec((TILE, width), lambda j: (j, 0)),
            columns(tokens),
            columns(tokens),
            columns(N),
            pl.BlockSpec((tokens, N), lambda j: (0, channels // N + 1)),
            whole((tokens, 256)),
            columns(256),
            columns(8),
        ],
        out_specs=[columns(tokens), columns(tokens), columns(tokens), whole((8, tokens))],
        out_shape=[sds((tokens, channels))] * 3 + [sds((8, tokens))],
        scratch_shapes=[pltpu.VMEM((tokens, 128), F32), pltpu.VMEM((tokens, 128), F32)],
        compiler_params=params(),
        cost_estimate=cost(16),
        name="gate_forward",
    )(normed, cot, w_gate, w_out, y0, act, early, act, grow, spread, vectors)


def mix_kernel(
    inner_channels, graw_ref, y_ref, gm_ref, x_ref, stats_ref, vec_ref,
    mixed_ref, gg_ref, dy_ref, sums_ref, stats_col,
):
    tokens = y_ref.shape[0]

    @pl.when(pl.program_id(0) == 0)
    def _():
        stats_col[...] = stats_ref[...].T

    gain = vec_ref[1:2, :]
    gain_sum = jnp.zeros((1, TILE), F32)
    skip_sum = jnp.zeros((1, TILE), F32)
    for row in range(0, tokens, Q):
        rows = slice(row, row + Q)
        inv = lax.rsqrt(stats_col[rows, 0:1] * (1.0 / inner_channels) + EPSILON)
        pull = inv * inv * inv * (stats_col[rows, 1:2] * (1.0 / inner_channels))
        raw = graw_ref[rows, :]
        y = y_ref[rows, :]
        gm = gm_ref[rows, :]
        sig = sigmoid(raw)
        act = raw * sig
        gated = y * act
        unit = gated * inv
        mixed_ref[rows, :] = (unit * gain).astype(BF)
        gain_sum = gain_sum + jnp.sum(gm * unit, axis=0, keepdims=True)
        grad_gated = inv * (gm * gain) - gated * pull
        dy = grad_gated * act
        dy_ref[rows, :] = dy
        gg_ref[rows, :] = (grad_gated * y * (sig * (1.0 + raw * (1.0 - sig)))).astype(BF)
        skip_sum = skip_sum + jnp.sum(dy * x_ref[rows, :].astype(F32), axis=0, keepdims=True)
    sums_ref[...] = jnp.zeros_like(sums_ref)
    sums_ref[0:1, :] = gain_sum
    sums_ref[1:2, :] = skip_sum


def mix_backward(inner_channels, graw, y, gm, act, stats, vectors):
    tokens, channels = y.shape
    return pl.pallas_call(
        partial(mix_kernel, inner_channels),
        grid=(channels // TILE,),
        in_specs=[columns(tokens)] * 4 + [whole((128, tokens)), columns(8)],
        out_specs=[columns(tokens)] * 3 + [columns(8)],
        out_shape=[
            sds((tokens, channels), BF),
            sds((tokens, channels), BF),
            sds((tokens, channels)),
            sds((8, channels)),
        ],
        scratch_shapes=[pltpu.VMEM((tokens, 128), F32)],
        compiler_params=params(),
        cost_estimate=cost(10),
        name="mix_backward",
    )(graw, y, gm, act, stats, vectors)


def conv_back_kernel(ga_ref, raw_ref, taps_ref, gv_ref, sums_ref, g_pad):
    tokens, width = ga_ref.shape
    taps = taps_ref[...]
    g_pad[0:HALO, :] = jnp.zeros((HALO, width), F32)
    g_pad[HALO + tokens :, :] = jnp.zeros((HALO, width), F32)
    sums = [jnp.zeros((1, width), F32)] * 5
    for row in range(0, tokens, Q):
        pre = conv_rows(raw_ref, taps, row, Q)
        sig = sigmoid(pre)
        g = ga_ref[row : row + Q, :] * (sig * (1.0 + pre * (1.0 - sig)))
        g_pad[HALO + row : HALO + row + Q, :] = g
        for k in range(4):
            moved = raw_ref[pl.ds(HALO - 3 + k + row, Q), :]
            sums[k] = sums[k] + jnp.sum(g * moved, axis=0, keepdims=True)
        sums[4] = sums[4] + jnp.sum(g, axis=0, keepdims=True)
    for row in list(range(HALO, HALO + tokens, Q)) + [0]:
        size = HALO if row == 0 else Q
        total = jnp.zeros((size, width), F32)
        for k in range(4):
            total = total + taps[k : k + 1, :] * g_pad[pl.ds(row + 3 - k, size), :]
        gv_ref[row : row + size, :] = total.astype(BF)
    sums_ref[...] = jnp.zeros_like(sums_ref)
    for k in range(5):
        sums_ref[k : k + 1, :] = sums[k]


def conv_back(ga, raw, taps):
    tokens, channels = ga.shape
    width = min(channels, TILE)
    return pl.pallas_call(
        conv_back_kernel,
        grid=(channels // width,),
        in_specs=[columns(tokens, width), columns(tokens + HALO, width), columns(8, width)],
        out_specs=[columns(tokens + HALO, width), columns(8, width)],
        out_shape=[sds((tokens + HALO, channels), BF), sds((8, channels))],
        scratch_shapes=[pltpu.VMEM((tokens + 2 * HALO, width), F32)],
        compiler_params=params(),
        cost_estimate=cost(8 * channels / 1536),
        name="conv_back",
    )(ga, raw, taps)


def flips(size, by):
    return [(i, i ^ by) for i in range(size)]


def butterfly(values, axis):
    size = lax.axis_size(axis)
    by = 1
    while by < size:
        values = values + lax.ppermute(values, axis, flips(size, by))
        by *= 2
    return values


def at_rows(values, index, size):
    return lax.dynamic_slice_in_dim(values, index * size, size, axis=0)


def collect_dp(piece, dp):
    size = lax.axis_size("dp")
    rows = piece.shape[0]
    out = jnp.zeros((size * rows,) + piece.shape[1:], piece.dtype)
    out = lax.dynamic_update_slice_in_dim(out, piece, dp * rows, 0)
    for by in range(1, size):
        other = lax.ppermute(piece, "dp", flips(size, by))
        out = lax.dynamic_update_slice_in_dim(out, other, (dp ^ by) * rows, 0)
    return out


def reduce_dp(values, dp):
    size = lax.axis_size("dp")
    total = lax.dynamic_index_in_dim(values, dp, 0, keepdims=False)
    for by in range(1, size):
        piece = lax.dynamic_index_in_dim(values, dp ^ by, 0, keepdims=False).astype(BF)
        total = total + lax.ppermute(piece, "dp", flips(size, by)).astype(F32)
    return total


def swap_core(values):
    return lax.ppermute(values, "row", [(0, 1), (1, 0)])


def per_device(
    tokens, norm_gain, w_gate, w_value, w_state, w_step, conv_value, bias_value, conv_state,
    bias_state, a_log, d_skip, dt_bias, mix_gain, w_out, cotangent,
):
    cols, rows_n, dps = lax.axis_size("col"), lax.axis_size("row"), lax.axis_size("dp")
    col, row, dp = lax.axis_index("col"), lax.axis_index("row"), lax.axis_index("dp")
    group = cols // 2
    place = lax.rem(col, group)
    local, width = tokens.shape
    span = local * group
    half_width = width // 2
    shard = w_value.shape[1]
    channels = 2 * shard
    heads = a_log.shape[0]
    inner_channels = shard * cols
    state_all = w_state.shape[1] * cols
    mirror = [(i, cols - 1 - i) for i in range(cols)]
    forth = [(i, cols - 1 - i) for i in range(group)]
    back = [(cols - 1 - i, i) for i in range(group)]

    def ring(by):
        return [(i, (i // group) * group + (i % group + by) % group) for i in range(cols)]

    def mine_first(values, axis):
        a, b = jnp.split(values, 2, axis=axis)
        return jnp.where(row == 0, values, jnp.concatenate([b, a], axis=axis))

    def own_then_mirror(own, other):
        return jnp.concatenate([own, other], axis=0)

    tokens_p = mine_first(tokens, 1)
    cot_p = mine_first(cotangent, 1)
    gain_p = mine_first(norm_gain.astype(F32), 0)

    def gather_tokens(values, first_rows):
        out = jnp.zeros((first_rows + span, width), values.dtype)
        out = lax.dynamic_update_slice_in_dim(out, values, first_rows + place * local, 0)
        for by in range(1, group):
            other = lax.ppermute(values, "col", ring(by))
            at = lax.rem(place - by + group, group)
            out = lax.dynamic_update_slice_in_dim(out, other, first_rows + at * local, 0)
        return out

    group_tokens = gather_tokens(tokens_p, HALO)
    halo = sum(
        lax.ppermute(tokens_p[local - HALO :], "col", [(group - 1, group + j)]) for j in range(group)
    )
    group_tokens = lax.dynamic_update_slice_in_dim(group_tokens, halo, 0, 0)

    def import_shard(values):
        piece = values.shape[0] // dps
        return collect_dp(lax.ppermute(at_rows(values, dp, piece), "col", mirror), dp)

    mirror_value = import_shard(w_value)
    value_rows = jnp.concatenate([w_value, mirror_value], axis=1)
    value_other = swap_core(value_rows)
    small = jnp.concatenate([w_state, w_step], axis=1)
    small = lax.all_gather(lax.all_gather(small, "col", axis=0), "row", axis=1, tiled=True)
    small = mine_first(small, 1)
    state_width = w_state.shape[1]
    state_full = jnp.transpose(small[:, :, :state_width], (1, 0, 2)).reshape(width, state_all)
    step_own = lax.dynamic_index_in_dim(small, col, 0, keepdims=False)[:, state_width:]
    step_mirror = lax.dynamic_index_in_dim(small, cols - 1 - col, 0, keepdims=False)[:, state_width:]
    step_full = jnp.pad(
        jnp.concatenate([step_own, step_mirror], axis=1), ((0, 0), (0, 128 - 2 * heads))
    )
    value_full = jnp.concatenate([value_rows, value_other], axis=0)
    weights = jnp.concatenate([value_full, state_full], axis=1)
    gate_out = import_shard(jnp.concatenate([w_gate.reshape(dps, -1, shard), w_out.reshape(dps, -1, half_width)], axis=1).reshape(-1, shard)) if shard == half_width else None
    if gate_out is None:
        mirror_gate, mirror_out = import_shard(w_gate), import_shard(w_out)
    else:
        gate_out = gate_out.reshape(dps, 2, -1, shard)
        mirror_gate = gate_out[:, 0].reshape(half_width, shard)
        mirror_out = gate_out[:, 1].reshape(shard, half_width)
    gate_rows = jnp.concatenate([w_gate, mirror_gate], axis=1)
    gate_full = jnp.concatenate([gate_rows, swap_core(gate_rows)], axis=0)
    out_rows = jnp.concatenate([w_out, mirror_out], axis=0)
    out_full = jnp.concatenate([out_rows, swap_core(out_rows)], axis=1)

    def per_channel(own_taps, own_bias):
        taps = jnp.concatenate([own_taps.astype(F32).T, own_bias.astype(F32)[None]], axis=0)
        return jnp.pad(taps, ((0, 3), (0, 0)))

    packed = jnp.concatenate(
        [
            per_channel(conv_value, bias_value)[:5],
            mix_gain.astype(F32)[None],
            jnp.repeat(d_skip.astype(F32), HEAD)[None],
            jnp.pad(
                jnp.concatenate([a_log.astype(F32), dt_bias.astype(F32)]), (0, shard - 2 * heads)
            )[None],
        ],
        axis=0,
    )
    packed_both = jnp.concatenate([packed, lax.ppermute(packed, "col", mirror)], axis=1)
    state_vec = per_channel(conv_state, bias_state)
    state_vecs = jnp.zeros((8, state_all), F32)
    state_vecs = lax.dynamic_update_slice_in_dim(state_vecs, state_vec, col * state_width, 1)
    state_vecs = butterfly(state_vecs, "col")
    value_taps = jnp.concatenate([packed_both[:5], jnp.zeros((3, channels), F32)], axis=0)
    taps = jnp.concatenate([value_taps, state_vecs], axis=1)
    vectors = jnp.concatenate(
        [packed_both[6:7], packed_both[5:6], jnp.zeros((6, channels), F32)], axis=0
    )
    head_own, head_mirror = packed_both[7, :shard], packed_both[7, shard:]
    a_both = jnp.concatenate([head_own[:heads], head_mirror[:heads]])
    dt_both = jnp.concatenate([head_own[heads : 2 * heads], head_mirror[heads : 2 * heads]])
    rate = -jnp.exp(a_both)
    head_rows = jnp.zeros((8, 128), F32)
    head_rows = head_rows.at[0, : 2 * heads].set(dt_both).at[1, : 2 * heads].set(rate)
    head_of = lax.broadcasted_iota(jnp.int32, (128, channels), 1) // HEAD
    spread_one = (head_of == lax.broadcasted_iota(jnp.int32, (128, channels), 0)).astype(BF)
    spread = jnp.concatenate([spread_one, spread_one], axis=0)
    gather = (
        lax.broadcasted_iota(jnp.int32, (channels, 128), 0) // HEAD
        == lax.broadcasted_iota(jnp.int32, (channels, 128), 1)
    ).astype(BF)

    rows_float = group_tokens.astype(F32)
    inv_rms = lax.rsqrt(jnp.mean(rows_float * rows_float, axis=-1, keepdims=True) + EPSILON)
    normed = (rows_float * inv_rms * gain_p).astype(BF)
    raw, act, step_in, step, cum, grow, offs = project(normed, weights, taps, step_full, head_rows)
    states, final_state = scan_states(act, step, cum, spread, channels)

    def cross(values, pairs):
        moved = lax.ppermute(values, "col", pairs)
        return jnp.concatenate([moved[:, shard:], moved[:, :shard]], axis=1)

    early = cross(final_state, forth)
    y0 = scan_forward(act, step, cum, spread, states, channels)
    group_cot = gather_tokens(cot_p, 0)
    graw, y, gm, stats = gate_forward(
        normed, group_cot, gate_full, out_full, y0, act, early, grow, spread, vectors
    )
    by = 1
    while by < group:
        stats = stats + lax.ppermute(stats, "col", flips(cols, by))
        by *= 2
    stats_pad = jnp.pad(stats, ((0, 120), (0, 0)))
    mixed, grad_gate, dy, mix_sums = mix_backward(inner_channels, graw, y, gm, act, stats_pad, vectors)

    def scatter_rows(make):
        parts = []
        for by in range(1, group):
            part = make(lax.rem(place + by, group)).astype(BF)
            parts.append(lax.ppermute(part, "col", ring(by)))
        total = make(place)
        for part in parts:
            total = total + part.astype(F32)
        return total

    after, first_grad = scan_grad_states(dy, act, cum, spread)
    late = cross(first_grad, back)
    branch = scatter_rows(lambda at: mm(at_rows(mixed, at, local), out_full))
    block_out = mine_first((tokens_p.astype(F32) + branch).astype(BF), 1)

    tn = (((0,), (0,)), ((), ()))

    def weight_grad(left, right):
        return lax.dot_general(left, right, tn, preferred_element_type=F32)

    def reduce_weight(values):
        mine, other = jnp.split(values, 2, axis=0)
        kept = mine + swap_core(other)
        return reduce_dp(kept.reshape(dps, -1, values.shape[1]), dp)

    def settle(own, other):
        total = own + lax.ppermute(other.astype(BF), "col", mirror).astype(F32)
        return collect_dp(total, dp)

    grad_out = weight_grad(mixed, group_cot)
    out_mine, out_other = jnp.split(grad_out, 2, axis=1)
    out_kept = (out_mine + swap_core(out_other)).reshape(2, dps, -1, half_width)
    out_piece = reduce_dp(jnp.transpose(out_kept, (1, 0, 2, 3)), dp)
    sum_out = settle(out_piece[0], out_piece[1])

    gate_piece = reduce_weight(weight_grad(normed[HALO:], grad_gate))
    sum_gate = settle(gate_piece[:, :shard], gate_piece[:, shard:])

    gx, gbc_near = scan_backward_near(dy, act, step, cum, spread, states, early, offs)
    ga, grad_step, gbc, head_sums = scan_backward_far(
        dy, act, y, gx, step, cum, step_in, spread, gather, after, late, states, early, offs,
        head_rows, vectors, gbc_near,
    )
    state_part = state_all // group

    def state_slice(values, at):
        return lax.dynamic_slice_in_dim(values, at * state_part, state_part, axis=1)

    gbc_own = state_slice(gbc, place)
    for by in range(1, group):
        gbc_own = gbc_own + lax.ppermute(state_slice(gbc, lax.rem(place + by, group)), "col", ring(by))
    gv, value_sums = conv_back(ga, raw, taps)
    state_taps = state_slice(state_vecs, place)
    gs, state_sums = conv_back(gbc_own, state_slice(raw[:, channels:], place), state_taps)

    state_here = state_slice(state_full, place)
    nt = (((1,), (1,)), ((), ()))

    def back_dot(left, right):
        return lax.dot_general(left, right, nt, preferred_element_type=F32)

    grad_normed = back_dot(gv, value_full) + back_dot(gs, state_here)
    token_part = back_dot(grad_gate, gate_full) + back_dot(grad_step, step_full)
    grad_normed = grad_normed + jnp.pad(token_part, ((HALO, 0), (0, 0)))
    norm_part = jnp.sum(grad_normed * (rows_float * inv_rms), axis=0)
    halo_part = sum(
        lax.ppermute(grad_normed[:HALO].astype(BF), "col", [(group + j, group - 1)]).astype(F32)
        for j in range(group)
    )
    own_grad = scatter_rows(lambda at: at_rows(grad_normed[HALO:], at, local))
    own_grad = own_grad + jnp.pad(halo_part, ((local - HALO, 0), (0, 0)))

    joint = weight_grad(normed, jnp.concatenate([gv, gs], axis=1))
    joint_step = weight_grad(normed[HALO:], grad_step)
    value_piece = reduce_weight(jnp.concatenate([joint, joint_step], axis=1))
    state_piece = jnp.zeros((half_width // dps, state_all), F32)
    state_piece = lax.dynamic_update_slice_in_dim(
        state_piece, value_piece[:, channels : channels + state_part], place * state_part, 1
    )
    state_piece = lax.dynamic_slice_in_dim(
        butterfly(state_piece, "col"), col * state_width, state_width, axis=1
    )
    step_piece = value_piece[:, channels + state_part :]
    settled = jnp.concatenate([value_piece[:, :shard], step_piece[:, :heads]], axis=1)
    leaving = jnp.concatenate([value_piece[:, shard:channels], step_piece[:, heads : 2 * heads]], axis=1)
    settled = settled + lax.ppermute(leaving.astype(BF), "col", mirror).astype(F32)
    sum_joint = collect_dp(jnp.concatenate([settled, state_piece], axis=1), dp)
    sum_value = sum_joint[:, :shard]
    sum_step = sum_joint[:, shard : shard + heads]
    sum_state = sum_joint[:, shard + heads :]

    wide = jnp.concatenate([value_sums[:5], mix_sums[0:1]], axis=0)
    wide_all = jnp.zeros((6, inner_channels), F32)
    wide_all = lax.dynamic_update_slice_in_dim(wide_all, wide[:, :shard], col * shard, 1)
    wide_all = lax.dynamic_update_slice_in_dim(wide_all, wide[:, shard:], (cols - 1 - col) * shard, 1)
    state_wide = jnp.zeros((5, state_all), F32)
    state_wide = lax.dynamic_update_slice_in_dim(state_wide, state_sums[:5], place * state_part, 1)
    skip_heads = jnp.sum(mix_sums[1].reshape(2 * heads, HEAD), axis=1)
    head_parts = jnp.stack([head_sums[0, : 2 * heads] * rate, skip_heads, head_sums[1, : 2 * heads]])
    head_all = jnp.zeros((3, heads * cols), F32)
    head_all = lax.dynamic_update_slice_in_dim(head_all, head_parts[:, :heads], col * heads, 1)
    head_all = lax.dynamic_update_slice_in_dim(head_all, head_parts[:, heads:], (cols - 1 - col) * heads, 1)
    lengths = [wide_all.size, state_wide.size, head_all.size, width]
    flat = jnp.concatenate(
        [wide_all.reshape(-1), state_wide.reshape(-1), head_all.reshape(-1), mine_first(norm_part, 0)]
    )
    flat = jnp.pad(flat, (0, -flat.size % 1024)).reshape(-1, 128)
    for axis in ("row", "dp", "col"):
        flat = butterfly(flat, axis)
    flat = flat.reshape(-1)
    ends = [sum(lengths[: i + 1]) for i in range(4)]
    wide_all = flat[: ends[0]].reshape(6, inner_channels)
    state_wide = flat[ends[0] : ends[1]].reshape(5, state_all)
    head_all = flat[ends[1] : ends[2]].reshape(3, heads * cols)
    norm_total = flat[ends[2] : ends[3]]
    wide_own = lax.dynamic_slice_in_dim(wide_all, col * shard, shard, axis=1)
    state_own = lax.dynamic_slice_in_dim(state_wide, col * state_width, state_width, axis=1)
    head_own = lax.dynamic_slice_in_dim(head_all, col * heads, heads, axis=1)

    own_float = tokens_p.astype(F32)
    own_inv = lax.rsqrt(jnp.mean(own_float * own_float, axis=-1, keepdims=True) + EPSILON)
    unit = own_float * own_inv
    pulled = own_grad * gain_p
    tokens_grad = cot_p.astype(F32) + own_inv * (
        pulled - unit * jnp.mean(pulled * unit, axis=-1, keepdims=True)
    )
    tokens_grad = mine_first(tokens_grad, 1)
    return (
        block_out,
        tokens_grad,
        norm_total,
        sum_gate,
        sum_value,
        sum_state,
        sum_step,
        wide_own[:4].T,
        wide_own[4],
        state_own[:4].T,
        state_own[4],
        head_own[0],
        head_own[1],
        head_own[2],
        wide_own[5],
        sum_out,
    )


def solution(mesh):
    rows = P(("dp", "row", "col"), None)
    grid = P("row", "col")
    vec = P("col")
    taps = P("col", None)
    return jax.shard_map(
        per_device,
        mesh=mesh,
        in_specs=(
            rows, P(), grid, grid, grid, grid, taps, vec, taps, vec, vec, vec, vec, vec,
            P("col", "row"), rows,
        ),
        out_specs=(
            rows, rows, P(), grid, grid, grid, grid, taps, vec, taps, vec, vec, vec, vec, vec,
            P("col", "row"),
        ),
        check_vma=False,
    )
```

```python
from functools import partial

import jax
import jax.numpy as jnp
from jax import lax
from jax.experimental import pallas as pl
from jax.experimental.pallas import tpu as pltpu
from jax.sharding import PartitionSpec as P

BF = jnp.bfloat16
F32 = jnp.float32
EPSILON = 1e-05
N = 128
Q = 128
HEAD = 64
HALO = 16
TILE = 256
HIGHEST = lax.Precision.HIGHEST
VMEM_LIMIT = 56 * 2**20


def mm(a, b):
    return lax.dot_general(a, b, (((1,), (0,)), ((), ())), preferred_element_type=F32)


def mm_nt(a, b):
    return lax.dot_general(a, b, (((1,), (1,)), ((), ())), preferred_element_type=F32)


def mm_exact(a, b):
    return lax.dot_general(
        a, b, (((1,), (0,)), ((), ())), precision=HIGHEST, preferred_element_type=F32
    )


def split2(values):
    high = values.astype(BF)
    return high, (values - high.astype(F32)).astype(BF)


def sigmoid(values):
    return 1.0 / (1.0 + jnp.exp(-values))


def iota2(shape, axis):
    return lax.broadcasted_iota(jnp.int32, shape, axis)


def params(*names):
    return pltpu.CompilerParams(
        dimension_semantics=names or ("arbitrary",), vmem_limit_bytes=VMEM_LIMIT
    )


def cost(micros):
    return pl.CostEstimate(flops=0, bytes_accessed=int(micros * 3.0e6), transcendentals=0)


def whole(shape):
    return pl.BlockSpec(shape, lambda *_: (0,) * len(shape))


def columns(rows, width=TILE):
    return pl.BlockSpec((rows, width), lambda j: (0, j))


def sds(shape, dtype=F32):
    return jax.ShapeDtypeStruct(shape, dtype)


def here():
    return lax.axis_index("dp"), lax.axis_index("row"), lax.axis_index("col")


def lanes_at(index, size):
    return pl.ds(pl.multiple_of(index * size, 128), size)


def greet(others):
    barrier = pltpu.get_barrier_semaphore()
    for other in others:
        pl.semaphore_signal(barrier, inc=1, device_id=other, device_id_type=pl.DeviceIdType.MESH)
    pl.semaphore_wait(barrier, len(others))


def import_kernel(
    cols, dps, tok, wv, wg, wo, sw, tg, vf, gf, of, sf, zeros, tok_vm, w_vm, wo_vm, s_vm, local, send, recv
):
    dp, row, col = here()
    group = cols // 2
    place = lax.rem(col, group)
    half, shard = wv.shape
    count = tok.shape[0]
    piece, piece_out = half // dps, wo.shape[0] // dps
    sibling = (dp, 1 - row, col)
    mirror = (dp, row, cols - 1 - col)
    col_peer = lambda by: (dp, row, col ^ by)
    dp_peer = lambda by: (dp ^ by, row, col)
    greet(
        [sibling]
        + [col_peer(by) for by in range(1, cols)]
        + [dp_peer(by) for by in range(1, dps)]
    )
    used = [0]
    started = []

    def remote(src, dst, device):
        i = used[0]
        used[0] += 1
        return pltpu.make_async_remote_copy(
            src_ref=src, dst_ref=dst, send_sem=send.at[i], recv_sem=recv.at[i],
            device_id=device, device_id_type=pl.DeviceIdType.MESH,
        )

    def launch(src, dst, device):
        copy = remote(src, dst, device)
        copy.start()
        started.append(copy)
        return copy

    def keep(i, src, dst):
        copy = pltpu.make_async_copy(src, dst, local.at[i])
        copy.start()
        return copy

    my_rows = pl.ds(row * half, half)
    my_piece = pl.ds(row * half + dp * piece, piece)
    out_piece = pl.ds(shard + dp * piece_out, piece_out)
    my_lanes = lanes_at(row, half)
    own, other = pl.ds(0, shard), pl.ds(shard, shard)
    src_piece, src_out = pl.ds(dp * piece, piece), pl.ds(dp * piece_out, piece_out)

    staged = [
        keep(0, sw.at[src_piece, :], s_vm),
        keep(2, tok, tok_vm),
        keep(3, wv, w_vm.at[0]),
        keep(4, wg, w_vm.at[1]),
        keep(5, wo, wo_vm),
    ]
    s_cross = [
        launch(sw.at[src_piece, :], sf.at[my_piece, lanes_at(col, 128)], col_peer(by))
        for by in range(1, cols)
    ]
    v_cross = launch(wv.at[src_piece, :], vf.at[my_piece, other], mirror)
    my_tokens = tg.at[pl.ds(HALO + place * count, count), :]
    tok_cross = [launch(tok, my_tokens, col_peer(by)) for by in range(1, group)]
    halo_src = tok.at[pl.ds(count - HALO, HALO), :]
    halo_dst = tg.at[pl.ds(0, HALO), :]
    halo_at = used[0]
    used[0] += group
    halos = [
        pltpu.make_async_remote_copy(
            src_ref=halo_src, dst_ref=halo_dst, send_sem=send.at[halo_at + j], recv_sem=recv.at[halo_at],
            device_id=(dp, row, group + j), device_id_type=pl.DeviceIdType.MESH,
        )
        for j in range(group)
    ]

    @pl.when(col == group - 1)
    def _():
        for copy in halos:
            copy.start()

    zeros[...] = jnp.zeros_like(zeros)

    @pl.when(col < group)
    def _():
        clear = pltpu.make_async_copy(zeros, halo_dst, local.at[1])
        clear.start()
        clear.wait()

    v_own = launch(wv, vf.at[my_rows, own], sibling)
    g_own = launch(wg, gf.at[my_rows, own], sibling)
    o_own = launch(wo, of.at[own, my_lanes], sibling)
    for copy in staged:
        copy.wait()
    small_own = keep(0, s_vm, sf.at[my_piece, lanes_at(col, 128)])
    kept = [
        keep(2, tok_vm, my_tokens),
        keep(3, w_vm.at[0], vf.at[my_rows, own]),
        keep(4, w_vm.at[1], gf.at[my_rows, own]),
        keep(5, wo_vm, of.at[own, my_lanes]),
    ]

    def spread_out(ref):
        return [launch(ref, ref, dp_peer(by)) for by in range(1, dps)]

    def arrive(copies):
        for copy in copies:
            copy.wait_recv()

    arrive(s_cross)
    small_own.wait()
    s_dp = spread_out(sf.at[my_piece, :])
    arrive([v_cross])
    g_cross = launch(wg.at[src_piece, :], gf.at[my_piece, other], mirror)
    v_dp = spread_out(vf.at[my_piece, other])
    arrive([g_cross])
    o_cross = launch(wo.at[src_out, :], of.at[out_piece, my_lanes], mirror)
    g_dp = spread_out(gf.at[my_piece, other])
    arrive(s_dp)
    last = [launch(sf.at[my_rows, :], sf.at[my_rows, :], sibling)]
    arrive(v_dp)
    last += [launch(vf.at[my_rows, other], vf.at[my_rows, other], sibling)]
    arrive([o_cross])
    o_dp = spread_out(of.at[out_piece, my_lanes])
    arrive(g_dp)
    last += [launch(gf.at[my_rows, other], gf.at[my_rows, other], sibling)]
    arrive(o_dp)
    last += [launch(of.at[other, my_lanes], of.at[other, my_lanes], sibling)]
    arrive(last)
    arrive([v_own, g_own, o_own])
    arrive(tok_cross)

    @pl.when(col >= group)
    def _():
        halos[0].wait_recv()

    @pl.when(col == group - 1)
    def _():
        for copy in halos:
            copy.wait_send()

    for copy in kept:
        copy.wait()
    for copy in started:
        copy.wait_send()


def import_all(cols, dps, tokens, w_value, w_gate, w_out, small):
    half, shard = w_value.shape
    count, width = tokens.shape
    any_spec = pl.BlockSpec(memory_space=pl.ANY)
    copies = 3 + (cols - 1) + (cols // 2 - 1) + cols // 2 + 3 + 4 * (dps - 1) + 4
    return pl.pallas_call(
        partial(import_kernel, cols, dps),
        in_specs=[any_spec] * 5,
        out_specs=[any_spec] * 5,
        out_shape=[
            sds((HALO + count * (cols // 2), width), BF),
            sds((2 * half, 2 * shard), BF),
            sds((2 * half, 2 * shard), BF),
            sds((2 * shard, 2 * half), BF),
            sds((2 * half, cols * 128), BF),
        ],
        scratch_shapes=[
            pltpu.VMEM((HALO, width), BF),
            pltpu.VMEM((count, width), BF),
            pltpu.VMEM((2, half, shard), BF),
            pltpu.VMEM((shard, half), BF),
            pltpu.VMEM((half // dps, 128), BF),
            pltpu.SemaphoreType.DMA((6,)),
            pltpu.SemaphoreType.DMA((copies,)),
            pltpu.SemaphoreType.DMA((copies,)),
        ],
        compiler_params=pltpu.CompilerParams(
            collective_id=1, has_side_effects=True, vmem_limit_bytes=VMEM_LIMIT
        ),
        cost_estimate=cost(55),
        name="import_all",
    )(tokens, w_value, w_gate, w_out, small)


def conv_rows(raw_ref, taps, start, size):
    total = taps[4:5, :] + jnp.zeros((size, taps.shape[1]), F32)
    for k in range(4):
        total = total + taps[k : k + 1, :] * raw_ref[pl.ds(HALO - 3 + k + start, size), :]
    return total


def project_kernel(
    tok_ref, gain_ref, w_ref, small_ref, pick_ref, taps_ref, head_ref,
    raw_ref, act_ref, normed_ref, stepin_ref, step_ref, cum_ref, grow_ref, offs_ref, inv_ref, picked_ref,
):
    tokens = act_ref.shape[0]
    at_tile = pl.program_id(0)
    last = pl.num_programs(0) - 1

    @pl.when(at_tile == 0)
    def _():
        for at in [0] + list(range(HALO, HALO + tokens, Q)):
            size = HALO if at == 0 else Q
            values = tok_ref[at : at + size, :].astype(F32)
            inv = lax.rsqrt(jnp.mean(values * values, axis=-1, keepdims=True) + EPSILON)
            normed_ref[at : at + size, :] = (values * inv * gain_ref[0:1, :]).astype(BF)
            inv_ref[at : at + size, :] = jnp.broadcast_to(inv, (size, 128))

    @pl.when(at_tile < last)
    def _():
        raw_ref[...] = mm(normed_ref[...], w_ref[...])

    @pl.when(at_tile == last)
    def _():
        picked = mm(small_ref[...], pick_ref[...]).astype(BF)
        picked_ref[...] = picked
        raw_ref[...] = mm(normed_ref[...], picked[:, :TILE])
        step_in = mm(normed_ref[HALO:, :], picked[:, TILE:]) + head_ref[0:1, :]
        small = jnp.exp(-jnp.abs(step_in))
        plus = 1.0 + small
        safe = jnp.where(plus == 1.0, 1.0, plus - 1.0)
        log_part = jnp.where(plus == 1.0, small, jnp.log(plus) * (small / safe))
        step = jnp.maximum(step_in, 0.0) + log_part
        stepin_ref[...] = step_in
        step_ref[...] = step
        falls = step * head_ref[1:2, :]
        lower = (iota2((Q, Q), 0) >= iota2((Q, Q), 1)).astype(F32)
        before = jnp.zeros((1, 128), F32)
        offs_ref[...] = jnp.zeros_like(offs_ref)
        for b in range(tokens // Q):
            rows = slice(b * Q, b * Q + Q)
            cum = mm_exact(lower, falls[rows, :])
            cum_ref[rows, :] = cum
            high, low = split2(jnp.exp(cum + before))
            grow_ref[rows, 0:128] = high
            grow_ref[rows, 128:256] = low
            before = before + cum[Q - 1 : Q, :]
            offs_ref[b + 1 : b + 2, :] = before

    taps = taps_ref[...]
    for at in range(0, tokens, Q):
        pre = conv_rows(raw_ref, taps, at, Q)
        act_ref[at : at + Q, :] = (pre * sigmoid(pre)).astype(BF)


def project(group_tokens, gain, weights, small, pick, taps, head_rows):
    rows, width = group_tokens.shape
    tokens = rows - HALO
    total = weights.shape[1] + TILE
    last = weights.shape[1] // TILE - 1
    return pl.pallas_call(
        project_kernel,
        grid=(total // TILE,),
        in_specs=[
            whole((rows, width)),
            whole((1, width)),
            pl.BlockSpec((width, TILE), lambda j: (0, jnp.minimum(j, last))),
            whole(small.shape),
            whole(pick.shape),
            columns(8),
            whole((8, 128)),
        ],
        out_specs=[
            columns(rows),
            columns(tokens),
            whole((rows, width)),
            whole((tokens, 128)),
            whole((tokens, 128)),
            whole((tokens, 128)),
            whole((tokens, 256)),
            whole((16, 128)),
            whole((rows, 128)),
            whole((width, TILE + 128)),
        ],
        out_shape=[
            sds((rows, total)),
            sds((tokens, total), BF),
            sds((rows, width), BF),
            sds((tokens, 128)),
            sds((tokens, 128)),
            sds((tokens, 128)),
            sds((tokens, 256), BF),
            sds((16, 128)),
            sds((rows, 128)),
            sds((width, TILE + 128), BF),
        ],
        compiler_params=params(),
        cost_estimate=cost(14),
        name="project",
    )(group_tokens, gain, weights, small, pick, taps, head_rows)


def expand(per_head, spread):
    high, low = split2(per_head)
    return mm(jnp.concatenate([high, low], 1), spread)


def transpose_bf(values):
    return values.astype(F32).T.astype(BF)


def states_kernel(x_ref, b_ref, step_ref, cum_ref, spread_ref, states_ref, final_ref, held):
    at = pl.program_id(0)
    last = pl.num_programs(0) - 1

    @pl.when(at == 0)
    def _():
        held[...] = jnp.zeros_like(held)

    states_ref[0] = held[...]

    @pl.when(at == last)
    def _():
        final_ref[...] = held[...]

    @pl.when(at < last)
    def _():
        cum = cum_ref[...]
        end = cum[Q - 1 : Q, :]
        tail = jnp.exp(end - cum) * step_ref[...]
        fall = jnp.broadcast_to(jnp.exp(end), (8, 128))
        b_t = transpose_bf(b_ref[...])
        b_t2 = jnp.concatenate([b_t, b_t], 1)
        for start in range(0, x_ref.shape[1], TILE):
            lanes = slice(start, start + TILE)
            spread = spread_ref[:, lanes]
            scaled = expand(tail, spread) * x_ref[:, lanes].astype(F32)
            high, low = split2(scaled)
            fresh = mm(b_t2, jnp.concatenate([high, low], 0))
            held[:, lanes] = held[:, lanes] * expand(fall, spread)[0:1, :] + fresh


def scan_states(act, step, cum, spread, channels):
    blocks = act.shape[0] // Q
    clamp = lambda i: jnp.minimum(i, blocks - 1)
    return pl.pallas_call(
        states_kernel,
        grid=(blocks + 1,),
        in_specs=[
            pl.BlockSpec((Q, channels), lambda i: (clamp(i), 0)),
            pl.BlockSpec((Q, N), lambda i: (clamp(i), channels // N)),
            pl.BlockSpec((Q, 128), lambda i: (clamp(i), 0)),
            pl.BlockSpec((Q, 128), lambda i: (clamp(i), 0)),
            whole((256, channels)),
        ],
        out_specs=[
            pl.BlockSpec((1, N, channels), lambda i: (i, 0, 0)),
            whole((N, channels)),
        ],
        out_shape=[sds((blocks + 1, N, channels)), sds((N, channels))],
        scratch_shapes=[pltpu.VMEM((N, channels), F32)],
        compiler_params=params(),
        cost_estimate=cost(6),
        name="scan_states",
    )(act, act, step, cum, spread)


def forward_kernel(x_ref, b_ref, c_ref, step_ref, cum_ref, spread_ref, state_ref, y_ref):
    b_blk, c_blk = b_ref[...], c_ref[...]
    affinity = mm_nt(c_blk, b_blk)
    causal = iota2((Q, Q), 0) >= iota2((Q, Q), 1)
    first = iota2((Q, 128), 1) < HEAD
    cum = cum_ref[...]
    cum_t = cum.T
    step_t = step_ref[...].T
    growth = jnp.exp(cum)
    c2 = jnp.concatenate([c_blk, c_blk], 1)
    zero = jnp.zeros((Q, 128), BF)
    for start in range(0, x_ref.shape[1], TILE):
        lanes = slice(start, start + TILE)
        s_high, s_low = split2(state_ref[0, :, lanes])
        reached = mm(c2, jnp.concatenate([s_high, s_low], 0)) * expand(growth, spread_ref[:, lanes])
        for pair in range(2):
            at = start + pair * 128
            x_pair = x_ref[:, at : at + 128]
            x0, x1 = jnp.where(first, x_pair, zero), jnp.where(first, zero, x_pair)
            pieces = []
            for half in range(2):
                h = at // HEAD + half
                spread_h = cum[:, h : h + 1] - cum_t[h : h + 1, :]
                decay = jnp.exp(jnp.where(causal, spread_h, -1e30))
                mixing = affinity * decay * step_t[h : h + 1, :]
                pieces += split2(mixing)
            intra = mm(jnp.concatenate(pieces, 1), jnp.concatenate([x0, x0, x1, x1], 0))
            y_ref[:, at : at + 128] = intra + reached[:, pair * 128 : pair * 128 + 128]


def scan_forward(act, step, cum, spread, states, channels):
    tokens = act.shape[0]
    return pl.pallas_call(
        forward_kernel,
        grid=(tokens // Q,),
        in_specs=[
            pl.BlockSpec((Q, channels), lambda i: (i, 0)),
            pl.BlockSpec((Q, N), lambda i: (i, channels // N)),
            pl.BlockSpec((Q, N), lambda i: (i, channels // N + 1)),
            pl.BlockSpec((Q, 128), lambda i: (i, 0)),
            pl.BlockSpec((Q, 128), lambda i: (i, 0)),
            whole((256, channels)),
            pl.BlockSpec((1, N, channels), lambda i: (i, 0, 0)),
        ],
        out_specs=pl.BlockSpec((Q, channels), lambda i: (i, 0)),
        out_shape=sds((tokens, channels)),
        compiler_params=params(),
        cost_estimate=cost(13),
        name="scan_forward",
    )(act, act, act, step, cum, spread, states)


def grad_states_kernel(dy_ref, c_ref, cum_ref, spread_ref, after_ref, first_ref, held):
    at = pl.program_id(0)

    @pl.when(at == 0)
    def _():
        held[...] = jnp.zeros_like(held)

    after_ref[0] = held[...]
    cum = cum_ref[...]
    growth = jnp.exp(cum)
    fall = jnp.broadcast_to(growth[Q - 1 : Q, :], (8, 128))
    c_t = transpose_bf(c_ref[...])
    c_t2 = jnp.concatenate([c_t, c_t], 1)
    for start in range(0, dy_ref.shape[1], TILE):
        lanes = slice(start, start + TILE)
        spread = spread_ref[:, lanes]
        high, low = split2(dy_ref[:, lanes] * expand(growth, spread))
        direct = mm(c_t2, jnp.concatenate([high, low], 0))
        held[:, lanes] = held[:, lanes] * expand(fall, spread)[0:1, :] + direct
    first_ref[...] = held[...]


def scan_grad_states(dy, act, cum, spread):
    tokens, channels = dy.shape
    blocks = tokens // Q
    return pl.pallas_call(
        grad_states_kernel,
        grid=(blocks,),
        in_specs=[
            pl.BlockSpec((Q, channels), lambda i: (blocks - 1 - i, 0)),
            pl.BlockSpec((Q, N), lambda i: (blocks - 1 - i, channels // N + 1)),
            pl.BlockSpec((Q, 128), lambda i: (blocks - 1 - i, 0)),
            whole((256, channels)),
        ],
        out_specs=[
            pl.BlockSpec((1, N, channels), lambda i: (blocks - 1 - i, 0, 0)),
            whole((N, channels)),
        ],
        out_shape=[sds((blocks, N, channels)), sds((N, channels))],
        scratch_shapes=[pltpu.VMEM((N, channels), F32)],
        compiler_params=params(),
        cost_estimate=cost(6),
        name="scan_grad_states",
    )(dy, act, cum, spread)


def backward_near_kernel(
    dy_ref, x_ref, b_ref, c_ref, step_ref, cum_ref, spread_ref, state_ref, early_ref, offs_ref,
    gx_ref, gbc_ref,
):
    at_block = pl.program_id(0)
    b_blk, c_blk = b_ref[...], c_ref[...]
    affinity_t = mm_nt(b_blk, c_blk)
    causal_t = iota2((Q, Q), 1) >= iota2((Q, Q), 0)
    first = iota2((Q, 128), 1) < HEAD
    cum = cum_ref[...]
    cum_t = cum.T
    step = step_ref[...]
    growth = jnp.exp(cum)
    early_fall = jnp.broadcast_to(jnp.exp(offs_ref[pl.ds(at_block, 1), :]), (8, 128))
    zero = jnp.zeros((Q, 128), BF)
    grad_affinity_t = jnp.zeros((Q, Q), F32)
    grad_c = jnp.zeros((Q, N), F32)
    for start in range(0, x_ref.shape[1], TILE):
        lanes = slice(start, start + TILE)
        spread = spread_ref[:, lanes]
        before = state_ref[0, :, lanes] + expand(early_fall, spread)[0:1, :] * early_ref[:, lanes]
        dy_quad = dy_ref[:, lanes]
        s_high, s_low = split2(before)
        g_high, g_low = split2(dy_quad * expand(growth, spread))
        grad_c = grad_c + mm_nt(
            jnp.concatenate([g_high, g_low, g_high], 1), jnp.concatenate([s_high, s_high, s_low], 1)
        )
        for pair in range(2):
            at = start + pair * 128
            d_high, d_low = split2(dy_quad[:, pair * 128 : pair * 128 + 128])
            x_pair = x_ref[:, at : at + 128]
            x0, x1 = jnp.where(first, x_pair, zero), jnp.where(first, zero, x_pair)
            grad_mixing = mm_nt(
                jnp.concatenate([jnp.concatenate([x0, x0], 1), jnp.concatenate([x1, x1], 1)], 0),
                jnp.concatenate([d_high, d_low], 1),
            )
            left, right = [], []
            for half in range(2):
                h = at // HEAD + half
                spread_h = cum_t[h : h + 1, :] - cum[:, h : h + 1]
                decay = jnp.exp(jnp.where(causal_t, spread_h, -1e30))
                m_high, m_low = split2(affinity_t * decay)
                grad_affinity_t = grad_affinity_t + (
                    grad_mixing[half * Q : half * Q + Q, :] * decay * step[:, h : h + 1]
                )
                keep = first if half == 0 else jnp.logical_not(first)
                dh, dl = jnp.where(keep, d_high, zero), jnp.where(keep, d_low, zero)
                left += [m_high, m_low, m_high]
                right += [dh, dh, dl]
            gx_ref[:, at : at + 128] = mm(jnp.concatenate(left, 1), jnp.concatenate(right, 0))
    a_high, a_low = split2(grad_affinity_t)
    gbc_ref[:, 0:N] = mm(jnp.concatenate([a_high, a_low], 1), jnp.concatenate([c_blk, c_blk], 0))
    t_high, t_low = split2(grad_affinity_t.T)
    gbc_ref[:, N : 2 * N] = grad_c + mm(
        jnp.concatenate([t_high, t_low], 1), jnp.concatenate([b_blk, b_blk], 0)
    )


def scan_backward_near(dy, act, step, cum, spread, states, early, offs):
    tokens, channels = dy.shape
    rows = pl.BlockSpec((Q, channels), lambda i: (i, 0))
    return pl.pallas_call(
        backward_near_kernel,
        grid=(tokens // Q,),
        in_specs=[
            rows,
            rows,
            pl.BlockSpec((Q, N), lambda i: (i, channels // N)),
            pl.BlockSpec((Q, N), lambda i: (i, channels // N + 1)),
            pl.BlockSpec((Q, 128), lambda i: (i, 0)),
            pl.BlockSpec((Q, 128), lambda i: (i, 0)),
            whole((256, channels)),
            pl.BlockSpec((1, N, channels), lambda i: (i, 0, 0)),
            whole((N, channels)),
            whole((16, 128)),
        ],
        out_specs=[rows, pl.BlockSpec((Q, 2 * N), lambda i: (i, 0))],
        out_shape=[sds((tokens, channels)), sds((tokens, 2 * N))],
        compiler_params=params(),
        cost_estimate=cost(20),
        name="scan_backward_near",
    )(dy, act, act, act, step, cum, spread, states, early, offs)


def backward_far_kernel(
    dy_ref, x_ref, y_ref, gx_ref, b_ref, step_ref, cum_ref, stepin_ref, spread_ref, gather_ref,
    after_ref, late_ref, state_ref, early_ref, offs_ref, head_ref, skip_ref, gbc_ref,
    ga_ref, gstep_ref, gbc_out_ref, sums_ref,
):
    blocks = pl.num_programs(0)
    at_block = pl.program_id(0)

    @pl.when(at_block == 0)
    def _():
        sums_ref[...] = jnp.zeros_like(sums_ref)

    b_blk = b_ref[...]
    b2 = jnp.concatenate([b_blk, b_blk], 1)
    cum, step = cum_ref[...], step_ref[...]
    tail = jnp.exp(cum[Q - 1 : Q, :] - cum)
    tail_step = tail * step
    offs_after = offs_ref[pl.ds(at_block + 1, 1), :]
    offs_end = offs_ref[pl.ds(blocks, 1), :]
    late_fall = jnp.broadcast_to(jnp.exp(offs_end - offs_after), (8, 128))
    early_fall = jnp.broadcast_to(jnp.exp(offs_after), (8, 128))
    row_dots = jnp.zeros((Q, 128), F32)
    col_dots = jnp.zeros((Q, 128), F32)
    last_add = jnp.zeros((8, 128), F32)
    grad_b = gbc_ref[:, 0:N]
    for start in range(0, x_ref.shape[1], TILE):
        lanes = slice(start, start + TILE)
        spread = spread_ref[:, lanes]
        gather = gather_ref[lanes, :]
        gather2 = jnp.concatenate([gather, gather], 0)
        x_quad = x_ref[:, lanes].astype(F32)
        dy_quad = dy_ref[:, lanes]
        skip = skip_ref[0:1, lanes]
        d_state = after_ref[0, :, lanes] + expand(late_fall, spread)[0:1, :] * late_ref[:, lanes]
        state = state_ref[0, :, lanes] + expand(early_fall, spread)[0:1, :] * early_ref[:, lanes]
        touch = jnp.broadcast_to(jnp.sum(d_state * state, axis=0, keepdims=True), (8, TILE))
        t_high, t_low = split2(touch)
        last_add = last_add + mm(jnp.concatenate([t_high, t_low], 1), gather2)
        s_high, s_low = split2(d_state)
        gx = gx_ref[:, lanes] + expand(tail, spread) * mm(b2, jnp.concatenate([s_high, s_low], 0))
        w_high, w_low = split2(expand(tail_step, spread) * x_quad)
        grad_b = grad_b + mm_nt(
            jnp.concatenate([w_high, w_low, w_high], 1), jnp.concatenate([s_high, s_high, s_low], 1)
        )
        p_high, p_low = split2(dy_quad * (y_ref[:, lanes] - skip * x_quad))
        row_dots = row_dots + mm(jnp.concatenate([p_high, p_low], 1), gather2)
        r_high, r_low = split2(x_quad * gx)
        col_dots = col_dots + mm(jnp.concatenate([r_high, r_low], 1), gather2)
        ga_ref[:, lanes] = expand(step, spread) * gx + skip * dy_quad
    last_row = iota2((Q, 128), 0) == Q - 1
    grad_cum = row_dots - step * col_dots + jnp.where(last_row, last_add[0:1, :], 0.0)
    upper = (iota2((Q, Q), 1) >= iota2((Q, Q), 0)).astype(F32)
    grad_rate = mm_exact(upper, grad_cum)
    grad_step = col_dots + grad_rate * head_ref[1:2, :]
    grad_raw = grad_step * sigmoid(stepin_ref[...])
    gstep_ref[...] = grad_raw.astype(BF)
    sums_ref[0:1, :] += jnp.sum(grad_rate * step, axis=0, keepdims=True)
    sums_ref[1:2, :] += jnp.sum(grad_raw, axis=0, keepdims=True)
    gbc_out_ref[:, 0:N] = grad_b
    gbc_out_ref[:, N : 2 * N] = gbc_ref[:, N : 2 * N]


def scan_backward_far(
    dy, act, y, gx, step, cum, step_in, spread, gather, after, late, states, early, offs, head_rows, skip, gbc
):
    tokens, channels = dy.shape
    rows = pl.BlockSpec((Q, channels), lambda i: (i, 0))
    heads = pl.BlockSpec((Q, 128), lambda i: (i, 0))
    pairs = pl.BlockSpec((Q, 2 * N), lambda i: (i, 0))
    return pl.pallas_call(
        backward_far_kernel,
        grid=(tokens // Q,),
        in_specs=[
            rows,
            rows,
            rows,
            rows,
            pl.BlockSpec((Q, N), lambda i: (i, channels // N)),
            heads,
            heads,
            heads,
            whole((256, channels)),
            whole((channels, 128)),
            pl.BlockSpec((1, N, channels), lambda i: (i, 0, 0)),
            whole((N, channels)),
            pl.BlockSpec((1, N, channels), lambda i: (i + 1, 0, 0)),
            whole((N, channels)),
            whole((16, 128)),
            whole((8, 128)),
            whole((8, channels)),
            pairs,
        ],
        out_specs=[rows, heads, pairs, whole((8, 128))],
        out_shape=[
            sds((tokens, channels)),
            sds((tokens, 128), BF),
            sds((tokens, 2 * N)),
            sds((8, 128)),
        ],
        compiler_params=params(),
        cost_estimate=cost(14),
        name="scan_backward_far",
    )(dy, act, y, gx, act, step, cum, step_in, spread, gather, after, late, states, early, offs, head_rows, skip, gbc)


def gate_kernel(
    normed_ref, cot_ref, wg_ref, wo_ref, y0_ref, x_ref, early_ref, c_ref, grow_ref, spread_ref, vec_ref,
    graw_ref, y_ref, gm_ref, stats_ref, squares, inners,
):
    at = pl.program_id(0)
    tokens = cot_ref.shape[0]

    @pl.when(at == 0)
    def _():
        squares[...] = jnp.zeros_like(squares)
        inners[...] = jnp.zeros_like(inners)

    graw_ref[...] = mm(normed_ref[HALO:, :], wg_ref[...])
    gm_ref[...] = mm_nt(cot_ref[...], wo_ref[...])
    s_high, s_low = split2(early_ref[...])
    s2 = jnp.concatenate([s_high, s_low], 0)
    spread = spread_ref[...]
    skip, gain = vec_ref[0:1, :], vec_ref[1:2, :]
    for row in range(0, tokens, Q):
        rows = slice(row, row + Q)
        c_blk = c_ref[rows, :]
        carried = mm(jnp.concatenate([c_blk, c_blk], 1), s2) * mm(grow_ref[rows, :], spread)
        y = y0_ref[rows, :] + carried + skip * x_ref[rows, :].astype(F32)
        y_ref[rows, :] = y
        raw = graw_ref[rows, :]
        gated = y * raw * sigmoid(raw)
        square = gated * gated
        inner = gm_ref[rows, :] * gain * gated
        squares[rows, :] += square[:, 0:128] + square[:, 128:256]
        inners[rows, :] += inner[:, 0:128] + inner[:, 128:256]

    @pl.when(at == pl.num_programs(0) - 1)
    def _():
        ones = jnp.ones((8, 128), F32)
        nt = (((1,), (1,)), ((), ()))
        square_row = lax.dot_general(ones, squares[...], nt, precision=HIGHEST, preferred_element_type=F32)
        inner_row = lax.dot_general(ones, inners[...], nt, precision=HIGHEST, preferred_element_type=F32)
        stats_ref[...] = jnp.where(iota2(square_row.shape, 0) == 0, square_row, inner_row)


def gate_forward(normed, cot, w_gate, w_out, y0, act, early, grow, spread, vectors):
    rows, width = normed.shape
    tokens, channels = y0.shape
    return pl.pallas_call(
        gate_kernel,
        grid=(channels // TILE,),
        in_specs=[
            whole((rows, width)),
            whole((tokens, width)),
            columns(width),
            pl.BlockSpec((TILE, width), lambda j: (j, 0)),
            columns(tokens),
            columns(tokens),
            columns(N),
            pl.BlockSpec((tokens, N), lambda j: (0, channels // N + 1)),
            whole((tokens, 256)),
            columns(256),
            columns(8),
        ],
        out_specs=[columns(tokens), columns(tokens), columns(tokens), whole((8, tokens))],
        out_shape=[sds((tokens, channels))] * 3 + [sds((8, tokens))],
        scratch_shapes=[pltpu.VMEM((tokens, 128), F32), pltpu.VMEM((tokens, 128), F32)],
        compiler_params=params(),
        cost_estimate=cost(16),
        name="gate_forward",
    )(normed, cot, w_gate, w_out, y0, act, early, act, grow, spread, vectors)


def mix_kernel(
    inner_channels, graw_ref, y_ref, gm_ref, x_ref, stats_ref, vec_ref,
    mixed_ref, gg_ref, dy_ref, sums_ref, stats_col,
):
    tokens = y_ref.shape[0]

    @pl.when(pl.program_id(0) == 0)
    def _():
        stats_col[...] = stats_ref[...].T

    gain = vec_ref[1:2, :]
    gain_sum = jnp.zeros((1, TILE), F32)
    skip_sum = jnp.zeros((1, TILE), F32)
    for row in range(0, tokens, Q):
        rows = slice(row, row + Q)
        inv = lax.rsqrt(stats_col[rows, 0:1] * (1.0 / inner_channels) + EPSILON)
        pull = inv * inv * inv * (stats_col[rows, 1:2] * (1.0 / inner_channels))
        raw = graw_ref[rows, :]
        y = y_ref[rows, :]
        gm = gm_ref[rows, :]
        sig = sigmoid(raw)
        act = raw * sig
        gated = y * act
        unit = gated * inv
        mixed_ref[rows, :] = (unit * gain).astype(BF)
        gain_sum = gain_sum + jnp.sum(gm * unit, axis=0, keepdims=True)
        grad_gated = inv * (gm * gain) - gated * pull
        dy = grad_gated * act
        dy_ref[rows, :] = dy
        gg_ref[rows, :] = (grad_gated * y * (sig * (1.0 + raw * (1.0 - sig)))).astype(BF)
        skip_sum = skip_sum + jnp.sum(dy * x_ref[rows, :].astype(F32), axis=0, keepdims=True)
    sums_ref[...] = jnp.zeros_like(sums_ref)
    sums_ref[0:1, :] = gain_sum
    sums_ref[1:2, :] = skip_sum


def mix_backward(inner_channels, graw, y, gm, act, stats, vectors):
    tokens, channels = y.shape
    return pl.pallas_call(
        partial(mix_kernel, inner_channels),
        grid=(channels // TILE,),
        in_specs=[columns(tokens)] * 4 + [whole((128, tokens)), columns(8)],
        out_specs=[columns(tokens)] * 3 + [columns(8)],
        out_shape=[
            sds((tokens, channels), BF),
            sds((tokens, channels), BF),
            sds((tokens, channels)),
            sds((8, channels)),
        ],
        scratch_shapes=[pltpu.VMEM((tokens, 128), F32)],
        compiler_params=params(),
        cost_estimate=cost(10),
        name="mix_backward",
    )(graw, y, gm, act, stats, vectors)


def conv_back_kernel(ga_ref, raw_ref, taps_ref, gv_ref, sums_ref, g_pad):
    tokens, width = ga_ref.shape
    taps = taps_ref[...]
    g_pad[0:HALO, :] = jnp.zeros((HALO, width), F32)
    g_pad[HALO + tokens :, :] = jnp.zeros((HALO, width), F32)
    sums = [jnp.zeros((1, width), F32)] * 5
    for row in range(0, tokens, Q):
        pre = conv_rows(raw_ref, taps, row, Q)
        sig = sigmoid(pre)
        g = ga_ref[row : row + Q, :] * (sig * (1.0 + pre * (1.0 - sig)))
        g_pad[HALO + row : HALO + row + Q, :] = g
        for k in range(4):
            moved = raw_ref[pl.ds(HALO - 3 + k + row, Q), :]
            sums[k] = sums[k] + jnp.sum(g * moved, axis=0, keepdims=True)
        sums[4] = sums[4] + jnp.sum(g, axis=0, keepdims=True)
    for row in list(range(HALO, HALO + tokens, Q)) + [0]:
        size = HALO if row == 0 else Q
        total = jnp.zeros((size, width), F32)
        for k in range(4):
            total = total + taps[k : k + 1, :] * g_pad[pl.ds(row + 3 - k, size), :]
        gv_ref[row : row + size, :] = total.astype(BF)
    sums_ref[...] = jnp.zeros_like(sums_ref)
    for k in range(5):
        sums_ref[k : k + 1, :] = sums[k]


def conv_back(ga, raw, taps):
    tokens, channels = ga.shape
    width = min(channels, TILE)
    return pl.pallas_call(
        conv_back_kernel,
        grid=(channels // width,),
        in_specs=[columns(tokens, width), columns(tokens + HALO, width), columns(8, width)],
        out_specs=[columns(tokens + HALO, width), columns(8, width)],
        out_shape=[sds((tokens + HALO, channels), BF), sds((8, channels))],
        scratch_shapes=[pltpu.VMEM((tokens + 2 * HALO, width), F32)],
        compiler_params=params(),
        cost_estimate=cost(8 * channels / 1536),
        name="conv_back",
    )(ga, raw, taps)


def mm_tn(a, b):
    return lax.dot_general(a, b, (((0,), (0,)), ((), ())), preferred_element_type=F32)


def weight_grad_kernel(skips, widths, left_ref, *refs):
    rights, out_ref = refs[:-1], refs[-1]
    rows = left_ref.shape[0]
    at = 0
    for skip, width, right in zip(skips, widths, rights):
        out_ref[:, at : at + width] = mm_tn(left_ref[skip:rows, :], right[...])
        at += width


def weight_grad(left, rights):
    rows, height = left.shape
    widths = [right.shape[1] for right in rights]
    skips = [rows - right.shape[0] for right in rights]
    return pl.pallas_call(
        partial(weight_grad_kernel, skips, widths),
        grid=(height // TILE,),
        in_specs=[columns(rows)] + [whole(right.shape) for right in rights],
        out_specs=pl.BlockSpec((TILE, sum(widths)), lambda j: (j, 0)),
        out_shape=sds((height, sum(widths))),
        compiler_params=params(),
        cost_estimate=cost(7),
        name="weight_grad",
    )(left, *rights)


def input_grad_kernel(
    gv_ref, gg_ref, gs_ref, gt_ref, v_ref, g_ref, s_ref, t_ref, tok_ref, inv_ref, out_ref, low_ref, sums_ref
):
    rows = gv_ref.shape[0]
    total = mm_nt(gv_ref[...], v_ref[...]) + mm_nt(gs_ref[...], s_ref[...])
    inner = mm_nt(gg_ref[...], g_ref[...]) + mm_nt(gt_ref[...], t_ref[...])
    out_ref[0:HALO, :] = total[0:HALO, :]
    out_ref[HALO:, :] = total[HALO:, :] + inner
    sums = jnp.zeros((1, TILE), F32)
    for at in [0] + list(range(HALO, rows, Q)):
        size = HALO if at == 0 else Q
        part = out_ref[at : at + size, :]
        low_ref[at : at + size, :] = part.astype(BF)
        unit = tok_ref[at : at + size, :].astype(F32) * inv_ref[at : at + size, 0:1]
        sums = sums + jnp.sum(part * unit, axis=0, keepdims=True)
    sums_ref[...] = jnp.broadcast_to(sums, (8, TILE))


def input_grad(gv, gg, gs, gt, w_value, w_gate, w_state, w_step, tokens, inv_rms):
    rows, channels = gv.shape
    width = tokens.shape[1]
    weight = lambda k: pl.BlockSpec((TILE, k), lambda j: (j, 0))
    return pl.pallas_call(
        input_grad_kernel,
        grid=(width // TILE,),
        in_specs=[
            whole(gv.shape), whole(gg.shape), whole(gs.shape), whole(gt.shape),
            weight(channels), weight(channels), weight(gs.shape[1]), weight(128),
            columns(rows), whole(inv_rms.shape),
        ],
        out_specs=[columns(rows), columns(rows), columns(8)],
        out_shape=[sds((rows, width)), sds((rows, width), BF), sds((8, width))],
        compiler_params=params(),
        cost_estimate=cost(12),
        name="input_grad",
    )(gv, gg, gs, gt, w_value, w_gate, w_state, w_step, tokens, inv_rms)


def settle_kernel(
    cols, dps, heads, gn, gnb, joint, flat, tok, cot, gain,
    tg_out, v_out, ext_out, flat_out,
    mine_a, land_a, mine_b, land_b, send_a, rec_a, send_b, rec_b, tot_a, tot_b,
    z_send, z_land, step_land, state_land, ext, acc, flat_land,
    gn_own, gn_land, halo_land, tok_vm, cot_vm, gain_vm, local, send, recv,
):
    dp, row, col = here()
    group = cols // 2
    place = lax.rem(col, group)
    half, wide_a = mine_a.shape
    shard = mine_b.shape[1]
    piece = tot_a.shape[0]
    count, width = gn_own.shape
    sibling = (dp, 1 - row, col)
    mirror = (dp, row, cols - 1 - col)
    col_peer = lambda by: (dp, row, col ^ by)
    dp_peer = lambda by: (dp ^ by, row, col)
    used = [0]
    started = []

    def remote(src, dst, device):
        i = used[0]
        used[0] += 1
        return pltpu.make_async_remote_copy(
            src_ref=src, dst_ref=dst, send_sem=send.at[i], recv_sem=recv.at[i],
            device_id=device, device_id_type=pl.DeviceIdType.MESH,
        )

    def launch(src, dst, device):
        copy = remote(src, dst, device)
        copy.start()
        started.append(copy)
        return copy

    def arrive(copies):
        for copy in copies:
            copy.wait_recv()

    kept = [0]

    def keep(src, dst):
        copy = pltpu.make_async_copy(src, dst, local.at[kept[0]])
        kept[0] += 1
        copy.start()
        return copy

    part_a, part_b = pl.ds(shard, wide_a), pl.ds(0, shard)
    my_rows, other_rows = pl.ds(row * half, half), pl.ds((1 - row) * half, half)
    load_a = keep(joint.at[my_rows, part_a], mine_a)
    load_b = keep(joint.at[my_rows, part_b], mine_b)
    load_flat = keep(flat, acc)
    loads = [
        keep(gn.at[pl.ds(HALO + place * count, count), :], gn_own),
        keep(tok, tok_vm),
        keep(cot, cot_vm),
        keep(gain, gain_vm),
    ]
    greet(
        [sibling]
        + [col_peer(by) for by in range(1, cols)]
        + [dp_peer(by) for by in range(1, dps)]
    )
    core_a = launch(joint.at[other_rows, part_a], land_a, sibling)
    core_b = launch(joint.at[other_rows, part_b], land_b, sibling)
    gn_moves = [
        launch(gnb.at[pl.ds(HALO + (place ^ by) * count, count), :], gn_land.at[by - 1], col_peer(by))
        for by in range(1, group)
    ]
    halo_at = used[0]
    used[0] += group
    halos = [
        pltpu.make_async_remote_copy(
            src_ref=gnb.at[pl.ds(0, HALO), :], dst_ref=halo_land.at[j], send_sem=send.at[halo_at + j],
            recv_sem=recv.at[halo_at + j], device_id=(dp, row, group - 1),
            device_id_type=pl.DeviceIdType.MESH,
        )
        for j in range(group)
    ]
    for j in range(group):
        pl.when(col == group + j)(halos[j].start)

    flat_steps = [sibling]
    by = 1
    while by < dps:
        flat_steps.append(dp_peer(by))
        by *= 2
    by = 1
    while by < cols:
        flat_steps.append(col_peer(by))
        by *= 2
    flat_moves = []
    flat_taken = [0]

    def flat_next():
        if flat_taken[0] < len(flat_moves):
            flat_moves[-1].wait_recv()
            flat_moves[-1].wait_send()
            acc[...] += flat_land[flat_taken[0]]
            flat_taken[0] += 1
        if len(flat_moves) < len(flat_steps):
            at = len(flat_moves)
            move = remote(acc, flat_land.at[at], flat_steps[at])
            move.start()
            flat_moves.append(move)

    load_flat.wait()
    flat_next()

    def hand_out(load, core, mine, land, total, sends, recs):
        load.wait()
        arrive([core])
        moves = []
        for by in range(1, dps):
            rows = pl.ds(pl.multiple_of((dp ^ by) * piece, 16), piece)
            sends[by - 1] = (mine[rows, :] + land[rows, :]).astype(BF)
            moves.append(launch(sends.at[by - 1], recs.at[by - 1], dp_peer(by)))
        rows = pl.ds(pl.multiple_of(dp * piece, 16), piece)
        total[...] = mine[rows, :] + land[rows, :]
        return moves

    moves_a = hand_out(load_a, core_a, mine_a, land_a, tot_a, send_a, rec_a)
    flat_next()
    moves_b = hand_out(load_b, core_b, mine_b, land_b, tot_b, send_b, rec_b)
    flat_next()
    arrive(moves_a)
    for by in range(1, dps):
        tot_a[...] += rec_a[by - 1].astype(F32)
    z_send[...] = tot_a[:, 0:shard].astype(BF)
    z_move = launch(z_send, z_land, mirror)
    step_move = launch(tot_a.at[:, pl.ds(shard + N, 128)], step_land, mirror)
    state_block = tot_a.at[:, pl.ds(shard, N)]
    state_moves = [launch(state_block, state_land.at[col], col_peer(by)) for by in range(1, cols)]
    state_land[col] = tot_a[:, shard : shard + N]
    flat_next()
    arrive(moves_b)
    for by in range(1, dps):
        tot_b[...] += rec_b[by - 1].astype(F32)
    arrive([z_move, step_move])
    tot_b[...] += z_land[...].astype(F32)
    ext[:, 0:128] = tot_a[:, shard + N : shard + N + 128] + pltpu.roll(step_land[...], 128 - heads, 1)
    out_rows = pl.ds(dp * piece, piece)
    v_moves = [launch(tot_b, v_out.at[out_rows, :], dp_peer(by)) for by in range(1, dps)]
    v_keep = keep(tot_b, v_out.at[out_rows, :])
    arrive(state_moves)
    part = col // 2
    ext[:, 128:256] = state_land[part] + state_land[part + group]
    e_moves = [launch(ext, ext_out.at[out_rows, :], dp_peer(by)) for by in range(1, dps)]
    e_keep = keep(ext, ext_out.at[out_rows, :])
    flat_next()
    for copy in loads:
        copy.wait()
    arrive(gn_moves)
    for by in range(1, group):
        gn_own[...] += gn_land[by - 1].astype(F32)

    @pl.when(col == group - 1)
    def _():
        for copy in halos:
            copy.wait_recv()
        for j in range(group):
            gn_own[count - HALO :, :] += halo_land[j].astype(F32)

    for j in range(group):
        pl.when(col == group + j)(halos[j].wait_send)
    flat_next()
    step = 64
    for at in range(0, count, step):
        rows = slice(at, at + step)
        values = tok_vm[rows, :].astype(F32)
        inv = lax.rsqrt(jnp.mean(values * values, axis=-1, keepdims=True) + EPSILON)
        unit = values * inv
        pulled = gn_own[rows, :] * gain_vm[0:1, :]
        mean = jnp.mean(pulled * unit, axis=-1, keepdims=True)
        gn_own[rows, :] = cot_vm[rows, :].astype(F32) + inv * (pulled - unit * mean)
    tg_keep = keep(gn_own, tg_out)
    while flat_taken[0] < len(flat_steps):
        flat_next()
    flat_keep = keep(acc, flat_out)
    arrive(v_moves)
    arrive(e_moves)
    for copy in [v_keep, e_keep, tg_keep, flat_keep]:
        copy.wait()
    for copy in started:
        copy.wait_send()


def settle(cols, dps, heads, gn, gnb, joint, flat, tokens, cotangent, gain, shard):
    width, wide = joint.shape
    half, wide_a = width // 2, wide - shard
    piece = half // dps
    count = tokens.shape[0]
    group = cols // 2
    any_spec = pl.BlockSpec(memory_space=pl.ANY)
    steps = (dps.bit_length() - 1) + (cols.bit_length() - 1) + 1
    copies = 2 + (group - 1) + group + steps + 4 * (dps - 1) + 2 + (cols - 1)
    vmem = pltpu.VMEM
    return pl.pallas_call(
        partial(settle_kernel, cols, dps, heads),
        in_specs=[any_spec] * 7,
        out_specs=[any_spec] * 4,
        out_shape=[
            sds((count, width)), sds((half, shard)), sds((half, 256)), sds(flat.shape),
        ],
        scratch_shapes=[
            vmem((half, wide_a), F32), vmem((half, wide_a), F32),
            vmem((half, shard), F32), vmem((half, shard), F32),
            vmem((dps - 1, piece, wide_a), BF), vmem((dps - 1, piece, wide_a), BF),
            vmem((dps - 1, piece, shard), BF), vmem((dps - 1, piece, shard), BF),
            vmem((piece, wide_a), F32), vmem((piece, shard), F32),
            vmem((piece, shard), BF), vmem((piece, shard), BF),
            vmem((piece, 128), F32), vmem((cols, piece, N), F32),
            vmem((piece, 256), F32),
            vmem(flat.shape, F32), vmem((steps,) + flat.shape, F32),
            vmem((count, width), F32), vmem((max(group - 1, 1), count, width), BF),
            vmem((group, HALO, width), BF),
            vmem((count, width), BF), vmem((count, width), BF), vmem((1, width), F32),
            pltpu.SemaphoreType.DMA((11,)),
            pltpu.SemaphoreType.DMA((copies,)),
            pltpu.SemaphoreType.DMA((copies,)),
        ],
        compiler_params=pltpu.CompilerParams(
            collective_id=2, has_side_effects=True, vmem_limit_bytes=VMEM_LIMIT
        ),
        cost_estimate=cost(90),
        name="settle",
    )(gn, gnb, joint, flat, tokens, cotangent, gain)


def flips(size, by):
    return [(i, i ^ by) for i in range(size)]


def butterfly(values, axis):
    size = lax.axis_size(axis)
    by = 1
    while by < size:
        values = values + lax.ppermute(values, axis, flips(size, by))
        by *= 2
    return values


def at_rows(values, index, size):
    return lax.dynamic_slice_in_dim(values, index * size, size, axis=0)


def collect_dp(piece, dp):
    size = lax.axis_size("dp")
    rows = piece.shape[0]
    out = jnp.zeros((size * rows,) + piece.shape[1:], piece.dtype)
    out = lax.dynamic_update_slice_in_dim(out, piece, dp * rows, 0)
    for by in range(1, size):
        other = lax.ppermute(piece, "dp", flips(size, by))
        out = lax.dynamic_update_slice_in_dim(out, other, (dp ^ by) * rows, 0)
    return out


def reduce_dp(values, dp):
    size = lax.axis_size("dp")
    total = lax.dynamic_index_in_dim(values, dp, 0, keepdims=False)
    for by in range(1, size):
        piece = lax.dynamic_index_in_dim(values, dp ^ by, 0, keepdims=False).astype(BF)
        total = total + lax.ppermute(piece, "dp", flips(size, by)).astype(F32)
    return total


def swap_core(values):
    return lax.ppermute(values, "row", [(0, 1), (1, 0)])


def per_device(
    tokens, norm_gain, w_gate, w_value, w_state, w_step, conv_value, bias_value, conv_state,
    bias_state, a_log, d_skip, dt_bias, mix_gain, w_out, cotangent,
):
    cols, rows_n, dps = lax.axis_size("col"), lax.axis_size("row"), lax.axis_size("dp")
    col, row, dp = lax.axis_index("col"), lax.axis_index("row"), lax.axis_index("dp")
    group = cols // 2
    place = lax.rem(col, group)
    local, width = tokens.shape
    span = local * group
    half_width = width // 2
    shard = w_value.shape[1]
    channels = 2 * shard
    heads = a_log.shape[0]
    inner_channels = shard * cols
    state_all = w_state.shape[1] * cols
    mirror = [(i, cols - 1 - i) for i in range(cols)]
    forth = [(i, cols - 1 - i) for i in range(group)]
    back = [(cols - 1 - i, i) for i in range(group)]

    def ring(by):
        return [(i, (i // group) * group + (i % group + by) % group) for i in range(cols)]

    state_width = w_state.shape[1]
    small = jnp.pad(
        jnp.concatenate([w_state, w_step], axis=1), ((0, 0), (0, 128 - state_width - heads))
    )
    group_tokens, value_full, gate_full, out_full, small_full = import_all(
        cols, dps, tokens, w_value, w_gate, w_out, small
    )
    from_col = lax.broadcasted_iota(jnp.int32, (cols * 128, TILE + 128), 0) // 128
    from_lane = lax.broadcasted_iota(jnp.int32, (cols * 128, TILE + 128), 0) % 128
    to = lax.broadcasted_iota(jnp.int32, (cols * 128, TILE + 128), 1)
    head_to = to - TILE
    is_state = (to < TILE) & (from_lane < state_width) & (from_col * state_width + from_lane == to)
    is_own = (from_col == col) & (head_to < heads) & (from_lane == state_width + head_to)
    is_mirror = (from_col == cols - 1 - col) & (head_to >= heads) & (head_to < 2 * heads)
    is_mirror = is_mirror & (from_lane == state_width + head_to - heads)
    pick = (is_state | ((head_to >= 0) & (is_own | is_mirror))).astype(BF)

    def gather_tokens(values):
        out = jnp.zeros((span, width), values.dtype)
        out = lax.dynamic_update_slice_in_dim(out, values, place * local, 0)
        for by in range(1, group):
            other = lax.ppermute(values, "col", ring(by))
            at = lax.rem(place - by + group, group)
            out = lax.dynamic_update_slice_in_dim(out, other, at * local, 0)
        return out

    def per_channel(own_taps, own_bias):
        taps = jnp.concatenate([own_taps.astype(F32).T, own_bias.astype(F32)[None]], axis=0)
        return jnp.pad(taps, ((0, 3), (0, 0)))

    packed = jnp.concatenate(
        [
            per_channel(conv_value, bias_value)[:5],
            mix_gain.astype(F32)[None],
            jnp.repeat(d_skip.astype(F32), HEAD)[None],
            jnp.pad(
                jnp.concatenate([a_log.astype(F32), dt_bias.astype(F32)]), (0, shard - 2 * heads)
            )[None],
        ],
        axis=0,
    )
    packed_both = jnp.concatenate([packed, lax.ppermute(packed, "col", mirror)], axis=1)
    state_vec = per_channel(conv_state, bias_state)
    state_vecs = jnp.zeros((8, state_all), F32)
    state_vecs = lax.dynamic_update_slice_in_dim(state_vecs, state_vec, col * state_width, 1)
    state_vecs = butterfly(state_vecs, "col")
    value_taps = jnp.concatenate([packed_both[:5], jnp.zeros((3, channels), F32)], axis=0)
    taps = jnp.concatenate([value_taps, state_vecs], axis=1)
    vectors = jnp.concatenate(
        [packed_both[6:7], packed_both[5:6], jnp.zeros((6, channels), F32)], axis=0
    )
    head_own, head_mirror = packed_both[7, :shard], packed_both[7, shard:]
    a_both = jnp.concatenate([head_own[:heads], head_mirror[:heads]])
    dt_both = jnp.concatenate([head_own[heads : 2 * heads], head_mirror[heads : 2 * heads]])
    rate = -jnp.exp(a_both)
    head_rows = jnp.zeros((8, 128), F32)
    head_rows = head_rows.at[0, : 2 * heads].set(dt_both).at[1, : 2 * heads].set(rate)
    head_of = lax.broadcasted_iota(jnp.int32, (128, channels), 1) // HEAD
    spread_one = (head_of == lax.broadcasted_iota(jnp.int32, (128, channels), 0)).astype(BF)
    spread = jnp.concatenate([spread_one, spread_one], axis=0)
    gather = (
        lax.broadcasted_iota(jnp.int32, (channels, 128), 0) // HEAD
        == lax.broadcasted_iota(jnp.int32, (channels, 128), 1)
    ).astype(BF)

    gain = norm_gain.astype(F32)
    raw, act, normed, step_in, step, cum, grow, offs, inv_rms, picked = project(
        group_tokens, gain[None], value_full, small_full, pick, taps, head_rows
    )
    states, final_state = scan_states(act, step, cum, spread, channels)

    def cross(values, pairs):
        moved = lax.ppermute(values, "col", pairs)
        return jnp.concatenate([moved[:, shard:], moved[:, :shard]], axis=1)

    early = cross(final_state, forth)
    y0 = scan_forward(act, step, cum, spread, states, channels)
    group_cot = gather_tokens(cotangent)
    graw, y, gm, stats = gate_forward(
        normed, group_cot, gate_full, out_full, y0, act, early, grow, spread, vectors
    )
    by = 1
    while by < group:
        stats = stats + lax.ppermute(stats, "col", flips(cols, by))
        by *= 2
    stats_pad = jnp.pad(stats, ((0, 120), (0, 0)))
    mixed, grad_gate, dy, mix_sums = mix_backward(inner_channels, graw, y, gm, act, stats_pad, vectors)

    def scatter_rows(make):
        parts = []
        for by in range(1, group):
            part = make(lax.rem(place + by, group)).astype(BF)
            parts.append(lax.ppermute(part, "col", ring(by)))
        total = make(place)
        for part in parts:
            total = total + part.astype(F32)
        return total

    after, first_grad = scan_grad_states(dy, act, cum, spread)
    late = cross(first_grad, back)
    branch = scatter_rows(lambda at: mm(at_rows(mixed, at, local), out_full))
    block_out = (tokens.astype(F32) + branch).astype(BF)

    def halves(values, axis):
        size = values.shape[axis] // 2
        mine = lax.dynamic_slice_in_dim(values, row * size, size, axis)
        return mine, lax.dynamic_slice_in_dim(values, (1 - row) * size, size, axis)

    def reduce_weight(values):
        mine, other = halves(values, 0)
        kept = mine + swap_core(other)
        return reduce_dp(kept.reshape(dps, -1, values.shape[1]), dp)

    def settle_shards(own, other):
        total = own + lax.ppermute(other.astype(BF), "col", mirror).astype(F32)
        return collect_dp(total, dp)

    grad_out = weight_grad(mixed, [group_cot])
    out_mine, out_other = halves(grad_out, 1)
    out_kept = (out_mine + swap_core(out_other)).reshape(2, dps, -1, half_width)
    out_piece = reduce_dp(jnp.transpose(out_kept, (1, 0, 2, 3)), dp)
    sum_out = settle_shards(out_piece[0], out_piece[1])

    gate_piece = reduce_weight(weight_grad(normed, [grad_gate]))
    sum_gate = settle_shards(gate_piece[:, :shard], gate_piece[:, shard:])

    gx, gbc_near = scan_backward_near(dy, act, step, cum, spread, states, early, offs)
    ga, grad_step, gbc, head_sums = scan_backward_far(
        dy, act, y, gx, step, cum, step_in, spread, gather, after, late, states, early, offs,
        head_rows, vectors, gbc_near,
    )
    state_part = state_all // group

    def state_slice(values, at):
        return lax.dynamic_slice_in_dim(values, at * state_part, state_part, axis=1)

    gbc_own = state_slice(gbc, place)
    for by in range(1, group):
        gbc_own = gbc_own + lax.ppermute(state_slice(gbc, lax.rem(place + by, group)), "col", ring(by))
    gv, value_sums = conv_back(ga, raw, taps)
    state_taps = state_slice(state_vecs, place)
    gs, state_sums = conv_back(gbc_own, state_slice(raw[:, channels:], place), state_taps)

    state_here, step_here = state_slice(picked, place), picked[:, TILE:]
    grad_normed, grad_normed_low, norm_sums = input_grad(
        gv, grad_gate, gs, grad_step, value_full, gate_full, state_here, step_here, group_tokens, inv_rms
    )
    joint = weight_grad(normed, [gv, jnp.pad(gs, ((0, 0), (0, N - state_part))), grad_step])

    wide = jnp.concatenate([value_sums[:5], mix_sums[0:1]], axis=0)
    wide_all = jnp.zeros((6, inner_channels), F32)
    wide_all = lax.dynamic_update_slice_in_dim(wide_all, wide[:, :shard], col * shard, 1)
    wide_all = lax.dynamic_update_slice_in_dim(wide_all, wide[:, shard:], (cols - 1 - col) * shard, 1)
    state_wide = jnp.zeros((5, state_all), F32)
    state_wide = lax.dynamic_update_slice_in_dim(state_wide, state_sums[:5], place * state_part, 1)
    skip_heads = jnp.sum(mix_sums[1].reshape(2 * heads, HEAD), axis=1)
    head_parts = jnp.stack([head_sums[0, : 2 * heads] * rate, skip_heads, head_sums[1, : 2 * heads]])
    head_all = jnp.zeros((3, heads * cols), F32)
    head_all = lax.dynamic_update_slice_in_dim(head_all, head_parts[:, :heads], col * heads, 1)
    head_all = lax.dynamic_update_slice_in_dim(head_all, head_parts[:, heads:], (cols - 1 - col) * heads, 1)
    lengths = [wide_all.size, state_wide.size, head_all.size, width]
    flat = jnp.concatenate(
        [wide_all.reshape(-1), state_wide.reshape(-1), head_all.reshape(-1), norm_sums[0]]
    )
    flat = jnp.pad(flat, (0, -flat.size % 1024)).reshape(-1, 128)
    tokens_grad, sum_value, extra, flat = settle(
        cols, dps, heads, grad_normed, grad_normed_low, joint, flat, tokens, cotangent, gain[None], shard
    )
    sum_step = extra[:, :heads]
    sum_state = lax.dynamic_slice_in_dim(
        extra, 128 + lax.rem(col, cols // group) * state_width, state_width, axis=1
    )
    flat = flat.reshape(-1)
    ends = [sum(lengths[: i + 1]) for i in range(4)]
    wide_all = flat[: ends[0]].reshape(6, inner_channels)
    state_wide = flat[ends[0] : ends[1]].reshape(5, state_all)
    head_all = flat[ends[1] : ends[2]].reshape(3, heads * cols)
    norm_total = flat[ends[2] : ends[3]]
    wide_own = lax.dynamic_slice_in_dim(wide_all, col * shard, shard, axis=1)
    state_own = lax.dynamic_slice_in_dim(state_wide, col * state_width, state_width, axis=1)
    head_own = lax.dynamic_slice_in_dim(head_all, col * heads, heads, axis=1)

    return (
        block_out,
        tokens_grad,
        norm_total,
        sum_gate,
        sum_value,
        sum_state,
        sum_step,
        wide_own[:4].T,
        wide_own[4],
        state_own[:4].T,
        state_own[4],
        head_own[0],
        head_own[1],
        head_own[2],
        wide_own[5],
        sum_out,
    )


def solution(mesh):
    rows = P(("dp", "row", "col"), None)
    grid = P("row", "col")
    vec = P("col")
    taps = P("col", None)
    return jax.shard_map(
        per_device,
        mesh=mesh,
        in_specs=(
            rows, P(), grid, grid, grid, grid, taps, vec, taps, vec, vec, vec, vec, vec,
            P("col", "row"), rows,
        ),
        out_specs=(
            rows, rows, P(), grid, grid, grid, grid, taps, vec, taps, vec, vec, vec, vec, vec,
            P("col", "row"),
        ),
        check_vma=False,
    )
```

```python
from functools import partial

import jax
import jax.numpy as jnp
import numpy as np
from jax import lax
from jax.experimental import pallas as pl
from jax.experimental.pallas import tpu as pltpu
from jax.sharding import PartitionSpec as P

BF = jnp.bfloat16
F32 = jnp.float32
EPSILON = 1e-05
N = 128
Q = 128
HEAD = 64
HALO = 16
TILE = 256
HIGHEST = lax.Precision.HIGHEST
VMEM_LIMIT = 56 * 2**20


def mm(a, b):
    return lax.dot_general(a, b, (((1,), (0,)), ((), ())), preferred_element_type=F32)


def mm_nt(a, b):
    return lax.dot_general(a, b, (((1,), (1,)), ((), ())), preferred_element_type=F32)


def mm_exact(a, b):
    return lax.dot_general(
        a, b, (((1,), (0,)), ((), ())), precision=HIGHEST, preferred_element_type=F32
    )


def split2(values):
    high = values.astype(BF)
    return high, (values - high.astype(F32)).astype(BF)


def sigmoid(values):
    return 1.0 / (1.0 + jnp.exp(-values))


def iota2(shape, axis):
    return lax.broadcasted_iota(jnp.int32, shape, axis)


def params(*names):
    return pltpu.CompilerParams(
        dimension_semantics=names or ("arbitrary",), vmem_limit_bytes=VMEM_LIMIT
    )


def cost(micros):
    return pl.CostEstimate(flops=0, bytes_accessed=int(micros * 3.0e6), transcendentals=0)


def whole(shape):
    return pl.BlockSpec(shape, lambda *_: (0,) * len(shape))


def columns(rows, width=TILE):
    return pl.BlockSpec((rows, width), lambda j: (0, j))


def sds(shape, dtype=F32):
    return jax.ShapeDtypeStruct(shape, dtype)


def here():
    return lax.axis_index("dp"), lax.axis_index("row"), lax.axis_index("col")


def lanes_at(index, size):
    return pl.ds(pl.multiple_of(index * size, 128), size)


def greet(others):
    barrier = pltpu.get_barrier_semaphore()
    for other in others:
        pl.semaphore_signal(barrier, inc=1, device_id=other, device_id_type=pl.DeviceIdType.MESH)
    pl.semaphore_wait(barrier, len(others))


def at_step(step):
    return pl.when(pl.program_id(0) == step)


def copy_to(src, dst, sems, i, device):
    return pltpu.make_async_remote_copy(
        src_ref=src, dst_ref=dst, send_sem=sems.at[0, i], recv_sem=sems.at[1, i],
        device_id=device, device_id_type=pl.DeviceIdType.MESH,
    )


def dp_copies(dps, sems, src_of, dst_of, first=0):
    dp, row, col = here()
    return [
        copy_to(src_of(dp ^ by, by - 1), dst_of(dp ^ by, by - 1), sems, first + by - 1, (dp ^ by, row, col))
        for by in range(1, dps)
    ]


def dp_peers(dps):
    dp, row, col = here()
    return [(dp ^ by, row, col) for by in range(1, dps)]


def mirror_of(cols):
    dp, row, col = here()
    return (dp, row, cols - 1 - col)


def remote_params(collective_id):
    return pltpu.CompilerParams(
        dimension_semantics=("arbitrary",), vmem_limit_bytes=VMEM_LIMIT, collective_id=collective_id,
        has_side_effects=True,
    )


ANY = pl.BlockSpec(memory_space=pl.ANY)


def import_kernel(
    cols, dps, tok, wv, wg, wo, sw, vec, tg, vf, gf, of, sf, vecs,
    zeros, tok_vm, w_vm, wo_vm, s_vm, vec_vm, local, send, recv,
):
    dp, row, col = here()
    group = cols // 2
    place = lax.rem(col, group)
    half, shard = wv.shape
    count = tok.shape[0]
    piece, piece_out = half // dps, wo.shape[0] // dps
    sibling = (dp, 1 - row, col)
    mirror = (dp, row, cols - 1 - col)
    col_peer = lambda by: (dp, row, col ^ by)
    dp_peer = lambda by: (dp ^ by, row, col)
    greet(
        [sibling]
        + [col_peer(by) for by in range(1, cols)]
        + [dp_peer(by) for by in range(1, dps)]
    )
    used = [0]
    started = []

    def remote(src, dst, device):
        i = used[0]
        used[0] += 1
        return pltpu.make_async_remote_copy(
            src_ref=src, dst_ref=dst, send_sem=send.at[i], recv_sem=recv.at[i],
            device_id=device, device_id_type=pl.DeviceIdType.MESH,
        )

    def launch(src, dst, device):
        copy = remote(src, dst, device)
        copy.start()
        started.append(copy)
        return copy

    def keep(i, src, dst):
        copy = pltpu.make_async_copy(src, dst, local.at[i])
        copy.start()
        return copy

    my_rows = pl.ds(row * half, half)
    my_piece = pl.ds(row * half + dp * piece, piece)
    out_piece = pl.ds(shard + dp * piece_out, piece_out)
    my_lanes = lanes_at(row, half)
    own, other = pl.ds(0, shard), pl.ds(shard, shard)
    src_piece, src_out = pl.ds(dp * piece, piece), pl.ds(dp * piece_out, piece_out)

    staged = [
        keep(6, vec, vec_vm),
        keep(0, sw.at[src_piece, :], s_vm),
        keep(2, tok, tok_vm),
        keep(3, wv, w_vm.at[0]),
        keep(4, wg, w_vm.at[1]),
        keep(5, wo, wo_vm),
    ]
    s_cross = [
        launch(sw.at[src_piece, :], sf.at[my_piece, lanes_at(col, 128)], col_peer(by))
        for by in range(1, cols)
    ]
    v_cross = launch(wv.at[src_piece, :], vf.at[my_piece, other], mirror)
    vec_cross = [launch(vec, vecs.at[col], col_peer(by)) for by in range(1, cols)]
    my_tokens = tg.at[pl.ds(HALO + place * count, count), :]
    tok_cross = [launch(tok, my_tokens, col_peer(by)) for by in range(1, group)]
    halo_src = tok.at[pl.ds(count - HALO, HALO), :]
    halo_dst = tg.at[pl.ds(0, HALO), :]
    halo_at = used[0]
    used[0] += group
    halos = [
        pltpu.make_async_remote_copy(
            src_ref=halo_src, dst_ref=halo_dst, send_sem=send.at[halo_at + j], recv_sem=recv.at[halo_at],
            device_id=(dp, row, group + j), device_id_type=pl.DeviceIdType.MESH,
        )
        for j in range(group)
    ]

    @pl.when(col == group - 1)
    def _():
        for copy in halos:
            copy.start()

    zeros[...] = jnp.zeros_like(zeros)

    @pl.when(col < group)
    def _():
        clear = pltpu.make_async_copy(zeros, halo_dst, local.at[1])
        clear.start()
        clear.wait()

    v_own = launch(wv, vf.at[my_rows, own], sibling)
    g_own = launch(wg, gf.at[my_rows, own], sibling)
    o_own = launch(wo, of.at[own, my_lanes], sibling)
    for copy in staged:
        copy.wait()
    small_own = keep(0, s_vm, sf.at[my_piece, lanes_at(col, 128)])
    kept = [
        keep(6, vec_vm, vecs.at[col]),
        keep(2, tok_vm, my_tokens),
        keep(3, w_vm.at[0], vf.at[my_rows, own]),
        keep(4, w_vm.at[1], gf.at[my_rows, own]),
        keep(5, wo_vm, of.at[own, my_lanes]),
    ]

    def spread_out(ref):
        return [launch(ref, ref, dp_peer(by)) for by in range(1, dps)]

    def arrive(copies):
        for copy in copies:
            copy.wait_recv()

    arrive(s_cross)
    small_own.wait()
    s_dp = spread_out(sf.at[my_piece, :])
    arrive([v_cross])
    g_cross = launch(wg.at[src_piece, :], gf.at[my_piece, other], mirror)
    v_dp = spread_out(vf.at[my_piece, other])
    arrive([g_cross])
    o_cross = launch(wo.at[src_out, :], of.at[out_piece, my_lanes], mirror)
    g_dp = spread_out(gf.at[my_piece, other])
    arrive(s_dp)
    last = [launch(sf.at[my_rows, :], sf.at[my_rows, :], sibling)]
    arrive(v_dp)
    last += [launch(vf.at[my_rows, other], vf.at[my_rows, other], sibling)]
    arrive([o_cross])
    o_dp = spread_out(of.at[out_piece, my_lanes])
    arrive(g_dp)
    last += [launch(gf.at[my_rows, other], gf.at[my_rows, other], sibling)]
    arrive(o_dp)
    last += [launch(of.at[other, my_lanes], of.at[other, my_lanes], sibling)]
    arrive(last)
    arrive([v_own, g_own, o_own])
    arrive(vec_cross)
    arrive(tok_cross)

    @pl.when(col >= group)
    def _():
        halos[0].wait_recv()

    @pl.when(col == group - 1)
    def _():
        for copy in halos:
            copy.wait_send()

    for copy in kept:
        copy.wait()
    for copy in started:
        copy.wait_send()


def import_all(cols, dps, tokens, w_value, w_gate, w_out, small, vec):
    half, shard = w_value.shape
    count, width = tokens.shape
    any_spec = pl.BlockSpec(memory_space=pl.ANY)
    copies = 3 + 2 * (cols - 1) + (cols // 2 - 1) + cols // 2 + 3 + 4 * (dps - 1) + 4
    return pl.pallas_call(
        partial(import_kernel, cols, dps),
        in_specs=[any_spec] * 6,
        out_specs=[any_spec] * 6,
        out_shape=[
            sds((HALO + count * (cols // 2), width), BF),
            sds((2 * half, 2 * shard), BF),
            sds((2 * half, 2 * shard), BF),
            sds((2 * shard, 2 * half), BF),
            sds((2 * half, cols * 128), BF),
            sds((cols,) + vec.shape, BF),
        ],
        scratch_shapes=[
            pltpu.VMEM((HALO, width), BF),
            pltpu.VMEM((count, width), BF),
            pltpu.VMEM((2, half, shard), BF),
            pltpu.VMEM((shard, half), BF),
            pltpu.VMEM((half // dps, 128), BF),
            pltpu.VMEM(vec.shape, BF),
            pltpu.SemaphoreType.DMA((7,)),
            pltpu.SemaphoreType.DMA((copies,)),
            pltpu.SemaphoreType.DMA((copies,)),
        ],
        compiler_params=pltpu.CompilerParams(
            collective_id=1, has_side_effects=True, vmem_limit_bytes=VMEM_LIMIT
        ),
        cost_estimate=cost(55),
        name="import_all",
    )(tokens, w_value, w_gate, w_out, small, vec)


def conv_rows(raw_ref, taps, start, size):
    total = taps[4:5, :] + jnp.zeros((size, taps.shape[1]), F32)
    for k in range(4):
        total = total + taps[k : k + 1, :] * raw_ref[pl.ds(HALO - 3 + k + start, size), :]
    return total


def project_kernel(
    tok_ref, gain_ref, w_ref, small_ref, pick_ref, taps_ref, head_ref,
    raw_ref, act_ref, normed_ref, stepin_ref, step_ref, cum_ref, grow_ref, offs_ref, inv_ref, picked_ref,
):
    tokens = act_ref.shape[0]
    at_tile = pl.program_id(0)
    last = pl.num_programs(0) - 1

    @pl.when(at_tile == 0)
    def _():
        for at in [0] + list(range(HALO, HALO + tokens, Q)):
            size = HALO if at == 0 else Q
            values = tok_ref[at : at + size, :].astype(F32)
            inv = lax.rsqrt(jnp.mean(values * values, axis=-1, keepdims=True) + EPSILON)
            normed_ref[at : at + size, :] = (values * inv * gain_ref[0:1, :]).astype(BF)
            inv_ref[at : at + size, :] = jnp.broadcast_to(inv, (size, 128))

    @pl.when(at_tile < last)
    def _():
        raw_ref[...] = mm(normed_ref[...], w_ref[...])

    @pl.when(at_tile == last)
    def _():
        picked = mm(small_ref[...], pick_ref[...]).astype(BF)
        picked_ref[...] = picked
        raw_ref[...] = mm(normed_ref[...], picked[:, :TILE])
        step_in = mm(normed_ref[HALO:, :], picked[:, TILE:]) + head_ref[0:1, :]
        small = jnp.exp(-jnp.abs(step_in))
        plus = 1.0 + small
        safe = jnp.where(plus == 1.0, 1.0, plus - 1.0)
        log_part = jnp.where(plus == 1.0, small, jnp.log(plus) * (small / safe))
        step = jnp.maximum(step_in, 0.0) + log_part
        stepin_ref[...] = step_in
        step_ref[...] = step
        falls = step * head_ref[1:2, :]
        lower = (iota2((Q, Q), 0) >= iota2((Q, Q), 1)).astype(F32)
        before = jnp.zeros((1, 128), F32)
        offs_ref[...] = jnp.zeros_like(offs_ref)
        for b in range(tokens // Q):
            rows = slice(b * Q, b * Q + Q)
            cum = mm_exact(lower, falls[rows, :])
            cum_ref[rows, :] = cum
            high, low = split2(jnp.exp(cum + before))
            grow_ref[rows, 0:128] = high
            grow_ref[rows, 128:256] = low
            before = before + cum[Q - 1 : Q, :]
            offs_ref[b + 1 : b + 2, :] = before

    taps = taps_ref[...]
    for at in range(0, tokens, Q):
        pre = conv_rows(raw_ref, taps, at, Q)
        act_ref[at : at + Q, :] = (pre * sigmoid(pre)).astype(BF)


def project(group_tokens, gain, weights, small, pick, taps, head_rows):
    rows, width = group_tokens.shape
    tokens = rows - HALO
    total = weights.shape[1] + TILE
    last = weights.shape[1] // TILE - 1
    return pl.pallas_call(
        project_kernel,
        grid=(total // TILE,),
        in_specs=[
            whole((rows, width)),
            whole((1, width)),
            pl.BlockSpec((width, TILE), lambda j: (0, jnp.minimum(j, last))),
            whole(small.shape),
            whole(pick.shape),
            columns(8),
            whole((8, 128)),
        ],
        out_specs=[
            columns(rows),
            columns(tokens),
            whole((rows, width)),
            whole((tokens, 128)),
            whole((tokens, 128)),
            whole((tokens, 128)),
            whole((tokens, 256)),
            whole((16, 128)),
            whole((rows, 128)),
            whole((width, TILE + 128)),
        ],
        out_shape=[
            sds((rows, total)),
            sds((tokens, total), BF),
            sds((rows, width), BF),
            sds((tokens, 128)),
            sds((tokens, 128)),
            sds((tokens, 128)),
            sds((tokens, 256), BF),
            sds((16, 128)),
            sds((rows, 128)),
            sds((width, TILE + 128), BF),
        ],
        compiler_params=params(),
        cost_estimate=cost(14),
        name="project",
    )(group_tokens, gain, weights, small, pick, taps, head_rows)


def expand(per_head, spread):
    high, low = split2(per_head)
    return mm(jnp.concatenate([high, low], 1), spread)


def transpose_bf(values):
    return values.astype(F32).T.astype(BF)


def states_kernel(x_ref, b_ref, step_ref, cum_ref, spread_ref, states_ref, final_ref, held):
    at = pl.program_id(0)
    last = pl.num_programs(0) - 1

    @pl.when(at == 0)
    def _():
        held[...] = jnp.zeros_like(held)

    states_ref[0] = held[...]

    @pl.when(at == last)
    def _():
        final_ref[...] = held[...]

    @pl.when(at < last)
    def _():
        cum = cum_ref[...]
        end = cum[Q - 1 : Q, :]
        tail = jnp.exp(end - cum) * step_ref[...]
        fall = jnp.broadcast_to(jnp.exp(end), (8, 128))
        b_t = transpose_bf(b_ref[...])
        b_t2 = jnp.concatenate([b_t, b_t], 1)
        for start in range(0, x_ref.shape[1], TILE):
            lanes = slice(start, start + TILE)
            spread = spread_ref[:, lanes]
            scaled = expand(tail, spread) * x_ref[:, lanes].astype(F32)
            high, low = split2(scaled)
            fresh = mm(b_t2, jnp.concatenate([high, low], 0))
            held[:, lanes] = held[:, lanes] * expand(fall, spread)[0:1, :] + fresh


def scan_states(act, step, cum, spread, channels):
    blocks = act.shape[0] // Q
    clamp = lambda i: jnp.minimum(i, blocks - 1)
    return pl.pallas_call(
        states_kernel,
        grid=(blocks + 1,),
        in_specs=[
            pl.BlockSpec((Q, channels), lambda i: (clamp(i), 0)),
            pl.BlockSpec((Q, N), lambda i: (clamp(i), channels // N)),
            pl.BlockSpec((Q, 128), lambda i: (clamp(i), 0)),
            pl.BlockSpec((Q, 128), lambda i: (clamp(i), 0)),
            whole((256, channels)),
        ],
        out_specs=[
            pl.BlockSpec((1, N, channels), lambda i: (i, 0, 0)),
            whole((N, channels)),
        ],
        out_shape=[sds((blocks + 1, N, channels)), sds((N, channels))],
        scratch_shapes=[pltpu.VMEM((N, channels), F32)],
        compiler_params=params(),
        cost_estimate=cost(6),
        name="scan_states",
    )(act, act, step, cum, spread)


def forward_kernel(x_ref, b_ref, c_ref, step_ref, cum_ref, spread_ref, state_ref, y_ref):
    b_blk, c_blk = b_ref[...], c_ref[...]
    affinity = mm_nt(c_blk, b_blk)
    causal = iota2((Q, Q), 0) >= iota2((Q, Q), 1)
    first = iota2((Q, 128), 1) < HEAD
    cum = cum_ref[...]
    cum_t = cum.T
    step_t = step_ref[...].T
    growth = jnp.exp(cum)
    c2 = jnp.concatenate([c_blk, c_blk], 1)
    zero = jnp.zeros((Q, 128), BF)
    for start in range(0, x_ref.shape[1], TILE):
        lanes = slice(start, start + TILE)
        s_high, s_low = split2(state_ref[0, :, lanes])
        reached = mm(c2, jnp.concatenate([s_high, s_low], 0)) * expand(growth, spread_ref[:, lanes])
        for pair in range(2):
            at = start + pair * 128
            x_pair = x_ref[:, at : at + 128]
            x0, x1 = jnp.where(first, x_pair, zero), jnp.where(first, zero, x_pair)
            pieces = []
            for half in range(2):
                h = at // HEAD + half
                spread_h = cum[:, h : h + 1] - cum_t[h : h + 1, :]
                decay = jnp.exp(jnp.where(causal, spread_h, -1e30))
                mixing = affinity * decay * step_t[h : h + 1, :]
                pieces += split2(mixing)
            intra = mm(jnp.concatenate(pieces, 1), jnp.concatenate([x0, x0, x1, x1], 0))
            y_ref[:, at : at + 128] = intra + reached[:, pair * 128 : pair * 128 + 128]


def scan_forward(act, step, cum, spread, states, channels):
    tokens = act.shape[0]
    return pl.pallas_call(
        forward_kernel,
        grid=(tokens // Q,),
        in_specs=[
            pl.BlockSpec((Q, channels), lambda i: (i, 0)),
            pl.BlockSpec((Q, N), lambda i: (i, channels // N)),
            pl.BlockSpec((Q, N), lambda i: (i, channels // N + 1)),
            pl.BlockSpec((Q, 128), lambda i: (i, 0)),
            pl.BlockSpec((Q, 128), lambda i: (i, 0)),
            whole((256, channels)),
            pl.BlockSpec((1, N, channels), lambda i: (i, 0, 0)),
        ],
        out_specs=pl.BlockSpec((Q, channels), lambda i: (i, 0)),
        out_shape=sds((tokens, channels)),
        compiler_params=params(),
        cost_estimate=cost(13),
        name="scan_forward",
    )(act, act, act, step, cum, spread, states)


def grad_states_kernel(dy_ref, c_ref, cum_ref, spread_ref, after_ref, first_ref, held):
    at = pl.program_id(0)

    @pl.when(at == 0)
    def _():
        held[...] = jnp.zeros_like(held)

    after_ref[0] = held[...]
    cum = cum_ref[...]
    growth = jnp.exp(cum)
    fall = jnp.broadcast_to(growth[Q - 1 : Q, :], (8, 128))
    c_t = transpose_bf(c_ref[...])
    c_t2 = jnp.concatenate([c_t, c_t], 1)
    for start in range(0, dy_ref.shape[1], TILE):
        lanes = slice(start, start + TILE)
        spread = spread_ref[:, lanes]
        high, low = split2(dy_ref[:, lanes] * expand(growth, spread))
        direct = mm(c_t2, jnp.concatenate([high, low], 0))
        held[:, lanes] = held[:, lanes] * expand(fall, spread)[0:1, :] + direct
    first_ref[...] = held[...]


def scan_grad_states(dy, act, cum, spread):
    tokens, channels = dy.shape
    blocks = tokens // Q
    return pl.pallas_call(
        grad_states_kernel,
        grid=(blocks,),
        in_specs=[
            pl.BlockSpec((Q, channels), lambda i: (blocks - 1 - i, 0)),
            pl.BlockSpec((Q, N), lambda i: (blocks - 1 - i, channels // N + 1)),
            pl.BlockSpec((Q, 128), lambda i: (blocks - 1 - i, 0)),
            whole((256, channels)),
        ],
        out_specs=[
            pl.BlockSpec((1, N, channels), lambda i: (blocks - 1 - i, 0, 0)),
            whole((N, channels)),
        ],
        out_shape=[sds((blocks, N, channels)), sds((N, channels))],
        scratch_shapes=[pltpu.VMEM((N, channels), F32)],
        compiler_params=params(),
        cost_estimate=cost(6),
        name="scan_grad_states",
    )(dy, act, cum, spread)


def near_block(
    at_block, here_rows, dy_ref, x_ref, b_ref, c_ref, step_ref, cum_ref, spread_ref, state_ref, early_ref,
    offs_ref, gx_ref, gbc_ref,
):
    b_blk, c_blk = b_ref[...], c_ref[...]
    affinity_t = mm_nt(b_blk, c_blk)
    causal_t = iota2((Q, Q), 1) >= iota2((Q, Q), 0)
    first = iota2((Q, 128), 1) < HEAD
    cum = cum_ref[...]
    cum_t = cum.T
    step = step_ref[...]
    growth = jnp.exp(cum)
    early_fall = jnp.broadcast_to(jnp.exp(offs_ref[pl.ds(at_block, 1), :]), (8, 128))
    zero = jnp.zeros((Q, 128), BF)
    grad_affinity_t = jnp.zeros((Q, Q), F32)
    grad_c = jnp.zeros((Q, N), F32)
    for start in range(0, x_ref.shape[1], TILE):
        lanes = slice(start, start + TILE)
        spread = spread_ref[:, lanes]
        before = state_ref[0, :, lanes] + expand(early_fall, spread)[0:1, :] * early_ref[:, lanes]
        dy_quad = dy_ref[:, lanes]
        s_high, s_low = split2(before)
        g_high, g_low = split2(dy_quad * expand(growth, spread))
        grad_c = grad_c + mm_nt(
            jnp.concatenate([g_high, g_low, g_high], 1), jnp.concatenate([s_high, s_high, s_low], 1)
        )
        for pair in range(2):
            at = start + pair * 128
            d_high, d_low = split2(dy_quad[:, pair * 128 : pair * 128 + 128])
            x_pair = x_ref[:, at : at + 128]
            x0, x1 = jnp.where(first, x_pair, zero), jnp.where(first, zero, x_pair)
            grad_mixing = mm_nt(
                jnp.concatenate([jnp.concatenate([x0, x0], 1), jnp.concatenate([x1, x1], 1)], 0),
                jnp.concatenate([d_high, d_low], 1),
            )
            left, right = [], []
            for half in range(2):
                h = at // HEAD + half
                spread_h = cum_t[h : h + 1, :] - cum[:, h : h + 1]
                decay = jnp.exp(jnp.where(causal_t, spread_h, -1e30))
                m_high, m_low = split2(affinity_t * decay)
                grad_affinity_t = grad_affinity_t + (
                    grad_mixing[half * Q : half * Q + Q, :] * decay * step[:, h : h + 1]
                )
                keep = first if half == 0 else jnp.logical_not(first)
                dh, dl = jnp.where(keep, d_high, zero), jnp.where(keep, d_low, zero)
                left += [m_high, m_low, m_high]
                right += [dh, dh, dl]
            gx_ref[here_rows, at : at + 128] = mm(jnp.concatenate(left, 1), jnp.concatenate(right, 0))
    a_high, a_low = split2(grad_affinity_t)
    gbc_ref[here_rows, 0:N] = mm(jnp.concatenate([a_high, a_low], 1), jnp.concatenate([c_blk, c_blk], 0))
    t_high, t_low = split2(grad_affinity_t.T)
    gbc_ref[here_rows, N : 2 * N] = grad_c + mm(
        jnp.concatenate([t_high, t_low], 1), jnp.concatenate([b_blk, b_blk], 0)
    )


def far_block(
    blocks, at_block, here_rows, dy_ref, x_ref, y_ref, gx_ref, b_ref, step_ref, cum_ref, stepin_ref, spread_ref,
    gather_ref, after_ref, late_ref, state_ref, early_ref, offs_ref, head_ref, skip_ref, gbc_ref,
    ga_ref, gstep_ref, gbc_out_ref, sums_ref,
):
    b_blk = b_ref[...]
    b2 = jnp.concatenate([b_blk, b_blk], 1)
    cum, step = cum_ref[...], step_ref[...]
    tail = jnp.exp(cum[Q - 1 : Q, :] - cum)
    tail_step = tail * step
    offs_after = offs_ref[pl.ds(at_block + 1, 1), :]
    offs_end = offs_ref[pl.ds(blocks, 1), :]
    late_fall = jnp.broadcast_to(jnp.exp(offs_end - offs_after), (8, 128))
    early_fall = jnp.broadcast_to(jnp.exp(offs_after), (8, 128))
    row_dots = jnp.zeros((Q, 128), F32)
    col_dots = jnp.zeros((Q, 128), F32)
    last_add = jnp.zeros((8, 128), F32)
    grad_b = gbc_ref[here_rows, 0:N]
    for start in range(0, x_ref.shape[1], TILE):
        lanes = slice(start, start + TILE)
        spread = spread_ref[:, lanes]
        gather = gather_ref[lanes, :]
        gather2 = jnp.concatenate([gather, gather], 0)
        x_quad = x_ref[:, lanes].astype(F32)
        dy_quad = dy_ref[:, lanes]
        skip = skip_ref[0:1, lanes]
        d_state = after_ref[0, :, lanes] + expand(late_fall, spread)[0:1, :] * late_ref[:, lanes]
        state = state_ref[0, :, lanes] + expand(early_fall, spread)[0:1, :] * early_ref[:, lanes]
        touch = jnp.broadcast_to(jnp.sum(d_state * state, axis=0, keepdims=True), (8, TILE))
        t_high, t_low = split2(touch)
        last_add = last_add + mm(jnp.concatenate([t_high, t_low], 1), gather2)
        s_high, s_low = split2(d_state)
        gx = gx_ref[here_rows, lanes] + expand(tail, spread) * mm(b2, jnp.concatenate([s_high, s_low], 0))
        w_high, w_low = split2(expand(tail_step, spread) * x_quad)
        grad_b = grad_b + mm_nt(
            jnp.concatenate([w_high, w_low, w_high], 1), jnp.concatenate([s_high, s_high, s_low], 1)
        )
        p_high, p_low = split2(dy_quad * (y_ref[:, lanes] - skip * x_quad))
        row_dots = row_dots + mm(jnp.concatenate([p_high, p_low], 1), gather2)
        r_high, r_low = split2(x_quad * gx)
        col_dots = col_dots + mm(jnp.concatenate([r_high, r_low], 1), gather2)
        ga_ref[:, lanes] = expand(step, spread) * gx + skip * dy_quad
    last_row = iota2((Q, 128), 0) == Q - 1
    grad_cum = row_dots - step * col_dots + jnp.where(last_row, last_add[0:1, :], 0.0)
    upper = (iota2((Q, Q), 1) >= iota2((Q, Q), 0)).astype(F32)
    grad_rate = mm_exact(upper, grad_cum)
    grad_step = col_dots + grad_rate * head_ref[1:2, :]
    grad_raw = grad_step * sigmoid(stepin_ref[...])
    gstep_ref[...] = grad_raw.astype(BF)
    sums_ref[0:1, :] += jnp.sum(grad_rate * step, axis=0, keepdims=True)
    sums_ref[1:2, :] += jnp.sum(grad_raw, axis=0, keepdims=True)
    gbc_out_ref[:, 0:N] = grad_b
    gbc_out_ref[:, N : 2 * N] = gbc_ref[here_rows, N : 2 * N]


def backward_kernel(
    cols, dps,
    dy_ref, x_ref, y_ref, b_ref, c_ref, step_ref, cum_ref, stepin_ref, spread_ref, gather_ref, after_ref,
    state_ref, early_ref, offs_ref, head_ref, skip_ref, o_low, o_full, g_low, g_full, late_ref, parts,
    ga_ref, gstep_ref, gbc_out_ref, sums_ref, o_total_ref, g_own_ref, g_cross_ref, branch_in,
    gx_ref, gbc_ref, o_own, o_land, o_cross, o_cross_land, g_own, g_land, sems, local,
):
    step_at = pl.program_id(0)
    blocks = pl.num_programs(0) // 2
    at_block = lax.rem(step_at, blocks)
    here_rows = pl.ds(pl.multiple_of(at_block * Q, Q), Q)
    dp, row, col = here()
    group = cols // 2
    shard = g_own_ref.shape[1]
    others = dps - 1
    own, other = pl.ds(0, shard), pl.ds(shard, shard)

    def o_moves():
        return dp_copies(dps, sems, lambda to, i: o_low.at[:, to], lambda to, i: o_land.at[i])

    def g_moves():
        return dp_copies(dps, sems, lambda to, i: g_low.at[to], lambda to, i: g_land.at[i], others)

    def cross_move():
        return copy_to(o_cross, o_cross_land, sems, 2 * others, mirror_of(cols))

    def part_moves():
        return [
            copy_to(
                parts.at[by - 1], branch_in.at[by - 1], sems, 2 * others + by, (dp, row, col ^ by)
            )
            for by in range(1, group)
        ]

    load_o = pltpu.make_async_copy(o_full.at[:, dp], o_own, local.at[0])
    load_g = pltpu.make_async_copy(g_full.at[dp], g_own, local.at[1])

    @at_step(0)
    def _():
        greet(dp_peers(dps) + [mirror_of(cols)] + [(dp, row, col ^ by) for by in range(1, group)])
        for move in o_moves() + part_moves():
            move.start()
        load_o.start()
        load_g.start()

        sums_ref[...] = jnp.zeros_like(sums_ref)

    @pl.when(step_at < blocks)
    def _():
        near_block(
            at_block, here_rows, dy_ref, x_ref, b_ref, c_ref, step_ref, cum_ref, spread_ref, state_ref,
            early_ref, offs_ref, gx_ref, gbc_ref,
        )

    @pl.when(step_at == blocks)
    def _():
        for move in o_moves():
            move.wait_recv()
        for move in g_moves():
            move.start()
        load_o.wait()
        for i in range(others):
            o_own[...] += o_land[i].astype(F32)
        o_cross[...] = o_own[1].astype(BF)
        cross_move().start()

    @pl.when(step_at >= blocks)
    def _():
        far_block(
            blocks, at_block, here_rows, dy_ref, x_ref, y_ref, gx_ref, b_ref, step_ref, cum_ref, stepin_ref,
            spread_ref, gather_ref, after_ref, late_ref, state_ref, early_ref, offs_ref, head_ref, skip_ref,
            gbc_ref, ga_ref, gstep_ref, gbc_out_ref, sums_ref,
        )

    @at_step(2 * blocks - 1)
    def _():
        cross_move().wait()
        o_total_ref[...] = o_own[0] + o_cross_land[...].astype(F32)
        load_g.wait()
        for move in g_moves():
            move.wait()
        for i in range(others):
            g_own[...] += g_land[i].astype(F32)
        g_own_ref[...] = g_own[:, :shard]
        g_cross_ref[...] = g_own[:, shard:].astype(BF)
        for move in part_moves():
            move.wait()
        for move in o_moves():
            move.wait_send()


def scan_backward(
    cols, dps, dy, act, y, step, cum, step_in, spread, gather, after, states, early, offs, head_rows, skip,
    o_low, o_full, g_low, g_full, late, parts,
):
    tokens, channels = dy.shape
    blocks, group, shard = tokens // Q, cols // 2, channels // 2
    piece, half = o_low.shape[2:]
    piece_g = g_low.shape[1]
    block = lambda i: lax.rem(i, blocks)
    second = lambda i: jnp.maximum(i - blocks, 0)
    rows = lambda at, width: pl.BlockSpec((Q, width), lambda i: (at(i), 0))
    vmem = pltpu.VMEM
    return pl.pallas_call(
        partial(backward_kernel, cols, dps),
        grid=(2 * blocks,),
        in_specs=[
            rows(block, channels),
            rows(block, channels),
            rows(second, channels),
            pl.BlockSpec((Q, N), lambda i: (block(i), channels // N)),
            pl.BlockSpec((Q, N), lambda i: (block(i), channels // N + 1)),
            rows(block, 128),
            rows(block, 128),
            rows(second, 128),
            whole(spread.shape),
            whole(gather.shape),
            pl.BlockSpec((1, N, channels), lambda i: (second(i), 0, 0)),
            pl.BlockSpec((1, N, channels), lambda i: (block(i) + lax.div(i, blocks), 0, 0)),
            whole(early.shape),
            whole((16, 128)),
            whole((8, 128)),
            whole((8, channels)),
        ] + [ANY] * 4 + [whole(late.shape), ANY],
        out_specs=[
            rows(second, channels),
            rows(second, 128),
            rows(second, 2 * N),
            whole((8, 128)),
            whole((piece, half)),
            whole((piece_g, shard)),
            whole((piece_g, shard)),
            ANY,
        ],
        out_shape=[
            sds((tokens, channels)),
            sds((tokens, 128), BF),
            sds((tokens, 2 * N)),
            sds((8, 128)),
            sds((piece, half)),
            sds((piece_g, shard)),
            sds((piece_g, shard), BF),
            sds(parts.shape, BF),
        ],
        scratch_shapes=[
            vmem((tokens, channels), F32), vmem((tokens, 2 * N), F32),
            vmem((2, piece, half), F32), vmem((dps - 1, 2, piece, half), BF),
            vmem((piece, half), BF), vmem((piece, half), BF),
            vmem((piece_g, channels), F32), vmem((dps - 1, piece_g, channels), BF),
            pltpu.SemaphoreType.DMA((2, 2 * (dps - 1) + group)),
            pltpu.SemaphoreType.DMA((2,)),
        ],
        compiler_params=remote_params(3),
        cost_estimate=cost(55),
        name="scan_backward",
    )(
        dy, act, y, act, act, step, cum, step_in, spread, gather, after, states, early, offs, head_rows, skip,
        o_low, o_full, g_low, g_full, late, parts,
    )


def gate_kernel(
    normed_ref, cot_ref, wg_ref, wo_ref, y0_ref, x_ref, early_ref, c_ref, grow_ref, spread_ref, vec_ref,
    graw_ref, y_ref, gm_ref, stats_ref, squares, inners,
):
    at = pl.program_id(0)
    tokens = cot_ref.shape[0]

    @pl.when(at == 0)
    def _():
        squares[...] = jnp.zeros_like(squares)
        inners[...] = jnp.zeros_like(inners)

    graw_ref[...] = mm(normed_ref[HALO:, :], wg_ref[...])
    gm_ref[...] = mm_nt(cot_ref[...], wo_ref[...])
    s_high, s_low = split2(early_ref[...])
    s2 = jnp.concatenate([s_high, s_low], 0)
    spread = spread_ref[...]
    skip, gain = vec_ref[0:1, :], vec_ref[1:2, :]
    for row in range(0, tokens, Q):
        rows = slice(row, row + Q)
        c_blk = c_ref[rows, :]
        carried = mm(jnp.concatenate([c_blk, c_blk], 1), s2) * mm(grow_ref[rows, :], spread)
        y = y0_ref[rows, :] + carried + skip * x_ref[rows, :].astype(F32)
        y_ref[rows, :] = y
        raw = graw_ref[rows, :]
        gated = y * raw * sigmoid(raw)
        square = gated * gated
        inner = gm_ref[rows, :] * gain * gated
        squares[rows, :] += square[:, 0:128] + square[:, 128:256]
        inners[rows, :] += inner[:, 0:128] + inner[:, 128:256]

    @pl.when(at == pl.num_programs(0) - 1)
    def _():
        ones = jnp.ones((8, 128), F32)
        nt = (((1,), (1,)), ((), ()))
        square_row = lax.dot_general(ones, squares[...], nt, precision=HIGHEST, preferred_element_type=F32)
        inner_row = lax.dot_general(ones, inners[...], nt, precision=HIGHEST, preferred_element_type=F32)
        stats_ref[...] = jnp.where(iota2(square_row.shape, 0) == 0, square_row, inner_row)


def gate_forward(normed, cot, w_gate, w_out, y0, act, early, grow, spread, vectors):
    rows, width = normed.shape
    tokens, channels = y0.shape
    return pl.pallas_call(
        gate_kernel,
        grid=(channels // TILE,),
        in_specs=[
            whole((rows, width)),
            whole((tokens, width)),
            columns(width),
            pl.BlockSpec((TILE, width), lambda j: (j, 0)),
            columns(tokens),
            columns(tokens),
            columns(N),
            pl.BlockSpec((tokens, N), lambda j: (0, channels // N + 1)),
            whole((tokens, 256)),
            columns(256),
            columns(8),
        ],
        out_specs=[columns(tokens), columns(tokens), columns(tokens), whole((8, tokens))],
        out_shape=[sds((tokens, channels))] * 3 + [sds((8, tokens))],
        scratch_shapes=[pltpu.VMEM((tokens, 128), F32), pltpu.VMEM((tokens, 128), F32)],
        compiler_params=params(),
        cost_estimate=cost(16),
        name="gate_forward",
    )(normed, cot, w_gate, w_out, y0, act, early, act, grow, spread, vectors)


def mix_kernel(
    inner_channels, graw_ref, y_ref, gm_ref, x_ref, stats_ref, vec_ref,
    mixed_ref, gg_ref, dy_ref, sums_ref, stats_col,
):
    tokens = y_ref.shape[0]

    @pl.when(pl.program_id(0) == 0)
    def _():
        stats_col[...] = stats_ref[...].T

    gain = vec_ref[1:2, :]
    gain_sum = jnp.zeros((1, TILE), F32)
    skip_sum = jnp.zeros((1, TILE), F32)
    for row in range(0, tokens, Q):
        rows = slice(row, row + Q)
        inv = lax.rsqrt(stats_col[rows, 0:1] * (1.0 / inner_channels) + EPSILON)
        pull = inv * inv * inv * (stats_col[rows, 1:2] * (1.0 / inner_channels))
        raw = graw_ref[rows, :]
        y = y_ref[rows, :]
        gm = gm_ref[rows, :]
        sig = sigmoid(raw)
        act = raw * sig
        gated = y * act
        unit = gated * inv
        mixed_ref[rows, :] = (unit * gain).astype(BF)
        gain_sum = gain_sum + jnp.sum(gm * unit, axis=0, keepdims=True)
        grad_gated = inv * (gm * gain) - gated * pull
        dy = grad_gated * act
        dy_ref[rows, :] = dy
        gg_ref[rows, :] = (grad_gated * y * (sig * (1.0 + raw * (1.0 - sig)))).astype(BF)
        skip_sum = skip_sum + jnp.sum(dy * x_ref[rows, :].astype(F32), axis=0, keepdims=True)
    sums_ref[...] = jnp.zeros_like(sums_ref)
    sums_ref[0:1, :] = gain_sum
    sums_ref[1:2, :] = skip_sum


def mix_backward(inner_channels, graw, y, gm, act, stats, vectors):
    tokens, channels = y.shape
    return pl.pallas_call(
        partial(mix_kernel, inner_channels),
        grid=(channels // TILE,),
        in_specs=[columns(tokens)] * 4 + [whole((128, tokens)), columns(8)],
        out_specs=[columns(tokens)] * 3 + [columns(8)],
        out_shape=[
            sds((tokens, channels), BF),
            sds((tokens, channels), BF),
            sds((tokens, channels)),
            sds((8, channels)),
        ],
        scratch_shapes=[pltpu.VMEM((tokens, 128), F32)],
        compiler_params=params(),
        cost_estimate=cost(10),
        name="mix_backward",
    )(graw, y, gm, act, stats, vectors)


def conv_back_tile(ga_ref, raw_ref, taps_ref, gv_ref, sums_ref, g_pad):
    tokens, width = ga_ref.shape
    taps = taps_ref[...]
    g_pad[0:HALO, :] = jnp.zeros((HALO, width), F32)
    g_pad[HALO + tokens :, :] = jnp.zeros((HALO, width), F32)
    sums = [jnp.zeros((1, width), F32)] * 5
    for row in range(0, tokens, Q):
        pre = conv_rows(raw_ref, taps, row, Q)
        sig = sigmoid(pre)
        g = ga_ref[row : row + Q, :] * (sig * (1.0 + pre * (1.0 - sig)))
        g_pad[HALO + row : HALO + row + Q, :] = g
        for k in range(4):
            moved = raw_ref[pl.ds(HALO - 3 + k + row, Q), :]
            sums[k] = sums[k] + jnp.sum(g * moved, axis=0, keepdims=True)
        sums[4] = sums[4] + jnp.sum(g, axis=0, keepdims=True)
    for row in list(range(HALO, HALO + tokens, Q)) + [0]:
        size = HALO if row == 0 else Q
        total = jnp.zeros((size, width), F32)
        for k in range(4):
            total = total + taps[k : k + 1, :] * g_pad[pl.ds(row + 3 - k, size), :]
        gv_ref[row : row + size, :] = total.astype(BF)
    sums_ref[...] = jnp.zeros_like(sums_ref)
    for k in range(5):
        sums_ref[k : k + 1, :] = sums[k]


def mm_tn(a, b):
    return lax.dot_general(a, b, (((0,), (0,)), ((), ())), preferred_element_type=F32)


def weight_grad_kernel(skips, widths, outs, *refs):
    out_ref = refs[-outs]
    sources = len(skips)
    lefts, rights = refs[:sources], refs[sources:-outs]
    at = 0
    for i, width in enumerate(widths):
        total = None
        for source in range(sources):
            left, right = lefts[source], rights[source * len(widths) + i]
            part = mm_tn(left[skips[source][i] :, :], right[...])
            total = part if total is None else total + part
        out_ref[:, at : at + width] = total
        if outs > 1:
            refs[-1][:, at : at + width] = total.astype(BF)
        at += width


def weight_grad(lefts, rights, low=False):
    height = lefts[0].shape[1]
    widths = [right.shape[1] for right in rights[0]]
    skips = [[left.shape[0] - r.shape[0] for r in group] for left, group in zip(lefts, rights)]
    flat = [r for group in rights for r in group]
    return pl.pallas_call(
        partial(weight_grad_kernel, skips, widths, 1 + low),
        grid=(height // TILE,),
        in_specs=[columns(left.shape[0]) for left in lefts] + [whole(r.shape) for r in flat],
        out_specs=[pl.BlockSpec((TILE, sum(widths)), lambda j: (j, 0))] * (1 + low),
        out_shape=[sds((height, sum(widths))), sds((height, sum(widths)), BF)][: 1 + low],
        compiler_params=params(),
        cost_estimate=cost(8),
        name="weight_grad",
    )(*lefts, *flat)


def input_grad_tile(
    gv_ref, gg_ref, gs_ref, gt_ref, v_ref, g_ref, s_ref, t_ref, tok_ref, inv_ref, out_ref, low_ref, sums_ref
):
    rows = gv_ref.shape[0]
    total = mm_nt(gv_ref[...], v_ref[...]) + mm_nt(gs_ref[...], s_ref[...])
    inner = mm_nt(gg_ref[...], g_ref[...]) + mm_nt(gt_ref[...], t_ref[...])
    out_ref[0:HALO, :] = total[0:HALO, :]
    out_ref[HALO:, :] = total[HALO:, :] + inner
    sums = jnp.zeros((1, TILE), F32)
    for at in [0] + list(range(HALO, rows, Q)):
        size = HALO if at == 0 else Q
        part = out_ref[at : at + size, :]
        low_ref[at : at + size, :] = part.astype(BF)
        unit = tok_ref[at : at + size, :].astype(F32) * inv_ref[at : at + size, 0:1]
        sums = sums + jnp.sum(part * unit, axis=0, keepdims=True)
    sums_ref[...] = jnp.broadcast_to(sums, (8, TILE))


def finish_kernel(
    cols, dps, part, whole_state,
    ga_ref, raw_ref, taps_ref, gg_ref, gt_ref, v_ref, g_ref, picked_ref, tok_ref, inv_ref, g_own_ref,
    o_total, g_cross, gbc, normed, gt_hbm,
    sums_ref, gn_ref, low_ref, norm_ref, joint_ref, o_out, g_out,
    gv_vm, gv_sib, gs_vm, gs_sib, gt_sib, bc_own, bc_land, g_pad,
    raw_part, taps_part, sums_part, g_pad_part, n_own, n_sib, o_vm, g_vm, g_land, sems, local,
):
    step = pl.program_id(0)
    conv_steps = gv_vm.shape[1] // TILE
    input_steps = 2 * n_own.shape[1] // TILE
    dp, row, col = here()
    group = cols // 2
    place = lax.rem(col, group)
    sibling = (dp, 1 - row, col)
    peers = [(dp, row, col ^ by) for by in range(1, group)]
    half = n_own.shape[1]
    piece = o_total.shape[0]
    span = gs_vm.shape[1]
    others = dps - 1
    out_rows = pl.ds(dp * piece, piece)
    g_rows = pl.ds(dp * g_vm.shape[0], g_vm.shape[0])

    def part_at(at):
        return pl.ds(0, span) if whole_state else lanes_at(at, span)

    def o_moves():
        return dp_copies(dps, sems, lambda to, i: o_total, lambda to, i: o_out.at[out_rows, :])

    def g_moves():
        return dp_copies(dps, sems, lambda to, i: g_vm, lambda to, i: g_out.at[g_rows, :], others)

    first = 2 * others
    g_move = lambda: copy_to(g_cross, g_land, sems, first, mirror_of(cols))
    n_move = lambda: copy_to(normed.at[:, lanes_at(1 - row, half)], n_sib, sems, first + 1, sibling)
    t_move = lambda: copy_to(gt_hbm, gt_sib, sems, first + 2, sibling)
    s_move = lambda: copy_to(gs_vm, gs_sib, sems, first + 3, sibling)

    def bc_moves():
        return [
            copy_to(gbc.at[:, part_at(place ^ by)], bc_land.at[by - 1], sems, first + 3 + by, peers[by - 1])
            for by in range(1, group)
        ]

    def v_move(tile):
        lanes = lanes_at(tile, TILE)
        return copy_to(gv_vm.at[:, lanes], gv_sib.at[:, lanes], sems, first + 3 + group + tile, sibling)

    load_bc = pltpu.make_async_copy(gbc.at[:, part_at(place)], bc_own, local.at[0])
    load_n = pltpu.make_async_copy(normed.at[:, lanes_at(row, half)], n_own, local.at[1])
    load_o = pltpu.make_async_copy(o_total, o_vm, local.at[2])
    store_o = pltpu.make_async_copy(o_vm, o_out.at[out_rows, :], local.at[3])
    store_g = pltpu.make_async_copy(g_vm, g_out.at[g_rows, :], local.at[4])

    @at_step(0)
    def _():
        load_o.start()
        load_bc.start()
        load_n.start()
        greet([sibling, mirror_of(cols)] + peers + dp_peers(dps))
        for move in bc_moves() + [g_move()] + o_moves() + [t_move(), n_move()]:
            move.start()
        load_o.wait()
        store_o.start()

    @pl.when(step < conv_steps)
    def _():
        conv_back_tile(
            ga_ref, raw_ref, taps_ref, gv_vm.at[:, lanes_at(step, TILE)], sums_ref, g_pad
        )
        v_move(step).start()

    @pl.when(step == conv_steps)
    def _():
        load_bc.wait()
        for move in bc_moves():
            move.wait_recv()
        for i in range(group - 1):
            bc_own[...] += bc_land[i]
        if whole_state:
            lane = iota2(bc_own.shape, 1)
            mine = (lane >= place * part) & (lane < place * part + part)
            bc_own[...] = jnp.where(mine, bc_own[...], 0.0)
        lanes = part_at(place)
        sums_ref[...] = jnp.zeros_like(sums_ref)
        raw_part[...] = raw_ref[:, lanes]
        taps_part[...] = taps_ref[:, lanes]
        conv_back_tile(bc_own, raw_part, taps_part, gs_vm, sums_part, g_pad_part)
        sums_ref[:, 0:span] = sums_part[...]
        s_move().start()
        g_move().wait_recv()
        g_vm[...] = g_own_ref[...] + g_land[...].astype(F32)
        for move in g_moves():
            move.start()
        store_g.start()

    @pl.when((step > conv_steps) & (step <= conv_steps + input_steps))
    def _():
        input_grad_tile(
            gv_vm, gg_ref, gs_vm, gt_ref, v_ref, g_ref, picked_ref.at[:, part_at(place)],
            picked_ref.at[:, pl.ds(TILE, 128)], tok_ref, inv_ref, gn_ref, low_ref, norm_ref,
        )

    @pl.when(step == conv_steps + input_steps + 1)
    def _():
        load_n.wait()
        for move in [n_move(), t_move(), s_move()]:
            move.wait_recv()
        for tile in range(conv_steps):
            v_move(tile).wait_recv()

    @pl.when(step > conv_steps + input_steps)
    def _():
        lanes = lanes_at(step - conv_steps - input_steps - 1, TILE)
        channels = gv_vm.shape[1]
        left, left_sib = n_own[:, lanes], n_sib[:, lanes]
        joint_ref[:, 0:channels] = mm_tn(left, gv_vm[...]) + mm_tn(left_sib, gv_sib[...])
        joint_ref[:, channels : channels + span] = mm_tn(left, gs_vm[...]) + mm_tn(left_sib, gs_sib[...])
        joint_ref[:, channels + span :] = mm_tn(left[HALO:, :], gt_ref[...]) + mm_tn(left_sib[HALO:, :], gt_sib[...])

    @at_step(pl.num_programs(0) - 1)
    def _():
        store_o.wait()
        store_g.wait()
        for move in o_moves() + g_moves():
            move.wait()
        for move in bc_moves() + [g_move(), n_move(), t_move(), s_move()]:
            move.wait_send()
        for tile in range(conv_steps):
            v_move(tile).wait_send()


def finish(
    cols, dps, part, ga, raw, taps, gg, gt, w_value, w_gate, picked, tokens_in, inv_rms, g_own, o_total, g_cross,
    gbc, normed,
):
    tokens, channels = ga.shape
    rows, width = normed.shape
    half = width // 2
    whole_state = part % 128 != 0
    span = 2 * N if whole_state else part
    group = cols // 2
    conv_steps, input_steps, weight_steps = channels // TILE, width // TILE, half // TILE
    piece = o_total.shape[0]
    joint_width = channels + span + 128

    def clamp(first, count):
        return lambda i: jnp.clip(i - first, 0, count - 1)

    conv, input_at = clamp(0, conv_steps), clamp(conv_steps + 1, input_steps)
    both = clamp(0, conv_steps + 1)
    weight_at = clamp(conv_steps + 1 + input_steps, weight_steps)
    lanes = lambda at, count: pl.BlockSpec((count, TILE), lambda i: (0, at(i)))
    slab = lambda at, size: pl.BlockSpec((TILE, size), lambda i: (at(i), 0))
    vmem = pltpu.VMEM
    copies = 2 * (dps - 1) + 3 + group + conv_steps
    return pl.pallas_call(
        partial(finish_kernel, cols, dps, part, whole_state),
        grid=(conv_steps + 1 + input_steps + weight_steps,),
        in_specs=[
            lanes(conv, tokens),
            lanes(both, rows),
            lanes(both, 8),
            whole(gg.shape),
            whole(gt.shape),
            slab(input_at, channels),
            slab(input_at, channels),
            slab(input_at, TILE + 128),
            lanes(input_at, rows),
            whole(inv_rms.shape),
            whole(g_own.shape),
        ] + [ANY] * 5,
        out_specs=[
            lanes(both, 8), lanes(input_at, rows), lanes(input_at, rows), lanes(input_at, 8),
            slab(weight_at, joint_width), ANY, ANY,
        ],
        out_shape=[
            sds((8, channels + TILE)), sds((rows, width)), sds((rows, width), BF), sds((8, width)),
            sds((half, joint_width)), sds((dps * piece, o_total.shape[1])),
            sds((dps * g_own.shape[0], g_own.shape[1])),
        ],
        scratch_shapes=[
            vmem((rows, channels), BF), vmem((rows, channels), BF), vmem((rows, span), BF), vmem((rows, span), BF),
            vmem((tokens, 128), BF), vmem((tokens, span), F32), vmem((max(group - 1, 1), tokens, span), F32),
            vmem((tokens + 2 * HALO, TILE), F32), vmem((rows, span), F32), vmem((8, span), F32),
            vmem((8, span), F32), vmem((tokens + 2 * HALO, span), F32),
            vmem((rows, half), BF), vmem((rows, half), BF),
            vmem(o_total.shape, F32), vmem(g_own.shape, F32), vmem(g_own.shape, BF),
            pltpu.SemaphoreType.DMA((2, copies)),
            pltpu.SemaphoreType.DMA((5,)),
        ],
        compiler_params=remote_params(5),
        cost_estimate=cost(55),
        name="finish",
    )(
        ga, raw, taps, gg, gt, w_value, w_gate, picked, tokens_in, inv_rms, g_own, o_total, g_cross, gbc, normed, gt,
    )


def settle_kernel(
    cols, dps, heads, span, gn, gnb, joint, flat, tok, cot, gain,
    tg_out, v_out, ext_out, flat_out,
    mine_a, mine_b, send_a, rec_a, send_b, rec_b, tot_a, tot_b,
    z_send, z_land, step_land, state_land, ext, acc, flat_land,
    gn_own, gn_land, halo_land, tok_vm, cot_vm, gain_vm, local, send, recv,
):
    dp, row, col = here()
    group = cols // 2
    place = lax.rem(col, group)
    half, wide_a = mine_a.shape
    shard = mine_b.shape[1]
    piece = tot_a.shape[0]
    count, width = gn_own.shape
    sibling = (dp, 1 - row, col)
    mirror = (dp, row, cols - 1 - col)
    col_peer = lambda by: (dp, row, col ^ by)
    dp_peer = lambda by: (dp ^ by, row, col)
    used = [0]
    started = []

    def remote(src, dst, device):
        i = used[0]
        used[0] += 1
        return pltpu.make_async_remote_copy(
            src_ref=src, dst_ref=dst, send_sem=send.at[i], recv_sem=recv.at[i],
            device_id=device, device_id_type=pl.DeviceIdType.MESH,
        )

    def launch(src, dst, device):
        copy = remote(src, dst, device)
        copy.start()
        started.append(copy)
        return copy

    def arrive(copies):
        for copy in copies:
            copy.wait_recv()

    kept = [0]

    def keep(src, dst):
        copy = pltpu.make_async_copy(src, dst, local.at[kept[0]])
        kept[0] += 1
        copy.start()
        return copy

    part_a, part_b = pl.ds(shard, wide_a), pl.ds(0, shard)
    load_a = keep(joint.at[:, part_a], mine_a)
    load_b = keep(joint.at[:, part_b], mine_b)
    load_flat = keep(flat, acc)
    loads = [
        keep(gn.at[pl.ds(HALO + place * count, count), :], gn_own),
        keep(tok, tok_vm),
        keep(cot, cot_vm),
        keep(gain, gain_vm),
    ]
    greet(
        [sibling]
        + [col_peer(by) for by in range(1, cols)]
        + [dp_peer(by) for by in range(1, dps)]
    )
    gn_moves = [
        launch(gnb.at[pl.ds(HALO + (place ^ by) * count, count), :], gn_land.at[by - 1], col_peer(by))
        for by in range(1, group)
    ]
    halo_at = used[0]
    used[0] += group
    halos = [
        pltpu.make_async_remote_copy(
            src_ref=gnb.at[pl.ds(0, HALO), :], dst_ref=halo_land.at[j], send_sem=send.at[halo_at + j],
            recv_sem=recv.at[halo_at + j], device_id=(dp, row, group - 1),
            device_id_type=pl.DeviceIdType.MESH,
        )
        for j in range(group)
    ]
    for j in range(group):
        pl.when(col == group + j)(halos[j].start)

    flat_steps = [sibling]
    by = 1
    while by < dps:
        flat_steps.append(dp_peer(by))
        by *= 2
    by = 1
    while by < cols:
        flat_steps.append(col_peer(by))
        by *= 2
    flat_moves = []
    flat_taken = [0]

    def flat_next():
        if flat_taken[0] < len(flat_moves):
            flat_moves[-1].wait_recv()
            flat_moves[-1].wait_send()
            acc[...] += flat_land[flat_taken[0]]
            flat_taken[0] += 1
        if len(flat_moves) < len(flat_steps):
            at = len(flat_moves)
            move = remote(acc, flat_land.at[at], flat_steps[at])
            move.start()
            flat_moves.append(move)

    load_flat.wait()
    flat_next()

    def hand_out(load, mine, total, sends, recs):
        load.wait()
        moves = []
        for by in range(1, dps):
            rows = pl.ds(pl.multiple_of((dp ^ by) * piece, 16), piece)
            sends[by - 1] = mine[rows, :].astype(BF)
            moves.append(launch(sends.at[by - 1], recs.at[by - 1], dp_peer(by)))
        total[...] = mine[pl.ds(pl.multiple_of(dp * piece, 16), piece), :]
        return moves

    moves_a = hand_out(load_a, mine_a, tot_a, send_a, rec_a)
    flat_next()
    moves_b = hand_out(load_b, mine_b, tot_b, send_b, rec_b)
    flat_next()
    arrive(moves_a)
    for by in range(1, dps):
        tot_a[...] += rec_a[by - 1].astype(F32)
    z_send[...] = tot_a[:, 0:shard].astype(BF)
    z_move = launch(z_send, z_land, mirror)
    step_move = launch(tot_a.at[:, pl.ds(shard + span, 128)], step_land, mirror)
    state_block = tot_a.at[:, pl.ds(shard, span)]
    state_moves = [launch(state_block, state_land.at[col], col_peer(by)) for by in range(1, cols)]
    state_land[col] = tot_a[:, shard : shard + span]
    flat_next()
    arrive(moves_b)
    for by in range(1, dps):
        tot_b[...] += rec_b[by - 1].astype(F32)
    arrive([z_move, step_move])
    tot_b[...] += z_land[...].astype(F32)
    ext[:, 0:128] = tot_a[:, shard + span : shard + span + 128] + pltpu.roll(step_land[...], 128 - heads, 1)
    out_rows = pl.ds(dp * piece, piece)
    v_moves = [launch(tot_b, v_out.at[out_rows, :], dp_peer(by)) for by in range(1, dps)]
    v_keep = keep(tot_b, v_out.at[out_rows, :])
    arrive(state_moves)
    if span == 2 * N:
        ext[:, 128:] = sum(state_land[i] for i in range(cols))
    else:
        part = col // 2
        ext[:, 128:] = state_land[part] + state_land[part + group]
    e_moves = [launch(ext, ext_out.at[out_rows, :], dp_peer(by)) for by in range(1, dps)]
    e_keep = keep(ext, ext_out.at[out_rows, :])
    flat_next()
    for copy in loads:
        copy.wait()
    arrive(gn_moves)
    for by in range(1, group):
        gn_own[...] += gn_land[by - 1].astype(F32)

    @pl.when(col == group - 1)
    def _():
        for copy in halos:
            copy.wait_recv()
        for j in range(group):
            gn_own[count - HALO :, :] += halo_land[j].astype(F32)

    for j in range(group):
        pl.when(col == group + j)(halos[j].wait_send)
    flat_next()
    step = 64
    for at in range(0, count, step):
        rows = slice(at, at + step)
        values = tok_vm[rows, :].astype(F32)
        inv = lax.rsqrt(jnp.mean(values * values, axis=-1, keepdims=True) + EPSILON)
        unit = values * inv
        pulled = gn_own[rows, :] * gain_vm[0:1, :]
        mean = jnp.mean(pulled * unit, axis=-1, keepdims=True)
        gn_own[rows, :] = cot_vm[rows, :].astype(F32) + inv * (pulled - unit * mean)
    tg_keep = keep(gn_own, tg_out)
    while flat_taken[0] < len(flat_steps):
        flat_next()
    flat_keep = keep(acc, flat_out)
    arrive(v_moves)
    arrive(e_moves)
    for copy in [v_keep, e_keep, tg_keep, flat_keep]:
        copy.wait()
    for copy in started:
        copy.wait_send()


def settle(cols, dps, heads, span, gn, gnb, joint, flat, tokens, cotangent, gain, shard):
    half, wide = joint.shape
    width, wide_a = 2 * half, wide - shard
    piece = half // dps
    count = tokens.shape[0]
    group = cols // 2
    any_spec = pl.BlockSpec(memory_space=pl.ANY)
    steps = (dps.bit_length() - 1) + (cols.bit_length() - 1) + 1
    copies = (group - 1) + group + steps + 4 * (dps - 1) + 2 + (cols - 1)
    vmem = pltpu.VMEM
    return pl.pallas_call(
        partial(settle_kernel, cols, dps, heads, span),
        in_specs=[any_spec] * 7,
        out_specs=[any_spec] * 4,
        out_shape=[
            sds((count, width)), sds((half, shard)), sds((half, 128 + span)), sds(flat.shape),
        ],
        scratch_shapes=[
            vmem((half, wide_a), F32), vmem((half, shard), F32),
            vmem((dps - 1, piece, wide_a), BF), vmem((dps - 1, piece, wide_a), BF),
            vmem((dps - 1, piece, shard), BF), vmem((dps - 1, piece, shard), BF),
            vmem((piece, wide_a), F32), vmem((piece, shard), F32),
            vmem((piece, shard), BF), vmem((piece, shard), BF),
            vmem((piece, 128), F32), vmem((cols, piece, span), F32),
            vmem((piece, 128 + span), F32),
            vmem(flat.shape, F32), vmem((steps,) + flat.shape, F32),
            vmem((count, width), F32), vmem((max(group - 1, 1), count, width), BF),
            vmem((group, HALO, width), BF),
            vmem((count, width), BF), vmem((count, width), BF), vmem((1, width), F32),
            pltpu.SemaphoreType.DMA((11,)),
            pltpu.SemaphoreType.DMA((copies,)),
            pltpu.SemaphoreType.DMA((copies,)),
        ],
        compiler_params=pltpu.CompilerParams(
            collective_id=2, has_side_effects=True, vmem_limit_bytes=VMEM_LIMIT
        ),
        cost_estimate=cost(90),
        name="settle",
    )(gn, gnb, joint, flat, tokens, cotangent, gain)


def flips(size, by):
    return [(i, i ^ by) for i in range(size)]


def butterfly(values, axis):
    size = lax.axis_size(axis)
    by = 1
    while by < size:
        values = values + lax.ppermute(values, axis, flips(size, by))
        by *= 2
    return values


def at_rows(values, index, size):
    return lax.dynamic_slice_in_dim(values, index * size, size, axis=0)


def collect_dp(piece, dp):
    size = lax.axis_size("dp")
    rows = piece.shape[0]
    out = jnp.zeros((size * rows,) + piece.shape[1:], piece.dtype)
    out = lax.dynamic_update_slice_in_dim(out, piece, dp * rows, 0)
    for by in range(1, size):
        other = lax.ppermute(piece, "dp", flips(size, by))
        out = lax.dynamic_update_slice_in_dim(out, other, (dp ^ by) * rows, 0)
    return out


def swap_core(values):
    return lax.ppermute(values, "row", [(0, 1), (1, 0)])


def per_device(
    tokens, norm_gain, w_gate, w_value, w_state, w_step, conv_value, bias_value, conv_state,
    bias_state, a_log, d_skip, dt_bias, mix_gain, w_out, cotangent,
):
    cols, rows_n, dps = lax.axis_size("col"), lax.axis_size("row"), lax.axis_size("dp")
    col, row, dp = lax.axis_index("col"), lax.axis_index("row"), lax.axis_index("dp")
    group = cols // 2
    place = lax.rem(col, group)
    local, width = tokens.shape
    span = local * group
    half_width = width // 2
    shard = w_value.shape[1]
    channels = 2 * shard
    heads = a_log.shape[0]
    inner_channels = shard * cols
    state_all = w_state.shape[1] * cols
    mirror = [(i, cols - 1 - i) for i in range(cols)]
    forth = [(i, cols - 1 - i) for i in range(group)]
    back = [(cols - 1 - i, i) for i in range(group)]

    def ring(by):
        return [(i, (i // group) * group + (i % group + by) % group) for i in range(cols)]

    state_width = w_state.shape[1]
    small = jnp.pad(
        jnp.concatenate([w_state, w_step], axis=1), ((0, 0), (0, 128 - state_width - heads))
    )
    heads_row = jnp.pad(
        jnp.concatenate([d_skip, a_log, dt_bias]), (0, shard - 3 * heads)
    )[None]
    state_rows = jnp.concatenate([conv_state.T, bias_state[None]], axis=0)
    vec = jnp.concatenate(
        [
            conv_value.T, bias_value[None], mix_gain[None], heads_row, jnp.zeros((1, shard), BF),
            jnp.pad(state_rows, ((0, 3), (0, shard - state_width))),
        ],
        axis=0,
    )
    group_tokens, value_full, gate_full, out_full, small_full, vecs = import_all(
        cols, dps, tokens, w_value, w_gate, w_out, small, vec
    )
    cotangent, group_tokens = lax.optimization_barrier((cotangent, group_tokens))
    from_col = lax.broadcasted_iota(jnp.int32, (cols * 128, TILE + 128), 0) // 128
    from_lane = lax.broadcasted_iota(jnp.int32, (cols * 128, TILE + 128), 0) % 128
    to = lax.broadcasted_iota(jnp.int32, (cols * 128, TILE + 128), 1)
    head_to = to - TILE
    is_state = (to < TILE) & (from_lane < state_width) & (from_col * state_width + from_lane == to)
    is_own = (from_col == col) & (head_to < heads) & (from_lane == state_width + head_to)
    is_mirror = (from_col == cols - 1 - col) & (head_to >= heads) & (head_to < 2 * heads)
    is_mirror = is_mirror & (from_lane == state_width + head_to - heads)
    pick = (is_state | ((head_to >= 0) & (is_own | is_mirror))).astype(BF)

    def gather_tokens(values):
        out = jnp.zeros((span, width), values.dtype)
        out = lax.dynamic_update_slice_in_dim(out, values, place * local, 0)
        for by in range(1, group):
            other = lax.ppermute(values, "col", ring(by))
            at = lax.rem(place - by + group, group)
            out = lax.dynamic_update_slice_in_dim(out, other, at * local, 0)
        return out

    vecs = vecs.astype(F32)
    both = jnp.concatenate(
        [
            lax.dynamic_index_in_dim(vecs, col, 0, keepdims=False),
            lax.dynamic_index_in_dim(vecs, cols - 1 - col, 0, keepdims=False),
        ],
        axis=1,
    )
    state_vecs = jnp.transpose(vecs[:, 8:16, :state_width], (1, 0, 2)).reshape(8, state_all)
    taps = jnp.concatenate([both[0:8], state_vecs], axis=1)

    def both_heads(at):
        return jnp.concatenate(
            [both[6, at * heads : (at + 1) * heads], both[6, shard + at * heads : shard + (at + 1) * heads]]
        )

    skip_both, a_both, dt_both = both_heads(0), both_heads(1), both_heads(2)
    vectors = jnp.concatenate(
        [jnp.repeat(skip_both, HEAD)[None], both[5:6], jnp.zeros((6, channels), F32)], axis=0
    )
    rate = -jnp.exp(a_both)
    head_rows = jnp.pad(jnp.stack([dt_both, rate]), ((0, 6), (0, 128 - 2 * heads)))
    head_of = np.arange(channels) // HEAD
    one_hot = (np.arange(128)[:, None] == head_of[None, :]).astype(np.float32)
    spread = jnp.asarray(np.concatenate([one_hot, one_hot], axis=0), BF)
    gather = jnp.asarray(one_hot.T, BF)

    gain = norm_gain.astype(F32)
    raw, act, normed, step_in, step, cum, grow, offs, inv_rms, picked = project(
        group_tokens, gain[None], value_full, small_full, pick, taps, head_rows
    )
    states, final_state = scan_states(act, step, cum, spread, channels)

    def cross(values, pairs):
        moved = lax.ppermute(values, "col", pairs)
        return jnp.concatenate([moved[:, shard:], moved[:, :shard]], axis=1)

    early = cross(final_state, forth)
    y0 = scan_forward(act, step, cum, spread, states, channels)
    group_cot = gather_tokens(cotangent)
    graw, y, gm, stats = gate_forward(
        normed, group_cot, gate_full, out_full, y0, act, early, grow, spread, vectors
    )
    by = 1
    while by < group:
        stats = stats + lax.ppermute(stats, "col", flips(cols, by))
        by *= 2
    stats_pad = jnp.pad(stats, ((0, 120), (0, 0)))
    mixed, grad_gate, dy, mix_sums = mix_backward(inner_channels, graw, y, gm, act, stats_pad, vectors)

    after, first_grad = scan_grad_states(dy, act, cum, spread)
    late = cross(first_grad, back)
    branch_rows = lambda at: mm(at_rows(mixed, at, local), out_full)
    parts = jnp.stack([branch_rows(place ^ by).astype(BF) for by in range(1, group)])
    branch = branch_rows(place)

    def my_half(values):
        mine = lax.dynamic_slice_in_dim(values, row * half_width, half_width, 1)
        return [mine, swap_core(lax.dynamic_slice_in_dim(values, (1 - row) * half_width, half_width, 1))]

    out_full_sum, out_low = weight_grad(
        [mixed, swap_core(mixed)], [[half] for half in my_half(group_cot)], low=True
    )
    normed_halves = my_half(normed)
    gate_full_sum, gate_low = weight_grad(normed_halves, [[grad_gate], [swap_core(grad_gate)]], low=True)
    by_out = (2, dps, shard // dps, half_width)
    by_gate = (dps, half_width // dps, channels)
    ga, grad_step, gbc, head_sums, out_total, gate_own, gate_cross, branch_in = scan_backward(
        cols, dps, dy, act, y, step, cum, step_in, spread, gather, after, states, early, offs, head_rows, vectors,
        out_low.reshape(by_out), out_full_sum.reshape(by_out), gate_low.reshape(by_gate),
        gate_full_sum.reshape(by_gate), late, parts,
    )
    block_out = (tokens.astype(F32) + branch + jnp.sum(branch_in.astype(F32), axis=0)).astype(BF)
    state_part = state_all // group

    value_sums, grad_normed, grad_normed_low, norm_sums, joint, sum_out, sum_gate = finish(
        cols, dps, state_part, ga, raw, taps, grad_gate, grad_step, value_full, gate_full, picked, group_tokens,
        inv_rms, gate_own, out_total, gate_cross, gbc, normed,
    )
    whole_state = state_part % 128 != 0
    span = state_all if whole_state else state_part

    wide = jnp.concatenate([value_sums[:5, :channels], mix_sums[0:1]], axis=0)
    wide_all = jnp.zeros((6, inner_channels), F32)
    wide_all = lax.dynamic_update_slice_in_dim(wide_all, wide[:, :shard], col * shard, 1)
    wide_all = lax.dynamic_update_slice_in_dim(wide_all, wide[:, shard:], (cols - 1 - col) * shard, 1)
    state_wide = jnp.zeros((5, state_all), F32)
    state_wide = lax.dynamic_update_slice_in_dim(
        state_wide, value_sums[:5, channels : channels + span], 0 if whole_state else place * state_part, 1
    )
    skip_heads = jnp.sum(mix_sums[1].reshape(2 * heads, HEAD), axis=1)
    head_parts = jnp.stack([head_sums[0, : 2 * heads] * rate, skip_heads, head_sums[1, : 2 * heads]])
    head_all = jnp.zeros((3, heads * cols), F32)
    head_all = lax.dynamic_update_slice_in_dim(head_all, head_parts[:, :heads], col * heads, 1)
    head_all = lax.dynamic_update_slice_in_dim(head_all, head_parts[:, heads:], (cols - 1 - col) * heads, 1)
    lengths = [wide_all.size, state_wide.size, head_all.size, width]
    flat = jnp.concatenate(
        [wide_all.reshape(-1), state_wide.reshape(-1), head_all.reshape(-1), norm_sums[0]]
    )
    flat = jnp.pad(flat, (0, -flat.size % 1024)).reshape(-1, 128)
    tokens_grad, sum_value, extra, flat = settle(
        cols, dps, heads, span, grad_normed, grad_normed_low, joint, flat, tokens, cotangent, gain[None], shard
    )
    sum_step = extra[:, :heads]
    sum_state = lax.dynamic_slice_in_dim(
        extra, 128 + (col if whole_state else lax.rem(col, cols // group)) * state_width, state_width, axis=1
    )
    flat = flat.reshape(-1)
    ends = [sum(lengths[: i + 1]) for i in range(4)]
    wide_all = flat[: ends[0]].reshape(6, inner_channels)
    state_wide = flat[ends[0] : ends[1]].reshape(5, state_all)
    head_all = flat[ends[1] : ends[2]].reshape(3, heads * cols)
    norm_total = flat[ends[2] : ends[3]]
    wide_own = lax.dynamic_slice_in_dim(wide_all, col * shard, shard, axis=1)
    state_own = lax.dynamic_slice_in_dim(state_wide, col * state_width, state_width, axis=1)
    head_own = lax.dynamic_slice_in_dim(head_all, col * heads, heads, axis=1)

    return (
        block_out,
        tokens_grad,
        norm_total,
        sum_gate,
        sum_value,
        sum_state,
        sum_step,
        wide_own[:4].T,
        wide_own[4],
        state_own[:4].T,
        state_own[4],
        head_own[0],
        head_own[1],
        head_own[2],
        wide_own[5],
        sum_out,
    )


def solution(mesh):
    rows = P(("dp", "row", "col"), None)
    grid = P("row", "col")
    vec = P("col")
    taps = P("col", None)
    return jax.shard_map(
        per_device,
        mesh=mesh,
        in_specs=(
            rows, P(), grid, grid, grid, grid, taps, vec, taps, vec, vec, vec, vec, vec,
            P("col", "row"), rows,
        ),
        out_specs=(
            rows, rows, P(), grid, grid, grid, grid, taps, vec, taps, vec, vec, vec, vec, vec,
            P("col", "row"),
        ),
        check_vma=False,
    )
```

```python
from functools import partial

import jax
import jax.numpy as jnp
import numpy as np
from jax import lax
from jax.experimental import pallas as pl
from jax.experimental.pallas import tpu as pltpu
from jax.sharding import PartitionSpec as P

BF = jnp.bfloat16
F32 = jnp.float32
EPSILON = 1e-05
N = 128
Q = 128
HEAD = 64
HALO = 16
TILE = 256
HIGHEST = lax.Precision.HIGHEST
VMEM_LIMIT = 56 * 2**20


def mm(a, b):
    return lax.dot_general(a, b, (((1,), (0,)), ((), ())), preferred_element_type=F32)


def mm_nt(a, b):
    return lax.dot_general(a, b, (((1,), (1,)), ((), ())), preferred_element_type=F32)


def mm_exact(a, b):
    return lax.dot_general(
        a, b, (((1,), (0,)), ((), ())), precision=HIGHEST, preferred_element_type=F32
    )


def split2(values):
    high = values.astype(BF)
    return high, (values - high.astype(F32)).astype(BF)


def sigmoid(values):
    return 1.0 / (1.0 + jnp.exp(-values))


def iota2(shape, axis):
    return lax.broadcasted_iota(jnp.int32, shape, axis)


def params(*names):
    return pltpu.CompilerParams(
        dimension_semantics=names or ("arbitrary",), vmem_limit_bytes=VMEM_LIMIT
    )


def cost(micros):
    return pl.CostEstimate(flops=0, bytes_accessed=int(micros * 3.0e6), transcendentals=0)


def whole(shape):
    return pl.BlockSpec(shape, lambda *_: (0,) * len(shape))


def columns(rows, width=TILE):
    return pl.BlockSpec((rows, width), lambda j: (0, j))


def sds(shape, dtype=F32):
    return jax.ShapeDtypeStruct(shape, dtype)


def here():
    return lax.axis_index("dp"), lax.axis_index("row"), lax.axis_index("col")


def lanes_at(index, size):
    return pl.ds(pl.multiple_of(index * size, 128), size)


def greet(others):
    barrier = pltpu.get_barrier_semaphore()
    for other in others:
        pl.semaphore_signal(barrier, inc=1, device_id=other, device_id_type=pl.DeviceIdType.MESH)
    pl.semaphore_wait(barrier, len(others))


def at_step(step):
    return pl.when(pl.program_id(0) == step)


def copy_to(src, dst, sems, i, device):
    return pltpu.make_async_remote_copy(
        src_ref=src, dst_ref=dst, send_sem=sems.at[0, i], recv_sem=sems.at[1, i],
        device_id=device, device_id_type=pl.DeviceIdType.MESH,
    )


def dp_copies(dps, sems, src_of, dst_of, first=0):
    dp, row, col = here()
    return [
        copy_to(src_of(dp ^ by, by - 1), dst_of(dp ^ by, by - 1), sems, first + by - 1, (dp ^ by, row, col))
        for by in range(1, dps)
    ]


def dp_peers(dps):
    dp, row, col = here()
    return [(dp ^ by, row, col) for by in range(1, dps)]


def mirror_of(cols):
    dp, row, col = here()
    return (dp, row, cols - 1 - col)


def remote_params(collective_id):
    return pltpu.CompilerParams(
        dimension_semantics=("arbitrary",), vmem_limit_bytes=VMEM_LIMIT, collective_id=collective_id,
        has_side_effects=True,
    )


ANY = pl.BlockSpec(memory_space=pl.ANY)


def import_kernel(
    cols, dps, tok, wv, sw, vec, tg, vf, sf, vecs, zeros, tok_vm, w_vm, s_vm, vec_vm, local, send, recv,
):
    dp, row, col = here()
    group = cols // 2
    place = lax.rem(col, group)
    half, shard = wv.shape
    count = tok.shape[0]
    piece = half // dps
    sibling = (dp, 1 - row, col)
    mirror = (dp, row, cols - 1 - col)
    col_peer = lambda by: (dp, row, col ^ by)
    dp_peer = lambda by: (dp ^ by, row, col)
    greet(
        [sibling]
        + [col_peer(by) for by in range(1, cols)]
        + [dp_peer(by) for by in range(1, dps)]
    )
    used = [0]
    started = []

    def remote(src, dst, device):
        i = used[0]
        used[0] += 1
        return pltpu.make_async_remote_copy(
            src_ref=src, dst_ref=dst, send_sem=send.at[i], recv_sem=recv.at[i],
            device_id=device, device_id_type=pl.DeviceIdType.MESH,
        )

    def launch(src, dst, device):
        copy = remote(src, dst, device)
        copy.start()
        started.append(copy)
        return copy

    def keep(i, src, dst):
        copy = pltpu.make_async_copy(src, dst, local.at[i])
        copy.start()
        return copy

    my_rows = pl.ds(row * half, half)
    my_piece = pl.ds(row * half + dp * piece, piece)
    own, other = pl.ds(0, shard), pl.ds(shard, shard)
    src_piece = pl.ds(dp * piece, piece)

    staged = [
        keep(6, vec, vec_vm),
        keep(0, sw.at[src_piece, :], s_vm),
        keep(2, tok, tok_vm),
        keep(3, wv, w_vm),
    ]
    s_cross = [
        launch(sw.at[src_piece, :], sf.at[my_piece, lanes_at(col, 128)], col_peer(by))
        for by in range(1, cols)
    ]
    v_cross = launch(wv.at[src_piece, :], vf.at[my_piece, other], mirror)
    vec_cross = [launch(vec, vecs.at[col], col_peer(by)) for by in range(1, cols)]
    my_tokens = tg.at[pl.ds(HALO + place * count, count), :]
    tok_cross = [launch(tok, my_tokens, col_peer(by)) for by in range(1, group)]
    halo_src = tok.at[pl.ds(count - HALO, HALO), :]
    halo_dst = tg.at[pl.ds(0, HALO), :]
    halo_at = used[0]
    used[0] += group
    halos = [
        pltpu.make_async_remote_copy(
            src_ref=halo_src, dst_ref=halo_dst, send_sem=send.at[halo_at + j], recv_sem=recv.at[halo_at],
            device_id=(dp, row, group + j), device_id_type=pl.DeviceIdType.MESH,
        )
        for j in range(group)
    ]

    @pl.when(col == group - 1)
    def _():
        for copy in halos:
            copy.start()

    zeros[...] = jnp.zeros_like(zeros)

    @pl.when(col < group)
    def _():
        clear = pltpu.make_async_copy(zeros, halo_dst, local.at[1])
        clear.start()
        clear.wait()

    v_own = launch(wv, vf.at[my_rows, own], sibling)
    for copy in staged:
        copy.wait()
    small_own = keep(0, s_vm, sf.at[my_piece, lanes_at(col, 128)])
    kept = [
        keep(6, vec_vm, vecs.at[col]),
        keep(2, tok_vm, my_tokens),
        keep(3, w_vm, vf.at[my_rows, own]),
    ]

    def spread_out(ref):
        return [launch(ref, ref, dp_peer(by)) for by in range(1, dps)]

    def arrive(copies):
        for copy in copies:
            copy.wait_recv()

    arrive(s_cross)
    small_own.wait()
    s_dp = spread_out(sf.at[my_piece, :])
    arrive([v_cross])
    v_dp = spread_out(vf.at[my_piece, other])
    arrive(s_dp)
    last = [launch(sf.at[my_rows, :], sf.at[my_rows, :], sibling)]
    arrive(v_dp)
    last += [launch(vf.at[my_rows, other], vf.at[my_rows, other], sibling)]
    arrive(last)
    arrive([v_own])
    arrive(vec_cross)
    arrive(tok_cross)

    @pl.when(col >= group)
    def _():
        halos[0].wait_recv()

    @pl.when(col == group - 1)
    def _():
        for copy in halos:
            copy.wait_send()

    for copy in kept:
        copy.wait()
    for copy in started:
        copy.wait_send()


def import_all(cols, dps, tokens, w_value, small, vec):
    half, shard = w_value.shape
    count, width = tokens.shape
    any_spec = pl.BlockSpec(memory_space=pl.ANY)
    copies = 1 + 2 * (cols - 1) + (cols // 2 - 1) + cols // 2 + 1 + 2 * (dps - 1) + 2
    return pl.pallas_call(
        partial(import_kernel, cols, dps),
        in_specs=[any_spec] * 4,
        out_specs=[any_spec] * 4,
        out_shape=[
            sds((HALO + count * (cols // 2), width), BF),
            sds((2 * half, 2 * shard), BF),
            sds((2 * half, cols * 128), BF),
            sds((cols,) + vec.shape, BF),
        ],
        scratch_shapes=[
            pltpu.VMEM((HALO, width), BF),
            pltpu.VMEM((count, width), BF),
            pltpu.VMEM((half, shard), BF),
            pltpu.VMEM((half // dps, 128), BF),
            pltpu.VMEM(vec.shape, BF),
            pltpu.SemaphoreType.DMA((7,)),
            pltpu.SemaphoreType.DMA((copies,)),
            pltpu.SemaphoreType.DMA((copies,)),
        ],
        compiler_params=pltpu.CompilerParams(
            collective_id=1, has_side_effects=True, vmem_limit_bytes=VMEM_LIMIT
        ),
        cost_estimate=cost(45),
        name="import_all",
    )(tokens, w_value, small, vec)


def conv_rows(raw_ref, taps, start, size):
    total = taps[4:5, :] + jnp.zeros((size, taps.shape[1]), F32)
    for k in range(4):
        total = total + taps[k : k + 1, :] * raw_ref[pl.ds(HALO - 3 + k + start, size), :]
    return total


def normalize(tok_ref, gain_ref, normed_ref, inv_ref):
    tokens = tok_ref.shape[0] - HALO
    for at in [0] + list(range(HALO, HALO + tokens, Q)):
        size = HALO if at == 0 else Q
        values = tok_ref[at : at + size, :].astype(F32)
        inv = lax.rsqrt(jnp.mean(values * values, axis=-1, keepdims=True) + EPSILON)
        normed_ref[at : at + size, :] = (values * inv * gain_ref[0:1, :]).astype(BF)
        inv_ref[at : at + size, :] = jnp.broadcast_to(inv, (size, 128))


def project_steps(
    small_ref, pick_ref, head_ref, normed_ref, raw_ref, stepin_ref, step_ref, cum_ref, grow_ref, offs_ref,
    picked_ref,
):
    tokens = step_ref.shape[0]
    picked = mm(small_ref[...], pick_ref[...]).astype(BF)
    picked_ref[...] = picked
    raw_ref[...] = mm(normed_ref[...], picked[:, :TILE])
    step_in = mm(normed_ref[HALO:, :], picked[:, TILE:]) + head_ref[0:1, :]
    small = jnp.exp(-jnp.abs(step_in))
    plus = 1.0 + small
    safe = jnp.where(plus == 1.0, 1.0, plus - 1.0)
    log_part = jnp.where(plus == 1.0, small, jnp.log(plus) * (small / safe))
    step = jnp.maximum(step_in, 0.0) + log_part
    stepin_ref[...] = step_in
    step_ref[...] = step
    falls = step * head_ref[1:2, :]
    lower = (iota2((Q, Q), 0) >= iota2((Q, Q), 1)).astype(F32)
    before = jnp.zeros((1, 128), F32)
    offs_ref[...] = jnp.zeros_like(offs_ref)
    for b in range(tokens // Q):
        rows = slice(b * Q, b * Q + Q)
        cum = mm_exact(lower, falls[rows, :])
        cum_ref[rows, :] = cum
        high, low = split2(jnp.exp(cum + before))
        grow_ref[rows, 0:128] = high
        grow_ref[rows, 128:256] = low
        before = before + cum[Q - 1 : Q, :]
        offs_ref[b + 1 : b + 2, :] = before


def activate(raw_ref, taps, act_ref, copy_ref):
    tokens = act_ref.shape[0]
    for at in range(0, tokens, Q):
        pre = conv_rows(raw_ref, taps, at, Q)
        act = (pre * sigmoid(pre)).astype(BF)
        act_ref[at : at + Q, :] = act
        copy_ref[at : at + Q, :] = act


def expand(per_head, spread):
    high, low = split2(per_head)
    return mm(jnp.concatenate([high, low], 1), spread)


def transpose_bf(values):
    return values.astype(F32).T.astype(BF)


def state_block(x_ref, b_ref, step_ref, cum_ref, spread_ref, held):
    cum = cum_ref[...]
    end = cum[Q - 1 : Q, :]
    tail = jnp.exp(end - cum) * step_ref[...]
    fall = jnp.broadcast_to(jnp.exp(end), (8, 128))
    b_t = transpose_bf(b_ref[...])
    b_t2 = jnp.concatenate([b_t, b_t], 1)
    for start in range(0, x_ref.shape[1], TILE):
        lanes = slice(start, start + TILE)
        spread = spread_ref[:, lanes]
        scaled = expand(tail, spread) * x_ref[:, lanes].astype(F32)
        high, low = split2(scaled)
        fresh = mm(b_t2, jnp.concatenate([high, low], 0))
        held[:, lanes] = held[:, lanes] * expand(fall, spread)[0:1, :] + fresh


def forward_block(x_ref, b_ref, c_ref, step_ref, cum_ref, spread_ref, state_ref, y_ref):
    b_blk, c_blk = b_ref[...], c_ref[...]
    affinity = mm_nt(c_blk, b_blk)
    causal = iota2((Q, Q), 0) >= iota2((Q, Q), 1)
    first = iota2((Q, 128), 1) < HEAD
    cum = cum_ref[...]
    cum_t = cum.T
    step_t = step_ref[...].T
    growth = jnp.exp(cum)
    c2 = jnp.concatenate([c_blk, c_blk], 1)
    zero = jnp.zeros((Q, 128), BF)
    for start in range(0, x_ref.shape[1], TILE):
        lanes = slice(start, start + TILE)
        s_high, s_low = split2(state_ref[0, :, lanes])
        reached = mm(c2, jnp.concatenate([s_high, s_low], 0)) * expand(growth, spread_ref[:, lanes])
        for pair in range(2):
            at = start + pair * 128
            x_pair = x_ref[:, at : at + 128]
            x0, x1 = jnp.where(first, x_pair, zero), jnp.where(first, zero, x_pair)
            pieces = []
            for half in range(2):
                h = at // HEAD + half
                spread_h = cum[:, h : h + 1] - cum_t[h : h + 1, :]
                decay = jnp.exp(jnp.where(causal, spread_h, -1e30))
                mixing = affinity * decay * step_t[h : h + 1, :]
                pieces += split2(mixing)
            intra = mm(jnp.concatenate(pieces, 1), jnp.concatenate([x0, x0, x1, x1], 0))
            y_ref[:, at : at + 128] = intra + reached[:, pair * 128 : pair * 128 + 128]


def forward_all_kernel(
    cols, dps,
    tok_ref, gain_ref, w_ref, small_ref, pick_ref, taps_ref, head_ref, spread_ref, cot, wg, wo,
    raw_ref, act_ref, normed_ref, stepin_ref, step_ref, cum_ref, grow_ref, offs_ref, inv_ref, picked_ref,
    states_ref, y_ref, graw_ref, gm_ref, early_ref, cot_out, gf, of,
    act_vm, states_vm, held, early_land, cot_vm, g_tiles, o_tiles, wg_vm, wo_vm, sems, local,
):
    step = pl.program_id(0)
    tokens, channels = states_vm.shape[0] * Q, held.shape[1]
    blocks = states_vm.shape[0]
    tiles = channels // TILE
    scan_at = tiles + 1
    out_at = scan_at + blocks
    gate_at = out_at + blocks
    dp, row, col = here()
    group = cols // 2
    place = lax.rem(col, group)
    half, shard = wg.shape
    count = cot.shape[0]
    others = dps - 1
    piece, piece_out = half // dps, wo.shape[0] // dps
    sibling, mirror = (dp, 1 - row, col), mirror_of(cols)
    peers = [(dp, row, col ^ by) for by in range(1, group)]
    my_rows = pl.ds(row * half, half)
    my_piece = pl.ds(row * half + dp * piece, piece)
    out_piece = pl.ds(shard + dp * piece_out, piece_out)
    my_lanes = lanes_at(row, half)
    own, other = pl.ds(0, shard), pl.ds(shard, shard)
    src_piece, src_out = pl.ds(dp * piece, piece), pl.ds(dp * piece_out, piece_out)
    my_cot = cot_vm.at[pl.ds(place * count, count), :]

    g_cross = lambda: copy_to(wg.at[src_piece, :], gf.at[my_piece, other], sems, 0, mirror)
    o_cross = lambda: copy_to(wo.at[src_out, :], of.at[out_piece, my_lanes], sems, 1, mirror)
    g_own = lambda: copy_to(wg, gf.at[my_rows, own], sems, 2, sibling)
    o_own = lambda: copy_to(wo, of.at[own, my_lanes], sems, 3, sibling)
    g_rest = lambda: copy_to(gf.at[my_rows, other], gf.at[my_rows, other], sems, 4, sibling)
    o_rest = lambda: copy_to(of.at[other, my_lanes], of.at[other, my_lanes], sems, 5, sibling)
    early_moves = lambda: [
        copy_to(held.at[:, own], early_land.at[:, other], sems, 6, mirror),
        copy_to(held.at[:, other], early_land.at[:, own], sems, 7, mirror),
    ]
    cot_moves = lambda: [copy_to(cot, my_cot, sems, 8 + i, peer) for i, peer in enumerate(peers)]
    first = 8 + group - 1

    def g_dp():
        ref = gf.at[my_piece, other]
        return dp_copies(dps, sems, lambda to, i: ref, lambda to, i: ref, first)

    def o_dp():
        ref = of.at[out_piece, my_lanes]
        return dp_copies(dps, sems, lambda to, i: ref, lambda to, i: ref, first + others)

    load_cot = pltpu.make_async_copy(cot, my_cot, local.at[0])
    load_g = pltpu.make_async_copy(wg, wg_vm, local.at[1])
    load_o = pltpu.make_async_copy(wo, wo_vm, local.at[2])
    store_g = pltpu.make_async_copy(wg_vm, gf.at[my_rows, own], local.at[1])
    store_o = pltpu.make_async_copy(wo_vm, of.at[own, my_lanes], local.at[2])
    store_cot = pltpu.make_async_copy(cot_vm, cot_out, local.at[0])

    def g_tile(at):
        return pltpu.make_async_copy(gf.at[:, lanes_at(at, TILE)], g_tiles.at[lax.rem(at, 2)], local.at[3])

    def o_tile(at):
        rows = pl.ds(pl.multiple_of(at * TILE, TILE), TILE)
        return pltpu.make_async_copy(of.at[rows, :], o_tiles.at[lax.rem(at, 2)], local.at[4])

    @at_step(0)
    def _():
        load_cot.start()
        load_g.start()
        load_o.start()
        greet([sibling, mirror] + peers + dp_peers(dps))
        for move in [g_cross(), o_cross(), g_own(), o_own()]:
            move.start()
        normalize(tok_ref, gain_ref, normed_ref, inv_ref)

    @at_step(1)
    def _():
        load_g.wait()
        store_g.start()
        load_o.wait()
        store_o.start()

    @at_step(tiles - 2)
    def _():
        for move in cot_moves():
            move.start()

    @at_step(scan_at + 2)
    def _():
        g_cross().wait_recv()
        for move in g_dp():
            move.start()

    @at_step(out_at)
    def _():
        o_cross().wait_recv()
        for move in o_dp():
            move.start()

    @at_step(out_at + blocks // 2)
    def _():
        for move in g_dp():
            move.wait_recv()
        g_rest().start()

    @at_step(gate_at + tiles // 2)
    def _():
        for move in o_dp():
            move.wait_recv()
        o_rest().start()

    @at_step(out_at)
    def _():
        @pl.when(col < group)
        def _():
            for move in early_moves():
                move.start()

    @pl.when(step < tiles)
    def _():
        raw_ref[...] = mm(normed_ref[...], w_ref[...])

    @pl.when(step == tiles)
    def _():
        project_steps(
            small_ref, pick_ref, head_ref, normed_ref, raw_ref, stepin_ref, step_ref, cum_ref, grow_ref, offs_ref,
            picked_ref,
        )

    @pl.when(step <= tiles)
    def _():
        activate(raw_ref, taps_ref[...], act_ref, act_vm.at[:, lanes_at(step, TILE)])

    def block_refs(at):
        rows = pl.ds(pl.multiple_of(at * Q, Q), Q)
        return (
            act_vm.at[rows, pl.ds(0, channels)], act_vm.at[rows, pl.ds(channels, N)],
            act_vm.at[rows, pl.ds(channels + N, N)], step_ref.at[rows, :], cum_ref.at[rows, :],
        )

    @pl.when(step == scan_at)
    def _():
        held[...] = jnp.zeros_like(held)

    @pl.when((step >= scan_at) & (step < out_at))
    def _():
        x_blk, b_blk, _, step_blk, cum_blk = block_refs(step - scan_at)
        states_ref[0] = held[...]
        states_vm[step - scan_at] = held[...]
        state_block(x_blk, b_blk, step_blk, cum_blk, spread_ref, held)

    @pl.when(step == out_at)
    def _():
        states_ref[0] = held[...]

    @pl.when((step >= out_at) & (step < gate_at))
    def _():
        x_blk, b_blk, c_blk, step_blk, cum_blk = block_refs(step - out_at)
        forward_block(
            x_blk, b_blk, c_blk, step_blk, cum_blk, spread_ref, states_vm.at[pl.ds(step - out_at, 1)], y_ref
        )

    @pl.when(step == gate_at)
    def _():
        for move in [g_own(), g_rest()]:
            move.wait_recv()
        store_g.wait()
        g_tile(0).start()

    @pl.when((step >= gate_at) & (step < gate_at + tiles))
    def _():
        at = step - gate_at
        g_tile(at).wait()

        @pl.when(at < tiles - 1)
        def _():
            g_tile(at + 1).start()

        graw_ref[...] = mm(normed_ref[HALO:, :], g_tiles[lax.rem(at, 2)])

    @pl.when(step == gate_at + tiles)
    def _():
        for move in [o_own(), o_rest()] + cot_moves():
            move.wait_recv()
        store_o.wait()
        load_cot.wait()
        store_cot.start()
        o_tile(0).start()

    @pl.when(step >= gate_at + tiles)
    def _():
        at = step - gate_at - tiles
        o_tile(at).wait()

        @pl.when(at < tiles - 1)
        def _():
            o_tile(at + 1).start()

        gm_ref[...] = mm_nt(cot_vm[...], o_tiles[lax.rem(at, 2)])

    @at_step(pl.num_programs(0) - 1)
    def _():
        store_cot.wait()
        for move in [g_cross(), o_cross(), g_own(), o_own(), g_rest(), o_rest()] + cot_moves() + g_dp() + o_dp():
            move.wait_send()

        @pl.when(col < group)
        def _():
            for move in early_moves():
                move.wait_send()
            early_ref[...] = jnp.zeros_like(early_ref)

        @pl.when(col >= group)
        def _():
            for move in early_moves():
                move.wait_recv()
            early_ref[...] = early_land[...]


def forward_all(cols, dps, group_tokens, gain, weights, small, pick, taps, head_rows, spread, cotangent, w_gate, w_out):
    rows, width = group_tokens.shape
    tokens = rows - HALO
    channels = weights.shape[1]
    total = channels + TILE
    blocks, tiles = tokens // Q, channels // TILE
    half, shard = w_gate.shape
    scan_at = tiles + 1
    out_at = scan_at + blocks
    gate_at = out_at + blocks

    def clamp(first, count):
        return lambda i: jnp.clip(i - first, 0, count - 1)

    lanes = lambda at, count: pl.BlockSpec((count, TILE), lambda i: (0, at(i)))
    both, value_at = clamp(0, tiles + 1), clamp(0, tiles)
    state_at, y_at = clamp(scan_at, blocks + 1), clamp(out_at, blocks)
    raw_tile, gm_tile = clamp(gate_at, tiles), clamp(gate_at + tiles, tiles)
    vmem = pltpu.VMEM
    return pl.pallas_call(
        partial(forward_all_kernel, cols, dps),
        grid=(gate_at + 2 * tiles,),
        in_specs=[
            whole((rows, width)),
            whole((1, width)),
            lanes(value_at, width),
            whole(small.shape),
            whole(pick.shape),
            lanes(both, 8),
            whole((8, 128)),
            whole(spread.shape),
            ANY, ANY, ANY,
        ],
        out_specs=[
            lanes(both, rows),
            lanes(both, tokens),
            whole((rows, width)),
            whole((tokens, 128)),
            whole((tokens, 128)),
            whole((tokens, 128)),
            whole((tokens, 256)),
            whole((16, 128)),
            whole((rows, 128)),
            whole((width, TILE + 128)),
            pl.BlockSpec((1, N, channels), lambda i: (state_at(i), 0, 0)),
            pl.BlockSpec((Q, channels), lambda i: (y_at(i), 0)),
            lanes(raw_tile, tokens),
            lanes(gm_tile, tokens),
            whole((N, channels)),
            ANY, ANY, ANY,
        ],
        out_shape=[
            sds((rows, total)),
            sds((tokens, total), BF),
            sds((rows, width), BF),
            sds((tokens, 128)),
            sds((tokens, 128)),
            sds((tokens, 128)),
            sds((tokens, 256), BF),
            sds((16, 128)),
            sds((rows, 128)),
            sds((width, TILE + 128), BF),
            sds((blocks + 1, N, channels)),
            sds((tokens, channels)),
            sds((tokens, channels)),
            sds((tokens, channels)),
            sds((N, channels)),
            sds((tokens, width), BF),
            sds((width, channels), BF),
            sds((channels, width), BF),
        ],
        scratch_shapes=[
            vmem((tokens, total), BF),
            vmem((blocks, N, channels), F32),
            vmem((N, channels), F32),
            vmem((N, channels), F32),
            vmem((tokens, width), BF),
            vmem((2, width, TILE), BF),
            vmem((2, TILE, width), BF),
            vmem((half, shard), BF),
            vmem((shard, half), BF),
            pltpu.SemaphoreType.DMA((2, 7 + cols // 2 + 2 * (dps - 1))),
            pltpu.SemaphoreType.DMA((5,)),
        ],
        compiler_params=remote_params(4),
        cost_estimate=cost(70),
        name="forward_all",
    )(group_tokens, gain, weights, small, pick, taps, head_rows, spread, cotangent, w_gate, w_out)


def grad_state_block(dy_tiles, c_ref, cum_ref, spread_ref, after_ref, held):
    after_ref[0] = held[...]
    cum = cum_ref[...]
    growth = jnp.exp(cum)
    fall = jnp.broadcast_to(growth[Q - 1 : Q, :], (8, 128))
    c_t = transpose_bf(c_ref[...])
    c_t2 = jnp.concatenate([c_t, c_t], 1)
    for tile in range(held.shape[1] // TILE):
        lanes = slice(tile * TILE, tile * TILE + TILE)
        spread = spread_ref[:, lanes]
        high, low = split2(dy_tiles[tile] * expand(growth, spread))
        direct = mm(c_t2, jnp.concatenate([high, low], 0))
        held[:, lanes] = held[:, lanes] * expand(fall, spread)[0:1, :] + direct


def near_block(
    at_block, here_rows, dy_ref, x_ref, b_ref, c_ref, step_ref, cum_ref, spread_ref, state_ref, early_ref,
    offs_ref, gx_ref, gbc_ref,
):
    b_blk, c_blk = b_ref[...], c_ref[...]
    affinity_t = mm_nt(b_blk, c_blk)
    causal_t = iota2((Q, Q), 1) >= iota2((Q, Q), 0)
    first = iota2((Q, 128), 1) < HEAD
    cum = cum_ref[...]
    cum_t = cum.T
    step = step_ref[...]
    growth = jnp.exp(cum)
    early_fall = jnp.broadcast_to(jnp.exp(offs_ref[pl.ds(at_block, 1), :]), (8, 128))
    zero = jnp.zeros((Q, 128), BF)
    grad_affinity_t = jnp.zeros((Q, Q), F32)
    grad_c = jnp.zeros((Q, N), F32)
    for start in range(0, x_ref.shape[1], TILE):
        lanes = slice(start, start + TILE)
        spread = spread_ref[:, lanes]
        before = state_ref[0, :, lanes] + expand(early_fall, spread)[0:1, :] * early_ref[:, lanes]
        dy_quad = dy_ref[:, lanes]
        s_high, s_low = split2(before)
        g_high, g_low = split2(dy_quad * expand(growth, spread))
        grad_c = grad_c + mm_nt(
            jnp.concatenate([g_high, g_low, g_high], 1), jnp.concatenate([s_high, s_high, s_low], 1)
        )
        for pair in range(2):
            at = start + pair * 128
            d_high, d_low = split2(dy_quad[:, pair * 128 : pair * 128 + 128])
            x_pair = x_ref[:, at : at + 128]
            x0, x1 = jnp.where(first, x_pair, zero), jnp.where(first, zero, x_pair)
            grad_mixing = mm_nt(
                jnp.concatenate([jnp.concatenate([x0, x0], 1), jnp.concatenate([x1, x1], 1)], 0),
                jnp.concatenate([d_high, d_low], 1),
            )
            left, right = [], []
            for half in range(2):
                h = at // HEAD + half
                spread_h = cum_t[h : h + 1, :] - cum[:, h : h + 1]
                decay = jnp.exp(jnp.where(causal_t, spread_h, -1e30))
                m_high, m_low = split2(affinity_t * decay)
                grad_affinity_t = grad_affinity_t + (
                    grad_mixing[half * Q : half * Q + Q, :] * decay * step[:, h : h + 1]
                )
                keep = first if half == 0 else jnp.logical_not(first)
                dh, dl = jnp.where(keep, d_high, zero), jnp.where(keep, d_low, zero)
                left += [m_high, m_low, m_high]
                right += [dh, dh, dl]
            gx_ref[here_rows, at : at + 128] = mm(jnp.concatenate(left, 1), jnp.concatenate(right, 0))
    a_high, a_low = split2(grad_affinity_t)
    gbc_ref[here_rows, 0:N] = mm(jnp.concatenate([a_high, a_low], 1), jnp.concatenate([c_blk, c_blk], 0))
    t_high, t_low = split2(grad_affinity_t.T)
    gbc_ref[here_rows, N : 2 * N] = grad_c + mm(
        jnp.concatenate([t_high, t_low], 1), jnp.concatenate([b_blk, b_blk], 0)
    )


def far_block(
    blocks, at_block, here_rows, dy_ref, x_ref, y_ref, gx_ref, b_ref, step_ref, cum_ref, stepin_ref, spread_ref,
    gather_ref, after_ref, late_ref, state_ref, early_ref, offs_ref, head_ref, skip_ref, gbc_ref,
    ga_ref, gstep_ref, gbc_out_ref, sums_ref,
):
    b_blk = b_ref[...]
    b2 = jnp.concatenate([b_blk, b_blk], 1)
    cum, step = cum_ref[...], step_ref[...]
    tail = jnp.exp(cum[Q - 1 : Q, :] - cum)
    tail_step = tail * step
    offs_after = offs_ref[pl.ds(at_block + 1, 1), :]
    offs_end = offs_ref[pl.ds(blocks, 1), :]
    late_fall = jnp.broadcast_to(jnp.exp(offs_end - offs_after), (8, 128))
    early_fall = jnp.broadcast_to(jnp.exp(offs_after), (8, 128))
    row_dots = jnp.zeros((Q, 128), F32)
    col_dots = jnp.zeros((Q, 128), F32)
    last_add = jnp.zeros((8, 128), F32)
    grad_b = gbc_ref[here_rows, 0:N]
    for start in range(0, x_ref.shape[1], TILE):
        lanes = slice(start, start + TILE)
        spread = spread_ref[:, lanes]
        gather = gather_ref[lanes, :]
        gather2 = jnp.concatenate([gather, gather], 0)
        x_quad = x_ref[:, lanes].astype(F32)
        dy_quad = dy_ref[:, lanes]
        skip = skip_ref[0:1, lanes]
        d_state = after_ref[0, :, lanes] + expand(late_fall, spread)[0:1, :] * late_ref[:, lanes]
        state = state_ref[0, :, lanes] + expand(early_fall, spread)[0:1, :] * early_ref[:, lanes]
        touch = jnp.broadcast_to(jnp.sum(d_state * state, axis=0, keepdims=True), (8, TILE))
        t_high, t_low = split2(touch)
        last_add = last_add + mm(jnp.concatenate([t_high, t_low], 1), gather2)
        s_high, s_low = split2(d_state)
        gx = gx_ref[here_rows, lanes] + expand(tail, spread) * mm(b2, jnp.concatenate([s_high, s_low], 0))
        w_high, w_low = split2(expand(tail_step, spread) * x_quad)
        grad_b = grad_b + mm_nt(
            jnp.concatenate([w_high, w_low, w_high], 1), jnp.concatenate([s_high, s_high, s_low], 1)
        )
        p_high, p_low = split2(dy_quad * (y_ref[:, lanes] - skip * x_quad))
        row_dots = row_dots + mm(jnp.concatenate([p_high, p_low], 1), gather2)
        r_high, r_low = split2(x_quad * gx)
        col_dots = col_dots + mm(jnp.concatenate([r_high, r_low], 1), gather2)
        ga_ref[:, lanes] = expand(step, spread) * gx + skip * dy_quad
    last_row = iota2((Q, 128), 0) == Q - 1
    grad_cum = row_dots - step * col_dots + jnp.where(last_row, last_add[0:1, :], 0.0)
    upper = (iota2((Q, Q), 1) >= iota2((Q, Q), 0)).astype(F32)
    grad_rate = mm_exact(upper, grad_cum)
    grad_step = col_dots + grad_rate * head_ref[1:2, :]
    grad_raw = grad_step * sigmoid(stepin_ref[...])
    gstep_ref[...] = grad_raw.astype(BF)
    sums_ref[0:1, :] += jnp.sum(grad_rate * step, axis=0, keepdims=True)
    sums_ref[1:2, :] += jnp.sum(grad_raw, axis=0, keepdims=True)
    gbc_out_ref[:, 0:N] = grad_b
    gbc_out_ref[:, N : 2 * N] = gbc_ref[here_rows, N : 2 * N]


WEIGHT_TILE = 384


def mm_tn(a, b):
    return lax.dot_general(a, b, (((0,), (0,)), ((), ())), preferred_element_type=F32)


def backward_kernel(
    cols, dps,
    dy_ref, x_ref, y_ref, b_ref, c_ref, step_ref, cum_ref, stepin_ref, spread_ref, gather_ref, after_ref,
    state_ref, early_ref, offs_ref, head_ref, skip_ref, mixed_ref, of_ref, gg_ref,
    first_grad, mixed_hbm, gg_hbm, cot, normed,
    ga_ref, gstep_ref, gbc_out_ref, sums_ref, o_total_ref, g_own_ref, g_cross_ref, branch_ref, branch_in,
    mixed_sib, gg_sib,
    gx_ref, gbc_ref, late_ref, o_low, o_own, o_land, o_cross, o_cross_land, g_low, g_own, g_land, parts,
    c_own, c_sib, n_own, n_sib, m_tiles, gg_tiles, sems, local,
):
    step_at = pl.program_id(0)
    blocks = gx_ref.shape[0] // Q
    dp, row, col = here()
    group = cols // 2
    place = lax.rem(col, group)
    shard, channels = g_own_ref.shape[1], gx_ref.shape[1]
    half = c_own.shape[1]
    count = branch_ref.shape[0]
    others = dps - 1
    own, other = pl.ds(0, shard), pl.ds(shard, shard)
    sibling, mirror = (dp, 1 - row, col), mirror_of(cols)
    peers = [(dp, row, col ^ by) for by in range(1, group)]
    out_steps, o_steps, g_steps = 2 * half // TILE, channels // WEIGHT_TILE, channels // TILE
    o_at = out_steps
    g_at = o_at + o_steps
    near_at = g_at + g_steps
    far_at = near_at + blocks
    last = far_at + blocks - 1

    def o_moves():
        return dp_copies(dps, sems, lambda to, i: o_low.at[:, to], lambda to, i: o_land.at[i])

    def g_moves():
        return dp_copies(dps, sems, lambda to, i: g_low.at[to], lambda to, i: g_land.at[i], others)

    at = 2 * others
    cross_move = lambda: copy_to(o_cross, o_cross_land, sems, at, mirror)
    late_moves = lambda: [
        copy_to(first_grad.at[:, own], late_ref.at[:, other], sems, at + 1, mirror),
        copy_to(first_grad.at[:, other], late_ref.at[:, own], sems, at + 2, mirror),
    ]
    core_moves = lambda: [
        copy_to(cot.at[:, lanes_at(1 - row, half)], c_sib, sems, at + 3, sibling),
        copy_to(mixed_hbm, mixed_sib, sems, at + 4, sibling),
        copy_to(normed.at[:, lanes_at(1 - row, half)], n_sib, sems, at + 5, sibling),
        copy_to(gg_hbm, gg_sib, sems, at + 6, sibling),
    ]
    part_moves = lambda: [
        copy_to(parts.at[i], branch_in.at[i], sems, at + 7 + i, peer) for i, peer in enumerate(peers)
    ]
    load_c = pltpu.make_async_copy(cot.at[:, lanes_at(row, half)], c_own, local.at[0])
    load_n = pltpu.make_async_copy(normed.at[:, lanes_at(row, half)], n_own, local.at[1])

    def m_tile(tile):
        lanes = lanes_at(tile, WEIGHT_TILE)
        return pltpu.make_async_copy(mixed_sib.at[:, lanes], m_tiles.at[lax.rem(tile, 2)], local.at[2])

    def gg_tile(tile):
        lanes = lanes_at(tile, TILE)
        return pltpu.make_async_copy(gg_sib.at[:, lanes], gg_tiles.at[lax.rem(tile, 2)], local.at[3])

    @at_step(0)
    def _():
        load_c.start()
        load_n.start()
        greet([sibling, mirror] + peers + dp_peers(dps))
        for move in core_moves():
            move.start()

        @pl.when(col >= group)
        def _():
            for move in late_moves():
                move.start()
            late_ref[...] = jnp.zeros_like(late_ref)

        sums_ref[...] = jnp.zeros_like(sums_ref)

    @pl.when(step_at < o_at)
    def _():
        rows = lambda index: pl.ds(pl.multiple_of(index * count, 128), count)
        branch_ref[...] = mm(mixed_ref[rows(place), :], of_ref[...])
        for by in range(1, group):
            parts[by - 1, :, lanes_at(step_at, TILE)] = mm(mixed_ref[rows(place ^ by), :], of_ref[...]).astype(BF)

    @pl.when(step_at == o_at)
    def _():
        load_c.wait()
        for move in core_moves()[:2]:
            move.wait_recv()
        m_tile(0).start()

    @pl.when((step_at >= o_at) & (step_at < g_at))
    def _():
        tile = step_at - o_at
        m_tile(tile).wait()

        @pl.when(tile < o_steps - 1)
        def _():
            m_tile(tile + 1).start()

        total = mm_tn(mixed_ref[:, lanes_at(tile, WEIGHT_TILE)], c_own[...])
        total = total + mm_tn(m_tiles[lax.rem(tile, 2)], c_sib[...])
        piece = o_own.shape[1]
        per, each = WEIGHT_TILE // piece, shard // WEIGHT_TILE
        which, inside = lax.div(tile, each), lax.rem(tile, each)
        for p in range(per):
            part = total[p * piece : p * piece + piece, :]
            o_low[which, inside * per + p] = part.astype(BF)

            @pl.when(dp == inside * per + p)
            def _():
                o_own[which] = part

    @pl.when(step_at == g_at)
    def _():
        for move in o_moves():
            move.start()
        load_n.wait()
        for move in core_moves()[2:]:
            move.wait_recv()
        gg_tile(0).start()

    @pl.when((step_at >= g_at) & (step_at < near_at))
    def _():
        tile = step_at - g_at
        gg_tile(tile).wait()

        @pl.when(tile < g_steps - 1)
        def _():
            gg_tile(tile + 1).start()

        lanes = lanes_at(tile, TILE)
        total = mm_tn(n_own[HALO:, :], gg_ref[...]) + mm_tn(n_sib[HALO:, :], gg_tiles[lax.rem(tile, 2)])
        piece = g_own.shape[0]
        for p in range(dps):
            part = total[p * piece : p * piece + piece, :]
            g_low[p, :, lanes] = part.astype(BF)

            @pl.when(dp == p)
            def _():
                g_own[:, lanes] = part

    at_block = lax.rem(jnp.maximum(step_at - near_at, 0), blocks)
    here_rows = pl.ds(pl.multiple_of(at_block * Q, Q), Q)

    @pl.when((step_at >= near_at) & (step_at < far_at))
    def _():
        near_block(
            at_block, here_rows, dy_ref, x_ref, b_ref, c_ref, step_ref, cum_ref, spread_ref, state_ref,
            early_ref, offs_ref, gx_ref, gbc_ref,
        )

    @pl.when(step_at == near_at + 2)
    def _():
        for move in part_moves():
            move.start()

    @pl.when(step_at == near_at + blocks // 2)
    def _():
        for move in o_moves():
            move.wait_recv()
        for move in g_moves():
            move.start()
        for i in range(others):
            o_own[...] += o_land[i].astype(F32)
        o_cross[...] = o_own[1].astype(BF)
        cross_move().start()

    @pl.when(step_at == far_at)
    def _():
        @pl.when(col < group)
        def _():
            for move in late_moves():
                move.wait_recv()

    @pl.when(step_at >= far_at)
    def _():
        far_block(
            blocks, at_block, here_rows, dy_ref, x_ref, y_ref, gx_ref, b_ref, step_ref, cum_ref, stepin_ref,
            spread_ref, gather_ref, after_ref, late_ref, state_ref, early_ref, offs_ref, head_ref, skip_ref,
            gbc_ref, ga_ref, gstep_ref, gbc_out_ref, sums_ref,
        )

    @at_step(last)
    def _():
        cross_move().wait()
        o_total_ref[...] = o_own[0] + o_cross_land[...].astype(F32)
        for move in g_moves():
            move.wait()
        for i in range(others):
            g_own[...] += g_land[i].astype(F32)
        g_own_ref[...] = g_own[:, :shard]
        g_cross_ref[...] = g_own[:, shard:].astype(BF)
        for move in part_moves():
            move.wait()
        for move in o_moves() + core_moves():
            move.wait_send()

        @pl.when(col >= group)
        def _():
            for move in late_moves():
                move.wait_send()


def scan_backward(
    cols, dps, dy, act, y, step, cum, step_in, spread, gather, after, states, early, offs, head_rows, skip,
    mixed, w_out, gg, first_grad, cot, normed,
):
    tokens, channels = dy.shape
    rows_n, width = normed.shape
    half = width // 2
    blocks, group, shard = tokens // Q, cols // 2, channels // 2
    count = tokens // group
    piece_o, piece_g = shard // dps, half // dps
    out_steps, o_steps, g_steps = width // TILE, channels // WEIGHT_TILE, channels // TILE
    g_at = out_steps + o_steps
    near_at = g_at + g_steps
    far_at = near_at + blocks

    def clamp(first, size):
        return lambda i: jnp.clip(i - first, 0, size - 1)

    block = lambda i: jnp.where(i < near_at, 0, lax.rem(jnp.maximum(i - near_at, 0), blocks))
    second = clamp(far_at, blocks)
    state_at = lambda i: block(i) + jnp.where(i < far_at, 0, 1)
    rows = lambda at, size: pl.BlockSpec((Q, size), lambda i: (at(i), 0))
    lanes = lambda at, size: pl.BlockSpec((size, TILE), lambda i: (0, at(i)))
    once = lambda shape: pl.BlockSpec(shape, lambda *_: (0,) * len(shape), pipeline_mode=pl.Buffered(1))
    vmem = pltpu.VMEM
    dma = pltpu.SemaphoreType.DMA
    return pl.pallas_call(
        partial(backward_kernel, cols, dps),
        grid=(far_at + blocks,),
        in_specs=[
            rows(block, channels),
            rows(block, channels),
            rows(second, channels),
            pl.BlockSpec((Q, N), lambda i: (block(i), channels // N)),
            pl.BlockSpec((Q, N), lambda i: (block(i), channels // N + 1)),
            rows(block, 128),
            rows(block, 128),
            rows(second, 128),
            once(spread.shape),
            once(gather.shape),
            pl.BlockSpec((1, N, channels), lambda i: (second(i), 0, 0)),
            pl.BlockSpec((1, N, channels), lambda i: (state_at(i), 0, 0)),
            once(early.shape),
            once((16, 128)),
            once((8, 128)),
            once((8, channels)),
            once(mixed.shape),
            lanes(clamp(0, out_steps), channels),
            lanes(clamp(g_at, g_steps), tokens),
        ] + [ANY] * 5,
        out_specs=[
            rows(second, channels),
            rows(second, 128),
            rows(second, 2 * N),
            whole((8, 128)),
            whole((piece_o, half)),
            whole((piece_g, shard)),
            whole((piece_g, shard)),
            lanes(clamp(0, out_steps), count),
            ANY, ANY, ANY,
        ],
        out_shape=[
            sds((tokens, channels)),
            sds((tokens, 128), BF),
            sds((tokens, 2 * N)),
            sds((8, 128)),
            sds((piece_o, half)),
            sds((piece_g, shard)),
            sds((piece_g, shard), BF),
            sds((count, width)),
            sds((max(group - 1, 1), count, width), BF),
            sds(mixed.shape, BF),
            sds(gg.shape, BF),
        ],
        scratch_shapes=[
            vmem((tokens, channels), F32), vmem((tokens, 2 * N), F32), vmem((N, channels), F32),
            vmem((2, dps, piece_o, half), BF), vmem((2, piece_o, half), F32),
            vmem((dps - 1, 2, piece_o, half), BF), vmem((piece_o, half), BF), vmem((piece_o, half), BF),
            vmem((dps, piece_g, channels), BF), vmem((piece_g, channels), F32),
            vmem((dps - 1, piece_g, channels), BF),
            vmem((max(group - 1, 1), count, width), BF),
            vmem((tokens, half), BF), vmem((tokens, half), BF),
            vmem((rows_n, half), BF), vmem((rows_n, half), BF),
            vmem((2, tokens, WEIGHT_TILE), BF), vmem((2, tokens, TILE), BF),
            dma((2, 2 * (dps - 1) + 6 + group)),
            dma((4,)),
        ],
        compiler_params=remote_params(3),
        cost_estimate=cost(80),
        name="scan_backward",
    )(
        dy, act, y, act, act, step, cum, step_in, spread, gather, after, states, early, offs, head_rows, skip,
        mixed, w_out, gg, first_grad, mixed, gg, cot, normed,
    )


def gate_kernel(
    cols, inner_channels,
    y0_ref, graw_ref, gm_ref, x_ref, early_ref, c_ref, grow_ref, spread_ref, vec_ref,
    cum_ref, c_block_ref, spread_all_ref,
    y_ref, mixed_ref, gg_ref, dy_ref, sums_ref, after_ref, first_ref,
    y_vm, graw_vm, gm_vm, squares, inners, stats, stats_land, stats_col, held, sems,
):
    step = pl.program_id(0)
    tiles = y_vm.shape[0]
    tokens = y0_ref.shape[0]
    dp, row, col = here()
    group = cols // 2
    peers = [(dp, row, col ^ by) for by in range(1, group)]
    gain = vec_ref[1:2, :]
    nt = (((1,), (1,)), ((), ()))
    moves = lambda: [copy_to(stats, stats_land.at[i], sems, i, peer) for i, peer in enumerate(peers)]

    @at_step(0)
    def _():
        greet(peers)
        squares[...] = jnp.zeros_like(squares)
        inners[...] = jnp.zeros_like(inners)

    @pl.when(step < tiles)
    def _():
        s_high, s_low = split2(early_ref[...])
        s2 = jnp.concatenate([s_high, s_low], 0)
        spread = spread_ref[...]
        skip = vec_ref[0:1, :]
        for at in range(0, tokens, Q):
            rows = slice(at, at + Q)
            c_blk = c_ref[rows, :]
            carried = mm(jnp.concatenate([c_blk, c_blk], 1), s2) * mm(grow_ref[rows, :], spread)
            y = y0_ref[rows, :] + carried + skip * x_ref[rows, :].astype(F32)
            raw, gm = graw_ref[rows, :], gm_ref[rows, :]
            y_ref[rows, :] = y
            y_vm[step, rows, :] = y
            graw_vm[step, rows, :] = raw
            gm_vm[step, rows, :] = gm
            gated = y * raw * sigmoid(raw)
            square = gated * gated
            inner = gm * gain * gated
            squares[rows, :] += square[:, 0:128] + square[:, 128:256]
            inners[rows, :] += inner[:, 0:128] + inner[:, 128:256]

    @at_step(tiles - 1)
    def _():
        ones = jnp.ones((8, 128), F32)
        square_row = lax.dot_general(ones, squares[...], nt, precision=HIGHEST, preferred_element_type=F32)
        inner_row = lax.dot_general(ones, inners[...], nt, precision=HIGHEST, preferred_element_type=F32)
        stats[...] = jnp.where(iota2(square_row.shape, 0) == 0, square_row, inner_row)
        for move in moves():
            move.start()
        for move in moves():
            move.wait_recv()
        total = stats[...]
        for i in range(group - 1):
            total = total + stats_land[i]
        wide = jnp.concatenate([total, jnp.zeros((120, tokens), F32)], 0)
        stats_col[...] = wide.T

    @pl.when((step >= tiles) & (step < 2 * tiles))
    def _():
        tile = step - tiles
        gain_sum = jnp.zeros((1, TILE), F32)
        skip_sum = jnp.zeros((1, TILE), F32)
        for at in range(0, tokens, Q):
            rows = slice(at, at + Q)
            inv = lax.rsqrt(stats_col[rows, 0:1] * (1.0 / inner_channels) + EPSILON)
            pull = inv * inv * inv * (stats_col[rows, 1:2] * (1.0 / inner_channels))
            raw, y, gm = graw_vm[tile, rows, :], y_vm[tile, rows, :], gm_vm[tile, rows, :]
            sig = sigmoid(raw)
            act = raw * sig
            gated = y * act
            unit = gated * inv
            mixed_ref[rows, :] = (unit * gain).astype(BF)
            gain_sum = gain_sum + jnp.sum(gm * unit, axis=0, keepdims=True)
            grad_gated = inv * (gm * gain) - gated * pull
            dy = grad_gated * act
            dy_ref[rows, :] = dy
            y_vm[tile, rows, :] = dy
            gg_ref[rows, :] = (grad_gated * y * (sig * (1.0 + raw * (1.0 - sig)))).astype(BF)
            skip_sum = skip_sum + jnp.sum(dy * x_ref[rows, :].astype(F32), axis=0, keepdims=True)
        sums_ref[...] = jnp.zeros_like(sums_ref)
        sums_ref[0:1, :] = gain_sum
        sums_ref[1:2, :] = skip_sum

    @pl.when(step == 2 * tiles)
    def _():
        for move in moves():
            move.wait_send()
        held[...] = jnp.zeros_like(held)

    @pl.when(step >= 2 * tiles)
    def _():
        at = pl.num_programs(0) - 1 - step
        rows = pl.ds(pl.multiple_of(at * Q, Q), Q)
        grad_state_block(y_vm.at[:, rows, :], c_block_ref, cum_ref, spread_all_ref, after_ref, held)
        first_ref[...] = held[...]


def gate_and_mix(cols, inner_channels, y0, graw, gm, act, early, grow, spread, vectors, cum):
    tokens, channels = y0.shape
    blocks = tokens // Q
    tiles, group = channels // TILE, cols // 2
    first = lambda i: jnp.minimum(i, tiles - 1)
    second = lambda i: jnp.clip(i - tiles, 0, tiles - 1)
    either = lambda i: jnp.where(i < 2 * tiles, lax.rem(i, tiles), tiles - 1)
    third = lambda i: blocks - 1 - jnp.maximum(i - 2 * tiles, 0)
    lanes = lambda at, count: pl.BlockSpec((count, TILE), lambda i: (0, at(i)))
    vmem = pltpu.VMEM
    return pl.pallas_call(
        partial(gate_kernel, cols, inner_channels),
        grid=(2 * tiles + blocks,),
        in_specs=[
            lanes(first, tokens), lanes(first, tokens), lanes(first, tokens), lanes(either, tokens),
            lanes(first, N),
            pl.BlockSpec((tokens, N), lambda i: (0, channels // N + 1)),
            whole((tokens, 256)),
            lanes(first, 256),
            lanes(either, 8),
            pl.BlockSpec((Q, 128), lambda i: (third(i), 0)),
            pl.BlockSpec((Q, N), lambda i: (third(i), channels // N + 1)),
            whole((256, channels)),
        ],
        out_specs=[
            lanes(first, tokens), lanes(second, tokens), lanes(second, tokens), lanes(second, tokens),
            lanes(second, 8),
            pl.BlockSpec((1, N, channels), lambda i: (third(i), 0, 0)),
            whole((N, channels)),
        ],
        out_shape=[
            sds((tokens, channels)), sds((tokens, channels), BF), sds((tokens, channels), BF),
            sds((tokens, channels)), sds((8, channels)), sds((blocks, N, channels)), sds((N, channels)),
        ],
        scratch_shapes=[
            vmem((tiles, tokens, TILE), F32), vmem((tiles, tokens, TILE), F32), vmem((tiles, tokens, TILE), F32),
            vmem((tokens, 128), F32), vmem((tokens, 128), F32),
            vmem((8, tokens), F32), vmem((max(group - 1, 1), 8, tokens), F32), vmem((tokens, 128), F32),
            vmem((N, channels), F32),
            pltpu.SemaphoreType.DMA((2, max(group - 1, 1))),
        ],
        compiler_params=remote_params(6),
        cost_estimate=cost(40),
        name="gate_and_mix",
    )(y0, graw, gm, act, early, act, grow, spread, vectors, cum, act, spread)


def conv_back_tile(ga_ref, raw_ref, taps_ref, gv_ref, sums_ref, g_pad):
    tokens, width = ga_ref.shape
    taps = taps_ref[...]
    g_pad[0:HALO, :] = jnp.zeros((HALO, width), F32)
    g_pad[HALO + tokens :, :] = jnp.zeros((HALO, width), F32)
    sums = [jnp.zeros((1, width), F32)] * 5
    for row in range(0, tokens, Q):
        pre = conv_rows(raw_ref, taps, row, Q)
        sig = sigmoid(pre)
        g = ga_ref[row : row + Q, :] * (sig * (1.0 + pre * (1.0 - sig)))
        g_pad[HALO + row : HALO + row + Q, :] = g
        for k in range(4):
            moved = raw_ref[pl.ds(HALO - 3 + k + row, Q), :]
            sums[k] = sums[k] + jnp.sum(g * moved, axis=0, keepdims=True)
        sums[4] = sums[4] + jnp.sum(g, axis=0, keepdims=True)
    for row in list(range(HALO, HALO + tokens, Q)) + [0]:
        size = HALO if row == 0 else Q
        total = jnp.zeros((size, width), F32)
        for k in range(4):
            total = total + taps[k : k + 1, :] * g_pad[pl.ds(row + 3 - k, size), :]
        gv_ref[row : row + size, :] = total.astype(BF)
    sums_ref[...] = jnp.zeros_like(sums_ref)
    for k in range(5):
        sums_ref[k : k + 1, :] = sums[k]


def input_grad_tile(
    gv_ref, gg_ref, gs_ref, gt_ref, v_ref, g_ref, s_ref, t_ref, tok_ref, inv_ref, out_ref, low_ref, sums_ref
):
    rows = gv_ref.shape[0]
    total = mm_nt(gv_ref[...], v_ref[...]) + mm_nt(gs_ref[...], s_ref[...])
    inner = mm_nt(gg_ref[...], g_ref[...]) + mm_nt(gt_ref[...], t_ref[...])
    out_ref[0:HALO, :] = total[0:HALO, :]
    out_ref[HALO:, :] = total[HALO:, :] + inner
    sums = jnp.zeros((1, TILE), F32)
    for at in [0] + list(range(HALO, rows, Q)):
        size = HALO if at == 0 else Q
        part = out_ref[at : at + size, :]
        low_ref[at : at + size, :] = part.astype(BF)
        unit = tok_ref[at : at + size, :].astype(F32) * inv_ref[at : at + size, 0:1]
        sums = sums + jnp.sum(part * unit, axis=0, keepdims=True)
    sums_ref[...] = jnp.broadcast_to(sums, (8, TILE))


def finish_kernel(
    cols, dps, part, whole_state,
    ga_ref, raw_ref, taps_ref, gg_ref, gt_ref, v_ref, g_ref, picked_ref, tok_ref, inv_ref, g_own_ref,
    o_total, g_cross, gbc, normed, gt_hbm,
    sums_ref, gn_ref, low_ref, norm_ref, joint_ref, o_out, g_out,
    gv_vm, gv_sib, gs_vm, gs_sib, gt_sib, bc_own, bc_land, g_pad,
    raw_part, taps_part, sums_part, g_pad_part, n_own, n_sib, o_vm, g_vm, g_land, sems, local,
):
    step = pl.program_id(0)
    conv_steps = gv_vm.shape[1] // TILE
    input_steps = 2 * n_own.shape[1] // TILE
    dp, row, col = here()
    group = cols // 2
    place = lax.rem(col, group)
    sibling = (dp, 1 - row, col)
    peers = [(dp, row, col ^ by) for by in range(1, group)]
    half = n_own.shape[1]
    piece = o_total.shape[0]
    span = gs_vm.shape[1]
    others = dps - 1
    out_rows = pl.ds(dp * piece, piece)
    g_rows = pl.ds(dp * g_vm.shape[0], g_vm.shape[0])

    def part_at(at):
        return pl.ds(0, span) if whole_state else lanes_at(at, span)

    def o_moves():
        return dp_copies(dps, sems, lambda to, i: o_total, lambda to, i: o_out.at[out_rows, :])

    def g_moves():
        return dp_copies(dps, sems, lambda to, i: g_vm, lambda to, i: g_out.at[g_rows, :], others)

    first = 2 * others
    g_move = lambda: copy_to(g_cross, g_land, sems, first, mirror_of(cols))
    n_move = lambda: copy_to(normed.at[:, lanes_at(1 - row, half)], n_sib, sems, first + 1, sibling)
    t_move = lambda: copy_to(gt_hbm, gt_sib, sems, first + 2, sibling)
    s_move = lambda: copy_to(gs_vm, gs_sib, sems, first + 3, sibling)

    def bc_moves():
        return [
            copy_to(gbc.at[:, part_at(place ^ by)], bc_land.at[by - 1], sems, first + 3 + by, peers[by - 1])
            for by in range(1, group)
        ]

    def v_move(tile):
        lanes = lanes_at(tile, TILE)
        return copy_to(gv_vm.at[:, lanes], gv_sib.at[:, lanes], sems, first + 3 + group + tile, sibling)

    load_bc = pltpu.make_async_copy(gbc.at[:, part_at(place)], bc_own, local.at[0])
    load_n = pltpu.make_async_copy(normed.at[:, lanes_at(row, half)], n_own, local.at[1])
    load_o = pltpu.make_async_copy(o_total, o_vm, local.at[2])
    store_o = pltpu.make_async_copy(o_vm, o_out.at[out_rows, :], local.at[3])
    store_g = pltpu.make_async_copy(g_vm, g_out.at[g_rows, :], local.at[4])

    @at_step(0)
    def _():
        load_o.start()
        load_bc.start()
        load_n.start()
        greet([sibling, mirror_of(cols)] + peers + dp_peers(dps))
        for move in bc_moves() + [g_move()] + o_moves() + [t_move(), n_move()]:
            move.start()
        load_o.wait()
        store_o.start()

    @pl.when(step < conv_steps)
    def _():
        conv_back_tile(
            ga_ref, raw_ref, taps_ref, gv_vm.at[:, lanes_at(step, TILE)], sums_ref, g_pad
        )
        v_move(step).start()

    @pl.when(step == conv_steps)
    def _():
        load_bc.wait()
        for move in bc_moves():
            move.wait_recv()
        for i in range(group - 1):
            bc_own[...] += bc_land[i]
        if whole_state:
            lane = iota2(bc_own.shape, 1)
            mine = (lane >= place * part) & (lane < place * part + part)
            bc_own[...] = jnp.where(mine, bc_own[...], 0.0)
        lanes = part_at(place)
        sums_ref[...] = jnp.zeros_like(sums_ref)
        raw_part[...] = raw_ref[:, lanes]
        taps_part[...] = taps_ref[:, lanes]
        conv_back_tile(bc_own, raw_part, taps_part, gs_vm, sums_part, g_pad_part)
        sums_ref[:, 0:span] = sums_part[...]
        s_move().start()
        g_move().wait_recv()
        g_vm[...] = g_own_ref[...] + g_land[...].astype(F32)
        for move in g_moves():
            move.start()
        store_g.start()

    @pl.when((step > conv_steps) & (step <= conv_steps + input_steps))
    def _():
        input_grad_tile(
            gv_vm, gg_ref, gs_vm, gt_ref, v_ref, g_ref, picked_ref.at[:, part_at(place)],
            picked_ref.at[:, pl.ds(TILE, 128)], tok_ref, inv_ref, gn_ref, low_ref, norm_ref,
        )

    @pl.when(step == conv_steps + input_steps + 1)
    def _():
        load_n.wait()
        for move in [n_move(), t_move(), s_move()]:
            move.wait_recv()
        for tile in range(conv_steps):
            v_move(tile).wait_recv()

    @pl.when(step > conv_steps + input_steps)
    def _():
        lanes = lanes_at(step - conv_steps - input_steps - 1, TILE)
        channels = gv_vm.shape[1]
        left, left_sib = n_own[:, lanes], n_sib[:, lanes]
        joint_ref[:, 0:channels] = mm_tn(left, gv_vm[...]) + mm_tn(left_sib, gv_sib[...])
        joint_ref[:, channels : channels + span] = mm_tn(left, gs_vm[...]) + mm_tn(left_sib, gs_sib[...])
        joint_ref[:, channels + span :] = mm_tn(left[HALO:, :], gt_ref[...]) + mm_tn(left_sib[HALO:, :], gt_sib[...])

    @at_step(pl.num_programs(0) - 1)
    def _():
        store_o.wait()
        store_g.wait()
        for move in o_moves() + g_moves():
            move.wait()
        for move in bc_moves() + [g_move(), n_move(), t_move(), s_move()]:
            move.wait_send()
        for tile in range(conv_steps):
            v_move(tile).wait_send()


def finish(
    cols, dps, part, ga, raw, taps, gg, gt, w_value, w_gate, picked, tokens_in, inv_rms, g_own, o_total, g_cross,
    gbc, normed,
):
    tokens, channels = ga.shape
    rows, width = normed.shape
    half = width // 2
    whole_state = part % 128 != 0
    span = 2 * N if whole_state else part
    group = cols // 2
    conv_steps, input_steps, weight_steps = channels // TILE, width // TILE, half // TILE
    piece = o_total.shape[0]
    joint_width = channels + span + 128

    def clamp(first, count):
        return lambda i: jnp.clip(i - first, 0, count - 1)

    conv, input_at = clamp(0, conv_steps), clamp(conv_steps + 1, input_steps)
    both = clamp(0, conv_steps + 1)
    weight_at = clamp(conv_steps + 1 + input_steps, weight_steps)
    lanes = lambda at, count: pl.BlockSpec((count, TILE), lambda i: (0, at(i)))
    slab = lambda at, size: pl.BlockSpec((TILE, size), lambda i: (at(i), 0))
    vmem = pltpu.VMEM
    copies = 2 * (dps - 1) + 3 + group + conv_steps
    return pl.pallas_call(
        partial(finish_kernel, cols, dps, part, whole_state),
        grid=(conv_steps + 1 + input_steps + weight_steps,),
        in_specs=[
            lanes(conv, tokens),
            lanes(both, rows),
            lanes(both, 8),
            whole(gg.shape),
            whole(gt.shape),
            slab(input_at, channels),
            slab(input_at, channels),
            slab(input_at, TILE + 128),
            lanes(input_at, rows),
            whole(inv_rms.shape),
            whole(g_own.shape),
        ] + [ANY] * 5,
        out_specs=[
            lanes(both, 8), lanes(input_at, rows), lanes(input_at, rows), lanes(input_at, 8),
            slab(weight_at, joint_width), ANY, ANY,
        ],
        out_shape=[
            sds((8, channels + TILE)), sds((rows, width)), sds((rows, width), BF), sds((8, width)),
            sds((half, joint_width)), sds((dps * piece, o_total.shape[1])),
            sds((dps * g_own.shape[0], g_own.shape[1])),
        ],
        scratch_shapes=[
            vmem((rows, channels), BF), vmem((rows, channels), BF), vmem((rows, span), BF), vmem((rows, span), BF),
            vmem((tokens, 128), BF), vmem((tokens, span), F32), vmem((max(group - 1, 1), tokens, span), F32),
            vmem((tokens + 2 * HALO, TILE), F32), vmem((rows, span), F32), vmem((8, span), F32),
            vmem((8, span), F32), vmem((tokens + 2 * HALO, span), F32),
            vmem((rows, half), BF), vmem((rows, half), BF),
            vmem(o_total.shape, F32), vmem(g_own.shape, F32), vmem(g_own.shape, BF),
            pltpu.SemaphoreType.DMA((2, copies)),
            pltpu.SemaphoreType.DMA((5,)),
        ],
        compiler_params=remote_params(5),
        cost_estimate=cost(55),
        name="finish",
    )(
        ga, raw, taps, gg, gt, w_value, w_gate, picked, tokens_in, inv_rms, g_own, o_total, g_cross, gbc, normed, gt,
    )


def settle_kernel(
    cols, dps, heads, span, gn, gnb, joint, flat, tok, cot, gain,
    tg_out, v_out, ext_out, flat_out,
    mine_a, mine_b, send_a, rec_a, send_b, rec_b, tot_a, tot_b,
    z_send, z_land, step_land, state_land, ext, acc, flat_land,
    gn_own, gn_land, halo_land, tok_vm, cot_vm, gain_vm, local, send, recv,
):
    dp, row, col = here()
    group = cols // 2
    place = lax.rem(col, group)
    half, wide_a = mine_a.shape
    shard = mine_b.shape[1]
    piece = tot_a.shape[0]
    count, width = gn_own.shape
    sibling = (dp, 1 - row, col)
    mirror = (dp, row, cols - 1 - col)
    col_peer = lambda by: (dp, row, col ^ by)
    dp_peer = lambda by: (dp ^ by, row, col)
    used = [0]
    started = []

    def remote(src, dst, device):
        i = used[0]
        used[0] += 1
        return pltpu.make_async_remote_copy(
            src_ref=src, dst_ref=dst, send_sem=send.at[i], recv_sem=recv.at[i],
            device_id=device, device_id_type=pl.DeviceIdType.MESH,
        )

    def launch(src, dst, device):
        copy = remote(src, dst, device)
        copy.start()
        started.append(copy)
        return copy

    def arrive(copies):
        for copy in copies:
            copy.wait_recv()

    kept = [0]

    def keep(src, dst):
        copy = pltpu.make_async_copy(src, dst, local.at[kept[0]])
        kept[0] += 1
        copy.start()
        return copy

    part_a, part_b = pl.ds(shard, wide_a), pl.ds(0, shard)
    load_a = keep(joint.at[:, part_a], mine_a)
    load_b = keep(joint.at[:, part_b], mine_b)
    load_flat = keep(flat, acc)
    loads = [
        keep(gn.at[pl.ds(HALO + place * count, count), :], gn_own),
        keep(tok, tok_vm),
        keep(cot, cot_vm),
        keep(gain, gain_vm),
    ]
    greet(
        [sibling]
        + [col_peer(by) for by in range(1, cols)]
        + [dp_peer(by) for by in range(1, dps)]
    )
    gn_moves = [
        launch(gnb.at[pl.ds(HALO + (place ^ by) * count, count), :], gn_land.at[by - 1], col_peer(by))
        for by in range(1, group)
    ]
    halo_at = used[0]
    used[0] += group
    halos = [
        pltpu.make_async_remote_copy(
            src_ref=gnb.at[pl.ds(0, HALO), :], dst_ref=halo_land.at[j], send_sem=send.at[halo_at + j],
            recv_sem=recv.at[halo_at + j], device_id=(dp, row, group - 1),
            device_id_type=pl.DeviceIdType.MESH,
        )
        for j in range(group)
    ]
    for j in range(group):
        pl.when(col == group + j)(halos[j].start)

    flat_steps = [sibling]
    by = 1
    while by < dps:
        flat_steps.append(dp_peer(by))
        by *= 2
    by = 1
    while by < cols:
        flat_steps.append(col_peer(by))
        by *= 2
    flat_moves = []
    flat_taken = [0]

    def flat_next():
        if flat_taken[0] < len(flat_moves):
            flat_moves[-1].wait_recv()
            flat_moves[-1].wait_send()
            acc[...] += flat_land[flat_taken[0]]
            flat_taken[0] += 1
        if len(flat_moves) < len(flat_steps):
            at = len(flat_moves)
            move = remote(acc, flat_land.at[at], flat_steps[at])
            move.start()
            flat_moves.append(move)

    load_flat.wait()
    flat_next()

    def hand_out(load, mine, total, sends, recs):
        load.wait()
        moves = []
        for by in range(1, dps):
            rows = pl.ds(pl.multiple_of((dp ^ by) * piece, 16), piece)
            sends[by - 1] = mine[rows, :].astype(BF)
            moves.append(launch(sends.at[by - 1], recs.at[by - 1], dp_peer(by)))
        total[...] = mine[pl.ds(pl.multiple_of(dp * piece, 16), piece), :]
        return moves

    moves_a = hand_out(load_a, mine_a, tot_a, send_a, rec_a)
    flat_next()
    moves_b = hand_out(load_b, mine_b, tot_b, send_b, rec_b)
    flat_next()
    arrive(moves_a)
    for by in range(1, dps):
        tot_a[...] += rec_a[by - 1].astype(F32)
    z_send[...] = tot_a[:, 0:shard].astype(BF)
    z_move = launch(z_send, z_land, mirror)
    step_move = launch(tot_a.at[:, pl.ds(shard + span, 128)], step_land, mirror)
    state_block = tot_a.at[:, pl.ds(shard, span)]
    state_moves = [launch(state_block, state_land.at[col], col_peer(by)) for by in range(1, cols)]
    state_land[col] = tot_a[:, shard : shard + span]
    flat_next()
    arrive(moves_b)
    for by in range(1, dps):
        tot_b[...] += rec_b[by - 1].astype(F32)
    arrive([z_move, step_move])
    tot_b[...] += z_land[...].astype(F32)
    ext[:, 0:128] = tot_a[:, shard + span : shard + span + 128] + pltpu.roll(step_land[...], 128 - heads, 1)
    out_rows = pl.ds(dp * piece, piece)
    v_moves = [launch(tot_b, v_out.at[out_rows, :], dp_peer(by)) for by in range(1, dps)]
    v_keep = keep(tot_b, v_out.at[out_rows, :])
    arrive(state_moves)
    if span == 2 * N:
        ext[:, 128:] = sum(state_land[i] for i in range(cols))
    else:
        part = col // 2
        ext[:, 128:] = state_land[part] + state_land[part + group]
    e_moves = [launch(ext, ext_out.at[out_rows, :], dp_peer(by)) for by in range(1, dps)]
    e_keep = keep(ext, ext_out.at[out_rows, :])
    flat_next()
    for copy in loads:
        copy.wait()
    arrive(gn_moves)
    for by in range(1, group):
        gn_own[...] += gn_land[by - 1].astype(F32)

    @pl.when(col == group - 1)
    def _():
        for copy in halos:
            copy.wait_recv()
        for j in range(group):
            gn_own[count - HALO :, :] += halo_land[j].astype(F32)

    for j in range(group):
        pl.when(col == group + j)(halos[j].wait_send)
    flat_next()
    step = 64
    for at in range(0, count, step):
        rows = slice(at, at + step)
        values = tok_vm[rows, :].astype(F32)
        inv = lax.rsqrt(jnp.mean(values * values, axis=-1, keepdims=True) + EPSILON)
        unit = values * inv
        pulled = gn_own[rows, :] * gain_vm[0:1, :]
        mean = jnp.mean(pulled * unit, axis=-1, keepdims=True)
        gn_own[rows, :] = cot_vm[rows, :].astype(F32) + inv * (pulled - unit * mean)
    tg_keep = keep(gn_own, tg_out)
    while flat_taken[0] < len(flat_steps):
        flat_next()
    flat_keep = keep(acc, flat_out)
    arrive(v_moves)
    arrive(e_moves)
    for copy in [v_keep, e_keep, tg_keep, flat_keep]:
        copy.wait()
    for copy in started:
        copy.wait_send()


def settle(cols, dps, heads, span, gn, gnb, joint, flat, tokens, cotangent, gain, shard):
    half, wide = joint.shape
    width, wide_a = 2 * half, wide - shard
    piece = half // dps
    count = tokens.shape[0]
    group = cols // 2
    any_spec = pl.BlockSpec(memory_space=pl.ANY)
    steps = (dps.bit_length() - 1) + (cols.bit_length() - 1) + 1
    copies = (group - 1) + group + steps + 4 * (dps - 1) + 2 + (cols - 1)
    vmem = pltpu.VMEM
    return pl.pallas_call(
        partial(settle_kernel, cols, dps, heads, span),
        in_specs=[any_spec] * 7,
        out_specs=[any_spec] * 4,
        out_shape=[
            sds((count, width)), sds((half, shard)), sds((half, 128 + span)), sds(flat.shape),
        ],
        scratch_shapes=[
            vmem((half, wide_a), F32), vmem((half, shard), F32),
            vmem((dps - 1, piece, wide_a), BF), vmem((dps - 1, piece, wide_a), BF),
            vmem((dps - 1, piece, shard), BF), vmem((dps - 1, piece, shard), BF),
            vmem((piece, wide_a), F32), vmem((piece, shard), F32),
            vmem((piece, shard), BF), vmem((piece, shard), BF),
            vmem((piece, 128), F32), vmem((cols, piece, span), F32),
            vmem((piece, 128 + span), F32),
            vmem(flat.shape, F32), vmem((steps,) + flat.shape, F32),
            vmem((count, width), F32), vmem((max(group - 1, 1), count, width), BF),
            vmem((group, HALO, width), BF),
            vmem((count, width), BF), vmem((count, width), BF), vmem((1, width), F32),
            pltpu.SemaphoreType.DMA((11,)),
            pltpu.SemaphoreType.DMA((copies,)),
            pltpu.SemaphoreType.DMA((copies,)),
        ],
        compiler_params=pltpu.CompilerParams(
            collective_id=2, has_side_effects=True, vmem_limit_bytes=VMEM_LIMIT
        ),
        cost_estimate=cost(90),
        name="settle",
    )(gn, gnb, joint, flat, tokens, cotangent, gain)


def flips(size, by):
    return [(i, i ^ by) for i in range(size)]


def butterfly(values, axis):
    size = lax.axis_size(axis)
    by = 1
    while by < size:
        values = values + lax.ppermute(values, axis, flips(size, by))
        by *= 2
    return values


def at_rows(values, index, size):
    return lax.dynamic_slice_in_dim(values, index * size, size, axis=0)


def collect_dp(piece, dp):
    size = lax.axis_size("dp")
    rows = piece.shape[0]
    out = jnp.zeros((size * rows,) + piece.shape[1:], piece.dtype)
    out = lax.dynamic_update_slice_in_dim(out, piece, dp * rows, 0)
    for by in range(1, size):
        other = lax.ppermute(piece, "dp", flips(size, by))
        out = lax.dynamic_update_slice_in_dim(out, other, (dp ^ by) * rows, 0)
    return out


def swap_core(values):
    return lax.ppermute(values, "row", [(0, 1), (1, 0)])


def per_device(
    tokens, norm_gain, w_gate, w_value, w_state, w_step, conv_value, bias_value, conv_state,
    bias_state, a_log, d_skip, dt_bias, mix_gain, w_out, cotangent,
):
    cols, rows_n, dps = lax.axis_size("col"), lax.axis_size("row"), lax.axis_size("dp")
    col, row, dp = lax.axis_index("col"), lax.axis_index("row"), lax.axis_index("dp")
    group = cols // 2
    place = lax.rem(col, group)
    local, width = tokens.shape
    span = local * group
    half_width = width // 2
    shard = w_value.shape[1]
    channels = 2 * shard
    heads = a_log.shape[0]
    inner_channels = shard * cols
    state_all = w_state.shape[1] * cols
    mirror = [(i, cols - 1 - i) for i in range(cols)]
    forth = [(i, cols - 1 - i) for i in range(group)]
    back = [(cols - 1 - i, i) for i in range(group)]

    def ring(by):
        return [(i, (i // group) * group + (i % group + by) % group) for i in range(cols)]

    state_width = w_state.shape[1]
    small = jnp.pad(
        jnp.concatenate([w_state, w_step], axis=1), ((0, 0), (0, 128 - state_width - heads))
    )
    heads_row = jnp.pad(
        jnp.concatenate([d_skip, a_log, dt_bias]), (0, shard - 3 * heads)
    )[None]
    state_rows = jnp.concatenate([conv_state.T, bias_state[None]], axis=0)
    vec = jnp.concatenate(
        [
            conv_value.T, bias_value[None], mix_gain[None], heads_row, jnp.zeros((1, shard), BF),
            jnp.pad(state_rows, ((0, 3), (0, shard - state_width))),
        ],
        axis=0,
    )
    group_tokens, value_full, small_full, vecs = import_all(cols, dps, tokens, w_value, small, vec)
    from_col = lax.broadcasted_iota(jnp.int32, (cols * 128, TILE + 128), 0) // 128
    from_lane = lax.broadcasted_iota(jnp.int32, (cols * 128, TILE + 128), 0) % 128
    to = lax.broadcasted_iota(jnp.int32, (cols * 128, TILE + 128), 1)
    head_to = to - TILE
    is_state = (to < TILE) & (from_lane < state_width) & (from_col * state_width + from_lane == to)
    is_own = (from_col == col) & (head_to < heads) & (from_lane == state_width + head_to)
    is_mirror = (from_col == cols - 1 - col) & (head_to >= heads) & (head_to < 2 * heads)
    is_mirror = is_mirror & (from_lane == state_width + head_to - heads)
    pick = (is_state | ((head_to >= 0) & (is_own | is_mirror))).astype(BF)

    vecs = vecs.astype(F32)
    both = jnp.concatenate(
        [
            lax.dynamic_index_in_dim(vecs, col, 0, keepdims=False),
            lax.dynamic_index_in_dim(vecs, cols - 1 - col, 0, keepdims=False),
        ],
        axis=1,
    )
    state_vecs = jnp.transpose(vecs[:, 8:16, :state_width], (1, 0, 2)).reshape(8, state_all)
    taps = jnp.concatenate([both[0:8], state_vecs], axis=1)

    def both_heads(at):
        return jnp.concatenate(
            [both[6, at * heads : (at + 1) * heads], both[6, shard + at * heads : shard + (at + 1) * heads]]
        )

    skip_both, a_both, dt_both = both_heads(0), both_heads(1), both_heads(2)
    vectors = jnp.concatenate(
        [jnp.repeat(skip_both, HEAD)[None], both[5:6], jnp.zeros((6, channels), F32)], axis=0
    )
    rate = -jnp.exp(a_both)
    head_rows = jnp.pad(jnp.stack([dt_both, rate]), ((0, 6), (0, 128 - 2 * heads)))
    head_of = np.arange(channels) // HEAD
    one_hot = (np.arange(128)[:, None] == head_of[None, :]).astype(np.float32)
    spread = jnp.asarray(np.concatenate([one_hot, one_hot], axis=0), BF)
    gather = jnp.asarray(one_hot.T, BF)

    gain = norm_gain.astype(F32)
    (
        raw, act, normed, step_in, step, cum, grow, offs, inv_rms, picked, states, y0, graw, gm, early,
        group_cot, gate_full, out_full,
    ) = forward_all(
        cols, dps, group_tokens, gain[None], value_full, small_full, pick, taps, head_rows, spread, cotangent,
        w_gate, w_out,
    )
    y, mixed, grad_gate, dy, mix_sums, after, first_grad = gate_and_mix(
        cols, inner_channels, y0, graw, gm, act, early, grow, spread, vectors, cum
    )
    (
        ga, grad_step, gbc, head_sums, out_total, gate_own, gate_cross, branch, branch_in, _, _,
    ) = scan_backward(
        cols, dps, dy, act, y, step, cum, step_in, spread, gather, after, states, early, offs, head_rows, vectors,
        mixed, out_full, grad_gate, first_grad, group_cot, normed,
    )
    block_out = (tokens.astype(F32) + branch + jnp.sum(branch_in.astype(F32), axis=0)).astype(BF)
    state_part = state_all // group

    value_sums, grad_normed, grad_normed_low, norm_sums, joint, sum_out, sum_gate = finish(
        cols, dps, state_part, ga, raw, taps, grad_gate, grad_step, value_full, gate_full, picked, group_tokens,
        inv_rms, gate_own, out_total, gate_cross, gbc, normed,
    )
    whole_state = state_part % 128 != 0
    span = state_all if whole_state else state_part

    wide = jnp.concatenate([value_sums[:5, :channels], mix_sums[0:1]], axis=0)
    wide_all = jnp.zeros((6, inner_channels), F32)
    wide_all = lax.dynamic_update_slice_in_dim(wide_all, wide[:, :shard], col * shard, 1)
    wide_all = lax.dynamic_update_slice_in_dim(wide_all, wide[:, shard:], (cols - 1 - col) * shard, 1)
    state_wide = jnp.zeros((5, state_all), F32)
    state_wide = lax.dynamic_update_slice_in_dim(
        state_wide, value_sums[:5, channels : channels + span], 0 if whole_state else place * state_part, 1
    )
    skip_heads = jnp.sum(mix_sums[1].reshape(2 * heads, HEAD), axis=1)
    head_parts = jnp.stack([head_sums[0, : 2 * heads] * rate, skip_heads, head_sums[1, : 2 * heads]])
    head_all = jnp.zeros((3, heads * cols), F32)
    head_all = lax.dynamic_update_slice_in_dim(head_all, head_parts[:, :heads], col * heads, 1)
    head_all = lax.dynamic_update_slice_in_dim(head_all, head_parts[:, heads:], (cols - 1 - col) * heads, 1)
    lengths = [wide_all.size, state_wide.size, head_all.size, width]
    flat = jnp.concatenate(
        [wide_all.reshape(-1), state_wide.reshape(-1), head_all.reshape(-1), norm_sums[0]]
    )
    flat = jnp.pad(flat, (0, -flat.size % 1024)).reshape(-1, 128)
    tokens_grad, sum_value, extra, flat = settle(
        cols, dps, heads, span, grad_normed, grad_normed_low, joint, flat, tokens, cotangent, gain[None], shard
    )
    sum_step = extra[:, :heads]
    sum_state = lax.dynamic_slice_in_dim(
        extra, 128 + (col if whole_state else lax.rem(col, cols // group)) * state_width, state_width, axis=1
    )
    flat = flat.reshape(-1)
    ends = [sum(lengths[: i + 1]) for i in range(4)]
    wide_all = flat[: ends[0]].reshape(6, inner_channels)
    state_wide = flat[ends[0] : ends[1]].reshape(5, state_all)
    head_all = flat[ends[1] : ends[2]].reshape(3, heads * cols)
    norm_total = flat[ends[2] : ends[3]]
    wide_own = lax.dynamic_slice_in_dim(wide_all, col * shard, shard, axis=1)
    state_own = lax.dynamic_slice_in_dim(state_wide, col * state_width, state_width, axis=1)
    head_own = lax.dynamic_slice_in_dim(head_all, col * heads, heads, axis=1)

    return (
        block_out,
        tokens_grad,
        norm_total,
        sum_gate,
        sum_value,
        sum_state,
        sum_step,
        wide_own[:4].T,
        wide_own[4],
        state_own[:4].T,
        state_own[4],
        head_own[0],
        head_own[1],
        head_own[2],
        wide_own[5],
        sum_out,
    )


def solution(mesh):
    rows = P(("dp", "row", "col"), None)
    grid = P("row", "col")
    vec = P("col")
    taps = P("col", None)
    return jax.shard_map(
        per_device,
        mesh=mesh,
        in_specs=(
            rows, P(), grid, grid, grid, grid, taps, vec, taps, vec, vec, vec, vec, vec,
            P("col", "row"), rows,
        ),
        out_specs=(
            rows, rows, P(), grid, grid, grid, grid, taps, vec, taps, vec, vec, vec, vec, vec,
            P("col", "row"),
        ),
        check_vma=False,
    )
```

```python
from functools import partial

import jax
import jax.numpy as jnp
import numpy as np
from jax import lax
from jax.experimental import pallas as pl
from jax.experimental.pallas import tpu as pltpu
from jax.sharding import PartitionSpec as P

BF = jnp.bfloat16
F32 = jnp.float32
EPSILON = 1e-05
N = 128
Q = 128
HEAD = 64
HALO = 16
ROWS = 64
TILE = 256
HIGHEST = lax.Precision.HIGHEST
VMEM_LIMIT = 56 * 2**20


def mm(a, b):
    return lax.dot_general(a, b, (((1,), (0,)), ((), ())), preferred_element_type=F32)


def mm_nt(a, b):
    return lax.dot_general(a, b, (((1,), (1,)), ((), ())), preferred_element_type=F32)


def mm_exact(a, b):
    return lax.dot_general(
        a, b, (((1,), (0,)), ((), ())), precision=HIGHEST, preferred_element_type=F32
    )


def split2(values):
    high = values.astype(BF)
    return high, (values - high.astype(F32)).astype(BF)


def sigmoid(values):
    return 1.0 / (1.0 + jnp.exp(-values))


def iota2(shape, axis):
    return lax.broadcasted_iota(jnp.int32, shape, axis)


def params(*names):
    return pltpu.CompilerParams(
        dimension_semantics=names or ("arbitrary",), vmem_limit_bytes=VMEM_LIMIT
    )


def cost(micros):
    return pl.CostEstimate(flops=0, bytes_accessed=int(micros * 3.0e6), transcendentals=0)


def whole(shape):
    return pl.BlockSpec(shape, lambda *_: (0,) * len(shape))


def columns(rows, width=TILE):
    return pl.BlockSpec((rows, width), lambda j: (0, j))


def sds(shape, dtype=F32):
    return jax.ShapeDtypeStruct(shape, dtype)


def here():
    return lax.axis_index("dp"), lax.axis_index("row"), lax.axis_index("col")


def lanes_at(index, size):
    return pl.ds(pl.multiple_of(index * size, 128), size)


def greet(others):
    barrier = pltpu.get_barrier_semaphore()
    for other in others:
        pl.semaphore_signal(barrier, inc=1, device_id=other, device_id_type=pl.DeviceIdType.MESH)
    pl.semaphore_wait(barrier, len(others))


def at_step(step):
    return pl.when(pl.program_id(0) == step)


def copy_to(src, dst, sems, i, device):
    return pltpu.make_async_remote_copy(
        src_ref=src, dst_ref=dst, send_sem=sems.at[0, i], recv_sem=sems.at[1, i],
        device_id=device, device_id_type=pl.DeviceIdType.MESH,
    )


def dp_copies(dps, sems, src_of, dst_of, first=0):
    dp, row, col = here()
    return [
        copy_to(src_of(dp ^ by, by - 1), dst_of(dp ^ by, by - 1), sems, first + by - 1, (dp ^ by, row, col))
        for by in range(1, dps)
    ]


def hand_out(dps, sems, first, src, out):
    dp, row, col = here()
    piece, lanes = src.shape
    rows = lambda d: pl.ds(d * piece, piece)
    if dps != 4:
        return dp_copies(dps, sems, lambda to, i: src, lambda to, i: out.at[rows(dp), :], first), []
    left, right = pl.ds(0, lanes // 2), pl.ds(lanes // 2, lanes // 2)
    near = [
        copy_to(src, out.at[rows(dp), :], sems, first + i, (dp ^ by, row, col)) for i, by in enumerate((1, 2))
    ]
    far = []
    for i, (by, half) in enumerate(((1, left), (2, right))):
        passed = out.at[rows(dp ^ by), half]
        far.append(copy_to(passed, passed, sems, first + 2 + i, (dp ^ 3 ^ by, row, col)))
    return near, far


def dp_peers(dps):
    dp, row, col = here()
    return [(dp ^ by, row, col) for by in range(1, dps)]


def mirror_of(cols):
    dp, row, col = here()
    return (dp, row, cols - 1 - col)


def remote_params(collective_id):
    return pltpu.CompilerParams(
        dimension_semantics=("arbitrary",), vmem_limit_bytes=VMEM_LIMIT, collective_id=collective_id,
        has_side_effects=True,
    )


ANY = pl.BlockSpec(memory_space=pl.ANY)


def import_kernel(
    cols, dps, tok, wv, sw, vec, tg, vf, sf, vecs, zeros, tok_vm, w_vm, s_vm, vec_vm, local, send, recv,
):
    dp, row, col = here()
    group = cols // 2
    place = lax.rem(col, group)
    half, shard = wv.shape
    count = tok.shape[0]
    piece = half // dps
    sibling = (dp, 1 - row, col)
    mirror = (dp, row, cols - 1 - col)
    col_peer = lambda by: (dp, row, col ^ by)
    dp_peer = lambda by: (dp ^ by, row, col)
    greet(
        [sibling]
        + [col_peer(by) for by in range(1, cols)]
        + [dp_peer(by) for by in range(1, dps)]
    )
    used = [0]
    started = []

    def remote(src, dst, device):
        i = used[0]
        used[0] += 1
        return pltpu.make_async_remote_copy(
            src_ref=src, dst_ref=dst, send_sem=send.at[i], recv_sem=recv.at[i],
            device_id=device, device_id_type=pl.DeviceIdType.MESH,
        )

    def launch(src, dst, device):
        copy = remote(src, dst, device)
        copy.start()
        started.append(copy)
        return copy

    def keep(i, src, dst):
        copy = pltpu.make_async_copy(src, dst, local.at[i])
        copy.start()
        return copy

    my_rows = pl.ds(row * half, half)
    my_piece = pl.ds(row * half + dp * piece, piece)
    own, other = pl.ds(0, shard), pl.ds(shard, shard)
    src_piece = pl.ds(dp * piece, piece)

    staged = [
        keep(6, vec, vec_vm),
        keep(0, sw.at[src_piece, :], s_vm),
        keep(2, tok, tok_vm),
        keep(3, wv, w_vm),
    ]
    s_cross = [
        launch(sw.at[src_piece, :], sf.at[my_piece, lanes_at(col, 128)], col_peer(by))
        for by in range(1, cols)
    ]
    v_cross = launch(wv.at[src_piece, :], vf.at[my_piece, other], mirror)
    vec_cross = [launch(vec, vecs.at[col], col_peer(by)) for by in range(1, cols)]
    my_tokens = tg.at[pl.ds(HALO + place * count, count), :]
    tok_cross = [launch(tok, my_tokens, col_peer(by)) for by in range(1, group)]
    halo_src = tok.at[pl.ds(count - HALO, HALO), :]
    halo_dst = tg.at[pl.ds(0, HALO), :]
    halo_at = used[0]
    used[0] += group
    halos = [
        pltpu.make_async_remote_copy(
            src_ref=halo_src, dst_ref=halo_dst, send_sem=send.at[halo_at + j], recv_sem=recv.at[halo_at],
            device_id=(dp, row, group + j), device_id_type=pl.DeviceIdType.MESH,
        )
        for j in range(group)
    ]

    @pl.when(col == group - 1)
    def _():
        for copy in halos:
            copy.start()

    zeros[...] = jnp.zeros_like(zeros)

    @pl.when(col < group)
    def _():
        clear = pltpu.make_async_copy(zeros, halo_dst, local.at[1])
        clear.start()
        clear.wait()

    v_own = launch(wv, vf.at[my_rows, own], sibling)
    for copy in staged:
        copy.wait()
    small_own = keep(0, s_vm, sf.at[my_piece, lanes_at(col, 128)])
    kept = [
        keep(6, vec_vm, vecs.at[col]),
        keep(2, tok_vm, my_tokens),
        keep(3, w_vm, vf.at[my_rows, own]),
    ]

    def spread_out(ref):
        return [launch(ref, ref, dp_peer(by)) for by in range(1, dps)]

    def arrive(copies):
        for copy in copies:
            copy.wait_recv()

    arrive(s_cross)
    small_own.wait()
    s_dp = spread_out(sf.at[my_piece, :])
    arrive([v_cross])
    v_dp = spread_out(vf.at[my_piece, other])
    arrive(s_dp)
    last = [launch(sf.at[my_rows, :], sf.at[my_rows, :], sibling)]
    arrive(v_dp)
    last += [launch(vf.at[my_rows, other], vf.at[my_rows, other], sibling)]
    arrive(last)
    arrive([v_own])
    arrive(vec_cross)
    arrive(tok_cross)

    @pl.when(col >= group)
    def _():
        halos[0].wait_recv()

    @pl.when(col == group - 1)
    def _():
        for copy in halos:
            copy.wait_send()

    for copy in kept:
        copy.wait()
    for copy in started:
        copy.wait_send()


def import_all(cols, dps, tokens, w_value, small, vec):
    half, shard = w_value.shape
    count, width = tokens.shape
    any_spec = pl.BlockSpec(memory_space=pl.ANY)
    copies = 1 + 2 * (cols - 1) + (cols // 2 - 1) + cols // 2 + 1 + 2 * (dps - 1) + 2
    return pl.pallas_call(
        partial(import_kernel, cols, dps),
        in_specs=[any_spec] * 4,
        out_specs=[any_spec] * 4,
        out_shape=[
            sds((HALO + count * (cols // 2), width), BF),
            sds((2 * half, 2 * shard), BF),
            sds((2 * half, cols * 128), BF),
            sds((cols,) + vec.shape, BF),
        ],
        scratch_shapes=[
            pltpu.VMEM((HALO, width), BF),
            pltpu.VMEM((count, width), BF),
            pltpu.VMEM((half, shard), BF),
            pltpu.VMEM((half // dps, 128), BF),
            pltpu.VMEM(vec.shape, BF),
            pltpu.SemaphoreType.DMA((7,)),
            pltpu.SemaphoreType.DMA((copies,)),
            pltpu.SemaphoreType.DMA((copies,)),
        ],
        compiler_params=pltpu.CompilerParams(
            collective_id=1, has_side_effects=True, vmem_limit_bytes=VMEM_LIMIT
        ),
        cost_estimate=cost(45),
        name="import_all",
    )(tokens, w_value, small, vec)


def conv_window(raw_ref, start, size):
    window = raw_ref[HALO + start - 8 : HALO + start + size, :]
    return [pltpu.roll(window, 3 - k, 0)[8:, :] for k in range(3)] + [window[8:, :]]


def conv_rows(moved, taps):
    total = taps[4:5, :] + taps[0:1, :] * moved[0]
    for k in range(1, 4):
        total = total + taps[k : k + 1, :] * moved[k]
    return total


def normalize(tok_ref, gain_ref, normed_ref, inv_ref):
    tokens = tok_ref.shape[0] - HALO
    for at in [0] + list(range(HALO, HALO + tokens, Q)):
        size = HALO if at == 0 else Q
        values = tok_ref[at : at + size, :].astype(F32)
        inv = lax.rsqrt(jnp.mean(values * values, axis=-1, keepdims=True) + EPSILON)
        normed_ref[at : at + size, :] = (values * inv * gain_ref[0:1, :]).astype(BF)
        inv_ref[at : at + size, :] = jnp.broadcast_to(inv, (size, 128))


def project_steps(
    small_ref, pick_ref, head_ref, normed_ref, raw_ref, stepin_ref, step_ref, cum_ref, grow_ref, offs_ref,
    picked_ref,
):
    tokens = step_ref.shape[0]
    picked = mm(small_ref[...], pick_ref[...]).astype(BF)
    picked_ref[...] = picked
    raw_ref[...] = mm(normed_ref[...], picked[:, :TILE])
    step_in = mm(normed_ref[HALO:, :], picked[:, TILE:]) + head_ref[0:1, :]
    small = jnp.exp(-jnp.abs(step_in))
    plus = 1.0 + small
    safe = jnp.where(plus == 1.0, 1.0, plus - 1.0)
    log_part = jnp.where(plus == 1.0, small, jnp.log(plus) * (small / safe))
    step = jnp.maximum(step_in, 0.0) + log_part
    stepin_ref[...] = step_in
    step_ref[...] = step
    falls = step * head_ref[1:2, :]
    lower = (iota2((Q, Q), 0) >= iota2((Q, Q), 1)).astype(F32)
    before = jnp.zeros((1, 128), F32)
    offs_ref[...] = jnp.zeros_like(offs_ref)
    for b in range(tokens // Q):
        rows = slice(b * Q, b * Q + Q)
        cum = mm_exact(lower, falls[rows, :])
        cum_ref[rows, :] = cum
        high, low = split2(jnp.exp(cum + before))
        grow_ref[rows, 0:128] = high
        grow_ref[rows, 128:256] = low
        before = before + cum[Q - 1 : Q, :]
        offs_ref[b + 1 : b + 2, :] = before


def activate(raw_ref, taps, act_ref, copy_ref):
    tokens = act_ref.shape[0]
    for at in range(0, tokens, ROWS):
        pre = conv_rows(conv_window(raw_ref, at, ROWS), taps)
        act = (pre * sigmoid(pre)).astype(BF)
        act_ref[at : at + ROWS, :] = act
        copy_ref[at : at + ROWS, :] = act


def expand(per_head, spread):
    high, low = split2(per_head)
    return mm(jnp.concatenate([high, low], 1), spread)


def transpose_bf(values):
    return values.astype(F32).T.astype(BF)


def expand_rows(per_head, spread):
    high, low = split2(jnp.concatenate(per_head, 0))
    return mm(jnp.concatenate([high, low], 1), spread)


def eight(row):
    return jnp.broadcast_to(row, (8, row.shape[1]))


def spans(total, size):
    size = min(size, total)
    return [slice(at, at + size) for at in range(0, total, size)]


def state_block(x_ref, b_ref, step_ref, cum_ref, spread_ref, held):
    cum = cum_ref[...]
    end = cum[Q - 1 : Q, :]
    tail = jnp.exp(end - cum) * step_ref[...]
    b_t = transpose_bf(b_ref[...])
    b_t2 = jnp.concatenate([b_t, b_t], 1)
    for lanes in spans(x_ref.shape[1], 1536):
        wide = expand_rows([tail, eight(jnp.exp(end))], spread_ref[:, lanes])
        high, low = split2(wide[:Q] * x_ref[:, lanes].astype(F32))
        fresh = mm(b_t2, jnp.concatenate([high, low], 0))
        held[:, lanes] = held[:, lanes] * wide[Q : Q + 1, :] + fresh


def forward_block(x_ref, b_ref, c_ref, step_ref, cum_ref, spread_ref, state_ref, y_ref):
    b_blk, c_blk = b_ref[...], c_ref[...]
    affinity = mm_nt(c_blk, b_blk)
    causal = iota2((Q, Q), 0) >= iota2((Q, Q), 1)
    first = iota2((Q, 128), 1) < HEAD
    cum = cum_ref[...]
    cum_t = cum.T
    step_t = step_ref[...].T
    growth = jnp.exp(cum)
    c2 = jnp.concatenate([c_blk, c_blk], 1)
    zero = jnp.zeros((Q, 128), BF)
    for lanes in spans(x_ref.shape[1], 1536):
        s_high, s_low = split2(state_ref[0, :, lanes])
        reached = mm(c2, jnp.concatenate([s_high, s_low], 0)) * expand_rows([growth], spread_ref[:, lanes])
        for at in range(lanes.start, lanes.stop, 128):
            x_pair = x_ref[:, at : at + 128]
            x0, x1 = jnp.where(first, x_pair, zero), jnp.where(first, zero, x_pair)
            pieces = []
            for half in range(2):
                h = at // HEAD + half
                spread_h = cum[:, h : h + 1] - cum_t[h : h + 1, :]
                decay = jnp.exp(jnp.where(causal, spread_h, -1e30))
                pieces += split2(affinity * decay * step_t[h : h + 1, :])
            intra = mm(jnp.concatenate(pieces, 1), jnp.concatenate([x0, x0, x1, x1], 0))
            inside = at - lanes.start
            y_ref[:, at : at + 128] = intra + reached[:, inside : inside + 128]


def forward_all_kernel(
    cols, dps,
    tok_ref, gain_ref, w_ref, small_ref, pick_ref, taps_ref, head_ref, spread_ref, cot, wg, wo,
    raw_ref, act_ref, normed_ref, stepin_ref, step_ref, cum_ref, grow_ref, offs_ref, inv_ref, picked_ref,
    states_ref, y_ref, graw_ref, gm_ref, early_ref, cot_out, gf, of,
    act_vm, states_vm, held, early_land, cot_vm, g_tiles, o_tiles, wg_vm, wo_vm, sems, local,
):
    step = pl.program_id(0)
    tokens, channels = states_vm.shape[0] * Q, held.shape[1]
    blocks = states_vm.shape[0]
    tiles = channels // TILE
    scan_at = tiles + 1
    out_at = scan_at + blocks
    gate_at = out_at + blocks
    dp, row, col = here()
    group = cols // 2
    place = lax.rem(col, group)
    half, shard = wg.shape
    count = cot.shape[0]
    others = dps - 1
    piece, piece_out = half // dps, wo.shape[0] // dps
    sibling, mirror = (dp, 1 - row, col), mirror_of(cols)
    peers = [(dp, row, col ^ by) for by in range(1, group)]
    my_rows = pl.ds(row * half, half)
    my_piece = pl.ds(row * half + dp * piece, piece)
    out_piece = pl.ds(shard + dp * piece_out, piece_out)
    my_lanes = lanes_at(row, half)
    own, other = pl.ds(0, shard), pl.ds(shard, shard)
    src_piece, src_out = pl.ds(dp * piece, piece), pl.ds(dp * piece_out, piece_out)
    my_cot = cot_vm.at[pl.ds(place * count, count), :]

    g_cross = lambda: copy_to(wg.at[src_piece, :], gf.at[my_piece, other], sems, 0, mirror)
    o_cross = lambda: copy_to(wo.at[src_out, :], of.at[out_piece, my_lanes], sems, 1, mirror)
    g_own = lambda: copy_to(wg, gf.at[my_rows, own], sems, 2, sibling)
    o_own = lambda: copy_to(wo, of.at[own, my_lanes], sems, 3, sibling)
    g_rest = lambda: copy_to(gf.at[my_rows, other], gf.at[my_rows, other], sems, 4, sibling)
    o_rest = lambda: copy_to(of.at[other, my_lanes], of.at[other, my_lanes], sems, 5, sibling)
    early_moves = lambda: [
        copy_to(held.at[:, own], early_land.at[:, other], sems, 6, mirror),
        copy_to(held.at[:, other], early_land.at[:, own], sems, 7, mirror),
    ]
    cot_moves = lambda: [copy_to(cot, my_cot, sems, 8 + i, peer) for i, peer in enumerate(peers)]
    first = 8 + group - 1

    def g_dp():
        ref = gf.at[my_piece, other]
        return dp_copies(dps, sems, lambda to, i: ref, lambda to, i: ref, first)

    def o_dp():
        ref = of.at[out_piece, my_lanes]
        return dp_copies(dps, sems, lambda to, i: ref, lambda to, i: ref, first + others)

    load_cot = pltpu.make_async_copy(cot, my_cot, local.at[0])
    load_g = pltpu.make_async_copy(wg, wg_vm, local.at[1])
    load_o = pltpu.make_async_copy(wo, wo_vm, local.at[2])
    store_g = pltpu.make_async_copy(wg_vm, gf.at[my_rows, own], local.at[1])
    store_o = pltpu.make_async_copy(wo_vm, of.at[own, my_lanes], local.at[2])
    store_cot = pltpu.make_async_copy(cot_vm, cot_out, local.at[0])

    def g_tile(at):
        return pltpu.make_async_copy(gf.at[:, lanes_at(at, TILE)], g_tiles.at[lax.rem(at, 2)], local.at[3])

    def o_tile(at):
        rows = pl.ds(pl.multiple_of(at * TILE, TILE), TILE)
        return pltpu.make_async_copy(of.at[rows, :], o_tiles.at[lax.rem(at, 2)], local.at[4])

    @at_step(0)
    def _():
        load_cot.start()
        load_g.start()
        load_o.start()
        greet([sibling, mirror] + peers + dp_peers(dps))
        for move in [g_cross(), o_cross(), g_own(), o_own()]:
            move.start()
        normalize(tok_ref, gain_ref, normed_ref, inv_ref)

    @at_step(1)
    def _():
        load_g.wait()
        store_g.start()
        load_o.wait()
        store_o.start()

    @at_step(tiles - 2)
    def _():
        for move in cot_moves():
            move.start()

    @at_step(scan_at + 2)
    def _():
        g_cross().wait_recv()
        for move in g_dp():
            move.start()

    @at_step(out_at)
    def _():
        o_cross().wait_recv()
        for move in o_dp():
            move.start()

    @at_step(out_at + blocks // 2)
    def _():
        for move in g_dp():
            move.wait_recv()
        g_rest().start()

    @at_step(gate_at + tiles // 2)
    def _():
        for move in o_dp():
            move.wait_recv()
        o_rest().start()

    @at_step(out_at)
    def _():
        @pl.when(col < group)
        def _():
            for move in early_moves():
                move.start()

    @pl.when(step < tiles)
    def _():
        raw_ref[...] = mm(normed_ref[...], w_ref[...])

    @pl.when(step == tiles)
    def _():
        project_steps(
            small_ref, pick_ref, head_ref, normed_ref, raw_ref, stepin_ref, step_ref, cum_ref, grow_ref, offs_ref,
            picked_ref,
        )

    @pl.when(step <= tiles)
    def _():
        activate(raw_ref, taps_ref[...], act_ref, act_vm.at[:, lanes_at(step, TILE)])

    def block_refs(at):
        rows = pl.ds(pl.multiple_of(at * Q, Q), Q)
        return (
            act_vm.at[rows, pl.ds(0, channels)], act_vm.at[rows, pl.ds(channels, N)],
            act_vm.at[rows, pl.ds(channels + N, N)], step_ref.at[rows, :], cum_ref.at[rows, :],
        )

    @pl.when(step == scan_at)
    def _():
        held[...] = jnp.zeros_like(held)

    @pl.when((step >= scan_at) & (step < out_at))
    def _():
        x_blk, b_blk, _, step_blk, cum_blk = block_refs(step - scan_at)
        states_ref[0] = held[...]
        states_vm[step - scan_at] = held[...]
        state_block(x_blk, b_blk, step_blk, cum_blk, spread_ref, held)

    @pl.when(step == out_at)
    def _():
        states_ref[0] = held[...]

    @pl.when((step >= out_at) & (step < gate_at))
    def _():
        x_blk, b_blk, c_blk, step_blk, cum_blk = block_refs(step - out_at)
        forward_block(
            x_blk, b_blk, c_blk, step_blk, cum_blk, spread_ref, states_vm.at[pl.ds(step - out_at, 1)], y_ref
        )

    @pl.when(step == gate_at)
    def _():
        for move in [g_own(), g_rest()]:
            move.wait_recv()
        store_g.wait()
        g_tile(0).start()

    @pl.when((step >= gate_at) & (step < gate_at + tiles))
    def _():
        at = step - gate_at
        g_tile(at).wait()

        @pl.when(at < tiles - 1)
        def _():
            g_tile(at + 1).start()

        graw_ref[...] = mm(normed_ref[HALO:, :], g_tiles[lax.rem(at, 2)])

    @pl.when(step == gate_at + tiles)
    def _():
        for move in [o_own(), o_rest()] + cot_moves():
            move.wait_recv()
        store_o.wait()
        load_cot.wait()
        store_cot.start()
        o_tile(0).start()

    @pl.when(step >= gate_at + tiles)
    def _():
        at = step - gate_at - tiles
        o_tile(at).wait()

        @pl.when(at < tiles - 1)
        def _():
            o_tile(at + 1).start()

        gm_ref[...] = mm_nt(cot_vm[...], o_tiles[lax.rem(at, 2)])

    @at_step(pl.num_programs(0) - 1)
    def _():
        store_cot.wait()
        for move in [g_cross(), o_cross(), g_own(), o_own(), g_rest(), o_rest()] + cot_moves() + g_dp() + o_dp():
            move.wait_send()

        @pl.when(col < group)
        def _():
            for move in early_moves():
                move.wait_send()
            early_ref[...] = jnp.zeros_like(early_ref)

        @pl.when(col >= group)
        def _():
            for move in early_moves():
                move.wait_recv()
            early_ref[...] = early_land[...]


def forward_all(cols, dps, group_tokens, gain, weights, small, pick, taps, head_rows, spread, cotangent, w_gate, w_out):
    rows, width = group_tokens.shape
    tokens = rows - HALO
    channels = weights.shape[1]
    total = channels + TILE
    blocks, tiles = tokens // Q, channels // TILE
    half, shard = w_gate.shape
    scan_at = tiles + 1
    out_at = scan_at + blocks
    gate_at = out_at + blocks

    def clamp(first, count):
        return lambda i: jnp.clip(i - first, 0, count - 1)

    lanes = lambda at, count: pl.BlockSpec((count, TILE), lambda i: (0, at(i)))
    both, value_at = clamp(0, tiles + 1), clamp(0, tiles)
    state_at, y_at = clamp(scan_at, blocks + 1), clamp(out_at, blocks)
    raw_tile, gm_tile = clamp(gate_at, tiles), clamp(gate_at + tiles, tiles)
    vmem = pltpu.VMEM
    return pl.pallas_call(
        partial(forward_all_kernel, cols, dps),
        grid=(gate_at + 2 * tiles,),
        in_specs=[
            whole((rows, width)),
            whole((1, width)),
            lanes(value_at, width),
            whole(small.shape),
            whole(pick.shape),
            lanes(both, 8),
            whole((8, 128)),
            whole(spread.shape),
            ANY, ANY, ANY,
        ],
        out_specs=[
            lanes(both, rows),
            lanes(both, tokens),
            whole((rows, width)),
            whole((tokens, 128)),
            whole((tokens, 128)),
            whole((tokens, 128)),
            whole((tokens, 256)),
            whole((16, 128)),
            whole((rows, 128)),
            whole((width, TILE + 128)),
            pl.BlockSpec((1, N, channels), lambda i: (state_at(i), 0, 0)),
            pl.BlockSpec((Q, channels), lambda i: (y_at(i), 0)),
            lanes(raw_tile, tokens),
            lanes(gm_tile, tokens),
            whole((N, channels)),
            ANY, ANY, ANY,
        ],
        out_shape=[
            sds((rows, total)),
            sds((tokens, total), BF),
            sds((rows, width), BF),
            sds((tokens, 128)),
            sds((tokens, 128)),
            sds((tokens, 128)),
            sds((tokens, 256), BF),
            sds((16, 128)),
            sds((rows, 128)),
            sds((width, TILE + 128), BF),
            sds((blocks + 1, N, channels)),
            sds((tokens, channels)),
            sds((tokens, channels)),
            sds((tokens, channels)),
            sds((N, channels)),
            sds((tokens, width), BF),
            sds((width, channels), BF),
            sds((channels, width), BF),
        ],
        scratch_shapes=[
            vmem((tokens, total), BF),
            vmem((blocks, N, channels), F32),
            vmem((N, channels), F32),
            vmem((N, channels), F32),
            vmem((tokens, width), BF),
            vmem((2, width, TILE), BF),
            vmem((2, TILE, width), BF),
            vmem((half, shard), BF),
            vmem((shard, half), BF),
            pltpu.SemaphoreType.DMA((2, 7 + cols // 2 + 2 * (dps - 1))),
            pltpu.SemaphoreType.DMA((5,)),
        ],
        compiler_params=remote_params(4),
        cost_estimate=cost(70),
        name="forward_all",
    )(group_tokens, gain, weights, small, pick, taps, head_rows, spread, cotangent, w_gate, w_out)


def grad_state_block(dy_tiles, c_ref, cum_ref, spread_ref, after_ref, held):
    after_ref[0] = held[...]
    growth = jnp.exp(cum_ref[...])
    c_t = transpose_bf(c_ref[...])
    c_t2 = jnp.concatenate([c_t, c_t], 1)
    wide = expand_rows([growth], spread_ref[...])
    for tile in range(held.shape[1] // TILE):
        lanes = slice(tile * TILE, tile * TILE + TILE)
        high, low = split2(dy_tiles[tile] * wide[:, lanes])
        direct = mm(c_t2, jnp.concatenate([high, low], 0))
        held[:, lanes] = held[:, lanes] * wide[Q - 1 : Q, lanes] + direct


def near_block(
    at_block, here_rows, dy_ref, x_ref, b_ref, c_ref, step_ref, cum_ref, spread_ref, state_ref, early_ref,
    offs_ref, gx_ref, gbc_ref,
):
    b_blk, c_blk = b_ref[...], c_ref[...]
    affinity_t = mm_nt(b_blk, c_blk)
    causal_t = iota2((Q, Q), 1) >= iota2((Q, Q), 0)
    first = iota2((Q, 128), 1) < HEAD
    cum = cum_ref[...]
    cum_t = cum.T
    step = step_ref[...]
    growth = jnp.exp(cum)
    early_fall = eight(jnp.exp(offs_ref[pl.ds(at_block, 1), :]))
    zero = jnp.zeros((Q, 128), BF)
    grad_affinity_t = jnp.zeros((Q, Q), F32)
    grad_c = jnp.zeros((Q, N), F32)
    for lanes in spans(x_ref.shape[1], 768):
        wide = expand_rows([growth, early_fall], spread_ref[:, lanes])
        before = state_ref[0, :, lanes] + wide[Q : Q + 1, :] * early_ref[:, lanes]
        dy_wide = dy_ref[:, lanes]
        s_high, s_low = split2(before)
        g_high, g_low = split2(dy_wide * wide[:Q])
        grad_c = grad_c + mm_nt(
            jnp.concatenate([g_high, g_low, g_high], 1), jnp.concatenate([s_high, s_high, s_low], 1)
        )
        for at in range(lanes.start, lanes.stop, 128):
            d_high, d_low = split2(dy_ref[:, at : at + 128])
            x_pair = x_ref[:, at : at + 128]
            x0, x1 = jnp.where(first, x_pair, zero), jnp.where(first, zero, x_pair)
            grad_mixing = mm_nt(
                jnp.concatenate([jnp.concatenate([x0, x0], 1), jnp.concatenate([x1, x1], 1)], 0),
                jnp.concatenate([d_high, d_low], 1),
            )
            left, right = [], []
            for half in range(2):
                h = at // HEAD + half
                spread_h = cum_t[h : h + 1, :] - cum[:, h : h + 1]
                decay = jnp.exp(jnp.where(causal_t, spread_h, -1e30))
                m_high, m_low = split2(affinity_t * decay)
                grad_affinity_t = grad_affinity_t + (
                    grad_mixing[half * Q : half * Q + Q, :] * decay * step[:, h : h + 1]
                )
                keep = first if half == 0 else jnp.logical_not(first)
                dh, dl = jnp.where(keep, d_high, zero), jnp.where(keep, d_low, zero)
                left += [m_high, m_low, m_high]
                right += [dh, dh, dl]
            gx_ref[here_rows, at : at + 128] = mm(jnp.concatenate(left, 1), jnp.concatenate(right, 0))
    a_high, a_low = split2(grad_affinity_t)
    gbc_ref[here_rows, 0:N] = mm(jnp.concatenate([a_high, a_low], 1), jnp.concatenate([c_blk, c_blk], 0))
    t_high, t_low = split2(grad_affinity_t.T)
    gbc_ref[here_rows, N : 2 * N] = grad_c + mm(
        jnp.concatenate([t_high, t_low], 1), jnp.concatenate([b_blk, b_blk], 0)
    )


def far_block(
    blocks, at_block, here_rows, dy_ref, x_ref, y_ref, gx_ref, b_ref, step_ref, cum_ref, stepin_ref, spread_ref,
    gather_ref, after_ref, late_ref, state_ref, early_ref, offs_ref, head_ref, skip_ref, gbc_ref,
    ga_ref, gstep_ref, gbc_out_ref, sums_ref,
):
    b_blk = b_ref[...]
    b2 = jnp.concatenate([b_blk, b_blk], 1)
    cum, step = cum_ref[...], step_ref[...]
    tail = jnp.exp(cum[Q - 1 : Q, :] - cum)
    offs_after = offs_ref[pl.ds(at_block + 1, 1), :]
    late_fall = eight(jnp.exp(offs_ref[pl.ds(blocks, 1), :] - offs_after))
    early_fall = eight(jnp.exp(offs_after))
    dots = jnp.zeros((2 * Q + 8, 128), F32)
    grad_b = gbc_ref[here_rows, 0:N]
    for lanes in spans(x_ref.shape[1], 512):
        wide = expand_rows([tail, step, late_fall, early_fall], spread_ref[:, lanes])
        tail_wide, step_wide = wide[:Q], wide[Q : 2 * Q]
        x = x_ref[:, lanes].astype(F32)
        dy = dy_ref[:, lanes]
        skip = skip_ref[0:1, lanes]
        d_state = after_ref[0, :, lanes] + wide[2 * Q : 2 * Q + 1, :] * late_ref[:, lanes]
        state = state_ref[0, :, lanes] + wide[2 * Q + 8 : 2 * Q + 9, :] * early_ref[:, lanes]
        touch = eight(jnp.sum(d_state * state, axis=0, keepdims=True))
        s_high, s_low = split2(d_state)
        gx = gx_ref[here_rows, lanes] + tail_wide * mm(b2, jnp.concatenate([s_high, s_low], 0))
        w_high, w_low = split2(tail_wide * step_wide * x)
        grad_b = grad_b + mm_nt(
            jnp.concatenate([w_high, w_low, w_high], 1), jnp.concatenate([s_high, s_high, s_low], 1)
        )
        ga_ref[:, lanes] = step_wide * gx + skip * dy
        high, low = split2(jnp.concatenate([dy * (y_ref[:, lanes] - skip * x), x * gx, touch], 0))
        gather = gather_ref[lanes, :]
        dots = dots + mm(jnp.concatenate([high, low], 1), jnp.concatenate([gather, gather], 0))
    row_dots, col_dots, last_add = dots[:Q], dots[Q : 2 * Q], dots[2 * Q :]
    last_row = iota2((Q, 128), 0) == Q - 1
    grad_cum = row_dots - step * col_dots + jnp.where(last_row, last_add[0:1, :], 0.0)
    upper = (iota2((Q, Q), 1) >= iota2((Q, Q), 0)).astype(F32)
    grad_rate = mm_exact(upper, grad_cum)
    grad_step = col_dots + grad_rate * head_ref[1:2, :]
    grad_raw = grad_step * sigmoid(stepin_ref[...])
    gstep_ref[...] = grad_raw.astype(BF)
    sums_ref[0:1, :] += jnp.sum(grad_rate * step, axis=0, keepdims=True)
    sums_ref[1:2, :] += jnp.sum(grad_raw, axis=0, keepdims=True)
    gbc_out_ref[:, 0:N] = grad_b
    gbc_out_ref[:, N : 2 * N] = gbc_ref[here_rows, N : 2 * N]


WEIGHT_TILE = 384


def mm_tn(a, b):
    return lax.dot_general(a, b, (((0,), (0,)), ((), ())), preferred_element_type=F32)


def backward_kernel(
    cols, dps,
    dy_ref, x_ref, y_ref, b_ref, c_ref, step_ref, cum_ref, stepin_ref, spread_ref, gather_ref, after_ref,
    state_ref, early_ref, offs_ref, head_ref, skip_ref, mixed_ref, of_ref, gg_ref,
    first_grad, mixed_hbm, gg_hbm, cot, normed,
    ga_ref, gstep_ref, gbc_out_ref, sums_ref, o_total_ref, g_own_ref, g_cross_ref, branch_ref, branch_in,
    mixed_sib, gg_sib,
    gx_ref, gbc_ref, late_ref, o_low, o_own, o_land, o_cross, o_cross_land, g_low, g_own, g_land, parts,
    c_own, c_sib, n_own, n_sib, m_tiles, gg_tiles, sems, local,
):
    step_at = pl.program_id(0)
    blocks = gx_ref.shape[0] // Q
    dp, row, col = here()
    group = cols // 2
    place = lax.rem(col, group)
    shard, channels = g_own_ref.shape[1], gx_ref.shape[1]
    half = c_own.shape[1]
    count = branch_ref.shape[0]
    others = dps - 1
    own, other = pl.ds(0, shard), pl.ds(shard, shard)
    sibling, mirror = (dp, 1 - row, col), mirror_of(cols)
    peers = [(dp, row, col ^ by) for by in range(1, group)]
    out_steps, o_steps, g_steps = 2 * half // TILE, channels // WEIGHT_TILE, channels // TILE
    o_at = out_steps
    g_at = o_at + o_steps
    near_at = g_at + g_steps
    far_at = near_at + blocks
    last = far_at + blocks - 1

    def o_moves():
        return dp_copies(dps, sems, lambda to, i: o_low.at[:, to], lambda to, i: o_land.at[i])

    def g_moves():
        return dp_copies(dps, sems, lambda to, i: g_low.at[to], lambda to, i: g_land.at[i], others)

    at = 2 * others
    cross_move = lambda: copy_to(o_cross, o_cross_land, sems, at, mirror)
    late_moves = lambda: [
        copy_to(first_grad.at[:, own], late_ref.at[:, other], sems, at + 1, mirror),
        copy_to(first_grad.at[:, other], late_ref.at[:, own], sems, at + 2, mirror),
    ]
    core_moves = lambda: [
        copy_to(cot.at[:, lanes_at(1 - row, half)], c_sib, sems, at + 3, sibling),
        copy_to(mixed_hbm, mixed_sib, sems, at + 4, sibling),
        copy_to(normed.at[:, lanes_at(1 - row, half)], n_sib, sems, at + 5, sibling),
        copy_to(gg_hbm, gg_sib, sems, at + 6, sibling),
    ]
    part_moves = lambda: [
        copy_to(parts.at[i], branch_in.at[i], sems, at + 7 + i, peer) for i, peer in enumerate(peers)
    ]
    load_c = pltpu.make_async_copy(cot.at[:, lanes_at(row, half)], c_own, local.at[0])
    load_n = pltpu.make_async_copy(normed.at[:, lanes_at(row, half)], n_own, local.at[1])

    def m_tile(tile):
        lanes = lanes_at(tile, WEIGHT_TILE)
        return pltpu.make_async_copy(mixed_sib.at[:, lanes], m_tiles.at[lax.rem(tile, 2)], local.at[2])

    def gg_tile(tile):
        lanes = lanes_at(tile, TILE)
        return pltpu.make_async_copy(gg_sib.at[:, lanes], gg_tiles.at[lax.rem(tile, 2)], local.at[3])

    @at_step(0)
    def _():
        load_c.start()
        load_n.start()
        greet([sibling, mirror] + peers + dp_peers(dps))
        for move in core_moves():
            move.start()

        @pl.when(col >= group)
        def _():
            for move in late_moves():
                move.start()
            late_ref[...] = jnp.zeros_like(late_ref)

        sums_ref[...] = jnp.zeros_like(sums_ref)

    @pl.when(step_at < o_at)
    def _():
        rows = lambda index: pl.ds(pl.multiple_of(index * count, 128), count)
        branch_ref[...] = mm(mixed_ref[rows(place), :], of_ref[...])
        for by in range(1, group):
            parts[by - 1, :, lanes_at(step_at, TILE)] = mm(mixed_ref[rows(place ^ by), :], of_ref[...]).astype(BF)

    @pl.when(step_at == o_at)
    def _():
        load_c.wait()
        for move in core_moves()[:2]:
            move.wait_recv()
        m_tile(0).start()

    @pl.when((step_at >= o_at) & (step_at < g_at))
    def _():
        tile = step_at - o_at
        m_tile(tile).wait()

        @pl.when(tile < o_steps - 1)
        def _():
            m_tile(tile + 1).start()

        total = mm_tn(mixed_ref[:, lanes_at(tile, WEIGHT_TILE)], c_own[...])
        total = total + mm_tn(m_tiles[lax.rem(tile, 2)], c_sib[...])
        piece = o_own.shape[1]
        per, each = WEIGHT_TILE // piece, shard // WEIGHT_TILE
        which, inside = lax.div(tile, each), lax.rem(tile, each)
        for p in range(per):
            part = total[p * piece : p * piece + piece, :]
            o_low[which, inside * per + p] = part.astype(BF)

            @pl.when(dp == inside * per + p)
            def _():
                o_own[which] = part

    @pl.when(step_at == g_at)
    def _():
        for move in o_moves():
            move.start()
        load_n.wait()
        for move in core_moves()[2:]:
            move.wait_recv()
        gg_tile(0).start()

    @pl.when((step_at >= g_at) & (step_at < near_at))
    def _():
        tile = step_at - g_at
        gg_tile(tile).wait()

        @pl.when(tile < g_steps - 1)
        def _():
            gg_tile(tile + 1).start()

        lanes = lanes_at(tile, TILE)
        total = mm_tn(n_own[HALO:, :], gg_ref[...]) + mm_tn(n_sib[HALO:, :], gg_tiles[lax.rem(tile, 2)])
        piece = g_own.shape[0]
        for p in range(dps):
            part = total[p * piece : p * piece + piece, :]
            g_low[p, :, lanes] = part.astype(BF)

            @pl.when(dp == p)
            def _():
                g_own[:, lanes] = part

    at_block = lax.rem(jnp.maximum(step_at - near_at, 0), blocks)
    here_rows = pl.ds(pl.multiple_of(at_block * Q, Q), Q)

    @pl.when((step_at >= near_at) & (step_at < far_at))
    def _():
        near_block(
            at_block, here_rows, dy_ref, x_ref, b_ref, c_ref, step_ref, cum_ref, spread_ref, state_ref,
            early_ref, offs_ref, gx_ref, gbc_ref,
        )

    @pl.when(step_at == near_at + 2)
    def _():
        for move in part_moves():
            move.start()

    @pl.when(step_at == near_at + blocks - 1)
    def _():
        for move in o_moves():
            move.wait_recv()
        for move in g_moves():
            move.start()
        for i in range(others):
            o_own[...] += o_land[i].astype(F32)
        o_cross[...] = o_own[1].astype(BF)
        cross_move().start()

    @pl.when(step_at == far_at)
    def _():
        @pl.when(col < group)
        def _():
            for move in late_moves():
                move.wait_recv()

    @pl.when(step_at >= far_at)
    def _():
        far_block(
            blocks, at_block, here_rows, dy_ref, x_ref, y_ref, gx_ref, b_ref, step_ref, cum_ref, stepin_ref,
            spread_ref, gather_ref, after_ref, late_ref, state_ref, early_ref, offs_ref, head_ref, skip_ref,
            gbc_ref, ga_ref, gstep_ref, gbc_out_ref, sums_ref,
        )

    @at_step(last)
    def _():
        cross_move().wait()
        o_total_ref[...] = o_own[0] + o_cross_land[...].astype(F32)
        for move in g_moves():
            move.wait()
        for i in range(others):
            g_own[...] += g_land[i].astype(F32)
        g_own_ref[...] = g_own[:, :shard]
        g_cross_ref[...] = g_own[:, shard:].astype(BF)
        for move in part_moves():
            move.wait()
        for move in o_moves() + core_moves():
            move.wait_send()

        @pl.when(col >= group)
        def _():
            for move in late_moves():
                move.wait_send()


def scan_backward(
    cols, dps, dy, act, y, step, cum, step_in, spread, gather, after, states, early, offs, head_rows, skip,
    mixed, w_out, gg, first_grad, cot, normed,
):
    tokens, channels = dy.shape
    rows_n, width = normed.shape
    half = width // 2
    blocks, group, shard = tokens // Q, cols // 2, channels // 2
    count = tokens // group
    piece_o, piece_g = shard // dps, half // dps
    out_steps, o_steps, g_steps = width // TILE, channels // WEIGHT_TILE, channels // TILE
    g_at = out_steps + o_steps
    near_at = g_at + g_steps
    far_at = near_at + blocks

    def clamp(first, size):
        return lambda i: jnp.clip(i - first, 0, size - 1)

    block = lambda i: jnp.where(i < near_at, 0, lax.rem(jnp.maximum(i - near_at, 0), blocks))
    second = clamp(far_at, blocks)
    state_at = lambda i: block(i) + jnp.where(i < far_at, 0, 1)
    rows = lambda at, size: pl.BlockSpec((Q, size), lambda i: (at(i), 0))
    lanes = lambda at, size: pl.BlockSpec((size, TILE), lambda i: (0, at(i)))
    once = lambda shape: pl.BlockSpec(shape, lambda *_: (0,) * len(shape), pipeline_mode=pl.Buffered(1))
    vmem = pltpu.VMEM
    dma = pltpu.SemaphoreType.DMA
    return pl.pallas_call(
        partial(backward_kernel, cols, dps),
        grid=(far_at + blocks,),
        in_specs=[
            rows(block, channels),
            rows(block, channels),
            rows(second, channels),
            pl.BlockSpec((Q, N), lambda i: (block(i), channels // N)),
            pl.BlockSpec((Q, N), lambda i: (block(i), channels // N + 1)),
            rows(block, 128),
            rows(block, 128),
            rows(second, 128),
            once(spread.shape),
            once(gather.shape),
            pl.BlockSpec((1, N, channels), lambda i: (second(i), 0, 0)),
            pl.BlockSpec((1, N, channels), lambda i: (state_at(i), 0, 0)),
            once(early.shape),
            once((16, 128)),
            once((8, 128)),
            once((8, channels)),
            once(mixed.shape),
            lanes(clamp(0, out_steps), channels),
            lanes(clamp(g_at, g_steps), tokens),
        ] + [ANY] * 5,
        out_specs=[
            rows(second, channels),
            rows(second, 128),
            rows(second, 2 * N),
            whole((8, 128)),
            whole((piece_o, half)),
            whole((piece_g, shard)),
            whole((piece_g, shard)),
            lanes(clamp(0, out_steps), count),
            ANY, ANY, ANY,
        ],
        out_shape=[
            sds((tokens, channels)),
            sds((tokens, 128), BF),
            sds((tokens, 2 * N)),
            sds((8, 128)),
            sds((piece_o, half)),
            sds((piece_g, shard)),
            sds((piece_g, shard), BF),
            sds((count, width)),
            sds((max(group - 1, 1), count, width), BF),
            sds(mixed.shape, BF),
            sds(gg.shape, BF),
        ],
        scratch_shapes=[
            vmem((tokens, channels), F32), vmem((tokens, 2 * N), F32), vmem((N, channels), F32),
            vmem((2, dps, piece_o, half), BF), vmem((2, piece_o, half), F32),
            vmem((dps - 1, 2, piece_o, half), BF), vmem((piece_o, half), BF), vmem((piece_o, half), BF),
            vmem((dps, piece_g, channels), BF), vmem((piece_g, channels), F32),
            vmem((dps - 1, piece_g, channels), BF),
            vmem((max(group - 1, 1), count, width), BF),
            vmem((tokens, half), BF), vmem((tokens, half), BF),
            vmem((rows_n, half), BF), vmem((rows_n, half), BF),
            vmem((2, tokens, WEIGHT_TILE), BF), vmem((2, tokens, TILE), BF),
            dma((2, 2 * (dps - 1) + 6 + group)),
            dma((4,)),
        ],
        compiler_params=remote_params(3),
        cost_estimate=cost(80),
        name="scan_backward",
    )(
        dy, act, y, act, act, step, cum, step_in, spread, gather, after, states, early, offs, head_rows, skip,
        mixed, w_out, gg, first_grad, mixed, gg, cot, normed,
    )


def gate_kernel(
    cols, inner_channels,
    y0_ref, graw_ref, gm_ref, x_ref, early_ref, c_ref, grow_ref, spread_ref, vec_ref,
    cum_ref, c_block_ref, spread_all_ref,
    y_ref, mixed_ref, gg_ref, dy_ref, sums_ref, after_ref, first_ref,
    y_vm, graw_vm, gm_vm, squares, inners, stats, stats_land, stats_col, held, sems,
):
    step = pl.program_id(0)
    tiles = y_vm.shape[0]
    tokens = y0_ref.shape[0]
    dp, row, col = here()
    group = cols // 2
    peers = [(dp, row, col ^ by) for by in range(1, group)]
    gain = vec_ref[1:2, :]
    nt = (((1,), (1,)), ((), ()))
    moves = lambda: [copy_to(stats, stats_land.at[i], sems, i, peer) for i, peer in enumerate(peers)]

    @at_step(0)
    def _():
        greet(peers)
        squares[...] = jnp.zeros_like(squares)
        inners[...] = jnp.zeros_like(inners)

    @pl.when(step < tiles)
    def _():
        s_high, s_low = split2(early_ref[...])
        s2 = jnp.concatenate([s_high, s_low], 0)
        spread = spread_ref[...]
        skip = vec_ref[0:1, :]
        for at in range(0, tokens, Q):
            rows = slice(at, at + Q)
            c_blk = c_ref[rows, :]
            carried = mm(jnp.concatenate([c_blk, c_blk], 1), s2) * mm(grow_ref[rows, :], spread)
            y = y0_ref[rows, :] + carried + skip * x_ref[rows, :].astype(F32)
            raw, gm = graw_ref[rows, :], gm_ref[rows, :]
            y_ref[rows, :] = y
            y_vm[step, rows, :] = y
            graw_vm[step, rows, :] = raw
            gm_vm[step, rows, :] = gm
            gated = y * raw * sigmoid(raw)
            square = gated * gated
            inner = gm * gain * gated
            squares[rows, :] += square[:, 0:128] + square[:, 128:256]
            inners[rows, :] += inner[:, 0:128] + inner[:, 128:256]

    @at_step(tiles - 1)
    def _():
        ones = jnp.ones((8, 128), F32)
        square_row = lax.dot_general(ones, squares[...], nt, precision=HIGHEST, preferred_element_type=F32)
        inner_row = lax.dot_general(ones, inners[...], nt, precision=HIGHEST, preferred_element_type=F32)
        stats[...] = jnp.where(iota2(square_row.shape, 0) == 0, square_row, inner_row)
        for move in moves():
            move.start()
        for move in moves():
            move.wait_recv()
        total = stats[...]
        for i in range(group - 1):
            total = total + stats_land[i]
        wide = jnp.concatenate([total, jnp.zeros((120, tokens), F32)], 0)
        stats_col[...] = wide.T

    @pl.when((step >= tiles) & (step < 2 * tiles))
    def _():
        tile = step - tiles
        gain_sum = jnp.zeros((1, TILE), F32)
        skip_sum = jnp.zeros((1, TILE), F32)
        for at in range(0, tokens, Q):
            rows = slice(at, at + Q)
            inv = lax.rsqrt(stats_col[rows, 0:1] * (1.0 / inner_channels) + EPSILON)
            pull = inv * inv * inv * (stats_col[rows, 1:2] * (1.0 / inner_channels))
            raw, y, gm = graw_vm[tile, rows, :], y_vm[tile, rows, :], gm_vm[tile, rows, :]
            sig = sigmoid(raw)
            act = raw * sig
            gated = y * act
            unit = gated * inv
            mixed_ref[rows, :] = (unit * gain).astype(BF)
            gain_sum = gain_sum + jnp.sum(gm * unit, axis=0, keepdims=True)
            grad_gated = inv * (gm * gain) - gated * pull
            dy = grad_gated * act
            dy_ref[rows, :] = dy
            y_vm[tile, rows, :] = dy
            gg_ref[rows, :] = (grad_gated * y * (sig * (1.0 + raw * (1.0 - sig)))).astype(BF)
            skip_sum = skip_sum + jnp.sum(dy * x_ref[rows, :].astype(F32), axis=0, keepdims=True)
        sums_ref[...] = jnp.zeros_like(sums_ref)
        sums_ref[0:1, :] = gain_sum
        sums_ref[1:2, :] = skip_sum

    @pl.when(step == 2 * tiles)
    def _():
        for move in moves():
            move.wait_send()
        held[...] = jnp.zeros_like(held)

    @pl.when(step >= 2 * tiles)
    def _():
        at = pl.num_programs(0) - 1 - step
        rows = pl.ds(pl.multiple_of(at * Q, Q), Q)
        grad_state_block(y_vm.at[:, rows, :], c_block_ref, cum_ref, spread_all_ref, after_ref, held)
        first_ref[...] = held[...]


def gate_and_mix(cols, inner_channels, y0, graw, gm, act, early, grow, spread, vectors, cum):
    tokens, channels = y0.shape
    blocks = tokens // Q
    tiles, group = channels // TILE, cols // 2
    first = lambda i: jnp.minimum(i, tiles - 1)
    second = lambda i: jnp.clip(i - tiles, 0, tiles - 1)
    either = lambda i: jnp.where(i < 2 * tiles, lax.rem(i, tiles), tiles - 1)
    third = lambda i: blocks - 1 - jnp.maximum(i - 2 * tiles, 0)
    lanes = lambda at, count: pl.BlockSpec((count, TILE), lambda i: (0, at(i)))
    vmem = pltpu.VMEM
    return pl.pallas_call(
        partial(gate_kernel, cols, inner_channels),
        grid=(2 * tiles + blocks,),
        in_specs=[
            lanes(first, tokens), lanes(first, tokens), lanes(first, tokens), lanes(either, tokens),
            lanes(first, N),
            pl.BlockSpec((tokens, N), lambda i: (0, channels // N + 1)),
            whole((tokens, 256)),
            lanes(first, 256),
            lanes(either, 8),
            pl.BlockSpec((Q, 128), lambda i: (third(i), 0)),
            pl.BlockSpec((Q, N), lambda i: (third(i), channels // N + 1)),
            whole((256, channels)),
        ],
        out_specs=[
            lanes(first, tokens), lanes(second, tokens), lanes(second, tokens), lanes(second, tokens),
            lanes(second, 8),
            pl.BlockSpec((1, N, channels), lambda i: (third(i), 0, 0)),
            whole((N, channels)),
        ],
        out_shape=[
            sds((tokens, channels)), sds((tokens, channels), BF), sds((tokens, channels), BF),
            sds((tokens, channels)), sds((8, channels)), sds((blocks, N, channels)), sds((N, channels)),
        ],
        scratch_shapes=[
            vmem((tiles, tokens, TILE), F32), vmem((tiles, tokens, TILE), F32), vmem((tiles, tokens, TILE), F32),
            vmem((tokens, 128), F32), vmem((tokens, 128), F32),
            vmem((8, tokens), F32), vmem((max(group - 1, 1), 8, tokens), F32), vmem((tokens, 128), F32),
            vmem((N, channels), F32),
            pltpu.SemaphoreType.DMA((2, max(group - 1, 1))),
        ],
        compiler_params=remote_params(6),
        cost_estimate=cost(40),
        name="gate_and_mix",
    )(y0, graw, gm, act, early, act, grow, spread, vectors, cum, act, spread)


def conv_back_tile(ga_ref, raw_ref, taps_ref, gv_ref, sums_ref, g_pad):
    tokens, width = ga_ref.shape
    taps = taps_ref[...]
    g_pad[0:HALO, :] = jnp.zeros((HALO, width), F32)
    g_pad[HALO + tokens :, :] = jnp.zeros((HALO, width), F32)
    sums = [jnp.zeros((8, width), F32)] * 5
    by_eight = lambda values: jnp.sum(values.reshape(ROWS // 8, 8, width), axis=0)
    for row in range(0, tokens, ROWS):
        moved = conv_window(raw_ref, row, ROWS)
        pre = conv_rows(moved, taps)
        sig = sigmoid(pre)
        g = ga_ref[row : row + ROWS, :] * (sig * (1.0 + pre * (1.0 - sig)))
        g_pad[HALO + row : HALO + row + ROWS, :] = g
        for k in range(4):
            sums[k] = sums[k] + by_eight(g * moved[k])
        sums[4] = sums[4] + by_eight(g)
    for row in list(range(HALO, HALO + tokens, ROWS)) + [0]:
        size = HALO if row == 0 else ROWS
        window = g_pad[row : row + size + 8, :]
        total = taps[3:4, :] * window[:size, :]
        for k in range(3):
            total = total + taps[k : k + 1, :] * pltpu.roll(window, size + 5 + k, 0)[:size, :]
        gv_ref[row : row + size, :] = total.astype(BF)
    for k in range(5):
        sums_ref[k : k + 1, :] = jnp.sum(sums[k], axis=0, keepdims=True)


SMALL_ROWS = 16


def finish_kernel(
    cols, dps, heads, part, whole_state,
    ga_ref, raw_ref, taps_ref, gg_ref, gt_ref, v_ref, g_ref, pick_v_ref, tok_ref, inv_ref, g_own_ref,
    mix_ref, headsum_ref, gain_ref, o_total, g_cross, gbc, normed, gt_hbm, tok, cot,
    tg_out, o_out, g_out, v_out, ext_out, sm_out,
    gv_vm, gv_sib, gs_vm, gs_sib, gt_sib, bc_own, bc_land, g_pad, raw_part, taps_part, g_pad_part,
    n_own, n_sib, o_vm, g_vm, g_land, gn_tile, gn_own, gn_parts, gn_land, gn_halo, halo_land,
    joint_low, rec, tot, z_send, z_land, step_land, state_land, ext, small, small_land, tok_vm, cot_vm, sems, local,
):
    step = pl.program_id(0)
    channels, half = gv_vm.shape[1], n_own.shape[1]
    shard, piece, span = channels // 2, tot.shape[0], gs_vm.shape[1]
    count, width = gn_own.shape
    tokens = bc_own.shape[0]
    tiles, weight_steps, input_steps = channels // TILE, half // WEIGHT_TILE, width // TILE
    weight_at = tiles + 1
    input_at = weight_at + weight_steps
    last = input_at + input_steps
    dp, row, col = here()
    group = cols // 2
    place = lax.rem(col, group)
    sibling, mirror = (dp, 1 - row, col), mirror_of(cols)
    col_peer = lambda by: (dp, row, col ^ by)
    peers = [col_peer(by) for by in range(1, group)]
    others = dps - 1
    o_rows = pl.ds(dp * piece_of(o_vm), piece_of(o_vm))
    g_rows = pl.ds(dp * piece, piece)
    cols_a, cols_b = pl.ds(shard, tot.shape[1] - shard), pl.ds(0, shard)
    used = [0]

    def take(size):
        used[0] += size
        return used[0] - size

    def part_at(at):
        return pl.ds(0, span) if whole_state else lanes_at(at, span)

    def to_dp(src_of, dst_of):
        first = take(others)
        return lambda: dp_copies(dps, sems, src_of, dst_of, first)

    def to_all_dp(src, out):
        first = take(max(others, 4))
        return (lambda: hand_out(dps, sems, first, src, out)[0]), (lambda: hand_out(dps, sems, first, src, out)[1])

    def one(src, dst, device):
        at = take(1)
        return lambda: [copy_to(src, dst, sems, at, device)]

    def to_peers(src_of, dst_of):
        first = take(group - 1)
        return lambda: [
            copy_to(src_of(by), dst_of(by), sems, first + by - 1, col_peer(by)) for by in range(1, group)
        ]

    def to_cols(src, dst):
        first = take(cols - 1)
        return lambda: [copy_to(src, dst, sems, first + by - 1, col_peer(by)) for by in range(1, cols)]

    o_moves, o_passed = to_all_dp(o_total, o_out)
    g_moves, g_passed = to_all_dp(g_vm, g_out)
    a_moves = to_dp(lambda to, i: joint_low.at[to, :, cols_a], lambda to, i: rec.at[i, :, cols_a])
    b_moves = to_dp(lambda to, i: joint_low.at[to, :, cols_b], lambda to, i: rec.at[i, :, cols_b])
    v_moves, v_passed = to_all_dp(tot.at[:, cols_b], v_out)
    e_moves, e_passed = to_all_dp(ext, ext_out)
    g_move = one(g_cross, g_land, mirror)
    n_move = one(normed.at[:, lanes_at(1 - row, half)], n_sib, sibling)
    t_move = one(gt_hbm, gt_sib, sibling)
    s_move = one(gs_vm, gs_sib, sibling)
    z_move = one(z_send, z_land, mirror)
    step_move = one(tot.at[:, pl.ds(channels + span, 128)], step_land, mirror)
    state_moves = to_cols(tot.at[:, pl.ds(channels, span)], state_land.at[col])
    bc_moves = to_peers(lambda by: gbc.at[:, part_at(place ^ by)], lambda by: bc_land.at[by - 1])
    early_rows, late_rows = pl.ds(0, count // 2), pl.ds(count // 2, count - count // 2)
    gn_early = to_peers(lambda by: gn_parts.at[by - 1, early_rows, :], lambda by: gn_land.at[by - 1, early_rows, :])
    gn_late = to_peers(lambda by: gn_parts.at[by - 1, late_rows, :], lambda by: gn_land.at[by - 1, late_rows, :])
    gn_moves = lambda: gn_early() + gn_late()
    tile_first = take(tiles)

    def v_tile(tile):
        lanes = lanes_at(tile, TILE)
        return copy_to(gv_vm.at[:, lanes], gv_sib.at[:, lanes], sems, tile_first + tile, sibling)

    halo_first = take(group)
    halos = lambda: [
        copy_to(gn_halo, halo_land.at[j], sems, halo_first + j, (dp, row, group - 1)) for j in range(group)
    ]
    small_steps = [sibling]
    by = 1
    while by < dps:
        small_steps.append((dp ^ by, row, col))
        by *= 2
    small_first = take(len(small_steps))
    small_move = lambda i: copy_to(small, small_land.at[i], sems, small_first + i, small_steps[i])
    small_cols = to_cols(small, sm_out.at[col])

    def small_next(i):
        move = small_move(i)
        move.wait()
        small[...] += small_land[i]
        if i + 1 < len(small_steps):
            small_move(i + 1).start()

    def start(moves):
        for move in moves:
            move.start()

    def arrive(moves):
        for move in moves:
            move.wait_recv()

    def sent(moves):
        for move in moves:
            move.wait_send()

    load_bc = pltpu.make_async_copy(gbc.at[:, part_at(place)], bc_own, local.at[0])
    load_n = pltpu.make_async_copy(normed.at[:, lanes_at(row, half)], n_own, local.at[1])
    load_o = pltpu.make_async_copy(o_total, o_vm, local.at[2])
    load_tok = pltpu.make_async_copy(tok, tok_vm, local.at[3])
    load_cot = pltpu.make_async_copy(cot, cot_vm, local.at[4])
    store_o = pltpu.make_async_copy(o_vm, o_out.at[o_rows, :], local.at[2])
    store_g = pltpu.make_async_copy(g_vm, g_out.at[g_rows, :], local.at[0])
    store_v = pltpu.make_async_copy(tot.at[:, cols_b], v_out.at[g_rows, :], local.at[1])
    store_e = pltpu.make_async_copy(ext, ext_out.at[g_rows, :], local.at[5])
    store_tg = pltpu.make_async_copy(gn_own, tg_out, local.at[3])
    store_small = pltpu.make_async_copy(small, sm_out.at[col], local.at[6])

    @at_step(0)
    def _():
        load_o.start()
        load_bc.start()
        load_n.start()
        load_tok.start()
        load_cot.start()
        greet([sibling] + [col_peer(by) for by in range(1, cols)] + dp_peers(dps))
        start(bc_moves() + o_moves() + t_move() + n_move() + g_move())
        small[...] = jnp.zeros_like(small)
        small[5:7, 0:channels] = mix_ref[0:2, :]
        small[7:9, 0:128] = headsum_ref[0:2, :]
        load_o.wait()
        store_o.start()

    @pl.when(step < tiles)
    def _():
        lanes = lanes_at(step, TILE)
        conv_back_tile(ga_ref, raw_ref, taps_ref, gv_vm.at[:, lanes], small.at[0:5, lanes], g_pad)
        v_tile(step).start()

    @pl.when(step == tiles - 1)
    def _():
        arrive(o_moves())
        start(o_passed())

    @pl.when(step == tiles)
    def _():
        load_bc.wait()
        arrive(bc_moves())
        for i in range(group - 1):
            bc_own[...] += bc_land[i]
        if whole_state:
            lane = iota2(bc_own.shape, 1)
            mine = (lane >= place * part) & (lane < place * part + part)
            bc_own[...] = jnp.where(mine, bc_own[...], 0.0)
        lanes = part_at(place)
        raw_part[...] = raw_ref[:, lanes]
        taps_part[...] = taps_ref[:, lanes]
        conv_back_tile(bc_own, raw_part, taps_part, gs_vm, small.at[10:15, 0:span], g_pad_part)
        start(s_move())
        arrive(g_move())
        g_vm[...] = g_own_ref[...] + g_land[...].astype(F32)
        start(g_moves())
        store_g.start()

    @pl.when(step == weight_at)
    def _():
        load_n.wait()
        arrive(n_move() + t_move() + s_move() + [v_tile(tile) for tile in range(tiles)])

    @pl.when((step >= weight_at) & (step < input_at))
    def _():
        at = step - weight_at
        lanes = lanes_at(at, WEIGHT_TILE)
        left, left_sib = n_own[:, lanes], n_sib[:, lanes]
        per = WEIGHT_TILE // piece

        def keep(first, size, total):
            for p in range(per):
                rows = total[p * piece : p * piece + piece, :]
                joint_low[at * per + p, :, first : first + size] = rows.astype(BF)

                @pl.when(dp == at * per + p)
                def _():
                    tot[:, first : first + size] = rows

        keep(0, channels, mm_tn(left, gv_vm[...]) + mm_tn(left_sib, gv_sib[...]))
        keep(channels, span, mm_tn(left, gs_vm[...]) + mm_tn(left_sib, gs_sib[...]))
        keep(
            channels + span, 128,
            mm_tn(left[HALO:, :], gt_ref[...]) + mm_tn(left_sib[HALO:, :], gt_sib[...]),
        )

    @pl.when(step == input_at)
    def _():
        start(a_moves())
        arrive(g_moves())
        start(g_passed())

    @pl.when((step >= input_at) & (step < last))
    def _():
        at = step - input_at
        lanes = lanes_at(at, TILE)
        gn_tile[...] = mm_nt(gv_vm[...], v_ref[...]) + mm_nt(gs_vm[...], pick_v_ref[:, part_at(place)])
        gn_tile[HALO:, :] += mm_nt(gg_ref[...], g_ref[...]) + mm_nt(gt_ref[...], pick_v_ref[:, TILE:])
        rows = lambda index: pl.ds(pl.multiple_of(HALO + index * count, HALO), count)
        gn_own[:, lanes] = gn_tile[rows(place), :]
        for by in range(1, group):
            gn_parts[by - 1, :, lanes] = gn_tile[rows(place ^ by), :].astype(BF)
        gn_halo[:, lanes] = gn_tile[0:HALO, :].astype(BF)
        sums = jnp.zeros((1, TILE), F32)
        for first in [0] + list(range(HALO, HALO + tokens, Q)):
            size = HALO if first == 0 else Q
            unit = tok_ref[first : first + size, :].astype(F32) * inv_ref[first : first + size, 0:1]
            sums = sums + jnp.sum(gn_tile[first : first + size, :] * unit, axis=0, keepdims=True)
        small[9:10, lanes] = sums

    @pl.when(step == last)
    def _():
        start(gn_early())
        for j in range(group):
            pl.when(col == group + j)(halos()[j].start)
        small_move(0).start()
        arrive(a_moves())
        start(b_moves())
        for i in range(others):
            tot[:, cols_a] += rec[i, :, cols_a].astype(F32)
        z_send[...] = tot[:, shard:channels].astype(BF)
        start(z_move() + step_move() + state_moves())
        state_land[col] = tot[:, channels : channels + span]
        small_next(0)
        arrive(b_moves())
        for i in range(others):
            tot[:, cols_b] += rec[i, :, cols_b].astype(F32)
        arrive(z_move() + step_move())
        start(gn_late())
        tot[:, cols_b] += z_land[...].astype(F32)
        start(v_moves())
        store_v.start()
        ext[:, 0:128] = tot[:, channels + span :] + pltpu.roll(step_land[...], 128 - heads, 1)
        arrive(state_moves())
        if whole_state:
            ext[:, 128:] = sum(state_land[i] for i in range(cols))
        else:
            ext[:, 128:] = state_land[col // 2] + state_land[col // 2 + group]
        start(e_moves())
        store_e.start()
        for i in range(1, len(small_steps)):
            small_next(i)
        start(small_cols())
        store_small.start()
        load_tok.wait()
        load_cot.wait()
        arrive(gn_moves())
        for i in range(group - 1):
            gn_own[...] += gn_land[i].astype(F32)

        @pl.when(col == group - 1)
        def _():
            arrive(halos())
            for j in range(group):
                gn_own[count - HALO :, :] += halo_land[j].astype(F32)

        for j in range(group):
            pl.when(col == group + j)(halos()[j].wait_send)
        for first in range(0, count, ROWS):
            rows = slice(first, first + ROWS)
            values = tok_vm[rows, :].astype(F32)
            inv = lax.rsqrt(jnp.mean(values * values, axis=-1, keepdims=True) + EPSILON)
            unit = values * inv
            pulled = gn_own[rows, :] * gain_ref[0:1, :]
            mean = jnp.mean(pulled * unit, axis=-1, keepdims=True)
            gn_own[rows, :] = cot_vm[rows, :].astype(F32) + inv * (pulled - unit * mean)
        store_tg.start()
        arrive(v_moves())
        start(v_passed())
        arrive(e_moves())
        start(e_passed())
        store_o.wait()
        store_g.wait()
        store_small.wait()
        store_v.wait()
        store_e.wait()
        arrive(o_passed() + g_passed() + v_passed() + e_passed() + small_cols())
        sent(o_passed() + g_passed() + v_passed() + e_passed())
        sent(bc_moves() + o_moves() + t_move() + n_move() + g_move() + s_move() + a_moves() + b_moves())
        sent([v_tile(tile) for tile in range(tiles)])
        sent(gn_moves() + z_move() + step_move() + state_moves() + g_moves() + v_moves() + e_moves() + small_cols())
        store_tg.wait()


def piece_of(ref):
    return ref.shape[0]


def finish(
    cols, dps, heads, part, ga, raw, taps, gg, gt, w_value, w_gate, picked, tokens_in, inv_rms, g_own, mix_sums,
    head_sums, gain, o_total, g_cross, gbc, normed, tokens_own, cotangent,
):
    tokens, channels = ga.shape
    rows, width = normed.shape
    half, shard = width // 2, channels // 2
    whole_state = part % 128 != 0
    span = 2 * N if whole_state else part
    group = cols // 2
    tiles, weight_steps, input_steps = channels // TILE, half // WEIGHT_TILE, width // TILE
    piece, wide = g_own.shape[0], channels + span + 128
    count = tokens_own.shape[0]
    input_at = tiles + 1 + weight_steps
    small_steps = dps.bit_length()

    def clamp(first, size):
        return lambda i: jnp.clip(i - first, 0, size - 1)

    conv, both, input_tile = clamp(0, tiles), clamp(0, tiles + 1), clamp(input_at, input_steps)
    lanes = lambda at, size: pl.BlockSpec((size, TILE), lambda i: (0, at(i)))
    slab = lambda at, size: pl.BlockSpec((TILE, size), lambda i: (at(i), 0))
    once = lambda values: pl.BlockSpec(
        values.shape, lambda *_: (0,) * len(values.shape), pipeline_mode=pl.Buffered(1)
    )
    vmem = pltpu.VMEM
    dma = pltpu.SemaphoreType.DMA
    more = max(group - 1, 1)
    copies = 2 * (dps - 1) + 4 * max(dps - 1, 4) + 6 + 2 * (cols - 1) + 3 * (group - 1) + tiles + group + small_steps
    return pl.pallas_call(
        partial(finish_kernel, cols, dps, heads, part, whole_state),
        grid=(input_at + input_steps + 1,),
        in_specs=[
            lanes(conv, tokens),
            lanes(both, rows),
            lanes(both, 8),
            once(gg),
            once(gt),
            slab(input_tile, channels),
            slab(input_tile, channels),
            slab(input_tile, TILE + 128),
            lanes(input_tile, rows),
            once(inv_rms),
            once(g_own),
            once(mix_sums),
            once(head_sums),
            once(gain),
        ] + [ANY] * 7,
        out_specs=[ANY] * 6,
        out_shape=[
            sds((count, width)), sds((dps * o_total.shape[0], o_total.shape[1])), sds((half, shard)),
            sds((half, shard)), sds((half, 128 + span)), sds((cols, SMALL_ROWS, width)),
        ],
        scratch_shapes=[
            vmem((rows, channels), BF), vmem((rows, channels), BF), vmem((rows, span), BF), vmem((rows, span), BF),
            vmem((tokens, 128), BF), vmem((tokens, span), F32), vmem((more, tokens, span), F32),
            vmem((tokens + 2 * HALO, TILE), F32), vmem((rows, span), F32), vmem((8, span), F32),
            vmem((tokens + 2 * HALO, span), F32),
            vmem((rows, half), BF), vmem((rows, half), BF),
            vmem(o_total.shape, F32), vmem(g_own.shape, F32), vmem(g_own.shape, BF),
            vmem((rows, TILE), F32),
            vmem((count, width), F32), vmem((more, count, width), BF), vmem((more, count, width), BF),
            vmem((HALO, width), BF), vmem((group, HALO, width), BF),
            vmem((dps, piece, wide), BF), vmem((dps - 1, piece, wide), BF), vmem((piece, wide), F32),
            vmem((piece, shard), BF), vmem((piece, shard), BF), vmem((piece, 128), F32),
            vmem((cols, piece, span), F32), vmem((piece, 128 + span), F32),
            vmem((SMALL_ROWS, width), F32), vmem((small_steps, SMALL_ROWS, width), F32),
            vmem((count, width), BF), vmem((count, width), BF),
            dma((2, copies)),
            dma((7,)),
        ],
        compiler_params=remote_params(5),
        cost_estimate=cost(110),
        name="finish",
    )(
        ga, raw, taps, gg, gt, w_value, w_gate, picked, tokens_in, inv_rms, g_own, mix_sums, head_sums, gain,
        o_total, g_cross, gbc, normed, gt, tokens_own, cotangent,
    )


def flips(size, by):
    return [(i, i ^ by) for i in range(size)]


def butterfly(values, axis):
    size = lax.axis_size(axis)
    by = 1
    while by < size:
        values = values + lax.ppermute(values, axis, flips(size, by))
        by *= 2
    return values


def at_rows(values, index, size):
    return lax.dynamic_slice_in_dim(values, index * size, size, axis=0)


def collect_dp(piece, dp):
    size = lax.axis_size("dp")
    rows = piece.shape[0]
    out = jnp.zeros((size * rows,) + piece.shape[1:], piece.dtype)
    out = lax.dynamic_update_slice_in_dim(out, piece, dp * rows, 0)
    for by in range(1, size):
        other = lax.ppermute(piece, "dp", flips(size, by))
        out = lax.dynamic_update_slice_in_dim(out, other, (dp ^ by) * rows, 0)
    return out


def swap_core(values):
    return lax.ppermute(values, "row", [(0, 1), (1, 0)])


def per_device(
    tokens, norm_gain, w_gate, w_value, w_state, w_step, conv_value, bias_value, conv_state,
    bias_state, a_log, d_skip, dt_bias, mix_gain, w_out, cotangent,
):
    cols, rows_n, dps = lax.axis_size("col"), lax.axis_size("row"), lax.axis_size("dp")
    col, row, dp = lax.axis_index("col"), lax.axis_index("row"), lax.axis_index("dp")
    group = cols // 2
    place = lax.rem(col, group)
    local, width = tokens.shape
    span = local * group
    half_width = width // 2
    shard = w_value.shape[1]
    channels = 2 * shard
    heads = a_log.shape[0]
    inner_channels = shard * cols
    state_all = w_state.shape[1] * cols
    mirror = [(i, cols - 1 - i) for i in range(cols)]
    forth = [(i, cols - 1 - i) for i in range(group)]
    back = [(cols - 1 - i, i) for i in range(group)]

    def ring(by):
        return [(i, (i // group) * group + (i % group + by) % group) for i in range(cols)]

    state_width = w_state.shape[1]
    small = jnp.pad(
        jnp.concatenate([w_state, w_step], axis=1), ((0, 0), (0, 128 - state_width - heads))
    )
    heads_row = jnp.pad(
        jnp.concatenate([d_skip, a_log, dt_bias]), (0, shard - 3 * heads)
    )[None]
    state_rows = jnp.concatenate([conv_state.T, bias_state[None]], axis=0)
    vec = jnp.concatenate(
        [
            conv_value.T, bias_value[None], mix_gain[None], heads_row, jnp.zeros((1, shard), BF),
            jnp.pad(state_rows, ((0, 3), (0, shard - state_width))),
        ],
        axis=0,
    )
    group_tokens, value_full, small_full, vecs = import_all(cols, dps, tokens, w_value, small, vec)
    from_col = lax.broadcasted_iota(jnp.int32, (cols * 128, TILE + 128), 0) // 128
    from_lane = lax.broadcasted_iota(jnp.int32, (cols * 128, TILE + 128), 0) % 128
    to = lax.broadcasted_iota(jnp.int32, (cols * 128, TILE + 128), 1)
    head_to = to - TILE
    is_state = (to < TILE) & (from_lane < state_width) & (from_col * state_width + from_lane == to)
    is_own = (from_col == col) & (head_to < heads) & (from_lane == state_width + head_to)
    is_mirror = (from_col == cols - 1 - col) & (head_to >= heads) & (head_to < 2 * heads)
    is_mirror = is_mirror & (from_lane == state_width + head_to - heads)
    pick = (is_state | ((head_to >= 0) & (is_own | is_mirror))).astype(BF)

    vecs = vecs.astype(F32)
    both = jnp.concatenate(
        [
            lax.dynamic_index_in_dim(vecs, col, 0, keepdims=False),
            lax.dynamic_index_in_dim(vecs, cols - 1 - col, 0, keepdims=False),
        ],
        axis=1,
    )
    state_vecs = jnp.transpose(vecs[:, 8:16, :state_width], (1, 0, 2)).reshape(8, state_all)
    taps = jnp.concatenate([both[0:8], state_vecs], axis=1)

    def both_heads(at):
        return jnp.concatenate(
            [both[6, at * heads : (at + 1) * heads], both[6, shard + at * heads : shard + (at + 1) * heads]]
        )

    skip_both, a_both, dt_both = both_heads(0), both_heads(1), both_heads(2)
    vectors = jnp.concatenate(
        [jnp.repeat(skip_both, HEAD)[None], both[5:6], jnp.zeros((6, channels), F32)], axis=0
    )
    rate = -jnp.exp(a_both)
    head_rows = jnp.pad(jnp.stack([dt_both, rate]), ((0, 6), (0, 128 - 2 * heads)))
    head_of = np.arange(channels) // HEAD
    one_hot = (np.arange(128)[:, None] == head_of[None, :]).astype(np.float32)
    spread = jnp.asarray(np.concatenate([one_hot, one_hot], axis=0), BF)
    gather = jnp.asarray(one_hot.T, BF)

    gain = norm_gain.astype(F32)
    (
        raw, act, normed, step_in, step, cum, grow, offs, inv_rms, picked, states, y0, graw, gm, early,
        group_cot, gate_full, out_full,
    ) = forward_all(
        cols, dps, group_tokens, gain[None], value_full, small_full, pick, taps, head_rows, spread, cotangent,
        w_gate, w_out,
    )
    y, mixed, grad_gate, dy, mix_sums, after, first_grad = gate_and_mix(
        cols, inner_channels, y0, graw, gm, act, early, grow, spread, vectors, cum
    )
    (
        ga, grad_step, gbc, head_sums, out_total, gate_own, gate_cross, branch, branch_in, _, _,
    ) = scan_backward(
        cols, dps, dy, act, y, step, cum, step_in, spread, gather, after, states, early, offs, head_rows, vectors,
        mixed, out_full, grad_gate, first_grad, group_cot, normed,
    )
    block_out = (tokens.astype(F32) + branch + jnp.sum(branch_in.astype(F32), axis=0)).astype(BF)
    state_part = state_all // group

    tokens_grad, sum_out, sum_gate, sum_value, extra, small_sums = finish(
        cols, dps, heads, state_part, ga, raw, taps, grad_gate, grad_step, value_full, gate_full, picked,
        group_tokens, inv_rms, gate_own, mix_sums, head_sums, gain[None], out_total, gate_cross, gbc, normed,
        tokens, cotangent,
    )
    sum_step = extra[:, :heads]
    whole_state = state_part % 128 != 0
    first = 128 + (col if whole_state else lax.rem(col, cols // group)) * state_width
    sum_state = lax.dynamic_slice_in_dim(extra, first, state_width, axis=1)
    own_sums = lax.dynamic_index_in_dim(small_sums, col, 0, keepdims=False)
    mirror_sums = lax.dynamic_index_in_dim(small_sums, cols - 1 - col, 0, keepdims=False)
    wide = own_sums[0:7, :shard] + mirror_sums[0:7, shard:channels]
    head_own = own_sums[7:9, :heads] + mirror_sums[7:9, heads : 2 * heads]
    skip_own = jnp.sum(wide[6].reshape(heads, HEAD), axis=1)
    norm_total = small_sums[0, 9]
    for i in range(1, cols):
        norm_total = norm_total + small_sums[i, 9]
    if whole_state:
        state_sums = jnp.sum(small_sums[:, 10:15, :state_all], axis=0)
        state_first = col * state_width
    else:
        half_at = col * state_width // state_part
        state_sums = lax.dynamic_index_in_dim(small_sums, half_at, 0, keepdims=False)[10:15, :state_part]
        state_sums = state_sums + lax.dynamic_index_in_dim(
            small_sums, half_at + group, 0, keepdims=False
        )[10:15, :state_part]
        state_first = lax.rem(col * state_width, state_part)
    state_own = lax.dynamic_slice_in_dim(state_sums, state_first, state_width, axis=1)

    return (
        block_out,
        tokens_grad,
        norm_total,
        sum_gate,
        sum_value,
        sum_state,
        sum_step,
        wide[:4].T,
        wide[4],
        state_own[:4].T,
        state_own[4],
        head_own[0] * rate[:heads],
        skip_own,
        head_own[1],
        wide[5],
        sum_out,
    )


def solution(mesh):
    rows = P(("dp", "row", "col"), None)
    grid = P("row", "col")
    vec = P("col")
    taps = P("col", None)
    return jax.shard_map(
        per_device,
        mesh=mesh,
        in_specs=(
            rows, P(), grid, grid, grid, grid, taps, vec, taps, vec, vec, vec, vec, vec,
            P("col", "row"), rows,
        ),
        out_specs=(
            rows, rows, P(), grid, grid, grid, grid, taps, vec, taps, vec, vec, vec, vec, vec,
            P("col", "row"),
        ),
        check_vma=False,
    )
```

```python
from functools import partial

import jax
import jax.numpy as jnp
import numpy as np
from jax import lax
from jax.experimental import pallas as pl
from jax.experimental.pallas import tpu as pltpu
from jax.sharding import PartitionSpec as P

BF = jnp.bfloat16
F32 = jnp.float32
EPSILON = 1e-05
N = 128
Q = 128
HEAD = 64
HALO = 16
ROWS = 64
TILE = 256
HIGHEST = lax.Precision.HIGHEST
VMEM_LIMIT = 56 * 2**20


def mm(a, b):
    return lax.dot_general(a, b, (((1,), (0,)), ((), ())), preferred_element_type=F32)


def mm_nt(a, b):
    return lax.dot_general(a, b, (((1,), (1,)), ((), ())), preferred_element_type=F32)


def mm_exact(a, b):
    return lax.dot_general(
        a, b, (((1,), (0,)), ((), ())), precision=HIGHEST, preferred_element_type=F32
    )


def split2(values):
    high = values.astype(BF)
    return high, (values - high.astype(F32)).astype(BF)


def sigmoid(values):
    return 1.0 / (1.0 + jnp.exp(-values))


def iota2(shape, axis):
    return lax.broadcasted_iota(jnp.int32, shape, axis)


def params(*names):
    return pltpu.CompilerParams(
        dimension_semantics=names or ("arbitrary",), vmem_limit_bytes=VMEM_LIMIT
    )


def cost(micros):
    return pl.CostEstimate(flops=0, bytes_accessed=int(micros * 3.0e6), transcendentals=0)


def whole(shape):
    return pl.BlockSpec(shape, lambda *_: (0,) * len(shape))


def columns(rows, width=TILE):
    return pl.BlockSpec((rows, width), lambda j: (0, j))


def sds(shape, dtype=F32):
    return jax.ShapeDtypeStruct(shape, dtype)


def here():
    return lax.axis_index("dp"), lax.axis_index("row"), lax.axis_index("col")


def lanes_at(index, size):
    return pl.ds(pl.multiple_of(index * size, 128), size)


def greet(others):
    barrier = pltpu.get_barrier_semaphore()
    for other in others:
        pl.semaphore_signal(barrier, inc=1, device_id=other, device_id_type=pl.DeviceIdType.MESH)
    pl.semaphore_wait(barrier, len(others))


def at_step(step):
    return pl.when(pl.program_id(0) == step)


def copy_to(src, dst, sems, i, device):
    return pltpu.make_async_remote_copy(
        src_ref=src, dst_ref=dst, send_sem=sems.at[0, i], recv_sem=sems.at[1, i],
        device_id=device, device_id_type=pl.DeviceIdType.MESH,
    )


def dp_copies(dps, sems, src_of, dst_of, first=0):
    dp, row, col = here()
    return [
        copy_to(src_of(dp ^ by, by - 1), dst_of(dp ^ by, by - 1), sems, first + by - 1, (dp ^ by, row, col))
        for by in range(1, dps)
    ]


def hand_out(dps, sems, first, src, out):
    dp, row, col = here()
    piece, lanes = src.shape
    rows = lambda d: pl.ds(d * piece, piece)
    if dps != 4:
        return dp_copies(dps, sems, lambda to, i: src, lambda to, i: out.at[rows(dp), :], first), []
    near = [
        copy_to(src, out.at[rows(dp), :], sems, first + i, (dp ^ by, row, col)) for i, by in enumerate((1, 2))
    ]
    far = []
    for i, by in enumerate((1, 2)):
        passed = out.at[pl.ds((dp ^ by) * piece + i * (piece // 2), piece // 2), :]
        far.append(copy_to(passed, passed, sems, first + 2 + i, (dp ^ 3 ^ by, row, col)))
    return near, far


def dp_peers(dps):
    dp, row, col = here()
    return [(dp ^ by, row, col) for by in range(1, dps)]


def mirror_of(cols):
    dp, row, col = here()
    return (dp, row, cols - 1 - col)


def remote_params(collective_id):
    return pltpu.CompilerParams(
        dimension_semantics=("arbitrary",), vmem_limit_bytes=VMEM_LIMIT, collective_id=collective_id,
        has_side_effects=True,
    )


ANY = pl.BlockSpec(memory_space=pl.ANY)


def import_kernel(
    cols, dps, tok, wv, sw, vec, tg, vf, sf, vecs, zeros, tok_vm, w_vm, s_vm, vec_vm, local, send, recv,
):
    dp, row, col = here()
    group = cols // 2
    place = lax.rem(col, group)
    half, shard = wv.shape
    count = tok.shape[0]
    piece = half // dps
    sibling = (dp, 1 - row, col)
    mirror = (dp, row, cols - 1 - col)
    col_peer = lambda by: (dp, row, col ^ by)
    dp_peer = lambda by: (dp ^ by, row, col)
    greet(
        [sibling]
        + [col_peer(by) for by in range(1, cols)]
        + [dp_peer(by) for by in range(1, dps)]
    )
    used = [0]
    started = []

    def remote(src, dst, device):
        i = used[0]
        used[0] += 1
        return pltpu.make_async_remote_copy(
            src_ref=src, dst_ref=dst, send_sem=send.at[i], recv_sem=recv.at[i],
            device_id=device, device_id_type=pl.DeviceIdType.MESH,
        )

    def launch(src, dst, device):
        copy = remote(src, dst, device)
        copy.start()
        started.append(copy)
        return copy

    def keep(i, src, dst):
        copy = pltpu.make_async_copy(src, dst, local.at[i])
        copy.start()
        return copy

    my_rows = pl.ds(row * half, half)
    my_piece = pl.ds(row * half + dp * piece, piece)
    own, other = pl.ds(0, shard), pl.ds(shard, shard)
    src_piece = pl.ds(dp * piece, piece)

    staged = [
        keep(6, vec, vec_vm),
        keep(0, sw.at[src_piece, :], s_vm),
        keep(2, tok, tok_vm),
        keep(3, wv, w_vm),
    ]
    s_cross = [
        launch(sw.at[src_piece, :], sf.at[my_piece, lanes_at(col, 128)], col_peer(by))
        for by in range(1, cols)
    ]
    v_cross = launch(wv.at[src_piece, :], vf.at[my_piece, other], mirror)
    vec_cross = [launch(vec, vecs.at[col], col_peer(by)) for by in range(1, cols)]
    my_tokens = tg.at[pl.ds(HALO + place * count, count), :]
    tok_cross = [launch(tok, my_tokens, col_peer(by)) for by in range(1, group)]
    halo_src = tok.at[pl.ds(count - HALO, HALO), :]
    halo_dst = tg.at[pl.ds(0, HALO), :]
    halo_at = used[0]
    used[0] += group
    halos = [
        pltpu.make_async_remote_copy(
            src_ref=halo_src, dst_ref=halo_dst, send_sem=send.at[halo_at + j], recv_sem=recv.at[halo_at],
            device_id=(dp, row, group + j), device_id_type=pl.DeviceIdType.MESH,
        )
        for j in range(group)
    ]

    @pl.when(col == group - 1)
    def _():
        for copy in halos:
            copy.start()

    zeros[...] = jnp.zeros_like(zeros)

    @pl.when(col < group)
    def _():
        clear = pltpu.make_async_copy(zeros, halo_dst, local.at[1])
        clear.start()
        clear.wait()

    v_own = launch(wv, vf.at[my_rows, own], sibling)
    for copy in staged:
        copy.wait()
    small_own = keep(0, s_vm, sf.at[my_piece, lanes_at(col, 128)])
    kept = [
        keep(6, vec_vm, vecs.at[col]),
        keep(2, tok_vm, my_tokens),
        keep(3, w_vm, vf.at[my_rows, own]),
    ]

    def spread_out(ref):
        return [launch(ref, ref, dp_peer(by)) for by in range(1, dps)]

    def arrive(copies):
        for copy in copies:
            copy.wait_recv()

    arrive(s_cross)
    small_own.wait()
    s_dp = spread_out(sf.at[my_piece, :])
    arrive([v_cross])
    v_dp = spread_out(vf.at[my_piece, other])
    arrive(s_dp)
    last = [launch(sf.at[my_rows, :], sf.at[my_rows, :], sibling)]
    arrive(v_dp)
    last += [launch(vf.at[my_rows, other], vf.at[my_rows, other], sibling)]
    arrive(last)
    arrive([v_own])
    arrive(vec_cross)
    arrive(tok_cross)

    @pl.when(col >= group)
    def _():
        halos[0].wait_recv()

    @pl.when(col == group - 1)
    def _():
        for copy in halos:
            copy.wait_send()

    for copy in kept:
        copy.wait()
    for copy in started:
        copy.wait_send()


def import_all(cols, dps, tokens, w_value, small, vec):
    half, shard = w_value.shape
    count, width = tokens.shape
    any_spec = pl.BlockSpec(memory_space=pl.ANY)
    copies = 1 + 2 * (cols - 1) + (cols // 2 - 1) + cols // 2 + 1 + 2 * (dps - 1) + 2
    return pl.pallas_call(
        partial(import_kernel, cols, dps),
        in_specs=[any_spec] * 4,
        out_specs=[any_spec] * 4,
        out_shape=[
            sds((HALO + count * (cols // 2), width), BF),
            sds((2 * half, 2 * shard), BF),
            sds((2 * half, cols * 128), BF),
            sds((cols,) + vec.shape, BF),
        ],
        scratch_shapes=[
            pltpu.VMEM((HALO, width), BF),
            pltpu.VMEM((count, width), BF),
            pltpu.VMEM((half, shard), BF),
            pltpu.VMEM((half // dps, 128), BF),
            pltpu.VMEM(vec.shape, BF),
            pltpu.SemaphoreType.DMA((7,)),
            pltpu.SemaphoreType.DMA((copies,)),
            pltpu.SemaphoreType.DMA((copies,)),
        ],
        compiler_params=pltpu.CompilerParams(
            collective_id=1, has_side_effects=True, vmem_limit_bytes=VMEM_LIMIT
        ),
        cost_estimate=cost(45),
        name="import_all",
    )(tokens, w_value, small, vec)


def conv_window(raw_ref, start, size):
    window = raw_ref[HALO + start - 8 : HALO + start + size, :]
    return [pltpu.roll(window, 3 - k, 0)[8:, :] for k in range(3)] + [window[8:, :]]


def conv_rows(moved, taps):
    total = taps[4:5, :] + taps[0:1, :] * moved[0]
    for k in range(1, 4):
        total = total + taps[k : k + 1, :] * moved[k]
    return total


def normalize(tok_ref, gain_ref, normed_ref, inv_ref):
    tokens = tok_ref.shape[0] - HALO
    for at in [0] + list(range(HALO, HALO + tokens, Q)):
        size = HALO if at == 0 else Q
        values = tok_ref[at : at + size, :].astype(F32)
        inv = lax.rsqrt(jnp.mean(values * values, axis=-1, keepdims=True) + EPSILON)
        normed_ref[at : at + size, :] = (values * inv * gain_ref[0:1, :]).astype(BF)
        inv_ref[at : at + size, :] = jnp.broadcast_to(inv, (size, 128))


def project_steps(
    small_ref, pick_ref, head_ref, normed_ref, raw_ref, stepin_ref, step_ref, cum_ref, grow_ref, offs_ref,
    picked_ref,
):
    tokens = step_ref.shape[0]
    picked = mm(small_ref[...], pick_ref[...]).astype(BF)
    picked_ref[...] = picked
    raw_ref[...] = mm(normed_ref[...], picked[:, :TILE])
    step_in = mm(normed_ref[HALO:, :], picked[:, TILE:]) + head_ref[0:1, :]
    small = jnp.exp(-jnp.abs(step_in))
    plus = 1.0 + small
    safe = jnp.where(plus == 1.0, 1.0, plus - 1.0)
    log_part = jnp.where(plus == 1.0, small, jnp.log(plus) * (small / safe))
    step = jnp.maximum(step_in, 0.0) + log_part
    stepin_ref[...] = step_in
    step_ref[...] = step
    falls = step * head_ref[1:2, :]
    lower = (iota2((Q, Q), 0) >= iota2((Q, Q), 1)).astype(F32)
    before = jnp.zeros((1, 128), F32)
    offs_ref[...] = jnp.zeros_like(offs_ref)
    for b in range(tokens // Q):
        rows = slice(b * Q, b * Q + Q)
        cum = mm_exact(lower, falls[rows, :])
        cum_ref[rows, :] = cum
        high, low = split2(jnp.exp(cum + before))
        grow_ref[rows, 0:128] = high
        grow_ref[rows, 128:256] = low
        before = before + cum[Q - 1 : Q, :]
        offs_ref[b + 1 : b + 2, :] = before


def activate(raw_ref, taps, act_ref, copy_ref):
    tokens = act_ref.shape[0]
    for at in range(0, tokens, ROWS):
        pre = conv_rows(conv_window(raw_ref, at, ROWS), taps)
        act = (pre * sigmoid(pre)).astype(BF)
        act_ref[at : at + ROWS, :] = act
        copy_ref[at : at + ROWS, :] = act


def expand(per_head, spread):
    high, low = split2(per_head)
    return mm(jnp.concatenate([high, low], 1), spread)


def transpose_bf(values):
    return values.astype(F32).T.astype(BF)


def expand_rows(per_head, spread):
    high, low = split2(jnp.concatenate(per_head, 0))
    return mm(jnp.concatenate([high, low], 1), spread)


def eight(row):
    return jnp.broadcast_to(row, (8, row.shape[1]))


def spans(total, size):
    size = min(size, total)
    return [slice(at, at + size) for at in range(0, total, size)]


def state_block(x_ref, b_ref, step_ref, cum_ref, spread_ref, held):
    cum = cum_ref[...]
    end = cum[Q - 1 : Q, :]
    tail = jnp.exp(end - cum) * step_ref[...]
    b_t = transpose_bf(b_ref[...])
    b_t2 = jnp.concatenate([b_t, b_t], 1)
    for lanes in spans(x_ref.shape[1], 1536):
        wide = expand_rows([tail, eight(jnp.exp(end))], spread_ref[:, lanes])
        high, low = split2(wide[:Q] * x_ref[:, lanes].astype(F32))
        fresh = mm(b_t2, jnp.concatenate([high, low], 0))
        held[:, lanes] = held[:, lanes] * wide[Q : Q + 1, :] + fresh


def forward_block(x_ref, b_ref, c_ref, step_ref, cum_ref, spread_ref, state_ref, y_ref):
    b_blk, c_blk = b_ref[...], c_ref[...]
    affinity = mm_nt(c_blk, b_blk)
    causal = iota2((Q, Q), 0) >= iota2((Q, Q), 1)
    first = iota2((Q, 128), 1) < HEAD
    cum = cum_ref[...]
    cum_t = cum.T
    step_t = step_ref[...].T
    growth = jnp.exp(cum)
    c2 = jnp.concatenate([c_blk, c_blk], 1)
    zero = jnp.zeros((Q, 128), BF)
    for lanes in spans(x_ref.shape[1], 1536):
        s_high, s_low = split2(state_ref[0, :, lanes])
        reached = mm(c2, jnp.concatenate([s_high, s_low], 0)) * expand_rows([growth], spread_ref[:, lanes])
        for at in range(lanes.start, lanes.stop, 128):
            x_pair = x_ref[:, at : at + 128]
            x0, x1 = jnp.where(first, x_pair, zero), jnp.where(first, zero, x_pair)
            pieces = []
            for half in range(2):
                h = at // HEAD + half
                spread_h = cum[:, h : h + 1] - cum_t[h : h + 1, :]
                decay = jnp.exp(jnp.where(causal, spread_h, -1e30))
                pieces += split2(affinity * decay * step_t[h : h + 1, :])
            intra = mm(jnp.concatenate(pieces, 1), jnp.concatenate([x0, x0, x1, x1], 0))
            inside = at - lanes.start
            y_ref[:, at : at + 128] = intra + reached[:, inside : inside + 128]


def forward_all_kernel(
    cols, dps,
    tok_ref, gain_ref, w_ref, small_ref, pick_ref, taps_ref, head_ref, spread_ref, cot, wg, wo,
    raw_ref, act_ref, normed_ref, stepin_ref, step_ref, cum_ref, grow_ref, offs_ref, inv_ref, picked_ref,
    states_ref, y_ref, graw_ref, gm_ref, early_ref, cot_out, gf, of,
    act_vm, states_vm, held, early_land, cot_vm, g_tiles, o_tiles, wg_vm, wo_vm, sems, local,
):
    step = pl.program_id(0)
    tokens, channels = states_vm.shape[0] * Q, held.shape[1]
    blocks = states_vm.shape[0]
    tiles = channels // TILE
    scan_at = tiles + 1
    out_at = scan_at + blocks
    gate_at = out_at + blocks
    dp, row, col = here()
    group = cols // 2
    place = lax.rem(col, group)
    half, shard = wg.shape
    count = cot.shape[0]
    others = dps - 1
    piece, piece_out = half // dps, wo.shape[0] // dps
    sibling, mirror = (dp, 1 - row, col), mirror_of(cols)
    peers = [(dp, row, col ^ by) for by in range(1, group)]
    my_rows = pl.ds(row * half, half)
    my_piece = pl.ds(row * half + dp * piece, piece)
    out_piece = pl.ds(shard + dp * piece_out, piece_out)
    my_lanes = lanes_at(row, half)
    own, other = pl.ds(0, shard), pl.ds(shard, shard)
    src_piece, src_out = pl.ds(dp * piece, piece), pl.ds(dp * piece_out, piece_out)
    my_cot = cot_vm.at[pl.ds(place * count, count), :]

    g_cross = lambda: copy_to(wg.at[src_piece, :], gf.at[my_piece, other], sems, 0, mirror)
    o_cross = lambda: copy_to(wo.at[src_out, :], of.at[out_piece, my_lanes], sems, 1, mirror)
    g_own = lambda: copy_to(wg, gf.at[my_rows, own], sems, 2, sibling)
    o_own = lambda: copy_to(wo, of.at[own, my_lanes], sems, 3, sibling)
    g_rest = lambda: copy_to(gf.at[my_rows, other], gf.at[my_rows, other], sems, 4, sibling)
    o_rest = lambda: copy_to(of.at[other, my_lanes], of.at[other, my_lanes], sems, 5, sibling)
    early_moves = lambda: [
        copy_to(held.at[:, own], early_land.at[:, other], sems, 6, mirror),
        copy_to(held.at[:, other], early_land.at[:, own], sems, 7, mirror),
    ]
    cot_moves = lambda: [copy_to(cot, my_cot, sems, 8 + i, peer) for i, peer in enumerate(peers)]
    first = 8 + group - 1

    def g_dp():
        ref = gf.at[my_piece, other]
        return dp_copies(dps, sems, lambda to, i: ref, lambda to, i: ref, first)

    def o_dp():
        ref = of.at[out_piece, my_lanes]
        return dp_copies(dps, sems, lambda to, i: ref, lambda to, i: ref, first + others)

    load_cot = pltpu.make_async_copy(cot, my_cot, local.at[0])
    load_g = pltpu.make_async_copy(wg, wg_vm, local.at[1])
    load_o = pltpu.make_async_copy(wo, wo_vm, local.at[2])
    store_g = pltpu.make_async_copy(wg_vm, gf.at[my_rows, own], local.at[1])
    store_o = pltpu.make_async_copy(wo_vm, of.at[own, my_lanes], local.at[2])
    store_cot = pltpu.make_async_copy(cot_vm, cot_out, local.at[0])

    def g_tile(at):
        return pltpu.make_async_copy(gf.at[:, lanes_at(at, TILE)], g_tiles.at[lax.rem(at, 2)], local.at[3])

    def o_tile(at):
        rows = pl.ds(pl.multiple_of(at * TILE, TILE), TILE)
        return pltpu.make_async_copy(of.at[rows, :], o_tiles.at[lax.rem(at, 2)], local.at[4])

    @at_step(0)
    def _():
        load_cot.start()
        load_g.start()
        load_o.start()
        greet([sibling, mirror] + peers + dp_peers(dps))
        for move in [g_cross(), o_cross(), g_own(), o_own()]:
            move.start()
        normalize(tok_ref, gain_ref, normed_ref, inv_ref)

    @at_step(1)
    def _():
        load_g.wait()
        store_g.start()
        load_o.wait()
        store_o.start()

    @at_step(tiles - 2)
    def _():
        for move in cot_moves():
            move.start()

    @at_step(scan_at + 2)
    def _():
        g_cross().wait_recv()
        for move in g_dp():
            move.start()

    @at_step(out_at)
    def _():
        o_cross().wait_recv()
        for move in o_dp():
            move.start()

    @at_step(out_at + blocks // 2)
    def _():
        for move in g_dp():
            move.wait_recv()
        g_rest().start()

    @at_step(gate_at + tiles // 2)
    def _():
        for move in o_dp():
            move.wait_recv()
        o_rest().start()

    @at_step(out_at)
    def _():
        @pl.when(col < group)
        def _():
            for move in early_moves():
                move.start()

    @pl.when(step < tiles)
    def _():
        raw_ref[...] = mm(normed_ref[...], w_ref[...])

    @pl.when(step == tiles)
    def _():
        project_steps(
            small_ref, pick_ref, head_ref, normed_ref, raw_ref, stepin_ref, step_ref, cum_ref, grow_ref, offs_ref,
            picked_ref,
        )

    @pl.when(step <= tiles)
    def _():
        activate(raw_ref, taps_ref[...], act_ref, act_vm.at[:, lanes_at(step, TILE)])

    def block_refs(at):
        rows = pl.ds(pl.multiple_of(at * Q, Q), Q)
        return (
            act_vm.at[rows, pl.ds(0, channels)], act_vm.at[rows, pl.ds(channels, N)],
            act_vm.at[rows, pl.ds(channels + N, N)], step_ref.at[rows, :], cum_ref.at[rows, :],
        )

    @pl.when(step == scan_at)
    def _():
        held[...] = jnp.zeros_like(held)

    @pl.when((step >= scan_at) & (step < out_at))
    def _():
        x_blk, b_blk, _, step_blk, cum_blk = block_refs(step - scan_at)
        states_ref[0] = held[...]
        states_vm[step - scan_at] = held[...]
        state_block(x_blk, b_blk, step_blk, cum_blk, spread_ref, held)

    @pl.when(step == out_at)
    def _():
        states_ref[0] = held[...]

    @pl.when((step >= out_at) & (step < gate_at))
    def _():
        x_blk, b_blk, c_blk, step_blk, cum_blk = block_refs(step - out_at)
        forward_block(
            x_blk, b_blk, c_blk, step_blk, cum_blk, spread_ref, states_vm.at[pl.ds(step - out_at, 1)], y_ref
        )

    @pl.when(step == gate_at)
    def _():
        for move in [g_own(), g_rest()]:
            move.wait_recv()
        store_g.wait()
        g_tile(0).start()

    @pl.when((step >= gate_at) & (step < gate_at + tiles))
    def _():
        at = step - gate_at
        g_tile(at).wait()

        @pl.when(at < tiles - 1)
        def _():
            g_tile(at + 1).start()

        graw_ref[...] = mm(normed_ref[HALO:, :], g_tiles[lax.rem(at, 2)])

    @pl.when(step == gate_at + tiles)
    def _():
        for move in [o_own(), o_rest()] + cot_moves():
            move.wait_recv()
        store_o.wait()
        load_cot.wait()
        store_cot.start()
        o_tile(0).start()

    @pl.when(step >= gate_at + tiles)
    def _():
        at = step - gate_at - tiles
        o_tile(at).wait()

        @pl.when(at < tiles - 1)
        def _():
            o_tile(at + 1).start()

        gm_ref[...] = mm_nt(cot_vm[...], o_tiles[lax.rem(at, 2)])

    @at_step(pl.num_programs(0) - 1)
    def _():
        store_cot.wait()
        for move in [g_cross(), o_cross(), g_own(), o_own(), g_rest(), o_rest()] + cot_moves() + g_dp() + o_dp():
            move.wait_send()

        @pl.when(col < group)
        def _():
            for move in early_moves():
                move.wait_send()
            early_ref[...] = jnp.zeros_like(early_ref)

        @pl.when(col >= group)
        def _():
            for move in early_moves():
                move.wait_recv()
            early_ref[...] = early_land[...]


def forward_all(cols, dps, group_tokens, gain, weights, small, pick, taps, head_rows, spread, cotangent, w_gate, w_out):
    rows, width = group_tokens.shape
    tokens = rows - HALO
    channels = weights.shape[1]
    total = channels + TILE
    blocks, tiles = tokens // Q, channels // TILE
    half, shard = w_gate.shape
    scan_at = tiles + 1
    out_at = scan_at + blocks
    gate_at = out_at + blocks

    def clamp(first, count):
        return lambda i: jnp.clip(i - first, 0, count - 1)

    lanes = lambda at, count: pl.BlockSpec((count, TILE), lambda i: (0, at(i)))
    both, value_at = clamp(0, tiles + 1), clamp(0, tiles)
    state_at, y_at = clamp(scan_at, blocks + 1), clamp(out_at, blocks)
    raw_tile, gm_tile = clamp(gate_at, tiles), clamp(gate_at + tiles, tiles)
    vmem = pltpu.VMEM
    return pl.pallas_call(
        partial(forward_all_kernel, cols, dps),
        grid=(gate_at + 2 * tiles,),
        in_specs=[
            whole((rows, width)),
            whole((1, width)),
            lanes(value_at, width),
            whole(small.shape),
            whole(pick.shape),
            lanes(both, 8),
            whole((8, 128)),
            whole(spread.shape),
            ANY, ANY, ANY,
        ],
        out_specs=[
            lanes(both, rows),
            lanes(both, tokens),
            whole((rows, width)),
            whole((tokens, 128)),
            whole((tokens, 128)),
            whole((tokens, 128)),
            whole((tokens, 256)),
            whole((16, 128)),
            whole((rows, 128)),
            whole((width, TILE + 128)),
            pl.BlockSpec((1, N, channels), lambda i: (state_at(i), 0, 0)),
            pl.BlockSpec((Q, channels), lambda i: (y_at(i), 0)),
            lanes(raw_tile, tokens),
            lanes(gm_tile, tokens),
            whole((N, channels)),
            ANY, ANY, ANY,
        ],
        out_shape=[
            sds((rows, total)),
            sds((tokens, total), BF),
            sds((rows, width), BF),
            sds((tokens, 128)),
            sds((tokens, 128)),
            sds((tokens, 128)),
            sds((tokens, 256), BF),
            sds((16, 128)),
            sds((rows, 128)),
            sds((width, TILE + 128), BF),
            sds((blocks + 1, N, channels)),
            sds((tokens, channels)),
            sds((tokens, channels)),
            sds((tokens, channels)),
            sds((N, channels)),
            sds((tokens, width), BF),
            sds((width, channels), BF),
            sds((channels, width), BF),
        ],
        scratch_shapes=[
            vmem((tokens, total), BF),
            vmem((blocks, N, channels), F32),
            vmem((N, channels), F32),
            vmem((N, channels), F32),
            vmem((tokens, width), BF),
            vmem((2, width, TILE), BF),
            vmem((2, TILE, width), BF),
            vmem((half, shard), BF),
            vmem((shard, half), BF),
            pltpu.SemaphoreType.DMA((2, 7 + cols // 2 + 2 * (dps - 1))),
            pltpu.SemaphoreType.DMA((5,)),
        ],
        compiler_params=remote_params(4),
        cost_estimate=cost(70),
        name="forward_all",
    )(group_tokens, gain, weights, small, pick, taps, head_rows, spread, cotangent, w_gate, w_out)


def grad_state_block(dy_tiles, c_ref, cum_ref, spread_ref, after_ref, held):
    after_ref[0] = held[...]
    growth = jnp.exp(cum_ref[...])
    c_t = transpose_bf(c_ref[...])
    c_t2 = jnp.concatenate([c_t, c_t], 1)
    wide = expand_rows([growth], spread_ref[...])
    for tile in range(held.shape[1] // TILE):
        lanes = slice(tile * TILE, tile * TILE + TILE)
        high, low = split2(dy_tiles[tile] * wide[:, lanes])
        direct = mm(c_t2, jnp.concatenate([high, low], 0))
        held[:, lanes] = held[:, lanes] * wide[Q - 1 : Q, lanes] + direct


def near_block(
    at_block, here_rows, dy_ref, x_ref, b_ref, c_ref, step_ref, cum_ref, spread_ref, state_ref, early_ref,
    offs_ref, gx_ref, gbc_ref,
):
    b_blk, c_blk = b_ref[...], c_ref[...]
    affinity_t = mm_nt(b_blk, c_blk)
    causal_t = iota2((Q, Q), 1) >= iota2((Q, Q), 0)
    first = iota2((Q, 128), 1) < HEAD
    cum = cum_ref[...]
    cum_t = cum.T
    step = step_ref[...]
    growth = jnp.exp(cum)
    early_fall = eight(jnp.exp(offs_ref[pl.ds(at_block, 1), :]))
    zero = jnp.zeros((Q, 128), BF)
    grad_affinity_t = jnp.zeros((Q, Q), F32)
    grad_c = jnp.zeros((Q, N), F32)
    for lanes in spans(x_ref.shape[1], 768):
        wide = expand_rows([growth, early_fall], spread_ref[:, lanes])
        before = state_ref[0, :, lanes] + wide[Q : Q + 1, :] * early_ref[:, lanes]
        dy_wide = dy_ref[:, lanes]
        s_high, s_low = split2(before)
        g_high, g_low = split2(dy_wide * wide[:Q])
        grad_c = grad_c + mm_nt(
            jnp.concatenate([g_high, g_low, g_high], 1), jnp.concatenate([s_high, s_high, s_low], 1)
        )
        for at in range(lanes.start, lanes.stop, 128):
            d_high, d_low = split2(dy_ref[:, at : at + 128])
            x_pair = x_ref[:, at : at + 128]
            x0, x1 = jnp.where(first, x_pair, zero), jnp.where(first, zero, x_pair)
            grad_mixing = mm_nt(
                jnp.concatenate([jnp.concatenate([x0, x0], 1), jnp.concatenate([x1, x1], 1)], 0),
                jnp.concatenate([d_high, d_low], 1),
            )
            left, right = [], []
            for half in range(2):
                h = at // HEAD + half
                spread_h = cum_t[h : h + 1, :] - cum[:, h : h + 1]
                decay = jnp.exp(jnp.where(causal_t, spread_h, -1e30))
                m_high, m_low = split2(affinity_t * decay)
                grad_affinity_t = grad_affinity_t + (
                    grad_mixing[half * Q : half * Q + Q, :] * decay * step[:, h : h + 1]
                )
                keep = first if half == 0 else jnp.logical_not(first)
                dh, dl = jnp.where(keep, d_high, zero), jnp.where(keep, d_low, zero)
                left += [m_high, m_low, m_high]
                right += [dh, dh, dl]
            gx_ref[here_rows, at : at + 128] = mm(jnp.concatenate(left, 1), jnp.concatenate(right, 0))
    a_high, a_low = split2(grad_affinity_t)
    gbc_ref[here_rows, 0:N] = mm(jnp.concatenate([a_high, a_low], 1), jnp.concatenate([c_blk, c_blk], 0))
    t_high, t_low = split2(grad_affinity_t.T)
    gbc_ref[here_rows, N : 2 * N] = grad_c + mm(
        jnp.concatenate([t_high, t_low], 1), jnp.concatenate([b_blk, b_blk], 0)
    )


def far_block(
    blocks, at_block, here_rows, dy_ref, x_ref, y_ref, gx_ref, b_ref, step_ref, cum_ref, stepin_ref, spread_ref,
    gather_ref, after_ref, late_ref, state_ref, early_ref, offs_ref, head_ref, skip_ref, gbc_ref,
    ga_ref, gstep_ref, gbc_out_ref, sums_ref,
):
    b_blk = b_ref[...]
    b2 = jnp.concatenate([b_blk, b_blk], 1)
    cum, step = cum_ref[...], step_ref[...]
    tail = jnp.exp(cum[Q - 1 : Q, :] - cum)
    offs_after = offs_ref[pl.ds(at_block + 1, 1), :]
    late_fall = eight(jnp.exp(offs_ref[pl.ds(blocks, 1), :] - offs_after))
    early_fall = eight(jnp.exp(offs_after))
    dots = jnp.zeros((2 * Q + 8, 128), F32)
    grad_b = gbc_ref[here_rows, 0:N]
    for lanes in spans(x_ref.shape[1], 512):
        wide = expand_rows([tail, step, late_fall, early_fall], spread_ref[:, lanes])
        tail_wide, step_wide = wide[:Q], wide[Q : 2 * Q]
        x = x_ref[:, lanes].astype(F32)
        dy = dy_ref[:, lanes]
        skip = skip_ref[0:1, lanes]
        d_state = after_ref[0, :, lanes] + wide[2 * Q : 2 * Q + 1, :] * late_ref[:, lanes]
        state = state_ref[0, :, lanes] + wide[2 * Q + 8 : 2 * Q + 9, :] * early_ref[:, lanes]
        touch = eight(jnp.sum(d_state * state, axis=0, keepdims=True))
        s_high, s_low = split2(d_state)
        gx = gx_ref[here_rows, lanes] + tail_wide * mm(b2, jnp.concatenate([s_high, s_low], 0))
        w_high, w_low = split2(tail_wide * step_wide * x)
        grad_b = grad_b + mm_nt(
            jnp.concatenate([w_high, w_low, w_high], 1), jnp.concatenate([s_high, s_high, s_low], 1)
        )
        ga_ref[:, lanes] = step_wide * gx + skip * dy
        high, low = split2(jnp.concatenate([dy * (y_ref[:, lanes] - skip * x), x * gx, touch], 0))
        gather = gather_ref[lanes, :]
        dots = dots + mm(jnp.concatenate([high, low], 1), jnp.concatenate([gather, gather], 0))
    row_dots, col_dots, last_add = dots[:Q], dots[Q : 2 * Q], dots[2 * Q :]
    last_row = iota2((Q, 128), 0) == Q - 1
    grad_cum = row_dots - step * col_dots + jnp.where(last_row, last_add[0:1, :], 0.0)
    upper = (iota2((Q, Q), 1) >= iota2((Q, Q), 0)).astype(F32)
    grad_rate = mm_exact(upper, grad_cum)
    grad_step = col_dots + grad_rate * head_ref[1:2, :]
    grad_raw = grad_step * sigmoid(stepin_ref[...])
    gstep_ref[...] = grad_raw.astype(BF)
    sums_ref[0:1, :] += jnp.sum(grad_rate * step, axis=0, keepdims=True)
    sums_ref[1:2, :] += jnp.sum(grad_raw, axis=0, keepdims=True)
    gbc_out_ref[:, 0:N] = grad_b
    gbc_out_ref[:, N : 2 * N] = gbc_ref[here_rows, N : 2 * N]


WEIGHT_TILE = 384


def mm_tn(a, b):
    return lax.dot_general(a, b, (((0,), (0,)), ((), ())), preferred_element_type=F32)


def backward_kernel(
    cols, dps,
    dy_ref, x_ref, y_ref, b_ref, c_ref, step_ref, cum_ref, stepin_ref, spread_ref, gather_ref, after_ref,
    state_ref, early_ref, offs_ref, head_ref, skip_ref, mixed_ref, of_ref, gg_ref,
    first_grad, mixed_hbm, gg_hbm, cot, normed,
    ga_ref, gstep_ref, gbc_out_ref, sums_ref, o_total_ref, g_own_ref, g_cross_ref, branch_ref, branch_in,
    mixed_sib, gg_sib,
    gx_ref, gbc_ref, late_ref, o_low, o_own, o_land, o_cross, o_cross_land, g_low, g_own, g_land, parts,
    c_own, c_sib, n_own, n_sib, m_tiles, gg_tiles, sems, local,
):
    step_at = pl.program_id(0)
    blocks = gx_ref.shape[0] // Q
    dp, row, col = here()
    group = cols // 2
    place = lax.rem(col, group)
    shard, channels = g_own_ref.shape[1], gx_ref.shape[1]
    half = c_own.shape[1]
    count = branch_ref.shape[0]
    others = dps - 1
    own, other = pl.ds(0, shard), pl.ds(shard, shard)
    sibling, mirror = (dp, 1 - row, col), mirror_of(cols)
    peers = [(dp, row, col ^ by) for by in range(1, group)]
    out_steps, o_steps, g_steps = 2 * half // TILE, channels // WEIGHT_TILE, channels // TILE
    o_at = out_steps
    g_at = o_at + o_steps
    near_at = g_at + g_steps
    far_at = near_at + blocks
    last = far_at + blocks - 1

    def o_moves():
        return dp_copies(dps, sems, lambda to, i: o_low.at[:, to], lambda to, i: o_land.at[i])

    def g_moves():
        return dp_copies(dps, sems, lambda to, i: g_low.at[to], lambda to, i: g_land.at[i], others)

    at = 2 * others
    cross_move = lambda: copy_to(o_cross, o_cross_land, sems, at, mirror)
    late_moves = lambda: [
        copy_to(first_grad.at[:, own], late_ref.at[:, other], sems, at + 1, mirror),
        copy_to(first_grad.at[:, other], late_ref.at[:, own], sems, at + 2, mirror),
    ]
    core_moves = lambda: [
        copy_to(cot.at[:, lanes_at(1 - row, half)], c_sib, sems, at + 3, sibling),
        copy_to(mixed_hbm, mixed_sib, sems, at + 4, sibling),
        copy_to(normed.at[:, lanes_at(1 - row, half)], n_sib, sems, at + 5, sibling),
        copy_to(gg_hbm, gg_sib, sems, at + 6, sibling),
    ]
    part_moves = lambda: [
        copy_to(parts.at[i], branch_in.at[i], sems, at + 7 + i, peer) for i, peer in enumerate(peers)
    ]
    load_c = pltpu.make_async_copy(cot.at[:, lanes_at(row, half)], c_own, local.at[0])
    load_n = pltpu.make_async_copy(normed.at[:, lanes_at(row, half)], n_own, local.at[1])

    def m_tile(tile):
        lanes = lanes_at(tile, WEIGHT_TILE)
        return pltpu.make_async_copy(mixed_sib.at[:, lanes], m_tiles.at[lax.rem(tile, 2)], local.at[2])

    def gg_tile(tile):
        lanes = lanes_at(tile, TILE)
        return pltpu.make_async_copy(gg_sib.at[:, lanes], gg_tiles.at[lax.rem(tile, 2)], local.at[3])

    @at_step(0)
    def _():
        load_c.start()
        load_n.start()
        greet([sibling, mirror] + peers + dp_peers(dps))
        for move in core_moves():
            move.start()

        @pl.when(col >= group)
        def _():
            for move in late_moves():
                move.start()
            late_ref[...] = jnp.zeros_like(late_ref)

        sums_ref[...] = jnp.zeros_like(sums_ref)

    @pl.when(step_at < o_at)
    def _():
        rows = lambda index: pl.ds(pl.multiple_of(index * count, 128), count)
        branch_ref[...] = mm(mixed_ref[rows(place), :], of_ref[...])
        for by in range(1, group):
            parts[by - 1, :, lanes_at(step_at, TILE)] = mm(mixed_ref[rows(place ^ by), :], of_ref[...]).astype(BF)

    @pl.when(step_at == o_at)
    def _():
        load_c.wait()
        for move in core_moves()[:2]:
            move.wait_recv()
        m_tile(0).start()

    @pl.when((step_at >= o_at) & (step_at < g_at))
    def _():
        tile = step_at - o_at
        m_tile(tile).wait()

        @pl.when(tile < o_steps - 1)
        def _():
            m_tile(tile + 1).start()

        total = mm_tn(mixed_ref[:, lanes_at(tile, WEIGHT_TILE)], c_own[...])
        total = total + mm_tn(m_tiles[lax.rem(tile, 2)], c_sib[...])
        piece = o_own.shape[1]
        per, each = WEIGHT_TILE // piece, shard // WEIGHT_TILE
        which, inside = lax.div(tile, each), lax.rem(tile, each)
        for p in range(per):
            part = total[p * piece : p * piece + piece, :]
            o_low[which, inside * per + p] = part.astype(BF)

            @pl.when(dp == inside * per + p)
            def _():
                o_own[which] = part

    @pl.when(step_at == g_at)
    def _():
        for move in o_moves():
            move.start()
        load_n.wait()
        for move in core_moves()[2:]:
            move.wait_recv()
        gg_tile(0).start()

    @pl.when((step_at >= g_at) & (step_at < near_at))
    def _():
        tile = step_at - g_at
        gg_tile(tile).wait()

        @pl.when(tile < g_steps - 1)
        def _():
            gg_tile(tile + 1).start()

        lanes = lanes_at(tile, TILE)
        total = mm_tn(n_own[HALO:, :], gg_ref[...]) + mm_tn(n_sib[HALO:, :], gg_tiles[lax.rem(tile, 2)])
        piece = g_own.shape[0]
        for p in range(dps):
            part = total[p * piece : p * piece + piece, :]
            g_low[p, :, lanes] = part.astype(BF)

            @pl.when(dp == p)
            def _():
                g_own[:, lanes] = part

    at_block = lax.rem(jnp.maximum(step_at - near_at, 0), blocks)
    here_rows = pl.ds(pl.multiple_of(at_block * Q, Q), Q)

    @pl.when((step_at >= near_at) & (step_at < far_at))
    def _():
        near_block(
            at_block, here_rows, dy_ref, x_ref, b_ref, c_ref, step_ref, cum_ref, spread_ref, state_ref,
            early_ref, offs_ref, gx_ref, gbc_ref,
        )

    @pl.when(step_at == g_at)
    def _():
        for move in part_moves():
            move.start()

    @pl.when(step_at == near_at + blocks - 1)
    def _():
        for move in o_moves():
            move.wait_recv()
        for move in g_moves():
            move.start()
        for i in range(others):
            o_own[...] += o_land[i].astype(F32)
        o_cross[...] = o_own[1].astype(BF)
        cross_move().start()

    @pl.when(step_at == far_at)
    def _():
        @pl.when(col < group)
        def _():
            for move in late_moves():
                move.wait_recv()

    @pl.when(step_at >= far_at)
    def _():
        far_block(
            blocks, at_block, here_rows, dy_ref, x_ref, y_ref, gx_ref, b_ref, step_ref, cum_ref, stepin_ref,
            spread_ref, gather_ref, after_ref, late_ref, state_ref, early_ref, offs_ref, head_ref, skip_ref,
            gbc_ref, ga_ref, gstep_ref, gbc_out_ref, sums_ref,
        )

    @at_step(last)
    def _():
        cross_move().wait()
        o_total_ref[...] = o_own[0] + o_cross_land[...].astype(F32)
        for move in g_moves():
            move.wait()
        for i in range(others):
            g_own[...] += g_land[i].astype(F32)
        g_own_ref[...] = g_own[:, :shard]
        g_cross_ref[...] = g_own[:, shard:].astype(BF)
        for move in part_moves():
            move.wait()
        for move in o_moves() + core_moves():
            move.wait_send()

        @pl.when(col >= group)
        def _():
            for move in late_moves():
                move.wait_send()


def scan_backward(
    cols, dps, dy, act, y, step, cum, step_in, spread, gather, after, states, early, offs, head_rows, skip,
    mixed, w_out, gg, first_grad, cot, normed,
):
    tokens, channels = dy.shape
    rows_n, width = normed.shape
    half = width // 2
    blocks, group, shard = tokens // Q, cols // 2, channels // 2
    count = tokens // group
    piece_o, piece_g = shard // dps, half // dps
    out_steps, o_steps, g_steps = width // TILE, channels // WEIGHT_TILE, channels // TILE
    g_at = out_steps + o_steps
    near_at = g_at + g_steps
    far_at = near_at + blocks

    def clamp(first, size):
        return lambda i: jnp.clip(i - first, 0, size - 1)

    block = lambda i: jnp.where(i < near_at, 0, lax.rem(jnp.maximum(i - near_at, 0), blocks))
    second = clamp(far_at, blocks)
    state_at = lambda i: block(i) + jnp.where(i < far_at, 0, 1)
    rows = lambda at, size: pl.BlockSpec((Q, size), lambda i: (at(i), 0))
    lanes = lambda at, size: pl.BlockSpec((size, TILE), lambda i: (0, at(i)))
    once = lambda shape: pl.BlockSpec(shape, lambda *_: (0,) * len(shape), pipeline_mode=pl.Buffered(1))
    vmem = pltpu.VMEM
    dma = pltpu.SemaphoreType.DMA
    return pl.pallas_call(
        partial(backward_kernel, cols, dps),
        grid=(far_at + blocks,),
        in_specs=[
            rows(block, channels),
            rows(block, channels),
            rows(second, channels),
            pl.BlockSpec((Q, N), lambda i: (block(i), channels // N)),
            pl.BlockSpec((Q, N), lambda i: (block(i), channels // N + 1)),
            rows(block, 128),
            rows(block, 128),
            rows(second, 128),
            once(spread.shape),
            once(gather.shape),
            pl.BlockSpec((1, N, channels), lambda i: (second(i), 0, 0)),
            pl.BlockSpec((1, N, channels), lambda i: (state_at(i), 0, 0)),
            once(early.shape),
            once((16, 128)),
            once((8, 128)),
            once((8, channels)),
            once(mixed.shape),
            lanes(clamp(0, out_steps), channels),
            lanes(clamp(g_at, g_steps), tokens),
        ] + [ANY] * 5,
        out_specs=[
            rows(second, channels),
            rows(second, 128),
            rows(second, 2 * N),
            whole((8, 128)),
            whole((piece_o, half)),
            whole((piece_g, shard)),
            whole((piece_g, shard)),
            lanes(clamp(0, out_steps), count),
            ANY, ANY, ANY,
        ],
        out_shape=[
            sds((tokens, channels)),
            sds((tokens, 128), BF),
            sds((tokens, 2 * N)),
            sds((8, 128)),
            sds((piece_o, half)),
            sds((piece_g, shard)),
            sds((piece_g, shard), BF),
            sds((count, width)),
            sds((max(group - 1, 1), count, width), BF),
            sds(mixed.shape, BF),
            sds(gg.shape, BF),
        ],
        scratch_shapes=[
            vmem((tokens, channels), F32), vmem((tokens, 2 * N), F32), vmem((N, channels), F32),
            vmem((2, dps, piece_o, half), BF), vmem((2, piece_o, half), F32),
            vmem((dps - 1, 2, piece_o, half), BF), vmem((piece_o, half), BF), vmem((piece_o, half), BF),
            vmem((dps, piece_g, channels), BF), vmem((piece_g, channels), F32),
            vmem((dps - 1, piece_g, channels), BF),
            vmem((max(group - 1, 1), count, width), BF),
            vmem((tokens, half), BF), vmem((tokens, half), BF),
            vmem((rows_n, half), BF), vmem((rows_n, half), BF),
            vmem((2, tokens, WEIGHT_TILE), BF), vmem((2, tokens, TILE), BF),
            dma((2, 2 * (dps - 1) + 6 + group)),
            dma((4,)),
        ],
        compiler_params=remote_params(3),
        cost_estimate=cost(80),
        name="scan_backward",
    )(
        dy, act, y, act, act, step, cum, step_in, spread, gather, after, states, early, offs, head_rows, skip,
        mixed, w_out, gg, first_grad, mixed, gg, cot, normed,
    )


def gate_kernel(
    cols, inner_channels,
    y0_ref, graw_ref, gm_ref, x_ref, early_ref, c_ref, grow_ref, spread_ref, vec_ref,
    cum_ref, c_block_ref, spread_all_ref,
    y_ref, mixed_ref, gg_ref, dy_ref, sums_ref, after_ref, first_ref,
    y_vm, graw_vm, gm_vm, squares, inners, stats, stats_land, stats_col, held, sems,
):
    step = pl.program_id(0)
    tiles = y_vm.shape[0]
    tokens = y0_ref.shape[0]
    dp, row, col = here()
    group = cols // 2
    peers = [(dp, row, col ^ by) for by in range(1, group)]
    gain = vec_ref[1:2, :]
    nt = (((1,), (1,)), ((), ()))
    moves = lambda: [copy_to(stats, stats_land.at[i], sems, i, peer) for i, peer in enumerate(peers)]

    @at_step(0)
    def _():
        greet(peers)
        squares[...] = jnp.zeros_like(squares)
        inners[...] = jnp.zeros_like(inners)

    @pl.when(step < tiles)
    def _():
        s_high, s_low = split2(early_ref[...])
        s2 = jnp.concatenate([s_high, s_low], 0)
        spread = spread_ref[...]
        skip = vec_ref[0:1, :]
        for at in range(0, tokens, Q):
            rows = slice(at, at + Q)
            c_blk = c_ref[rows, :]
            carried = mm(jnp.concatenate([c_blk, c_blk], 1), s2) * mm(grow_ref[rows, :], spread)
            y = y0_ref[rows, :] + carried + skip * x_ref[rows, :].astype(F32)
            raw, gm = graw_ref[rows, :], gm_ref[rows, :]
            y_ref[rows, :] = y
            y_vm[step, rows, :] = y
            graw_vm[step, rows, :] = raw
            gm_vm[step, rows, :] = gm
            gated = y * raw * sigmoid(raw)
            square = gated * gated
            inner = gm * gain * gated
            squares[rows, :] += square[:, 0:128] + square[:, 128:256]
            inners[rows, :] += inner[:, 0:128] + inner[:, 128:256]

    @at_step(tiles - 1)
    def _():
        ones = jnp.ones((8, 128), F32)
        square_row = lax.dot_general(ones, squares[...], nt, precision=HIGHEST, preferred_element_type=F32)
        inner_row = lax.dot_general(ones, inners[...], nt, precision=HIGHEST, preferred_element_type=F32)
        stats[...] = jnp.where(iota2(square_row.shape, 0) == 0, square_row, inner_row)
        for move in moves():
            move.start()
        for move in moves():
            move.wait_recv()
        total = stats[...]
        for i in range(group - 1):
            total = total + stats_land[i]
        wide = jnp.concatenate([total, jnp.zeros((120, tokens), F32)], 0)
        stats_col[...] = wide.T

    @pl.when((step >= tiles) & (step < 2 * tiles))
    def _():
        tile = step - tiles
        gain_sum = jnp.zeros((1, TILE), F32)
        skip_sum = jnp.zeros((1, TILE), F32)
        for at in range(0, tokens, Q):
            rows = slice(at, at + Q)
            inv = lax.rsqrt(stats_col[rows, 0:1] * (1.0 / inner_channels) + EPSILON)
            pull = inv * inv * inv * (stats_col[rows, 1:2] * (1.0 / inner_channels))
            raw, y, gm = graw_vm[tile, rows, :], y_vm[tile, rows, :], gm_vm[tile, rows, :]
            sig = sigmoid(raw)
            act = raw * sig
            gated = y * act
            unit = gated * inv
            mixed_ref[rows, :] = (unit * gain).astype(BF)
            gain_sum = gain_sum + jnp.sum(gm * unit, axis=0, keepdims=True)
            grad_gated = inv * (gm * gain) - gated * pull
            dy = grad_gated * act
            dy_ref[rows, :] = dy
            y_vm[tile, rows, :] = dy
            gg_ref[rows, :] = (grad_gated * y * (sig * (1.0 + raw * (1.0 - sig)))).astype(BF)
            skip_sum = skip_sum + jnp.sum(dy * x_ref[rows, :].astype(F32), axis=0, keepdims=True)
        sums_ref[...] = jnp.zeros_like(sums_ref)
        sums_ref[0:1, :] = gain_sum
        sums_ref[1:2, :] = skip_sum

    @pl.when(step == 2 * tiles)
    def _():
        for move in moves():
            move.wait_send()
        held[...] = jnp.zeros_like(held)

    @pl.when(step >= 2 * tiles)
    def _():
        at = pl.num_programs(0) - 1 - step
        rows = pl.ds(pl.multiple_of(at * Q, Q), Q)
        grad_state_block(y_vm.at[:, rows, :], c_block_ref, cum_ref, spread_all_ref, after_ref, held)
        first_ref[...] = held[...]


def gate_and_mix(cols, inner_channels, y0, graw, gm, act, early, grow, spread, vectors, cum):
    tokens, channels = y0.shape
    blocks = tokens // Q
    tiles, group = channels // TILE, cols // 2
    first = lambda i: jnp.minimum(i, tiles - 1)
    second = lambda i: jnp.clip(i - tiles, 0, tiles - 1)
    either = lambda i: jnp.where(i < 2 * tiles, lax.rem(i, tiles), tiles - 1)
    third = lambda i: blocks - 1 - jnp.maximum(i - 2 * tiles, 0)
    lanes = lambda at, count: pl.BlockSpec((count, TILE), lambda i: (0, at(i)))
    vmem = pltpu.VMEM
    return pl.pallas_call(
        partial(gate_kernel, cols, inner_channels),
        grid=(2 * tiles + blocks,),
        in_specs=[
            lanes(first, tokens), lanes(first, tokens), lanes(first, tokens), lanes(either, tokens),
            lanes(first, N),
            pl.BlockSpec((tokens, N), lambda i: (0, channels // N + 1)),
            whole((tokens, 256)),
            lanes(first, 256),
            lanes(either, 8),
            pl.BlockSpec((Q, 128), lambda i: (third(i), 0)),
            pl.BlockSpec((Q, N), lambda i: (third(i), channels // N + 1)),
            whole((256, channels)),
        ],
        out_specs=[
            lanes(first, tokens), lanes(second, tokens), lanes(second, tokens), lanes(second, tokens),
            lanes(second, 8),
            pl.BlockSpec((1, N, channels), lambda i: (third(i), 0, 0)),
            whole((N, channels)),
        ],
        out_shape=[
            sds((tokens, channels)), sds((tokens, channels), BF), sds((tokens, channels), BF),
            sds((tokens, channels)), sds((8, channels)), sds((blocks, N, channels)), sds((N, channels)),
        ],
        scratch_shapes=[
            vmem((tiles, tokens, TILE), F32), vmem((tiles, tokens, TILE), F32), vmem((tiles, tokens, TILE), F32),
            vmem((tokens, 128), F32), vmem((tokens, 128), F32),
            vmem((8, tokens), F32), vmem((max(group - 1, 1), 8, tokens), F32), vmem((tokens, 128), F32),
            vmem((N, channels), F32),
            pltpu.SemaphoreType.DMA((2, max(group - 1, 1))),
        ],
        compiler_params=remote_params(6),
        cost_estimate=cost(40),
        name="gate_and_mix",
    )(y0, graw, gm, act, early, act, grow, spread, vectors, cum, act, spread)


def conv_back_tile(ga_ref, raw_ref, taps_ref, gv_ref, sums_ref, g_pad):
    tokens, width = ga_ref.shape
    taps = taps_ref[...]
    g_pad[0:HALO, :] = jnp.zeros((HALO, width), F32)
    g_pad[HALO + tokens :, :] = jnp.zeros((HALO, width), F32)
    sums = [jnp.zeros((8, width), F32)] * 5
    by_eight = lambda values: jnp.sum(values.reshape(ROWS // 8, 8, width), axis=0)
    for row in range(0, tokens, ROWS):
        moved = conv_window(raw_ref, row, ROWS)
        pre = conv_rows(moved, taps)
        sig = sigmoid(pre)
        g = ga_ref[row : row + ROWS, :] * (sig * (1.0 + pre * (1.0 - sig)))
        g_pad[HALO + row : HALO + row + ROWS, :] = g
        for k in range(4):
            sums[k] = sums[k] + by_eight(g * moved[k])
        sums[4] = sums[4] + by_eight(g)
    for row in list(range(HALO, HALO + tokens, ROWS)) + [0]:
        size = HALO if row == 0 else ROWS
        window = g_pad[row : row + size + 8, :]
        total = taps[3:4, :] * window[:size, :]
        for k in range(3):
            total = total + taps[k : k + 1, :] * pltpu.roll(window, size + 5 + k, 0)[:size, :]
        gv_ref[row : row + size, :] = total.astype(BF)
    for k in range(5):
        sums_ref[k : k + 1, :] = jnp.sum(sums[k], axis=0, keepdims=True)


SMALL_ROWS = 16
A_TAKEN = 4


def finish_kernel(
    cols, dps, heads, part, whole_state,
    ga_ref, raw_ref, taps_ref, gg_ref, gt_ref, v_ref, g_ref, pick_v_ref, tok_ref, inv_ref, g_own_ref,
    mix_ref, headsum_ref, gain_ref, o_total, g_cross, gbc, normed, gt_hbm, tok, cot,
    tg_out, o_out, g_out, v_out, ext_out, sm_out,
    gv_vm, gv_sib, gs_vm, gs_sib, gt_sib, bc_own, bc_land, g_pad, raw_part, taps_part, g_pad_part,
    n_own, n_sib, o_vm, g_vm, g_land, gn_tile, gn_own, gn_parts, gn_land, gn_halo, halo_land,
    joint_low, rec, tot, z_send, z_land, state_send, state_land, ext, small, small_land, tok_vm, cot_vm, sems, local,
):
    step = pl.program_id(0)
    channels, half = gv_vm.shape[1], n_own.shape[1]
    shard, piece, span = channels // 2, tot.shape[0], gs_vm.shape[1]
    count, width = gn_own.shape
    tokens = bc_own.shape[0]
    tiles, weight_steps, input_steps = channels // TILE, 2, width // TILE
    weight_at = tiles + 1
    input_at = weight_at + weight_steps
    last = input_at + input_steps
    dp, row, col = here()
    group = cols // 2
    place = lax.rem(col, group)
    sibling, mirror = (dp, 1 - row, col), mirror_of(cols)
    col_peer = lambda by: (dp, row, col ^ by)
    peers = [col_peer(by) for by in range(1, group)]
    others = dps - 1
    o_rows = pl.ds(dp * piece_of(o_vm), piece_of(o_vm))
    g_rows = pl.ds(dp * piece, piece)
    cols_a, cols_b = pl.ds(shard, tot.shape[1] - shard), pl.ds(0, shard)
    used = [0]

    def take(size):
        used[0] += size
        return used[0] - size

    def part_at(at):
        return pl.ds(0, span) if whole_state else lanes_at(at, span)

    def to_dp(src_of, dst_of):
        first = take(others)
        return lambda: dp_copies(dps, sems, src_of, dst_of, first)

    def to_all_dp(src, out):
        first = take(max(others, 4))
        return (lambda: hand_out(dps, sems, first, src, out)[0]), (lambda: hand_out(dps, sems, first, src, out)[1])

    def one(src, dst, device):
        at = take(1)
        return lambda: [copy_to(src, dst, sems, at, device)]

    def to_peers(src_of, dst_of):
        first = take(group - 1)
        return lambda: [
            copy_to(src_of(by), dst_of(by), sems, first + by - 1, col_peer(by)) for by in range(1, group)
        ]

    def to_cols(src, dst):
        first = take(cols - 1)
        return lambda: [copy_to(src, dst, sems, first + by - 1, col_peer(by)) for by in range(1, cols)]

    o_moves, o_passed = to_all_dp(o_total, o_out)
    g_moves, g_passed = to_all_dp(g_vm, g_out)
    a_moves = to_dp(lambda to, i: joint_low.at[to, :, cols_a], lambda to, i: rec.at[i, :, cols_a])
    b_moves = to_dp(lambda to, i: joint_low.at[to, :, cols_b], lambda to, i: rec.at[i, :, cols_b])
    v_moves, v_passed = to_all_dp(tot.at[:, cols_b], v_out)
    e_moves, e_passed = to_all_dp(ext, ext_out)
    g_move = one(g_cross, g_land, mirror)
    n_move = one(normed.at[:, lanes_at(1 - row, half)], n_sib, sibling)
    t_move = one(gt_hbm, gt_sib, sibling)
    s_move = one(gs_vm, gs_sib, sibling)
    z_move = one(z_send, z_land, mirror)
    state_moves = to_cols(state_send, state_land.at[col])
    bc_moves = to_peers(lambda by: gbc.at[:, part_at(place ^ by)], lambda by: bc_land.at[by - 1])
    early_rows, late_rows = pl.ds(0, count // 2), pl.ds(count // 2, count - count // 2)
    gn_early = to_peers(lambda by: gn_parts.at[by - 1, early_rows, :], lambda by: gn_land.at[by - 1, early_rows, :])
    gn_late = to_peers(lambda by: gn_parts.at[by - 1, late_rows, :], lambda by: gn_land.at[by - 1, late_rows, :])
    gn_moves = lambda: gn_early() + gn_late()
    tile_first = take(tiles)

    def v_tile(tile):
        lanes = lanes_at(tile, TILE)
        return copy_to(gv_vm.at[:, lanes], gv_sib.at[:, lanes], sems, tile_first + tile, sibling)

    halo_first = take(group)
    halos = lambda: [
        copy_to(gn_halo, halo_land.at[j], sems, halo_first + j, (dp, row, group - 1)) for j in range(group)
    ]
    small_steps = [sibling]
    by = 1
    while by < dps:
        small_steps.append((dp ^ by, row, col))
        by *= 2
    small_first = take(len(small_steps))
    small_move = lambda i: copy_to(small, small_land.at[i], sems, small_first + i, small_steps[i])
    small_cols = to_cols(small, sm_out.at[col])

    def small_next(i):
        move = small_move(i)
        move.wait()
        small[...] += small_land[i]
        if i + 1 < len(small_steps):
            small_move(i + 1).start()

    def start(moves):
        for move in moves:
            move.start()

    def arrive(moves):
        for move in moves:
            move.wait_recv()

    def sent(moves):
        for move in moves:
            move.wait_send()

    load_bc = pltpu.make_async_copy(gbc.at[:, part_at(place)], bc_own, local.at[0])
    load_n = pltpu.make_async_copy(normed.at[:, lanes_at(row, half)], n_own, local.at[1])
    load_o = pltpu.make_async_copy(o_total, o_vm, local.at[2])
    load_tok = pltpu.make_async_copy(tok, tok_vm, local.at[3])
    load_cot = pltpu.make_async_copy(cot, cot_vm, local.at[4])
    store_o = pltpu.make_async_copy(o_vm, o_out.at[o_rows, :], local.at[2])
    store_g = pltpu.make_async_copy(g_vm, g_out.at[g_rows, :], local.at[0])
    store_v = pltpu.make_async_copy(tot.at[:, cols_b], v_out.at[g_rows, :], local.at[1])
    store_e = pltpu.make_async_copy(ext, ext_out.at[g_rows, :], local.at[5])
    store_tg = pltpu.make_async_copy(gn_own, tg_out, local.at[3])
    store_small = pltpu.make_async_copy(small, sm_out.at[col], local.at[6])

    @at_step(0)
    def _():
        load_o.start()
        load_bc.start()
        load_n.start()
        load_tok.start()
        load_cot.start()
        greet([sibling] + [col_peer(by) for by in range(1, cols)] + dp_peers(dps))
        start(bc_moves() + o_moves() + t_move() + n_move() + g_move())
        small[...] = jnp.zeros_like(small)
        small[5:7, 0:channels] = mix_ref[0:2, :]
        small[7:9, 0:128] = headsum_ref[0:2, :]
        load_o.wait()
        store_o.start()

    @pl.when(step < tiles)
    def _():
        lanes = lanes_at(step, TILE)
        conv_back_tile(ga_ref, raw_ref, taps_ref, gv_vm.at[:, lanes], small.at[0:5, lanes], g_pad)
        v_tile(step).start()

    @pl.when(step == tiles - 1)
    def _():
        arrive(o_moves())
        start(o_passed())

    @pl.when(step == tiles)
    def _():
        load_bc.wait()
        arrive(bc_moves())
        for i in range(group - 1):
            bc_own[...] += bc_land[i]
        if whole_state:
            lane = iota2(bc_own.shape, 1)
            mine = (lane >= place * part) & (lane < place * part + part)
            bc_own[...] = jnp.where(mine, bc_own[...], 0.0)
        lanes = part_at(place)
        raw_part[...] = raw_ref[:, lanes]
        taps_part[...] = taps_ref[:, lanes]
        conv_back_tile(bc_own, raw_part, taps_part, gs_vm, small.at[10:15, 0:span], g_pad_part)
        start(s_move())
        arrive(g_move())
        g_vm[...] = g_own_ref[...] + g_land[...].astype(F32)
        start(g_moves())
        store_g.start()

    @pl.when(step == weight_at)
    def _():
        load_n.wait()
        arrive(n_move() + t_move() + s_move() + [v_tile(tile) for tile in range(tiles)])

    def keep(first, size, total):
        for p in range(dps):
            rows = total[p * piece : p * piece + piece, :]
            joint_low[p, :, first : first + size] = rows.astype(BF)

            @pl.when(dp == p)
            def _():
                tot[:, first : first + size] = rows

    @pl.when(step == weight_at)
    def _():
        keep(shard, shard, mm_tn(n_own[...], gv_vm[:, shard:]) + mm_tn(n_sib[...], gv_sib[:, shard:]))
        keep(channels, span, mm_tn(n_own[...], gs_vm[...]) + mm_tn(n_sib[...], gs_sib[...]))
        keep(channels + span, 128, mm_tn(n_own[HALO:, :], gt_ref[...]) + mm_tn(n_sib[HALO:, :], gt_sib[...]))
        start(a_moves())

    @pl.when(step == weight_at + 1)
    def _():
        keep(0, shard, mm_tn(n_own[...], gv_vm[:, :shard]) + mm_tn(n_sib[...], gv_sib[:, :shard]))

    @pl.when(step == input_at)
    def _():
        arrive(g_moves())
        start(g_passed())

    @pl.when(step == input_at + A_TAKEN)
    def _():
        arrive(a_moves())
        start(b_moves())
        for i in range(others):
            tot[:, cols_a] += rec[i, :, cols_a].astype(F32)
        z_send[:, 0:shard] = tot[:, shard:channels].astype(BF)
        z_send[:, shard:] = tot[:, channels + span :].astype(BF)
        state_send[...] = tot[:, channels : channels + span].astype(BF)
        start(z_move() + state_moves())
        state_land[col] = state_send[...]

    @pl.when((step >= input_at) & (step < last))
    def _():
        at = step - input_at
        lanes = lanes_at(at, TILE)
        gn_tile[...] = mm_nt(gv_vm[...], v_ref[...]) + mm_nt(gs_vm[...], pick_v_ref[:, part_at(place)])
        gn_tile[HALO:, :] += mm_nt(gg_ref[...], g_ref[...]) + mm_nt(gt_ref[...], pick_v_ref[:, TILE:])
        rows = lambda index: pl.ds(pl.multiple_of(HALO + index * count, HALO), count)
        gn_own[:, lanes] = gn_tile[rows(place), :]
        for by in range(1, group):
            gn_parts[by - 1, :, lanes] = gn_tile[rows(place ^ by), :].astype(BF)
        gn_halo[:, lanes] = gn_tile[0:HALO, :].astype(BF)
        sums = jnp.zeros((1, TILE), F32)
        for first in [0] + list(range(HALO, HALO + tokens, Q)):
            size = HALO if first == 0 else Q
            unit = tok_ref[first : first + size, :].astype(F32) * inv_ref[first : first + size, 0:1]
            sums = sums + jnp.sum(gn_tile[first : first + size, :] * unit, axis=0, keepdims=True)
        small[9:10, lanes] = sums

    @pl.when(step == last)
    def _():
        start(gn_early())
        for j in range(group):
            pl.when(col == group + j)(halos()[j].start)
        small_move(0).start()
        small_next(0)
        arrive(b_moves())
        for i in range(others):
            tot[:, cols_b] += rec[i, :, cols_b].astype(F32)
        arrive(z_move())
        start(gn_late())
        tot[:, cols_b] += z_land[:, 0:shard].astype(F32)
        start(v_moves())
        store_v.start()
        steps = tot[:, channels + span :] + pltpu.roll(z_land[:, shard:].astype(F32), 128 - heads, 1)
        arrive(state_moves())
        if whole_state:
            ext[:, 0:128] = steps
            ext[:, 128:] = sum(state_land[i].astype(F32) for i in range(cols))
        else:
            states = state_land[col // 2].astype(F32) + state_land[col // 2 + group].astype(F32)
            moved = jnp.where(lax.rem(col, 2) == 1, states, pltpu.roll(states, 64, 1))
            ext[...] = jnp.where(iota2(steps.shape, 1) < 64, steps, moved)
        start(e_moves())
        store_e.start()
        for i in range(1, len(small_steps)):
            small_next(i)
        start(small_cols())
        store_small.start()
        arrive(v_moves())
        start(v_passed())
        arrive(e_moves())
        start(e_passed())
        load_tok.wait()
        load_cot.wait()
        arrive(gn_moves())
        for i in range(group - 1):
            gn_own[...] += gn_land[i].astype(F32)

        @pl.when(col == group - 1)
        def _():
            arrive(halos())
            for j in range(group):
                gn_own[count - HALO :, :] += halo_land[j].astype(F32)

        for j in range(group):
            pl.when(col == group + j)(halos()[j].wait_send)
        for first in range(0, count, ROWS):
            rows = slice(first, first + ROWS)
            values = tok_vm[rows, :].astype(F32)
            inv = lax.rsqrt(jnp.mean(values * values, axis=-1, keepdims=True) + EPSILON)
            unit = values * inv
            pulled = gn_own[rows, :] * gain_ref[0:1, :]
            mean = jnp.mean(pulled * unit, axis=-1, keepdims=True)
            gn_own[rows, :] = cot_vm[rows, :].astype(F32) + inv * (pulled - unit * mean)
        store_tg.start()
        store_o.wait()
        store_g.wait()
        store_small.wait()
        store_v.wait()
        store_e.wait()
        arrive(o_passed() + g_passed() + v_passed() + e_passed() + small_cols())
        sent(o_passed() + g_passed() + v_passed() + e_passed())
        sent(bc_moves() + o_moves() + t_move() + n_move() + g_move() + s_move() + a_moves() + b_moves())
        sent([v_tile(tile) for tile in range(tiles)])
        sent(gn_moves() + z_move() + state_moves() + g_moves() + v_moves() + e_moves() + small_cols())
        store_tg.wait()


def piece_of(ref):
    return ref.shape[0]


def finish(
    cols, dps, heads, part, ga, raw, taps, gg, gt, w_value, w_gate, picked, tokens_in, inv_rms, g_own, mix_sums,
    head_sums, gain, o_total, g_cross, gbc, normed, tokens_own, cotangent,
):
    tokens, channels = ga.shape
    rows, width = normed.shape
    half, shard = width // 2, channels // 2
    whole_state = part % 128 != 0
    span = 2 * N if whole_state else part
    extra = 128 + span if whole_state else 128
    group = cols // 2
    tiles, weight_steps, input_steps = channels // TILE, 2, width // TILE
    piece, wide = g_own.shape[0], channels + span + 128
    count = tokens_own.shape[0]
    input_at = tiles + 1 + weight_steps
    small_steps = dps.bit_length()

    def clamp(first, size):
        return lambda i: jnp.clip(i - first, 0, size - 1)

    conv, both, input_tile = clamp(0, tiles), clamp(0, tiles + 1), clamp(input_at, input_steps)
    lanes = lambda at, size: pl.BlockSpec((size, TILE), lambda i: (0, at(i)))
    slab = lambda at, size: pl.BlockSpec((TILE, size), lambda i: (at(i), 0))
    once = lambda values: pl.BlockSpec(
        values.shape, lambda *_: (0,) * len(values.shape), pipeline_mode=pl.Buffered(1)
    )
    vmem = pltpu.VMEM
    dma = pltpu.SemaphoreType.DMA
    more = max(group - 1, 1)
    copies = 2 * (dps - 1) + 4 * max(dps - 1, 4) + 6 + 2 * (cols - 1) + 3 * (group - 1) + tiles + group + small_steps
    return pl.pallas_call(
        partial(finish_kernel, cols, dps, heads, part, whole_state),
        grid=(input_at + input_steps + 1,),
        in_specs=[
            lanes(conv, tokens),
            lanes(both, rows),
            lanes(both, 8),
            once(gg),
            once(gt),
            slab(input_tile, channels),
            slab(input_tile, channels),
            slab(input_tile, TILE + 128),
            lanes(input_tile, rows),
            once(inv_rms),
            once(g_own),
            once(mix_sums),
            once(head_sums),
            once(gain),
        ] + [ANY] * 7,
        out_specs=[ANY] * 6,
        out_shape=[
            sds((count, width)), sds((dps * o_total.shape[0], o_total.shape[1])), sds((half, shard)),
            sds((half, shard)), sds((half, extra)), sds((cols, SMALL_ROWS, width)),
        ],
        scratch_shapes=[
            vmem((rows, channels), BF), vmem((rows, channels), BF), vmem((rows, span), BF), vmem((rows, span), BF),
            vmem((tokens, 128), BF), vmem((tokens, span), F32), vmem((more, tokens, span), F32),
            vmem((tokens + 2 * HALO, TILE), F32), vmem((rows, span), F32), vmem((8, span), F32),
            vmem((tokens + 2 * HALO, span), F32),
            vmem((rows, half), BF), vmem((rows, half), BF),
            vmem(o_total.shape, F32), vmem(g_own.shape, F32), vmem(g_own.shape, BF),
            vmem((rows, TILE), F32),
            vmem((count, width), F32), vmem((more, count, width), BF), vmem((more, count, width), BF),
            vmem((HALO, width), BF), vmem((group, HALO, width), BF),
            vmem((dps, piece, wide), BF), vmem((dps - 1, piece, wide), BF), vmem((piece, wide), F32),
            vmem((piece, shard + 128), BF), vmem((piece, shard + 128), BF), vmem((piece, span), BF),
            vmem((cols, piece, span), BF), vmem((piece, extra), F32),
            vmem((SMALL_ROWS, width), F32), vmem((small_steps, SMALL_ROWS, width), F32),
            vmem((count, width), BF), vmem((count, width), BF),
            dma((2, copies)),
            dma((7,)),
        ],
        compiler_params=remote_params(5),
        cost_estimate=cost(110),
        name="finish",
    )(
        ga, raw, taps, gg, gt, w_value, w_gate, picked, tokens_in, inv_rms, g_own, mix_sums, head_sums, gain,
        o_total, g_cross, gbc, normed, gt, tokens_own, cotangent,
    )


def flips(size, by):
    return [(i, i ^ by) for i in range(size)]


def butterfly(values, axis):
    size = lax.axis_size(axis)
    by = 1
    while by < size:
        values = values + lax.ppermute(values, axis, flips(size, by))
        by *= 2
    return values


def at_rows(values, index, size):
    return lax.dynamic_slice_in_dim(values, index * size, size, axis=0)


def collect_dp(piece, dp):
    size = lax.axis_size("dp")
    rows = piece.shape[0]
    out = jnp.zeros((size * rows,) + piece.shape[1:], piece.dtype)
    out = lax.dynamic_update_slice_in_dim(out, piece, dp * rows, 0)
    for by in range(1, size):
        other = lax.ppermute(piece, "dp", flips(size, by))
        out = lax.dynamic_update_slice_in_dim(out, other, (dp ^ by) * rows, 0)
    return out


def swap_core(values):
    return lax.ppermute(values, "row", [(0, 1), (1, 0)])


def per_device(
    tokens, norm_gain, w_gate, w_value, w_state, w_step, conv_value, bias_value, conv_state,
    bias_state, a_log, d_skip, dt_bias, mix_gain, w_out, cotangent,
):
    cols, rows_n, dps = lax.axis_size("col"), lax.axis_size("row"), lax.axis_size("dp")
    col, row, dp = lax.axis_index("col"), lax.axis_index("row"), lax.axis_index("dp")
    group = cols // 2
    place = lax.rem(col, group)
    local, width = tokens.shape
    span = local * group
    half_width = width // 2
    shard = w_value.shape[1]
    channels = 2 * shard
    heads = a_log.shape[0]
    inner_channels = shard * cols
    state_all = w_state.shape[1] * cols
    mirror = [(i, cols - 1 - i) for i in range(cols)]
    forth = [(i, cols - 1 - i) for i in range(group)]
    back = [(cols - 1 - i, i) for i in range(group)]

    def ring(by):
        return [(i, (i // group) * group + (i % group + by) % group) for i in range(cols)]

    state_width = w_state.shape[1]
    small = jnp.pad(
        jnp.concatenate([w_state, w_step], axis=1), ((0, 0), (0, 128 - state_width - heads))
    )
    heads_row = jnp.pad(
        jnp.concatenate([d_skip, a_log, dt_bias]), (0, shard - 3 * heads)
    )[None]
    state_rows = jnp.concatenate([conv_state.T, bias_state[None]], axis=0)
    vec = jnp.concatenate(
        [
            conv_value.T, bias_value[None], mix_gain[None], heads_row, jnp.zeros((1, shard), BF),
            jnp.pad(state_rows, ((0, 3), (0, shard - state_width))),
        ],
        axis=0,
    )
    group_tokens, value_full, small_full, vecs = import_all(cols, dps, tokens, w_value, small, vec)
    from_col = lax.broadcasted_iota(jnp.int32, (cols * 128, TILE + 128), 0) // 128
    from_lane = lax.broadcasted_iota(jnp.int32, (cols * 128, TILE + 128), 0) % 128
    to = lax.broadcasted_iota(jnp.int32, (cols * 128, TILE + 128), 1)
    head_to = to - TILE
    is_state = (to < TILE) & (from_lane < state_width) & (from_col * state_width + from_lane == to)
    is_own = (from_col == col) & (head_to < heads) & (from_lane == state_width + head_to)
    is_mirror = (from_col == cols - 1 - col) & (head_to >= heads) & (head_to < 2 * heads)
    is_mirror = is_mirror & (from_lane == state_width + head_to - heads)
    pick = (is_state | ((head_to >= 0) & (is_own | is_mirror))).astype(BF)

    vecs = vecs.astype(F32)
    both = jnp.concatenate(
        [
            lax.dynamic_index_in_dim(vecs, col, 0, keepdims=False),
            lax.dynamic_index_in_dim(vecs, cols - 1 - col, 0, keepdims=False),
        ],
        axis=1,
    )
    state_vecs = jnp.transpose(vecs[:, 8:16, :state_width], (1, 0, 2)).reshape(8, state_all)
    taps = jnp.concatenate([both[0:8], state_vecs], axis=1)

    def both_heads(at):
        return jnp.concatenate(
            [both[6, at * heads : (at + 1) * heads], both[6, shard + at * heads : shard + (at + 1) * heads]]
        )

    skip_both, a_both, dt_both = both_heads(0), both_heads(1), both_heads(2)
    vectors = jnp.concatenate(
        [jnp.repeat(skip_both, HEAD)[None], both[5:6], jnp.zeros((6, channels), F32)], axis=0
    )
    rate = -jnp.exp(a_both)
    head_rows = jnp.pad(jnp.stack([dt_both, rate]), ((0, 6), (0, 128 - 2 * heads)))
    head_of = np.arange(channels) // HEAD
    one_hot = (np.arange(128)[:, None] == head_of[None, :]).astype(np.float32)
    spread = jnp.asarray(np.concatenate([one_hot, one_hot], axis=0), BF)
    gather = jnp.asarray(one_hot.T, BF)

    gain = norm_gain.astype(F32)
    (
        raw, act, normed, step_in, step, cum, grow, offs, inv_rms, picked, states, y0, graw, gm, early,
        group_cot, gate_full, out_full,
    ) = forward_all(
        cols, dps, group_tokens, gain[None], value_full, small_full, pick, taps, head_rows, spread, cotangent,
        w_gate, w_out,
    )
    y, mixed, grad_gate, dy, mix_sums, after, first_grad = gate_and_mix(
        cols, inner_channels, y0, graw, gm, act, early, grow, spread, vectors, cum
    )
    (
        ga, grad_step, gbc, head_sums, out_total, gate_own, gate_cross, branch, branch_in, _, _,
    ) = scan_backward(
        cols, dps, dy, act, y, step, cum, step_in, spread, gather, after, states, early, offs, head_rows, vectors,
        mixed, out_full, grad_gate, first_grad, group_cot, normed,
    )
    block_out = (tokens.astype(F32) + branch + jnp.sum(branch_in.astype(F32), axis=0)).astype(BF)
    state_part = state_all // group

    tokens_grad, sum_out, sum_gate, sum_value, extra, small_sums = finish(
        cols, dps, heads, state_part, ga, raw, taps, grad_gate, grad_step, value_full, gate_full, picked,
        group_tokens, inv_rms, gate_own, mix_sums, head_sums, gain[None], out_total, gate_cross, gbc, normed,
        tokens, cotangent,
    )
    sum_step = extra[:, :heads]
    whole_state = state_part % 128 != 0
    if whole_state:
        sum_state = lax.dynamic_slice_in_dim(extra, 128 + col * state_width, state_width, axis=1)
    else:
        sum_state = extra[:, 64:]
    own_sums = lax.dynamic_index_in_dim(small_sums, col, 0, keepdims=False)
    mirror_sums = lax.dynamic_index_in_dim(small_sums, cols - 1 - col, 0, keepdims=False)
    wide = own_sums[0:7, :shard] + mirror_sums[0:7, shard:channels]
    head_own = own_sums[7:9, :heads] + mirror_sums[7:9, heads : 2 * heads]
    skip_own = jnp.sum(wide[6].reshape(heads, HEAD), axis=1)
    norm_total = small_sums[0, 9]
    for i in range(1, cols):
        norm_total = norm_total + small_sums[i, 9]
    if whole_state:
        state_sums = jnp.sum(small_sums[:, 10:15, :state_all], axis=0)
        state_first = col * state_width
    else:
        half_at = col * state_width // state_part
        state_sums = lax.dynamic_index_in_dim(small_sums, half_at, 0, keepdims=False)[10:15, :state_part]
        state_sums = state_sums + lax.dynamic_index_in_dim(
            small_sums, half_at + group, 0, keepdims=False
        )[10:15, :state_part]
        state_first = lax.rem(col * state_width, state_part)
    state_own = lax.dynamic_slice_in_dim(state_sums, state_first, state_width, axis=1)

    return (
        block_out,
        tokens_grad,
        norm_total,
        sum_gate,
        sum_value,
        sum_state,
        sum_step,
        wide[:4].T,
        wide[4],
        state_own[:4].T,
        state_own[4],
        head_own[0] * rate[:heads],
        skip_own,
        head_own[1],
        wide[5],
        sum_out,
    )


def solution(mesh):
    rows = P(("dp", "row", "col"), None)
    grid = P("row", "col")
    vec = P("col")
    taps = P("col", None)
    return jax.shard_map(
        per_device,
        mesh=mesh,
        in_specs=(
            rows, P(), grid, grid, grid, grid, taps, vec, taps, vec, vec, vec, vec, vec,
            P("col", "row"), rows,
        ),
        out_specs=(
            rows, rows, P(), grid, grid, grid, grid, taps, vec, taps, vec, vec, vec, vec, vec,
            P("col", "row"),
        ),
        check_vma=False,
    )
```

```python
from functools import partial

import jax
import jax.numpy as jnp
import numpy as np
from jax import lax
from jax.experimental import pallas as pl
from jax.experimental.pallas import tpu as pltpu
from jax.sharding import PartitionSpec as P

BF = jnp.bfloat16
F32 = jnp.float32
EPSILON = 1e-05
N = 128
Q = 128
HEAD = 64
HALO = 16
ROWS = 64
TILE = 256
HIGHEST = lax.Precision.HIGHEST
VMEM_LIMIT = 56 * 2**20


def mm(a, b):
    return lax.dot_general(a, b, (((1,), (0,)), ((), ())), preferred_element_type=F32)


def mm_nt(a, b):
    return lax.dot_general(a, b, (((1,), (1,)), ((), ())), preferred_element_type=F32)


def mm_exact(a, b):
    return lax.dot_general(
        a, b, (((1,), (0,)), ((), ())), precision=HIGHEST, preferred_element_type=F32
    )


def split2(values):
    high = values.astype(BF)
    return high, (values - high.astype(F32)).astype(BF)


def sigmoid(values):
    return 1.0 / (1.0 + jnp.exp(-values))


def iota2(shape, axis):
    return lax.broadcasted_iota(jnp.int32, shape, axis)


def params(*names):
    return pltpu.CompilerParams(
        dimension_semantics=names or ("arbitrary",), vmem_limit_bytes=VMEM_LIMIT
    )


def cost(micros):
    return pl.CostEstimate(flops=0, bytes_accessed=int(micros * 3.0e6), transcendentals=0)


def whole(shape):
    return pl.BlockSpec(shape, lambda *_: (0,) * len(shape))


def columns(rows, width=TILE):
    return pl.BlockSpec((rows, width), lambda j: (0, j))


def sds(shape, dtype=F32):
    return jax.ShapeDtypeStruct(shape, dtype)


def here():
    return lax.axis_index("dp"), lax.axis_index("row"), lax.axis_index("col")


def lanes_at(index, size):
    return pl.ds(pl.multiple_of(index * size, 128), size)


def greet(others):
    barrier = pltpu.get_barrier_semaphore()
    for other in others:
        pl.semaphore_signal(barrier, inc=1, device_id=other, device_id_type=pl.DeviceIdType.MESH)
    pl.semaphore_wait(barrier, len(others))


def at_step(step):
    return pl.when(pl.program_id(0) == step)


def copy_to(src, dst, sems, i, device):
    return pltpu.make_async_remote_copy(
        src_ref=src, dst_ref=dst, send_sem=sems.at[0, i], recv_sem=sems.at[1, i],
        device_id=device, device_id_type=pl.DeviceIdType.MESH,
    )


def dp_copies(dps, sems, src_of, dst_of, first=0):
    dp, row, col = here()
    return [
        copy_to(src_of(dp ^ by, by - 1), dst_of(dp ^ by, by - 1), sems, first + by - 1, (dp ^ by, row, col))
        for by in range(1, dps)
    ]


def hand_out(dps, sems, first, src, out):
    dp, row, col = here()
    piece, lanes = src.shape
    rows = lambda d: pl.ds(d * piece, piece)
    if dps != 4:
        return dp_copies(dps, sems, lambda to, i: src, lambda to, i: out.at[rows(dp), :], first), []
    near = [
        copy_to(src, out.at[rows(dp), :], sems, first + i, (dp ^ by, row, col)) for i, by in enumerate((1, 2))
    ]
    far = []
    for i, by in enumerate((1, 2)):
        passed = out.at[pl.ds((dp ^ by) * piece + i * (piece // 2), piece // 2), :]
        far.append(copy_to(passed, passed, sems, first + 2 + i, (dp ^ 3 ^ by, row, col)))
    return near, far


def dp_peers(dps):
    dp, row, col = here()
    return [(dp ^ by, row, col) for by in range(1, dps)]


def mirror_of(cols):
    dp, row, col = here()
    return (dp, row, cols - 1 - col)


def remote_params(collective_id):
    return pltpu.CompilerParams(
        dimension_semantics=("arbitrary",), vmem_limit_bytes=VMEM_LIMIT, collective_id=collective_id,
        has_side_effects=True,
    )


ANY = pl.BlockSpec(memory_space=pl.ANY)


def import_kernel(
    cols, dps, tok, wv, sw, vec, tg, vf, sf, vecs, zeros, tok_vm, w_vm, s_vm, vec_vm, local, send, recv,
):
    dp, row, col = here()
    group = cols // 2
    place = lax.rem(col, group)
    half, shard = wv.shape
    count = tok.shape[0]
    piece = half // dps
    sibling = (dp, 1 - row, col)
    mirror = (dp, row, cols - 1 - col)
    col_peer = lambda by: (dp, row, col ^ by)
    dp_peer = lambda by: (dp ^ by, row, col)
    greet(
        [sibling]
        + [col_peer(by) for by in range(1, cols)]
        + [dp_peer(by) for by in range(1, dps)]
    )
    used = [0]
    started = []

    def remote(src, dst, device):
        i = used[0]
        used[0] += 1
        return pltpu.make_async_remote_copy(
            src_ref=src, dst_ref=dst, send_sem=send.at[i], recv_sem=recv.at[i],
            device_id=device, device_id_type=pl.DeviceIdType.MESH,
        )

    def launch(src, dst, device):
        copy = remote(src, dst, device)
        copy.start()
        started.append(copy)
        return copy

    def keep(i, src, dst):
        copy = pltpu.make_async_copy(src, dst, local.at[i])
        copy.start()
        return copy

    my_rows = pl.ds(row * half, half)
    my_piece = pl.ds(row * half + dp * piece, piece)
    own, other = pl.ds(0, shard), pl.ds(shard, shard)
    src_piece = pl.ds(dp * piece, piece)

    staged = [
        keep(6, vec, vec_vm),
        keep(0, sw.at[src_piece, :], s_vm),
        keep(2, tok, tok_vm),
        keep(3, wv, w_vm),
    ]
    s_cross = [
        launch(sw.at[src_piece, :], sf.at[my_piece, lanes_at(col, 128)], col_peer(by))
        for by in range(1, cols)
    ]
    v_cross = launch(wv.at[src_piece, :], vf.at[my_piece, other], mirror)
    vec_cross = [launch(vec, vecs.at[col], col_peer(by)) for by in range(1, cols)]
    my_tokens = tg.at[pl.ds(HALO + place * count, count), :]
    tok_cross = [launch(tok, my_tokens, col_peer(by)) for by in range(1, group)]
    halo_src = tok.at[pl.ds(count - HALO, HALO), :]
    halo_dst = tg.at[pl.ds(0, HALO), :]
    halo_at = used[0]
    used[0] += group
    halos = [
        pltpu.make_async_remote_copy(
            src_ref=halo_src, dst_ref=halo_dst, send_sem=send.at[halo_at + j], recv_sem=recv.at[halo_at],
            device_id=(dp, row, group + j), device_id_type=pl.DeviceIdType.MESH,
        )
        for j in range(group)
    ]

    @pl.when(col == group - 1)
    def _():
        for copy in halos:
            copy.start()

    zeros[...] = jnp.zeros_like(zeros)

    @pl.when(col < group)
    def _():
        clear = pltpu.make_async_copy(zeros, halo_dst, local.at[1])
        clear.start()
        clear.wait()

    v_own = launch(wv, vf.at[my_rows, own], sibling)
    for copy in staged:
        copy.wait()
    small_own = keep(0, s_vm, sf.at[my_piece, lanes_at(col, 128)])
    kept = [
        keep(6, vec_vm, vecs.at[col]),
        keep(2, tok_vm, my_tokens),
        keep(3, w_vm, vf.at[my_rows, own]),
    ]

    def spread_out(ref):
        return [launch(ref, ref, dp_peer(by)) for by in range(1, dps)]

    def arrive(copies):
        for copy in copies:
            copy.wait_recv()

    arrive(s_cross)
    small_own.wait()
    s_dp = spread_out(sf.at[my_piece, :])
    arrive([v_cross])
    v_dp = spread_out(vf.at[my_piece, other])
    arrive(s_dp)
    last = [launch(sf.at[my_rows, :], sf.at[my_rows, :], sibling)]
    arrive(v_dp)
    last += [launch(vf.at[my_rows, other], vf.at[my_rows, other], sibling)]
    arrive(last)
    arrive([v_own])
    arrive(vec_cross)
    arrive(tok_cross)

    @pl.when(col >= group)
    def _():
        halos[0].wait_recv()

    @pl.when(col == group - 1)
    def _():
        for copy in halos:
            copy.wait_send()

    for copy in kept:
        copy.wait()
    for copy in started:
        copy.wait_send()


def import_all(cols, dps, tokens, w_value, small, vec):
    half, shard = w_value.shape
    count, width = tokens.shape
    any_spec = pl.BlockSpec(memory_space=pl.ANY)
    copies = 1 + 2 * (cols - 1) + (cols // 2 - 1) + cols // 2 + 1 + 2 * (dps - 1) + 2
    return pl.pallas_call(
        partial(import_kernel, cols, dps),
        in_specs=[any_spec] * 4,
        out_specs=[any_spec] * 4,
        out_shape=[
            sds((HALO + count * (cols // 2), width), BF),
            sds((2 * half, 2 * shard), BF),
            sds((2 * half, cols * 128), BF),
            sds((cols,) + vec.shape, BF),
        ],
        scratch_shapes=[
            pltpu.VMEM((HALO, width), BF),
            pltpu.VMEM((count, width), BF),
            pltpu.VMEM((half, shard), BF),
            pltpu.VMEM((half // dps, 128), BF),
            pltpu.VMEM(vec.shape, BF),
            pltpu.SemaphoreType.DMA((7,)),
            pltpu.SemaphoreType.DMA((copies,)),
            pltpu.SemaphoreType.DMA((copies,)),
        ],
        compiler_params=pltpu.CompilerParams(
            collective_id=1, has_side_effects=True, vmem_limit_bytes=VMEM_LIMIT
        ),
        cost_estimate=cost(45),
        name="import_all",
    )(tokens, w_value, small, vec)


def conv_window(raw_ref, start, size):
    window = raw_ref[HALO + start - 8 : HALO + start + size, :]
    return [pltpu.roll(window, 3 - k, 0)[8:, :] for k in range(3)] + [window[8:, :]]


def conv_rows(moved, taps):
    total = taps[4:5, :] + taps[0:1, :] * moved[0]
    for k in range(1, 4):
        total = total + taps[k : k + 1, :] * moved[k]
    return total


def normalize(tok_ref, gain_ref, normed_ref, inv_ref):
    tokens = tok_ref.shape[0] - HALO
    for at in [0] + list(range(HALO, HALO + tokens, Q)):
        size = HALO if at == 0 else Q
        values = tok_ref[at : at + size, :].astype(F32)
        inv = lax.rsqrt(jnp.mean(values * values, axis=-1, keepdims=True) + EPSILON)
        normed_ref[at : at + size, :] = (values * inv * gain_ref[0:1, :]).astype(BF)
        inv_ref[at : at + size, :] = jnp.broadcast_to(inv, (size, 128))


def project_steps(
    small_ref, pick_ref, head_ref, normed_ref, raw_ref, stepin_ref, step_ref, cum_ref, grow_ref, offs_ref,
    picked_ref,
):
    tokens = step_ref.shape[0]
    picked = mm(small_ref[...], pick_ref[...]).astype(BF)
    picked_ref[...] = picked
    raw_ref[...] = mm(normed_ref[...], picked[:, :TILE])
    step_in = mm(normed_ref[HALO:, :], picked[:, TILE:]) + head_ref[0:1, :]
    small = jnp.exp(-jnp.abs(step_in))
    plus = 1.0 + small
    safe = jnp.where(plus == 1.0, 1.0, plus - 1.0)
    log_part = jnp.where(plus == 1.0, small, jnp.log(plus) * (small / safe))
    step = jnp.maximum(step_in, 0.0) + log_part
    stepin_ref[...] = step_in
    step_ref[...] = step
    falls = step * head_ref[1:2, :]
    lower = (iota2((Q, Q), 0) >= iota2((Q, Q), 1)).astype(F32)
    before = jnp.zeros((1, 128), F32)
    offs_ref[...] = jnp.zeros_like(offs_ref)
    for b in range(tokens // Q):
        rows = slice(b * Q, b * Q + Q)
        cum = mm_exact(lower, falls[rows, :])
        cum_ref[rows, :] = cum
        high, low = split2(jnp.exp(cum + before))
        grow_ref[rows, 0:128] = high
        grow_ref[rows, 128:256] = low
        before = before + cum[Q - 1 : Q, :]
        offs_ref[b + 1 : b + 2, :] = before


def activate(raw_ref, taps, act_ref, copy_ref):
    tokens = act_ref.shape[0]
    for at in range(0, tokens, ROWS):
        pre = conv_rows(conv_window(raw_ref, at, ROWS), taps)
        act = (pre * sigmoid(pre)).astype(BF)
        act_ref[at : at + ROWS, :] = act
        copy_ref[at : at + ROWS, :] = act


def expand(per_head, spread):
    high, low = split2(per_head)
    return mm(jnp.concatenate([high, low], 1), spread)


def transpose_bf(values):
    return values.astype(F32).T.astype(BF)


def expand_rows(per_head, spread):
    high, low = split2(jnp.concatenate(per_head, 0))
    return mm(jnp.concatenate([high, low], 1), spread)


def eight(row):
    return jnp.broadcast_to(row, (8, row.shape[1]))


def spans(total, size):
    size = min(size, total)
    return [slice(at, at + size) for at in range(0, total, size)]


def state_block(x_ref, b_ref, step_ref, cum_ref, spread_ref, held):
    cum = cum_ref[...]
    end = cum[Q - 1 : Q, :]
    tail = jnp.exp(end - cum) * step_ref[...]
    b_t = transpose_bf(b_ref[...])
    b_t2 = jnp.concatenate([b_t, b_t], 1)
    for lanes in spans(x_ref.shape[1], 1536):
        wide = expand_rows([tail, eight(jnp.exp(end))], spread_ref[:, lanes])
        high, low = split2(wide[:Q] * x_ref[:, lanes].astype(F32))
        fresh = mm(b_t2, jnp.concatenate([high, low], 0))
        held[:, lanes] = held[:, lanes] * wide[Q : Q + 1, :] + fresh


def forward_block(x_ref, b_ref, c_ref, step_ref, cum_ref, spread_ref, state_ref, y_ref):
    b_blk, c_blk = b_ref[...], c_ref[...]
    affinity = mm_nt(c_blk, b_blk)
    causal = iota2((Q, Q), 0) >= iota2((Q, Q), 1)
    first = iota2((Q, 128), 1) < HEAD
    cum = cum_ref[...]
    cum_t = cum.T
    step_t = step_ref[...].T
    growth = jnp.exp(cum)
    c2 = jnp.concatenate([c_blk, c_blk], 1)
    zero = jnp.zeros((Q, 128), BF)
    for lanes in spans(x_ref.shape[1], 1536):
        s_high, s_low = split2(state_ref[0, :, lanes])
        reached = mm(c2, jnp.concatenate([s_high, s_low], 0)) * expand_rows([growth], spread_ref[:, lanes])
        for at in range(lanes.start, lanes.stop, 128):
            x_pair = x_ref[:, at : at + 128]
            x0, x1 = jnp.where(first, x_pair, zero), jnp.where(first, zero, x_pair)
            pieces = []
            for half in range(2):
                h = at // HEAD + half
                spread_h = cum[:, h : h + 1] - cum_t[h : h + 1, :]
                decay = jnp.exp(jnp.where(causal, spread_h, -1e30))
                pieces += split2(affinity * decay * step_t[h : h + 1, :])
            intra = mm(jnp.concatenate(pieces, 1), jnp.concatenate([x0, x0, x1, x1], 0))
            inside = at - lanes.start
            y_ref[:, at : at + 128] = intra + reached[:, inside : inside + 128]


def forward_all_kernel(
    cols, dps,
    tok_ref, gain_ref, w_ref, small_ref, pick_ref, taps_ref, head_ref, spread_ref, cot, wg, wo,
    raw_ref, act_ref, normed_ref, stepin_ref, step_ref, cum_ref, grow_ref, offs_ref, inv_ref, picked_ref,
    states_ref, y_ref, graw_ref, gm_ref, early_ref, cot_out, gf, of,
    act_vm, states_vm, held, early_land, cot_vm, g_tiles, o_tiles, wg_vm, wo_vm, sems, local,
):
    step = pl.program_id(0)
    tokens, channels = states_vm.shape[0] * Q, held.shape[1]
    blocks = states_vm.shape[0]
    tiles = channels // TILE
    scan_at = tiles + 1
    out_at = scan_at + blocks
    gate_at = out_at + blocks
    dp, row, col = here()
    group = cols // 2
    place = lax.rem(col, group)
    half, shard = wg.shape
    count = cot.shape[0]
    others = dps - 1
    piece, piece_out = half // dps, wo.shape[0] // dps
    sibling, mirror = (dp, 1 - row, col), mirror_of(cols)
    peers = [(dp, row, col ^ by) for by in range(1, group)]
    my_rows = pl.ds(row * half, half)
    my_piece = pl.ds(row * half + dp * piece, piece)
    out_piece = pl.ds(shard + dp * piece_out, piece_out)
    my_lanes = lanes_at(row, half)
    own, other = pl.ds(0, shard), pl.ds(shard, shard)
    src_piece, src_out = pl.ds(dp * piece, piece), pl.ds(dp * piece_out, piece_out)
    my_cot = cot_vm.at[pl.ds(place * count, count), :]

    g_cross = lambda: copy_to(wg.at[src_piece, :], gf.at[my_piece, other], sems, 0, mirror)
    o_cross = lambda: copy_to(wo.at[src_out, :], of.at[out_piece, my_lanes], sems, 1, mirror)
    g_own = lambda: copy_to(wg, gf.at[my_rows, own], sems, 2, sibling)
    o_own = lambda: copy_to(wo, of.at[own, my_lanes], sems, 3, sibling)
    g_rest = lambda: copy_to(gf.at[my_rows, other], gf.at[my_rows, other], sems, 4, sibling)
    o_rest = lambda: copy_to(of.at[other, my_lanes], of.at[other, my_lanes], sems, 5, sibling)
    early_moves = lambda: [
        copy_to(held.at[:, own], early_land.at[:, other], sems, 6, mirror),
        copy_to(held.at[:, other], early_land.at[:, own], sems, 7, mirror),
    ]
    cot_moves = lambda: [copy_to(cot, my_cot, sems, 8 + i, peer) for i, peer in enumerate(peers)]
    first = 8 + group - 1

    def g_dp():
        ref = gf.at[my_piece, other]
        return dp_copies(dps, sems, lambda to, i: ref, lambda to, i: ref, first)

    def o_dp():
        ref = of.at[out_piece, my_lanes]
        return dp_copies(dps, sems, lambda to, i: ref, lambda to, i: ref, first + others)

    load_cot = pltpu.make_async_copy(cot, my_cot, local.at[0])
    load_g = pltpu.make_async_copy(wg, wg_vm, local.at[1])
    load_o = pltpu.make_async_copy(wo, wo_vm, local.at[2])
    store_g = pltpu.make_async_copy(wg_vm, gf.at[my_rows, own], local.at[1])
    store_o = pltpu.make_async_copy(wo_vm, of.at[own, my_lanes], local.at[2])
    store_cot = pltpu.make_async_copy(cot_vm, cot_out, local.at[0])

    def g_tile(at):
        return pltpu.make_async_copy(gf.at[:, lanes_at(at, TILE)], g_tiles.at[lax.rem(at, 2)], local.at[3])

    def o_tile(at):
        rows = pl.ds(pl.multiple_of(at * TILE, TILE), TILE)
        return pltpu.make_async_copy(of.at[rows, :], o_tiles.at[lax.rem(at, 2)], local.at[4])

    @at_step(0)
    def _():
        load_cot.start()
        load_g.start()
        load_o.start()
        greet([sibling, mirror] + peers + dp_peers(dps))
        for move in [g_cross(), o_cross(), g_own(), o_own()]:
            move.start()
        normalize(tok_ref, gain_ref, normed_ref, inv_ref)

    @at_step(1)
    def _():
        load_g.wait()
        store_g.start()
        load_o.wait()
        store_o.start()

    @at_step(tiles - 2)
    def _():
        for move in cot_moves():
            move.start()

    @at_step(scan_at + 2)
    def _():
        g_cross().wait_recv()
        for move in g_dp():
            move.start()

    @at_step(out_at)
    def _():
        o_cross().wait_recv()
        for move in o_dp():
            move.start()

    @at_step(out_at + blocks // 2)
    def _():
        for move in g_dp():
            move.wait_recv()
        g_rest().start()

    @at_step(gate_at + tiles // 2)
    def _():
        for move in o_dp():
            move.wait_recv()
        o_rest().start()

    @at_step(out_at)
    def _():
        @pl.when(col < group)
        def _():
            for move in early_moves():
                move.start()

    @pl.when(step < tiles)
    def _():
        raw_ref[...] = mm(normed_ref[...], w_ref[...])

    @pl.when(step == tiles)
    def _():
        project_steps(
            small_ref, pick_ref, head_ref, normed_ref, raw_ref, stepin_ref, step_ref, cum_ref, grow_ref, offs_ref,
            picked_ref,
        )

    @pl.when(step <= tiles)
    def _():
        activate(raw_ref, taps_ref[...], act_ref, act_vm.at[:, lanes_at(step, TILE)])

    def block_refs(at):
        rows = pl.ds(pl.multiple_of(at * Q, Q), Q)
        return (
            act_vm.at[rows, pl.ds(0, channels)], act_vm.at[rows, pl.ds(channels, N)],
            act_vm.at[rows, pl.ds(channels + N, N)], step_ref.at[rows, :], cum_ref.at[rows, :],
        )

    @pl.when(step == scan_at)
    def _():
        held[...] = jnp.zeros_like(held)

    @pl.when((step >= scan_at) & (step < out_at))
    def _():
        x_blk, b_blk, _, step_blk, cum_blk = block_refs(step - scan_at)
        states_ref[0] = held[...]
        states_vm[step - scan_at] = held[...]
        state_block(x_blk, b_blk, step_blk, cum_blk, spread_ref, held)

    @pl.when(step == out_at)
    def _():
        states_ref[0] = held[...]

    @pl.when((step >= out_at) & (step < gate_at))
    def _():
        x_blk, b_blk, c_blk, step_blk, cum_blk = block_refs(step - out_at)
        forward_block(
            x_blk, b_blk, c_blk, step_blk, cum_blk, spread_ref, states_vm.at[pl.ds(step - out_at, 1)], y_ref
        )

    @pl.when(step == gate_at)
    def _():
        for move in [g_own(), g_rest()]:
            move.wait_recv()
        store_g.wait()
        g_tile(0).start()

    @pl.when((step >= gate_at) & (step < gate_at + tiles))
    def _():
        at = step - gate_at
        g_tile(at).wait()

        @pl.when(at < tiles - 1)
        def _():
            g_tile(at + 1).start()

        graw_ref[...] = mm(normed_ref[HALO:, :], g_tiles[lax.rem(at, 2)])

    @pl.when(step == gate_at + tiles)
    def _():
        for move in [o_own(), o_rest()] + cot_moves():
            move.wait_recv()
        store_o.wait()
        load_cot.wait()
        store_cot.start()
        o_tile(0).start()

    @pl.when(step >= gate_at + tiles)
    def _():
        at = step - gate_at - tiles
        o_tile(at).wait()

        @pl.when(at < tiles - 1)
        def _():
            o_tile(at + 1).start()

        gm_ref[...] = mm_nt(cot_vm[...], o_tiles[lax.rem(at, 2)])

    @at_step(pl.num_programs(0) - 1)
    def _():
        store_cot.wait()
        for move in [g_cross(), o_cross(), g_own(), o_own(), g_rest(), o_rest()] + cot_moves() + g_dp() + o_dp():
            move.wait_send()

        @pl.when(col < group)
        def _():
            for move in early_moves():
                move.wait_send()
            early_ref[...] = jnp.zeros_like(early_ref)

        @pl.when(col >= group)
        def _():
            for move in early_moves():
                move.wait_recv()
            early_ref[...] = early_land[...]


def forward_all(cols, dps, group_tokens, gain, weights, small, pick, taps, head_rows, spread, cotangent, w_gate, w_out):
    rows, width = group_tokens.shape
    tokens = rows - HALO
    channels = weights.shape[1]
    total = channels + TILE
    blocks, tiles = tokens // Q, channels // TILE
    half, shard = w_gate.shape
    scan_at = tiles + 1
    out_at = scan_at + blocks
    gate_at = out_at + blocks

    def clamp(first, count):
        return lambda i: jnp.clip(i - first, 0, count - 1)

    lanes = lambda at, count: pl.BlockSpec((count, TILE), lambda i: (0, at(i)))
    both, value_at = clamp(0, tiles + 1), clamp(0, tiles)
    state_at, y_at = clamp(scan_at, blocks + 1), clamp(out_at, blocks)
    raw_tile, gm_tile = clamp(gate_at, tiles), clamp(gate_at + tiles, tiles)
    vmem = pltpu.VMEM
    return pl.pallas_call(
        partial(forward_all_kernel, cols, dps),
        grid=(gate_at + 2 * tiles,),
        in_specs=[
            whole((rows, width)),
            whole((1, width)),
            lanes(value_at, width),
            whole(small.shape),
            whole(pick.shape),
            lanes(both, 8),
            whole((8, 128)),
            whole(spread.shape),
            ANY, ANY, ANY,
        ],
        out_specs=[
            lanes(both, rows),
            lanes(both, tokens),
            whole((rows, width)),
            whole((tokens, 128)),
            whole((tokens, 128)),
            whole((tokens, 128)),
            whole((tokens, 256)),
            whole((16, 128)),
            whole((rows, 128)),
            whole((width, TILE + 128)),
            pl.BlockSpec((1, N, channels), lambda i: (state_at(i), 0, 0)),
            pl.BlockSpec((Q, channels), lambda i: (y_at(i), 0)),
            lanes(raw_tile, tokens),
            lanes(gm_tile, tokens),
            whole((N, channels)),
            ANY, ANY, ANY,
        ],
        out_shape=[
            sds((rows, total)),
            sds((tokens, total), BF),
            sds((rows, width), BF),
            sds((tokens, 128)),
            sds((tokens, 128)),
            sds((tokens, 128)),
            sds((tokens, 256), BF),
            sds((16, 128)),
            sds((rows, 128)),
            sds((width, TILE + 128), BF),
            sds((blocks + 1, N, channels)),
            sds((tokens, channels)),
            sds((tokens, channels)),
            sds((tokens, channels)),
            sds((N, channels)),
            sds((tokens, width), BF),
            sds((width, channels), BF),
            sds((channels, width), BF),
        ],
        scratch_shapes=[
            vmem((tokens, total), BF),
            vmem((blocks, N, channels), F32),
            vmem((N, channels), F32),
            vmem((N, channels), F32),
            vmem((tokens, width), BF),
            vmem((2, width, TILE), BF),
            vmem((2, TILE, width), BF),
            vmem((half, shard), BF),
            vmem((shard, half), BF),
            pltpu.SemaphoreType.DMA((2, 7 + cols // 2 + 2 * (dps - 1))),
            pltpu.SemaphoreType.DMA((5,)),
        ],
        compiler_params=remote_params(4),
        cost_estimate=cost(70),
        name="forward_all",
    )(group_tokens, gain, weights, small, pick, taps, head_rows, spread, cotangent, w_gate, w_out)


def grad_state_block(dy_tiles, c_ref, cum_ref, spread_ref, after_ref, held):
    after_ref[0] = held[...]
    growth = jnp.exp(cum_ref[...])
    c_t = transpose_bf(c_ref[...])
    c_t2 = jnp.concatenate([c_t, c_t], 1)
    wide = expand_rows([growth], spread_ref[...])
    for tile in range(held.shape[1] // TILE):
        lanes = slice(tile * TILE, tile * TILE + TILE)
        high, low = split2(dy_tiles[tile] * wide[:, lanes])
        direct = mm(c_t2, jnp.concatenate([high, low], 0))
        held[:, lanes] = held[:, lanes] * wide[Q - 1 : Q, lanes] + direct


def near_block(
    at_block, here_rows, dy_ref, x_ref, b_ref, c_ref, step_ref, cum_ref, spread_ref, state_ref, early_ref,
    offs_ref, gx_ref, gbc_ref,
):
    b_blk, c_blk = b_ref[...], c_ref[...]
    affinity_t = mm_nt(b_blk, c_blk)
    causal_t = iota2((Q, Q), 1) >= iota2((Q, Q), 0)
    first = iota2((Q, 128), 1) < HEAD
    cum = cum_ref[...]
    cum_t = cum.T
    step = step_ref[...]
    growth = jnp.exp(cum)
    early_fall = eight(jnp.exp(offs_ref[pl.ds(at_block, 1), :]))
    zero = jnp.zeros((Q, 128), BF)
    grad_affinity_t = jnp.zeros((Q, Q), F32)
    grad_c = jnp.zeros((Q, N), F32)
    for lanes in spans(x_ref.shape[1], 768):
        wide = expand_rows([growth, early_fall], spread_ref[:, lanes])
        before = state_ref[0, :, lanes] + wide[Q : Q + 1, :] * early_ref[:, lanes]
        dy_wide = dy_ref[:, lanes]
        s_high, s_low = split2(before)
        g_high, g_low = split2(dy_wide * wide[:Q])
        grad_c = grad_c + mm_nt(
            jnp.concatenate([g_high, g_low, g_high], 1), jnp.concatenate([s_high, s_high, s_low], 1)
        )
        for at in range(lanes.start, lanes.stop, 128):
            d_high, d_low = split2(dy_ref[:, at : at + 128])
            x_pair = x_ref[:, at : at + 128]
            x0, x1 = jnp.where(first, x_pair, zero), jnp.where(first, zero, x_pair)
            grad_mixing = mm_nt(
                jnp.concatenate([jnp.concatenate([x0, x0], 1), jnp.concatenate([x1, x1], 1)], 0),
                jnp.concatenate([d_high, d_low], 1),
            )
            left, right = [], []
            for half in range(2):
                h = at // HEAD + half
                spread_h = cum_t[h : h + 1, :] - cum[:, h : h + 1]
                decay = jnp.exp(jnp.where(causal_t, spread_h, -1e30))
                m_high, m_low = split2(affinity_t * decay)
                grad_affinity_t = grad_affinity_t + (
                    grad_mixing[half * Q : half * Q + Q, :] * decay * step[:, h : h + 1]
                )
                keep = first if half == 0 else jnp.logical_not(first)
                dh, dl = jnp.where(keep, d_high, zero), jnp.where(keep, d_low, zero)
                left += [m_high, m_low, m_high]
                right += [dh, dh, dl]
            gx_ref[here_rows, at : at + 128] = mm(jnp.concatenate(left, 1), jnp.concatenate(right, 0))
    a_high, a_low = split2(grad_affinity_t)
    gbc_ref[here_rows, 0:N] = mm(jnp.concatenate([a_high, a_low], 1), jnp.concatenate([c_blk, c_blk], 0))
    t_high, t_low = split2(grad_affinity_t.T)
    gbc_ref[here_rows, N : 2 * N] = grad_c + mm(
        jnp.concatenate([t_high, t_low], 1), jnp.concatenate([b_blk, b_blk], 0)
    )


def far_block(
    blocks, at_block, here_rows, dy_ref, x_ref, y_ref, gx_ref, b_ref, step_ref, cum_ref, stepin_ref, spread_ref,
    gather_ref, after_ref, late_ref, state_ref, early_ref, offs_ref, head_ref, skip_ref, gbc_ref,
    ga_ref, gstep_ref, gbc_out_ref, sums_ref,
):
    b_blk = b_ref[...]
    b2 = jnp.concatenate([b_blk, b_blk], 1)
    cum, step = cum_ref[...], step_ref[...]
    tail = jnp.exp(cum[Q - 1 : Q, :] - cum)
    offs_after = offs_ref[pl.ds(at_block + 1, 1), :]
    late_fall = eight(jnp.exp(offs_ref[pl.ds(blocks, 1), :] - offs_after))
    early_fall = eight(jnp.exp(offs_after))
    dots = jnp.zeros((2 * Q + 8, 128), F32)
    grad_b = gbc_ref[here_rows, 0:N]
    for lanes in spans(x_ref.shape[1], 512):
        wide = expand_rows([tail, step, late_fall, early_fall], spread_ref[:, lanes])
        tail_wide, step_wide = wide[:Q], wide[Q : 2 * Q]
        x = x_ref[:, lanes].astype(F32)
        dy = dy_ref[:, lanes]
        skip = skip_ref[0:1, lanes]
        d_state = after_ref[0, :, lanes] + wide[2 * Q : 2 * Q + 1, :] * late_ref[:, lanes]
        state = state_ref[0, :, lanes] + wide[2 * Q + 8 : 2 * Q + 9, :] * early_ref[:, lanes]
        touch = eight(jnp.sum(d_state * state, axis=0, keepdims=True))
        s_high, s_low = split2(d_state)
        gx = gx_ref[here_rows, lanes] + tail_wide * mm(b2, jnp.concatenate([s_high, s_low], 0))
        w_high, w_low = split2(tail_wide * step_wide * x)
        grad_b = grad_b + mm_nt(
            jnp.concatenate([w_high, w_low, w_high], 1), jnp.concatenate([s_high, s_high, s_low], 1)
        )
        ga_ref[:, lanes] = step_wide * gx + skip * dy
        high, low = split2(jnp.concatenate([dy * (y_ref[:, lanes] - skip * x), x * gx, touch], 0))
        gather = gather_ref[lanes, :]
        dots = dots + mm(jnp.concatenate([high, low], 1), jnp.concatenate([gather, gather], 0))
    row_dots, col_dots, last_add = dots[:Q], dots[Q : 2 * Q], dots[2 * Q :]
    last_row = iota2((Q, 128), 0) == Q - 1
    grad_cum = row_dots - step * col_dots + jnp.where(last_row, last_add[0:1, :], 0.0)
    upper = (iota2((Q, Q), 1) >= iota2((Q, Q), 0)).astype(F32)
    grad_rate = mm_exact(upper, grad_cum)
    grad_step = col_dots + grad_rate * head_ref[1:2, :]
    grad_raw = grad_step * sigmoid(stepin_ref[...])
    gstep_ref[...] = grad_raw.astype(BF)
    sums_ref[0:1, :] += jnp.sum(grad_rate * step, axis=0, keepdims=True)
    sums_ref[1:2, :] += jnp.sum(grad_raw, axis=0, keepdims=True)
    gbc_out_ref[:, 0:N] = grad_b
    gbc_out_ref[:, N : 2 * N] = gbc_ref[here_rows, N : 2 * N]


WEIGHT_TILE = 384


def mm_tn(a, b):
    return lax.dot_general(a, b, (((0,), (0,)), ((), ())), preferred_element_type=F32)


def backward_kernel(
    cols, dps,
    dy_ref, x_ref, y_ref, b_ref, c_ref, step_ref, cum_ref, stepin_ref, spread_ref, gather_ref, after_ref,
    state_ref, early_ref, offs_ref, head_ref, skip_ref, mixed_ref, of_ref, gg_ref,
    first_grad, mixed_hbm, gg_hbm, cot, normed,
    ga_ref, gstep_ref, gbc_out_ref, sums_ref, o_total_ref, g_own_ref, g_cross_ref, branch_ref, branch_in,
    mixed_sib, gg_sib,
    gx_ref, gbc_ref, late_ref, o_low, o_own, o_land, o_cross, o_cross_land, g_low, g_own, g_land, parts,
    c_own, c_sib, n_own, n_sib, m_tiles, gg_tiles, sems, local,
):
    step_at = pl.program_id(0)
    blocks = gx_ref.shape[0] // Q
    dp, row, col = here()
    group = cols // 2
    place = lax.rem(col, group)
    shard, channels = g_own_ref.shape[1], gx_ref.shape[1]
    half = c_own.shape[1]
    count = branch_ref.shape[0]
    others = dps - 1
    own, other = pl.ds(0, shard), pl.ds(shard, shard)
    sibling, mirror = (dp, 1 - row, col), mirror_of(cols)
    peers = [(dp, row, col ^ by) for by in range(1, group)]
    out_steps, o_steps, g_steps = 2 * half // TILE, channels // WEIGHT_TILE, channels // TILE
    o_at = out_steps
    g_at = o_at + o_steps
    near_at = g_at + g_steps
    far_at = near_at + blocks
    last = far_at + blocks - 1

    def o_moves():
        return dp_copies(dps, sems, lambda to, i: o_low.at[:, to], lambda to, i: o_land.at[i])

    def g_moves():
        return dp_copies(dps, sems, lambda to, i: g_low.at[to], lambda to, i: g_land.at[i], others)

    at = 2 * others
    cross_move = lambda: copy_to(o_cross, o_cross_land, sems, at, mirror)
    late_moves = lambda: [
        copy_to(first_grad.at[:, own], late_ref.at[:, other], sems, at + 1, mirror),
        copy_to(first_grad.at[:, other], late_ref.at[:, own], sems, at + 2, mirror),
    ]
    core_moves = lambda: [
        copy_to(cot.at[:, lanes_at(1 - row, half)], c_sib, sems, at + 3, sibling),
        copy_to(mixed_hbm, mixed_sib, sems, at + 4, sibling),
        copy_to(normed.at[:, lanes_at(1 - row, half)], n_sib, sems, at + 5, sibling),
        copy_to(gg_hbm, gg_sib, sems, at + 6, sibling),
    ]
    part_moves = lambda: [
        copy_to(parts.at[i], branch_in.at[i], sems, at + 7 + i, peer) for i, peer in enumerate(peers)
    ]
    load_c = pltpu.make_async_copy(cot.at[:, lanes_at(row, half)], c_own, local.at[0])
    load_n = pltpu.make_async_copy(normed.at[:, lanes_at(row, half)], n_own, local.at[1])

    def m_tile(tile):
        lanes = lanes_at(tile, WEIGHT_TILE)
        return pltpu.make_async_copy(mixed_sib.at[:, lanes], m_tiles.at[lax.rem(tile, 2)], local.at[2])

    def gg_tile(tile):
        lanes = lanes_at(tile, TILE)
        return pltpu.make_async_copy(gg_sib.at[:, lanes], gg_tiles.at[lax.rem(tile, 2)], local.at[3])

    @at_step(0)
    def _():
        load_c.start()
        load_n.start()
        greet([sibling, mirror] + peers + dp_peers(dps))
        for move in core_moves():
            move.start()

        @pl.when(col >= group)
        def _():
            for move in late_moves():
                move.start()
            late_ref[...] = jnp.zeros_like(late_ref)

        sums_ref[...] = jnp.zeros_like(sums_ref)

    @pl.when(step_at < o_at)
    def _():
        rows = lambda index: pl.ds(pl.multiple_of(index * count, 128), count)
        branch_ref[...] = mm(mixed_ref[rows(place), :], of_ref[...])
        for by in range(1, group):
            parts[by - 1, :, lanes_at(step_at, TILE)] = mm(mixed_ref[rows(place ^ by), :], of_ref[...]).astype(BF)

    @pl.when(step_at == o_at)
    def _():
        load_c.wait()
        for move in core_moves()[:2]:
            move.wait_recv()
        m_tile(0).start()

    @pl.when((step_at >= o_at) & (step_at < g_at))
    def _():
        tile = step_at - o_at
        m_tile(tile).wait()

        @pl.when(tile < o_steps - 1)
        def _():
            m_tile(tile + 1).start()

        total = mm_tn(mixed_ref[:, lanes_at(tile, WEIGHT_TILE)], c_own[...])
        total = total + mm_tn(m_tiles[lax.rem(tile, 2)], c_sib[...])
        piece = o_own.shape[1]
        per, each = WEIGHT_TILE // piece, shard // WEIGHT_TILE
        which, inside = lax.div(tile, each), lax.rem(tile, each)
        for p in range(per):
            part = total[p * piece : p * piece + piece, :]
            o_low[which, inside * per + p] = part.astype(BF)

            @pl.when(dp == inside * per + p)
            def _():
                o_own[which] = part

    @pl.when(step_at == g_at)
    def _():
        for move in o_moves():
            move.start()
        load_n.wait()
        for move in core_moves()[2:]:
            move.wait_recv()
        gg_tile(0).start()

    @pl.when((step_at >= g_at) & (step_at < near_at))
    def _():
        tile = step_at - g_at
        gg_tile(tile).wait()

        @pl.when(tile < g_steps - 1)
        def _():
            gg_tile(tile + 1).start()

        lanes = lanes_at(tile, TILE)
        total = mm_tn(n_own[HALO:, :], gg_ref[...]) + mm_tn(n_sib[HALO:, :], gg_tiles[lax.rem(tile, 2)])
        piece = g_own.shape[0]
        for p in range(dps):
            part = total[p * piece : p * piece + piece, :]
            g_low[p, :, lanes] = part.astype(BF)

            @pl.when(dp == p)
            def _():
                g_own[:, lanes] = part

    at_block = lax.rem(jnp.maximum(step_at - near_at, 0), blocks)
    here_rows = pl.ds(pl.multiple_of(at_block * Q, Q), Q)

    @pl.when((step_at >= near_at) & (step_at < far_at))
    def _():
        near_block(
            at_block, here_rows, dy_ref, x_ref, b_ref, c_ref, step_ref, cum_ref, spread_ref, state_ref,
            early_ref, offs_ref, gx_ref, gbc_ref,
        )

    @pl.when(step_at == g_at)
    def _():
        for move in part_moves():
            move.start()

    @pl.when(step_at == near_at + blocks // 2 + 1)
    def _():
        for move in o_moves():
            move.wait_recv()
        for move in g_moves():
            move.start()
        for i in range(others):
            o_own[...] += o_land[i].astype(F32)
        o_cross[...] = o_own[1].astype(BF)
        cross_move().start()

    @pl.when(step_at == far_at)
    def _():
        @pl.when(col < group)
        def _():
            for move in late_moves():
                move.wait_recv()

    @pl.when(step_at >= far_at)
    def _():
        far_block(
            blocks, at_block, here_rows, dy_ref, x_ref, y_ref, gx_ref, b_ref, step_ref, cum_ref, stepin_ref,
            spread_ref, gather_ref, after_ref, late_ref, state_ref, early_ref, offs_ref, head_ref, skip_ref,
            gbc_ref, ga_ref, gstep_ref, gbc_out_ref, sums_ref,
        )

    @at_step(last)
    def _():
        cross_move().wait()
        o_total_ref[...] = o_own[0] + o_cross_land[...].astype(F32)
        for move in g_moves():
            move.wait()
        for i in range(others):
            g_own[...] += g_land[i].astype(F32)
        g_own_ref[...] = g_own[:, :shard]
        g_cross_ref[...] = g_own[:, shard:].astype(BF)
        for move in part_moves():
            move.wait()
        for move in o_moves() + core_moves():
            move.wait_send()

        @pl.when(col >= group)
        def _():
            for move in late_moves():
                move.wait_send()


def scan_backward(
    cols, dps, dy, act, y, step, cum, step_in, spread, gather, after, states, early, offs, head_rows, skip,
    mixed, w_out, gg, first_grad, cot, normed,
):
    tokens, channels = dy.shape
    rows_n, width = normed.shape
    half = width // 2
    blocks, group, shard = tokens // Q, cols // 2, channels // 2
    count = tokens // group
    piece_o, piece_g = shard // dps, half // dps
    out_steps, o_steps, g_steps = width // TILE, channels // WEIGHT_TILE, channels // TILE
    g_at = out_steps + o_steps
    near_at = g_at + g_steps
    far_at = near_at + blocks

    def clamp(first, size):
        return lambda i: jnp.clip(i - first, 0, size - 1)

    block = lambda i: jnp.where(i < near_at, 0, lax.rem(jnp.maximum(i - near_at, 0), blocks))
    second = clamp(far_at, blocks)
    state_at = lambda i: block(i) + jnp.where(i < far_at, 0, 1)
    rows = lambda at, size: pl.BlockSpec((Q, size), lambda i: (at(i), 0))
    lanes = lambda at, size: pl.BlockSpec((size, TILE), lambda i: (0, at(i)))
    once = lambda shape: pl.BlockSpec(shape, lambda *_: (0,) * len(shape), pipeline_mode=pl.Buffered(1))
    vmem = pltpu.VMEM
    dma = pltpu.SemaphoreType.DMA
    return pl.pallas_call(
        partial(backward_kernel, cols, dps),
        grid=(far_at + blocks,),
        in_specs=[
            rows(block, channels),
            rows(block, channels),
            rows(second, channels),
            pl.BlockSpec((Q, N), lambda i: (block(i), channels // N)),
            pl.BlockSpec((Q, N), lambda i: (block(i), channels // N + 1)),
            rows(block, 128),
            rows(block, 128),
            rows(second, 128),
            once(spread.shape),
            once(gather.shape),
            pl.BlockSpec((1, N, channels), lambda i: (second(i), 0, 0)),
            pl.BlockSpec((1, N, channels), lambda i: (state_at(i), 0, 0)),
            once(early.shape),
            once((16, 128)),
            once((8, 128)),
            once((8, channels)),
            once(mixed.shape),
            lanes(clamp(0, out_steps), channels),
            lanes(clamp(g_at, g_steps), tokens),
        ] + [ANY] * 5,
        out_specs=[
            rows(second, channels),
            rows(second, 128),
            rows(second, 2 * N),
            whole((8, 128)),
            whole((piece_o, half)),
            whole((piece_g, shard)),
            whole((piece_g, shard)),
            lanes(clamp(0, out_steps), count),
            ANY, ANY, ANY,
        ],
        out_shape=[
            sds((tokens, channels)),
            sds((tokens, 128), BF),
            sds((tokens, 2 * N)),
            sds((8, 128)),
            sds((piece_o, half)),
            sds((piece_g, shard)),
            sds((piece_g, shard), BF),
            sds((count, width)),
            sds((max(group - 1, 1), count, width), BF),
            sds(mixed.shape, BF),
            sds(gg.shape, BF),
        ],
        scratch_shapes=[
            vmem((tokens, channels), F32), vmem((tokens, 2 * N), F32), vmem((N, channels), F32),
            vmem((2, dps, piece_o, half), BF), vmem((2, piece_o, half), F32),
            vmem((dps - 1, 2, piece_o, half), BF), vmem((piece_o, half), BF), vmem((piece_o, half), BF),
            vmem((dps, piece_g, channels), BF), vmem((piece_g, channels), F32),
            vmem((dps - 1, piece_g, channels), BF),
            vmem((max(group - 1, 1), count, width), BF),
            vmem((tokens, half), BF), vmem((tokens, half), BF),
            vmem((rows_n, half), BF), vmem((rows_n, half), BF),
            vmem((2, tokens, WEIGHT_TILE), BF), vmem((2, tokens, TILE), BF),
            dma((2, 2 * (dps - 1) + 6 + group)),
            dma((4,)),
        ],
        compiler_params=remote_params(3),
        cost_estimate=cost(80),
        name="scan_backward",
    )(
        dy, act, y, act, act, step, cum, step_in, spread, gather, after, states, early, offs, head_rows, skip,
        mixed, w_out, gg, first_grad, mixed, gg, cot, normed,
    )


def gate_kernel(
    cols, inner_channels,
    y0_ref, graw_ref, gm_ref, x_ref, early_ref, c_ref, grow_ref, spread_ref, vec_ref,
    cum_ref, c_block_ref, spread_all_ref,
    y_ref, mixed_ref, gg_ref, dy_ref, sums_ref, after_ref, first_ref,
    y_vm, graw_vm, gm_vm, squares, inners, stats, stats_land, stats_col, held, sems,
):
    step = pl.program_id(0)
    tiles = y_vm.shape[0]
    tokens = y0_ref.shape[0]
    dp, row, col = here()
    group = cols // 2
    peers = [(dp, row, col ^ by) for by in range(1, group)]
    gain = vec_ref[1:2, :]
    nt = (((1,), (1,)), ((), ()))
    moves = lambda: [copy_to(stats, stats_land.at[i], sems, i, peer) for i, peer in enumerate(peers)]

    @at_step(0)
    def _():
        greet(peers)
        squares[...] = jnp.zeros_like(squares)
        inners[...] = jnp.zeros_like(inners)

    @pl.when(step < tiles)
    def _():
        s_high, s_low = split2(early_ref[...])
        s2 = jnp.concatenate([s_high, s_low], 0)
        spread = spread_ref[...]
        skip = vec_ref[0:1, :]
        for at in range(0, tokens, Q):
            rows = slice(at, at + Q)
            c_blk = c_ref[rows, :]
            carried = mm(jnp.concatenate([c_blk, c_blk], 1), s2) * mm(grow_ref[rows, :], spread)
            y = y0_ref[rows, :] + carried + skip * x_ref[rows, :].astype(F32)
            raw, gm = graw_ref[rows, :], gm_ref[rows, :]
            y_ref[rows, :] = y
            y_vm[step, rows, :] = y
            graw_vm[step, rows, :] = raw
            gm_vm[step, rows, :] = gm
            gated = y * raw * sigmoid(raw)
            square = gated * gated
            inner = gm * gain * gated
            squares[rows, :] += square[:, 0:128] + square[:, 128:256]
            inners[rows, :] += inner[:, 0:128] + inner[:, 128:256]

    @at_step(tiles - 1)
    def _():
        ones = jnp.ones((8, 128), F32)
        square_row = lax.dot_general(ones, squares[...], nt, precision=HIGHEST, preferred_element_type=F32)
        inner_row = lax.dot_general(ones, inners[...], nt, precision=HIGHEST, preferred_element_type=F32)
        stats[...] = jnp.where(iota2(square_row.shape, 0) == 0, square_row, inner_row)
        for move in moves():
            move.start()
        for move in moves():
            move.wait_recv()
        total = stats[...]
        for i in range(group - 1):
            total = total + stats_land[i]
        wide = jnp.concatenate([total, jnp.zeros((120, tokens), F32)], 0)
        stats_col[...] = wide.T

    @pl.when((step >= tiles) & (step < 2 * tiles))
    def _():
        tile = step - tiles
        gain_sum = jnp.zeros((1, TILE), F32)
        skip_sum = jnp.zeros((1, TILE), F32)
        for at in range(0, tokens, Q):
            rows = slice(at, at + Q)
            inv = lax.rsqrt(stats_col[rows, 0:1] * (1.0 / inner_channels) + EPSILON)
            pull = inv * inv * inv * (stats_col[rows, 1:2] * (1.0 / inner_channels))
            raw, y, gm = graw_vm[tile, rows, :], y_vm[tile, rows, :], gm_vm[tile, rows, :]
            sig = sigmoid(raw)
            act = raw * sig
            gated = y * act
            unit = gated * inv
            mixed_ref[rows, :] = (unit * gain).astype(BF)
            gain_sum = gain_sum + jnp.sum(gm * unit, axis=0, keepdims=True)
            grad_gated = inv * (gm * gain) - gated * pull
            dy = grad_gated * act
            dy_ref[rows, :] = dy
            y_vm[tile, rows, :] = dy
            gg_ref[rows, :] = (grad_gated * y * (sig * (1.0 + raw * (1.0 - sig)))).astype(BF)
            skip_sum = skip_sum + jnp.sum(dy * x_ref[rows, :].astype(F32), axis=0, keepdims=True)
        sums_ref[...] = jnp.zeros_like(sums_ref)
        sums_ref[0:1, :] = gain_sum
        sums_ref[1:2, :] = skip_sum

    @pl.when(step == 2 * tiles)
    def _():
        for move in moves():
            move.wait_send()
        held[...] = jnp.zeros_like(held)

    @pl.when(step >= 2 * tiles)
    def _():
        at = pl.num_programs(0) - 1 - step
        rows = pl.ds(pl.multiple_of(at * Q, Q), Q)
        grad_state_block(y_vm.at[:, rows, :], c_block_ref, cum_ref, spread_all_ref, after_ref, held)
        first_ref[...] = held[...]


def gate_and_mix(cols, inner_channels, y0, graw, gm, act, early, grow, spread, vectors, cum):
    tokens, channels = y0.shape
    blocks = tokens // Q
    tiles, group = channels // TILE, cols // 2
    first = lambda i: jnp.minimum(i, tiles - 1)
    second = lambda i: jnp.clip(i - tiles, 0, tiles - 1)
    either = lambda i: jnp.where(i < 2 * tiles, lax.rem(i, tiles), tiles - 1)
    third = lambda i: blocks - 1 - jnp.maximum(i - 2 * tiles, 0)
    lanes = lambda at, count: pl.BlockSpec((count, TILE), lambda i: (0, at(i)))
    vmem = pltpu.VMEM
    return pl.pallas_call(
        partial(gate_kernel, cols, inner_channels),
        grid=(2 * tiles + blocks,),
        in_specs=[
            lanes(first, tokens), lanes(first, tokens), lanes(first, tokens), lanes(either, tokens),
            lanes(first, N),
            pl.BlockSpec((tokens, N), lambda i: (0, channels // N + 1)),
            whole((tokens, 256)),
            lanes(first, 256),
            lanes(either, 8),
            pl.BlockSpec((Q, 128), lambda i: (third(i), 0)),
            pl.BlockSpec((Q, N), lambda i: (third(i), channels // N + 1)),
            whole((256, channels)),
        ],
        out_specs=[
            lanes(first, tokens), lanes(second, tokens), lanes(second, tokens), lanes(second, tokens),
            lanes(second, 8),
            pl.BlockSpec((1, N, channels), lambda i: (third(i), 0, 0)),
            whole((N, channels)),
        ],
        out_shape=[
            sds((tokens, channels)), sds((tokens, channels), BF), sds((tokens, channels), BF),
            sds((tokens, channels)), sds((8, channels)), sds((blocks, N, channels)), sds((N, channels)),
        ],
        scratch_shapes=[
            vmem((tiles, tokens, TILE), F32), vmem((tiles, tokens, TILE), F32), vmem((tiles, tokens, TILE), F32),
            vmem((tokens, 128), F32), vmem((tokens, 128), F32),
            vmem((8, tokens), F32), vmem((max(group - 1, 1), 8, tokens), F32), vmem((tokens, 128), F32),
            vmem((N, channels), F32),
            pltpu.SemaphoreType.DMA((2, max(group - 1, 1))),
        ],
        compiler_params=remote_params(6),
        cost_estimate=cost(40),
        name="gate_and_mix",
    )(y0, graw, gm, act, early, act, grow, spread, vectors, cum, act, spread)


def conv_back_tile(ga_ref, raw_ref, taps_ref, gv_ref, sums_ref, g_pad):
    tokens, width = ga_ref.shape
    taps = taps_ref[...]
    g_pad[0:HALO, :] = jnp.zeros((HALO, width), F32)
    g_pad[HALO + tokens :, :] = jnp.zeros((HALO, width), F32)
    sums = [jnp.zeros((8, width), F32)] * 5
    by_eight = lambda values: jnp.sum(values.reshape(ROWS // 8, 8, width), axis=0)
    for row in range(0, tokens, ROWS):
        moved = conv_window(raw_ref, row, ROWS)
        pre = conv_rows(moved, taps)
        sig = sigmoid(pre)
        g = ga_ref[row : row + ROWS, :] * (sig * (1.0 + pre * (1.0 - sig)))
        g_pad[HALO + row : HALO + row + ROWS, :] = g
        for k in range(4):
            sums[k] = sums[k] + by_eight(g * moved[k])
        sums[4] = sums[4] + by_eight(g)
    for row in list(range(HALO, HALO + tokens, ROWS)) + [0]:
        size = HALO if row == 0 else ROWS
        window = g_pad[row : row + size + 8, :]
        total = taps[3:4, :] * window[:size, :]
        for k in range(3):
            total = total + taps[k : k + 1, :] * pltpu.roll(window, size + 5 + k, 0)[:size, :]
        gv_ref[row : row + size, :] = total.astype(BF)
    for k in range(5):
        sums_ref[k : k + 1, :] = jnp.sum(sums[k], axis=0, keepdims=True)


SMALL_ROWS = 16
A_TAKEN = 4


def finish_kernel(
    cols, dps, heads, part, whole_state,
    ga_ref, raw_ref, taps_ref, gg_ref, gt_ref, v_ref, g_ref, pick_v_ref, tok_ref, inv_ref, g_own_ref,
    mix_ref, headsum_ref, gain_ref, o_total, g_cross, gbc, normed, gt_hbm, tok, cot,
    tg_out, o_out, g_out, v_out, ext_out, sm_out,
    gv_vm, gv_sib, gs_vm, gs_sib, gt_sib, bc_own, bc_land, g_pad, raw_part, taps_part, g_pad_part,
    n_own, n_sib, o_vm, g_vm, g_land, gn_tile, gn_own, gn_parts, gn_land, gn_halo, halo_land,
    joint_low, rec, tot, z_send, z_land, state_land, ext, small, small_land, tok_vm, cot_vm, sems, local,
):
    step = pl.program_id(0)
    channels, half = gv_vm.shape[1], n_own.shape[1]
    shard, piece, span = channels // 2, tot.shape[0], gs_vm.shape[1]
    count, width = gn_own.shape
    tokens = bc_own.shape[0]
    tiles, weight_steps, input_steps = channels // TILE, 2, width // TILE
    weight_at = tiles + 1
    input_at = weight_at + weight_steps
    last = input_at + input_steps
    dp, row, col = here()
    group = cols // 2
    place = lax.rem(col, group)
    sibling, mirror = (dp, 1 - row, col), mirror_of(cols)
    col_peer = lambda by: (dp, row, col ^ by)
    peers = [col_peer(by) for by in range(1, group)]
    others = dps - 1
    o_rows = pl.ds(dp * piece_of(o_vm), piece_of(o_vm))
    g_rows = pl.ds(dp * piece, piece)
    cols_a, cols_b = pl.ds(shard, tot.shape[1] - shard), pl.ds(0, shard)
    used = [0]

    def take(size):
        used[0] += size
        return used[0] - size

    def part_at(at):
        return pl.ds(0, span) if whole_state else lanes_at(at, span)

    def to_dp(src_of, dst_of):
        first = take(others)
        return lambda: dp_copies(dps, sems, src_of, dst_of, first)

    def to_all_dp(src, out):
        first = take(max(others, 4))
        return (lambda: hand_out(dps, sems, first, src, out)[0]), (lambda: hand_out(dps, sems, first, src, out)[1])

    def one(src, dst, device):
        at = take(1)
        return lambda: [copy_to(src, dst, sems, at, device)]

    def to_peers(src_of, dst_of):
        first = take(group - 1)
        return lambda: [
            copy_to(src_of(by), dst_of(by), sems, first + by - 1, col_peer(by)) for by in range(1, group)
        ]

    def to_cols(src, dst):
        first = take(cols - 1)
        return lambda: [copy_to(src, dst, sems, first + by - 1, col_peer(by)) for by in range(1, cols)]

    o_moves, o_passed = to_all_dp(o_total, o_out)
    g_moves, g_passed = to_all_dp(g_vm, g_out)
    a_moves = to_dp(lambda to, i: joint_low.at[to, :, cols_a], lambda to, i: rec.at[i, :, cols_a])
    b_moves = to_dp(lambda to, i: joint_low.at[to, :, cols_b], lambda to, i: rec.at[i, :, cols_b])
    v_moves, v_passed = to_all_dp(tot.at[:, cols_b], v_out)
    e_moves, e_passed = to_all_dp(ext, ext_out)
    g_move = one(g_cross, g_land, mirror)
    n_move = one(normed.at[:, lanes_at(1 - row, half)], n_sib, sibling)
    t_move = one(gt_hbm, gt_sib, sibling)
    s_move = one(gs_vm, gs_sib, sibling)
    z_move = one(z_send, z_land, mirror)
    state_moves = to_cols(tot.at[:, pl.ds(channels, span)], state_land.at[col])

    def state_each(sending, act):
        for by, move in enumerate(state_moves(), 1):
            if whole_state:
                act(move)
            else:
                there = col ^ by
                needed = lax.div(there, 2) == place if sending else lax.rem(there, group) == lax.div(col, 2)
                pl.when(needed)(partial(act, move))

    bc_moves = to_peers(lambda by: gbc.at[:, part_at(place ^ by)], lambda by: bc_land.at[by - 1])
    early_rows, late_rows = pl.ds(0, count // 2), pl.ds(count // 2, count - count // 2)
    gn_early = to_peers(lambda by: gn_parts.at[by - 1, early_rows, :], lambda by: gn_land.at[by - 1, early_rows, :])
    gn_late = to_peers(lambda by: gn_parts.at[by - 1, late_rows, :], lambda by: gn_land.at[by - 1, late_rows, :])
    gn_moves = lambda: gn_early() + gn_late()
    tile_first = take(tiles)

    def v_tile(tile):
        lanes = lanes_at(tile, TILE)
        return copy_to(gv_vm.at[:, lanes], gv_sib.at[:, lanes], sems, tile_first + tile, sibling)

    halo_first = take(group)
    halos = lambda: [
        copy_to(gn_halo, halo_land.at[j], sems, halo_first + j, (dp, row, group - 1)) for j in range(group)
    ]
    small_steps = [sibling]
    by = 1
    while by < dps:
        small_steps.append((dp ^ by, row, col))
        by *= 2
    small_first = take(len(small_steps))
    small_move = lambda i: copy_to(small, small_land.at[i], sems, small_first + i, small_steps[i])
    small_cols = to_cols(small, sm_out.at[col])

    def small_next(i):
        move = small_move(i)
        move.wait()
        small[...] += small_land[i]
        if i + 1 < len(small_steps):
            small_move(i + 1).start()

    def start(moves):
        for move in moves:
            move.start()

    def arrive(moves):
        for move in moves:
            move.wait_recv()

    def sent(moves):
        for move in moves:
            move.wait_send()

    load_bc = pltpu.make_async_copy(gbc.at[:, part_at(place)], bc_own, local.at[0])
    load_n = pltpu.make_async_copy(normed.at[:, lanes_at(row, half)], n_own, local.at[1])
    load_o = pltpu.make_async_copy(o_total, o_vm, local.at[2])
    load_tok = pltpu.make_async_copy(tok, tok_vm, local.at[3])
    load_cot = pltpu.make_async_copy(cot, cot_vm, local.at[4])
    store_o = pltpu.make_async_copy(o_vm, o_out.at[o_rows, :], local.at[2])
    store_g = pltpu.make_async_copy(g_vm, g_out.at[g_rows, :], local.at[0])
    store_v = pltpu.make_async_copy(tot.at[:, cols_b], v_out.at[g_rows, :], local.at[1])
    store_e = pltpu.make_async_copy(ext, ext_out.at[g_rows, :], local.at[5])
    store_tg = pltpu.make_async_copy(gn_own, tg_out, local.at[3])
    store_small = pltpu.make_async_copy(small, sm_out.at[col], local.at[6])

    @at_step(0)
    def _():
        load_o.start()
        load_bc.start()
        load_n.start()
        load_tok.start()
        load_cot.start()
        greet([sibling] + [col_peer(by) for by in range(1, cols)] + dp_peers(dps))
        start(bc_moves() + o_moves() + t_move() + n_move() + g_move())
        small[...] = jnp.zeros_like(small)
        small[5:7, 0:channels] = mix_ref[0:2, :]
        small[7:9, 0:128] = headsum_ref[0:2, :]
        load_o.wait()
        store_o.start()

    @pl.when(step < tiles)
    def _():
        lanes = lanes_at(step, TILE)
        conv_back_tile(ga_ref, raw_ref, taps_ref, gv_vm.at[:, lanes], small.at[0:5, lanes], g_pad)
        v_tile(step).start()

    @pl.when(step == tiles - 1)
    def _():
        arrive(o_moves())
        start(o_passed())

    @pl.when(step == tiles)
    def _():
        load_bc.wait()
        arrive(bc_moves())
        for i in range(group - 1):
            bc_own[...] += bc_land[i]
        if whole_state:
            lane = iota2(bc_own.shape, 1)
            mine = (lane >= place * part) & (lane < place * part + part)
            bc_own[...] = jnp.where(mine, bc_own[...], 0.0)
        lanes = part_at(place)
        raw_part[...] = raw_ref[:, lanes]
        taps_part[...] = taps_ref[:, lanes]
        conv_back_tile(bc_own, raw_part, taps_part, gs_vm, small.at[10:15, 0:span], g_pad_part)
        start(s_move())
        arrive(g_move())
        g_vm[...] = g_own_ref[...] + g_land[...].astype(F32)
        start(g_moves())
        store_g.start()

    @pl.when(step == weight_at)
    def _():
        load_n.wait()
        arrive(n_move() + t_move() + s_move() + [v_tile(tile) for tile in range(tiles)])

    def keep(first, size, total):
        for p in range(dps):
            rows = total[p * piece : p * piece + piece, :]
            joint_low[p, :, first : first + size] = rows.astype(BF)

            @pl.when(dp == p)
            def _():
                tot[:, first : first + size] = rows

    @pl.when(step == weight_at)
    def _():
        keep(shard, shard, mm_tn(n_own[...], gv_vm[:, shard:]) + mm_tn(n_sib[...], gv_sib[:, shard:]))
        keep(channels, span, mm_tn(n_own[...], gs_vm[...]) + mm_tn(n_sib[...], gs_sib[...]))
        keep(channels + span, 128, mm_tn(n_own[HALO:, :], gt_ref[...]) + mm_tn(n_sib[HALO:, :], gt_sib[...]))
        start(a_moves())

    @pl.when(step == weight_at + 1)
    def _():
        keep(0, shard, mm_tn(n_own[...], gv_vm[:, :shard]) + mm_tn(n_sib[...], gv_sib[:, :shard]))

    @pl.when(step == input_at)
    def _():
        arrive(g_moves())
        start(g_passed())

    @pl.when(step == input_at + A_TAKEN)
    def _():
        arrive(a_moves())
        start(b_moves())
        for i in range(others):
            tot[:, cols_a] += rec[i, :, cols_a].astype(F32)
        z_send[:, 0:shard] = tot[:, shard:channels].astype(BF)
        z_send[:, shard:] = tot[:, channels + span :].astype(BF)
        start(z_move())
        state_each(True, lambda move: move.start())
        state_land[col] = tot[:, channels : channels + span]

    @pl.when((step >= input_at) & (step < last))
    def _():
        at = step - input_at
        lanes = lanes_at(at, TILE)
        gn_tile[...] = mm_nt(gv_vm[...], v_ref[...]) + mm_nt(gs_vm[...], pick_v_ref[:, part_at(place)])
        gn_tile[HALO:, :] += mm_nt(gg_ref[...], g_ref[...]) + mm_nt(gt_ref[...], pick_v_ref[:, TILE:])
        rows = lambda index: pl.ds(pl.multiple_of(HALO + index * count, HALO), count)
        gn_own[:, lanes] = gn_tile[rows(place), :]
        for by in range(1, group):
            gn_parts[by - 1, :, lanes] = gn_tile[rows(place ^ by), :].astype(BF)
        gn_halo[:, lanes] = gn_tile[0:HALO, :].astype(BF)
        sums = jnp.zeros((1, TILE), F32)
        for first in [0] + list(range(HALO, HALO + tokens, Q)):
            size = HALO if first == 0 else Q
            unit = tok_ref[first : first + size, :].astype(F32) * inv_ref[first : first + size, 0:1]
            sums = sums + jnp.sum(gn_tile[first : first + size, :] * unit, axis=0, keepdims=True)
        small[9:10, lanes] = sums

    @pl.when(step == last)
    def _():
        start(gn_early())
        for j in range(group):
            pl.when(col == group + j)(halos()[j].start)
        small_move(0).start()
        small_next(0)
        arrive(b_moves())
        for i in range(others):
            tot[:, cols_b] += rec[i, :, cols_b].astype(F32)
        arrive(z_move())
        start(gn_late())
        tot[:, cols_b] += z_land[:, 0:shard].astype(F32)
        start(v_moves())
        store_v.start()
        steps = tot[:, channels + span :] + pltpu.roll(z_land[:, shard:].astype(F32), 128 - heads, 1)
        state_each(False, lambda move: move.wait_recv())
        if whole_state:
            ext[:, 0:128] = steps
            ext[:, 128:] = sum(state_land[i] for i in range(cols))
        else:
            states = state_land[lax.div(col, 2)] + state_land[lax.div(col, 2) + group]
            moved = jnp.where(lax.rem(col, 2) == 1, states, pltpu.roll(states, 64, 1))
            ext[...] = jnp.where(iota2(steps.shape, 1) < 64, steps, moved)
        start(e_moves())
        store_e.start()
        for i in range(1, len(small_steps)):
            small_next(i)
        start(small_cols())
        store_small.start()
        arrive(v_moves())
        start(v_passed())
        arrive(e_moves())
        start(e_passed())
        load_tok.wait()
        load_cot.wait()
        arrive(gn_moves())
        for i in range(group - 1):
            gn_own[...] += gn_land[i].astype(F32)

        @pl.when(col == group - 1)
        def _():
            arrive(halos())
            for j in range(group):
                gn_own[count - HALO :, :] += halo_land[j].astype(F32)

        for j in range(group):
            pl.when(col == group + j)(halos()[j].wait_send)
        for first in range(0, count, ROWS):
            rows = slice(first, first + ROWS)
            values = tok_vm[rows, :].astype(F32)
            inv = lax.rsqrt(jnp.mean(values * values, axis=-1, keepdims=True) + EPSILON)
            unit = values * inv
            pulled = gn_own[rows, :] * gain_ref[0:1, :]
            mean = jnp.mean(pulled * unit, axis=-1, keepdims=True)
            gn_own[rows, :] = cot_vm[rows, :].astype(F32) + inv * (pulled - unit * mean)
        store_tg.start()
        store_o.wait()
        store_g.wait()
        store_small.wait()
        store_v.wait()
        store_e.wait()
        arrive(o_passed() + g_passed() + v_passed() + e_passed() + small_cols())
        sent(o_passed() + g_passed() + v_passed() + e_passed())
        sent(bc_moves() + o_moves() + t_move() + n_move() + g_move() + s_move() + a_moves() + b_moves())
        sent([v_tile(tile) for tile in range(tiles)])
        state_each(True, lambda move: move.wait_send())
        sent(gn_moves() + z_move() + g_moves() + v_moves() + e_moves() + small_cols())
        store_tg.wait()


def piece_of(ref):
    return ref.shape[0]


def finish(
    cols, dps, heads, part, ga, raw, taps, gg, gt, w_value, w_gate, picked, tokens_in, inv_rms, g_own, mix_sums,
    head_sums, gain, o_total, g_cross, gbc, normed, tokens_own, cotangent,
):
    tokens, channels = ga.shape
    rows, width = normed.shape
    half, shard = width // 2, channels // 2
    whole_state = part % 128 != 0
    span = 2 * N if whole_state else part
    extra = 128 + span if whole_state else 128
    group = cols // 2
    tiles, weight_steps, input_steps = channels // TILE, 2, width // TILE
    piece, wide = g_own.shape[0], channels + span + 128
    count = tokens_own.shape[0]
    input_at = tiles + 1 + weight_steps
    small_steps = dps.bit_length()

    def clamp(first, size):
        return lambda i: jnp.clip(i - first, 0, size - 1)

    conv, both, input_tile = clamp(0, tiles), clamp(0, tiles + 1), clamp(input_at, input_steps)
    lanes = lambda at, size: pl.BlockSpec((size, TILE), lambda i: (0, at(i)))
    slab = lambda at, size: pl.BlockSpec((TILE, size), lambda i: (at(i), 0))
    once = lambda values: pl.BlockSpec(
        values.shape, lambda *_: (0,) * len(values.shape), pipeline_mode=pl.Buffered(1)
    )
    vmem = pltpu.VMEM
    dma = pltpu.SemaphoreType.DMA
    more = max(group - 1, 1)
    copies = 2 * (dps - 1) + 4 * max(dps - 1, 4) + 6 + 2 * (cols - 1) + 3 * (group - 1) + tiles + group + small_steps
    return pl.pallas_call(
        partial(finish_kernel, cols, dps, heads, part, whole_state),
        grid=(input_at + input_steps + 1,),
        in_specs=[
            lanes(conv, tokens),
            lanes(both, rows),
            lanes(both, 8),
            once(gg),
            once(gt),
            slab(input_tile, channels),
            slab(input_tile, channels),
            slab(input_tile, TILE + 128),
            lanes(input_tile, rows),
            once(inv_rms),
            once(g_own),
            once(mix_sums),
            once(head_sums),
            once(gain),
        ] + [ANY] * 7,
        out_specs=[ANY] * 6,
        out_shape=[
            sds((count, width)), sds((dps * o_total.shape[0], o_total.shape[1])), sds((half, shard)),
            sds((half, shard)), sds((half, extra)), sds((cols, SMALL_ROWS, width)),
        ],
        scratch_shapes=[
            vmem((rows, channels), BF), vmem((rows, channels), BF), vmem((rows, span), BF), vmem((rows, span), BF),
            vmem((tokens, 128), BF), vmem((tokens, span), F32), vmem((more, tokens, span), F32),
            vmem((tokens + 2 * HALO, TILE), F32), vmem((rows, span), F32), vmem((8, span), F32),
            vmem((tokens + 2 * HALO, span), F32),
            vmem((rows, half), BF), vmem((rows, half), BF),
            vmem(o_total.shape, F32), vmem(g_own.shape, F32), vmem(g_own.shape, BF),
            vmem((rows, TILE), F32),
            vmem((count, width), F32), vmem((more, count, width), BF), vmem((more, count, width), BF),
            vmem((HALO, width), BF), vmem((group, HALO, width), BF),
            vmem((dps, piece, wide), BF), vmem((dps - 1, piece, wide), BF), vmem((piece, wide), F32),
            vmem((piece, shard + 128), BF), vmem((piece, shard + 128), BF),
            vmem((cols, piece, span), F32), vmem((piece, extra), F32),
            vmem((SMALL_ROWS, width), F32), vmem((small_steps, SMALL_ROWS, width), F32),
            vmem((count, width), BF), vmem((count, width), BF),
            dma((2, copies)),
            dma((7,)),
        ],
        compiler_params=remote_params(5),
        cost_estimate=cost(110),
        name="finish",
    )(
        ga, raw, taps, gg, gt, w_value, w_gate, picked, tokens_in, inv_rms, g_own, mix_sums, head_sums, gain,
        o_total, g_cross, gbc, normed, gt, tokens_own, cotangent,
    )


def collect_kernel(tok_ref, branch_ref, in_ref, *refs):
    half = (len(refs) - 1) // 2
    refs[half][...] = (
        tok_ref[...].astype(F32) + branch_ref[...] + jnp.sum(in_ref[...].astype(F32), axis=0)
    ).astype(BF)
    for source, target in zip(refs[:half], refs[half + 1 :]):
        target[...] = source[...]


def collect(tokens, branch, branch_in, results):
    steps = 4
    slab = lambda v: pl.BlockSpec((v.shape[0] // steps, v.shape[1]), lambda i: (i, 0))
    more, count, width = branch_in.shape
    return pl.pallas_call(
        collect_kernel,
        grid=(steps,),
        in_specs=[
            slab(tokens), slab(branch), pl.BlockSpec((more, count // steps, width), lambda i: (0, i, 0)),
        ] + [slab(v) for v in results],
        out_specs=[slab(tokens)] + [slab(v) for v in results],
        out_shape=[sds(tokens.shape, BF)] + [sds(v.shape) for v in results],
        compiler_params=params(),
        cost_estimate=cost(8),
        name="collect",
    )(tokens, branch, branch_in, *results)


def flips(size, by):
    return [(i, i ^ by) for i in range(size)]


def butterfly(values, axis):
    size = lax.axis_size(axis)
    by = 1
    while by < size:
        values = values + lax.ppermute(values, axis, flips(size, by))
        by *= 2
    return values


def at_rows(values, index, size):
    return lax.dynamic_slice_in_dim(values, index * size, size, axis=0)


def collect_dp(piece, dp):
    size = lax.axis_size("dp")
    rows = piece.shape[0]
    out = jnp.zeros((size * rows,) + piece.shape[1:], piece.dtype)
    out = lax.dynamic_update_slice_in_dim(out, piece, dp * rows, 0)
    for by in range(1, size):
        other = lax.ppermute(piece, "dp", flips(size, by))
        out = lax.dynamic_update_slice_in_dim(out, other, (dp ^ by) * rows, 0)
    return out


def swap_core(values):
    return lax.ppermute(values, "row", [(0, 1), (1, 0)])


def per_device(
    tokens, norm_gain, w_gate, w_value, w_state, w_step, conv_value, bias_value, conv_state,
    bias_state, a_log, d_skip, dt_bias, mix_gain, w_out, cotangent,
):
    cols, rows_n, dps = lax.axis_size("col"), lax.axis_size("row"), lax.axis_size("dp")
    col, row, dp = lax.axis_index("col"), lax.axis_index("row"), lax.axis_index("dp")
    group = cols // 2
    place = lax.rem(col, group)
    local, width = tokens.shape
    span = local * group
    half_width = width // 2
    shard = w_value.shape[1]
    channels = 2 * shard
    heads = a_log.shape[0]
    inner_channels = shard * cols
    state_all = w_state.shape[1] * cols
    mirror = [(i, cols - 1 - i) for i in range(cols)]
    forth = [(i, cols - 1 - i) for i in range(group)]
    back = [(cols - 1 - i, i) for i in range(group)]

    def ring(by):
        return [(i, (i // group) * group + (i % group + by) % group) for i in range(cols)]

    state_width = w_state.shape[1]
    small = jnp.pad(
        jnp.concatenate([w_state, w_step], axis=1), ((0, 0), (0, 128 - state_width - heads))
    )
    heads_row = jnp.pad(
        jnp.concatenate([d_skip, a_log, dt_bias]), (0, shard - 3 * heads)
    )[None]
    state_rows = jnp.concatenate([conv_state.T, bias_state[None]], axis=0)
    vec = jnp.concatenate(
        [
            conv_value.T, bias_value[None], mix_gain[None], heads_row, jnp.zeros((1, shard), BF),
            jnp.pad(state_rows, ((0, 3), (0, shard - state_width))),
        ],
        axis=0,
    )
    group_tokens, value_full, small_full, vecs = import_all(cols, dps, tokens, w_value, small, vec)
    from_col = lax.broadcasted_iota(jnp.int32, (cols * 128, TILE + 128), 0) // 128
    from_lane = lax.broadcasted_iota(jnp.int32, (cols * 128, TILE + 128), 0) % 128
    to = lax.broadcasted_iota(jnp.int32, (cols * 128, TILE + 128), 1)
    head_to = to - TILE
    is_state = (to < TILE) & (from_lane < state_width) & (from_col * state_width + from_lane == to)
    is_own = (from_col == col) & (head_to < heads) & (from_lane == state_width + head_to)
    is_mirror = (from_col == cols - 1 - col) & (head_to >= heads) & (head_to < 2 * heads)
    is_mirror = is_mirror & (from_lane == state_width + head_to - heads)
    pick = (is_state | ((head_to >= 0) & (is_own | is_mirror))).astype(BF)

    vecs = vecs.astype(F32)
    both = jnp.concatenate(
        [
            lax.dynamic_index_in_dim(vecs, col, 0, keepdims=False),
            lax.dynamic_index_in_dim(vecs, cols - 1 - col, 0, keepdims=False),
        ],
        axis=1,
    )
    state_vecs = jnp.transpose(vecs[:, 8:16, :state_width], (1, 0, 2)).reshape(8, state_all)
    taps = jnp.concatenate([both[0:8], state_vecs], axis=1)

    def both_heads(at):
        return jnp.concatenate(
            [both[6, at * heads : (at + 1) * heads], both[6, shard + at * heads : shard + (at + 1) * heads]]
        )

    skip_both, a_both, dt_both = both_heads(0), both_heads(1), both_heads(2)
    vectors = jnp.concatenate(
        [jnp.repeat(skip_both, HEAD)[None], both[5:6], jnp.zeros((6, channels), F32)], axis=0
    )
    rate = -jnp.exp(a_both)
    head_rows = jnp.pad(jnp.stack([dt_both, rate]), ((0, 6), (0, 128 - 2 * heads)))
    head_of = np.arange(channels) // HEAD
    one_hot = (np.arange(128)[:, None] == head_of[None, :]).astype(np.float32)
    spread = jnp.asarray(np.concatenate([one_hot, one_hot], axis=0), BF)
    gather = jnp.asarray(one_hot.T, BF)

    gain = norm_gain.astype(F32)
    (
        raw, act, normed, step_in, step, cum, grow, offs, inv_rms, picked, states, y0, graw, gm, early,
        group_cot, gate_full, out_full,
    ) = forward_all(
        cols, dps, group_tokens, gain[None], value_full, small_full, pick, taps, head_rows, spread, cotangent,
        w_gate, w_out,
    )
    y, mixed, grad_gate, dy, mix_sums, after, first_grad = gate_and_mix(
        cols, inner_channels, y0, graw, gm, act, early, grow, spread, vectors, cum
    )
    (
        ga, grad_step, gbc, head_sums, out_total, gate_own, gate_cross, branch, branch_in, _, _,
    ) = scan_backward(
        cols, dps, dy, act, y, step, cum, step_in, spread, gather, after, states, early, offs, head_rows, vectors,
        mixed, out_full, grad_gate, first_grad, group_cot, normed,
    )
    state_part = state_all // group

    tokens_grad, sum_out, sum_gate, sum_value, extra, small_sums = finish(
        cols, dps, heads, state_part, ga, raw, taps, grad_gate, grad_step, value_full, gate_full, picked,
        group_tokens, inv_rms, gate_own, mix_sums, head_sums, gain[None], out_total, gate_cross, gbc, normed,
        tokens, cotangent,
    )
    block_out, tokens_grad, sum_out, sum_gate, sum_value = collect(
        tokens, branch, branch_in, [tokens_grad, sum_out, sum_gate, sum_value]
    )
    sum_step = extra[:, :heads]
    whole_state = state_part % 128 != 0
    if whole_state:
        sum_state = lax.dynamic_slice_in_dim(extra, 128 + col * state_width, state_width, axis=1)
    else:
        sum_state = extra[:, 64:]
    own_sums = lax.dynamic_index_in_dim(small_sums, col, 0, keepdims=False)
    mirror_sums = lax.dynamic_index_in_dim(small_sums, cols - 1 - col, 0, keepdims=False)
    wide = own_sums[0:7, :shard] + mirror_sums[0:7, shard:channels]
    head_own = own_sums[7:9, :heads] + mirror_sums[7:9, heads : 2 * heads]
    skip_own = jnp.sum(wide[6].reshape(heads, HEAD), axis=1)
    norm_total = small_sums[0, 9]
    for i in range(1, cols):
        norm_total = norm_total + small_sums[i, 9]
    if whole_state:
        state_sums = jnp.sum(small_sums[:, 10:15, :state_all], axis=0)
        state_first = col * state_width
    else:
        half_at = col * state_width // state_part
        state_sums = lax.dynamic_index_in_dim(small_sums, half_at, 0, keepdims=False)[10:15, :state_part]
        state_sums = state_sums + lax.dynamic_index_in_dim(
            small_sums, half_at + group, 0, keepdims=False
        )[10:15, :state_part]
        state_first = lax.rem(col * state_width, state_part)
    state_own = lax.dynamic_slice_in_dim(state_sums, state_first, state_width, axis=1)

    return (
        block_out,
        tokens_grad,
        norm_total,
        sum_gate,
        sum_value,
        sum_state,
        sum_step,
        wide[:4].T,
        wide[4],
        state_own[:4].T,
        state_own[4],
        head_own[0] * rate[:heads],
        skip_own,
        head_own[1],
        wide[5],
        sum_out,
    )


def solution(mesh):
    rows = P(("dp", "row", "col"), None)
    grid = P("row", "col")
    vec = P("col")
    taps = P("col", None)
    return jax.shard_map(
        per_device,
        mesh=mesh,
        in_specs=(
            rows, P(), grid, grid, grid, grid, taps, vec, taps, vec, vec, vec, vec, vec,
            P("col", "row"), rows,
        ),
        out_specs=(
            rows, rows, P(), grid, grid, grid, grid, taps, vec, taps, vec, vec, vec, vec, vec,
            P("col", "row"),
        ),
        check_vma=False,
    )
```

```python
from functools import partial

import jax
import jax.numpy as jnp
import numpy as np
from jax import lax
from jax.experimental import pallas as pl
from jax.experimental.pallas import tpu as pltpu
from jax.sharding import PartitionSpec as P

BF = jnp.bfloat16
F32 = jnp.float32
EPSILON = 1e-05
N = 128
Q = 128
HEAD = 64
HALO = 16
ROWS = 64
TILE = 256
HIGHEST = lax.Precision.HIGHEST
VMEM_LIMIT = 56 * 2**20


def mm(a, b):
    return lax.dot_general(a, b, (((1,), (0,)), ((), ())), preferred_element_type=F32)


def mm_nt(a, b):
    return lax.dot_general(a, b, (((1,), (1,)), ((), ())), preferred_element_type=F32)


def mm_exact(a, b):
    return lax.dot_general(
        a, b, (((1,), (0,)), ((), ())), precision=HIGHEST, preferred_element_type=F32
    )


def split2(values):
    high = values.astype(BF)
    return high, (values - high.astype(F32)).astype(BF)


def sigmoid(values):
    return 1.0 / (1.0 + jnp.exp(-values))


def iota2(shape, axis):
    return lax.broadcasted_iota(jnp.int32, shape, axis)


def params(*names):
    return pltpu.CompilerParams(
        dimension_semantics=names or ("arbitrary",), vmem_limit_bytes=VMEM_LIMIT
    )


def cost(micros):
    return pl.CostEstimate(flops=0, bytes_accessed=int(micros * 3.0e6), transcendentals=0)


def whole(shape):
    return pl.BlockSpec(shape, lambda *_: (0,) * len(shape))


def columns(rows, width=TILE):
    return pl.BlockSpec((rows, width), lambda j: (0, j))


def sds(shape, dtype=F32):
    return jax.ShapeDtypeStruct(shape, dtype)


def here():
    return lax.axis_index("dp"), lax.axis_index("row"), lax.axis_index("col")


def lanes_at(index, size):
    return pl.ds(pl.multiple_of(index * size, 128), size)


def greet(others):
    barrier = pltpu.get_barrier_semaphore()
    for other in others:
        pl.semaphore_signal(barrier, inc=1, device_id=other, device_id_type=pl.DeviceIdType.MESH)
    pl.semaphore_wait(barrier, len(others))


def at_step(step):
    return pl.when(pl.program_id(0) == step)


def copy_to(src, dst, sems, i, device):
    return pltpu.make_async_remote_copy(
        src_ref=src, dst_ref=dst, send_sem=sems.at[0, i], recv_sem=sems.at[1, i],
        device_id=device, device_id_type=pl.DeviceIdType.MESH,
    )


def dp_copies(dps, sems, src_of, dst_of, first=0):
    dp, row, col = here()
    return [
        copy_to(src_of(dp ^ by, by - 1), dst_of(dp ^ by, by - 1), sems, first + by - 1, (dp ^ by, row, col))
        for by in range(1, dps)
    ]


def hand_out(dps, sems, first, src, out):
    dp, row, col = here()
    piece, lanes = src.shape
    rows = lambda d: pl.ds(d * piece, piece)
    if dps != 4:
        return dp_copies(dps, sems, lambda to, i: src, lambda to, i: out.at[rows(dp), :], first), []
    near = [
        copy_to(src, out.at[rows(dp), :], sems, first + i, (dp ^ by, row, col)) for i, by in enumerate((1, 2))
    ]
    far = []
    for i, by in enumerate((1, 2)):
        passed = out.at[pl.ds((dp ^ by) * piece + i * (piece // 2), piece // 2), :]
        far.append(copy_to(passed, passed, sems, first + 2 + i, (dp ^ 3 ^ by, row, col)))
    return near, far


def dp_peers(dps):
    dp, row, col = here()
    return [(dp ^ by, row, col) for by in range(1, dps)]


def mirror_of(cols):
    dp, row, col = here()
    return (dp, row, cols - 1 - col)


def remote_params(collective_id):
    return pltpu.CompilerParams(
        dimension_semantics=("arbitrary",), vmem_limit_bytes=VMEM_LIMIT, collective_id=collective_id,
        has_side_effects=True,
    )


ANY = pl.BlockSpec(memory_space=pl.ANY)


def import_kernel(
    cols, dps, tok, wv, sw, vec, tg, vf, sf, vecs, zeros, tok_vm, w_vm, s_vm, vec_vm, local, send, recv,
):
    dp, row, col = here()
    group = cols // 2
    place = lax.rem(col, group)
    half, shard = wv.shape
    count = tok.shape[0]
    piece = half // dps
    sibling = (dp, 1 - row, col)
    mirror = (dp, row, cols - 1 - col)
    col_peer = lambda by: (dp, row, col ^ by)
    dp_peer = lambda by: (dp ^ by, row, col)
    greet(
        [sibling]
        + [col_peer(by) for by in range(1, cols)]
        + [dp_peer(by) for by in range(1, dps)]
    )
    used = [0]
    started = []

    def remote(src, dst, device):
        i = used[0]
        used[0] += 1
        return pltpu.make_async_remote_copy(
            src_ref=src, dst_ref=dst, send_sem=send.at[i], recv_sem=recv.at[i],
            device_id=device, device_id_type=pl.DeviceIdType.MESH,
        )

    def launch(src, dst, device):
        copy = remote(src, dst, device)
        copy.start()
        started.append(copy)
        return copy

    def keep(i, src, dst):
        copy = pltpu.make_async_copy(src, dst, local.at[i])
        copy.start()
        return copy

    my_rows = pl.ds(row * half, half)
    my_piece = pl.ds(row * half + dp * piece, piece)
    own, other = pl.ds(0, shard), pl.ds(shard, shard)
    src_piece = pl.ds(dp * piece, piece)

    staged = [
        keep(6, vec, vec_vm),
        keep(0, sw.at[src_piece, :], s_vm),
        keep(2, tok, tok_vm),
        keep(3, wv, w_vm),
    ]
    s_cross = [
        launch(sw.at[src_piece, :], sf.at[my_piece, lanes_at(col, 128)], col_peer(by))
        for by in range(1, cols)
    ]
    v_cross = launch(wv.at[src_piece, :], vf.at[my_piece, other], mirror)
    vec_cross = [launch(vec, vecs.at[col], col_peer(by)) for by in range(1, cols)]
    my_tokens = tg.at[pl.ds(HALO + place * count, count), :]
    tok_cross = [launch(tok, my_tokens, col_peer(by)) for by in range(1, group)]
    halo_src = tok.at[pl.ds(count - HALO, HALO), :]
    halo_dst = tg.at[pl.ds(0, HALO), :]
    halo_at = used[0]
    used[0] += group
    halos = [
        pltpu.make_async_remote_copy(
            src_ref=halo_src, dst_ref=halo_dst, send_sem=send.at[halo_at + j], recv_sem=recv.at[halo_at],
            device_id=(dp, row, group + j), device_id_type=pl.DeviceIdType.MESH,
        )
        for j in range(group)
    ]

    @pl.when(col == group - 1)
    def _():
        for copy in halos:
            copy.start()

    zeros[...] = jnp.zeros_like(zeros)

    @pl.when(col < group)
    def _():
        clear = pltpu.make_async_copy(zeros, halo_dst, local.at[1])
        clear.start()
        clear.wait()

    v_own = launch(wv, vf.at[my_rows, own], sibling)
    for copy in staged:
        copy.wait()
    small_own = keep(0, s_vm, sf.at[my_piece, lanes_at(col, 128)])
    kept = [
        keep(6, vec_vm, vecs.at[col]),
        keep(2, tok_vm, my_tokens),
        keep(3, w_vm, vf.at[my_rows, own]),
    ]

    def spread_out(ref):
        return [launch(ref, ref, dp_peer(by)) for by in range(1, dps)]

    def arrive(copies):
        for copy in copies:
            copy.wait_recv()

    arrive(s_cross)
    small_own.wait()
    s_dp = spread_out(sf.at[my_piece, :])
    arrive([v_cross])
    v_dp = spread_out(vf.at[my_piece, other])
    arrive(s_dp)
    last = [launch(sf.at[my_rows, :], sf.at[my_rows, :], sibling)]
    arrive(v_dp)
    last += [launch(vf.at[my_rows, other], vf.at[my_rows, other], sibling)]
    arrive(last)
    arrive([v_own])
    arrive(vec_cross)
    arrive(tok_cross)

    @pl.when(col >= group)
    def _():
        halos[0].wait_recv()

    @pl.when(col == group - 1)
    def _():
        for copy in halos:
            copy.wait_send()

    for copy in kept:
        copy.wait()
    for copy in started:
        copy.wait_send()


def import_all(cols, dps, tokens, w_value, small, vec):
    half, shard = w_value.shape
    count, width = tokens.shape
    any_spec = pl.BlockSpec(memory_space=pl.ANY)
    copies = 1 + 2 * (cols - 1) + (cols // 2 - 1) + cols // 2 + 1 + 2 * (dps - 1) + 2
    return pl.pallas_call(
        partial(import_kernel, cols, dps),
        in_specs=[any_spec] * 4,
        out_specs=[any_spec] * 4,
        out_shape=[
            sds((HALO + count * (cols // 2), width), BF),
            sds((2 * half, 2 * shard), BF),
            sds((2 * half, cols * 128), BF),
            sds((cols,) + vec.shape, BF),
        ],
        scratch_shapes=[
            pltpu.VMEM((HALO, width), BF),
            pltpu.VMEM((count, width), BF),
            pltpu.VMEM((half, shard), BF),
            pltpu.VMEM((half // dps, 128), BF),
            pltpu.VMEM(vec.shape, BF),
            pltpu.SemaphoreType.DMA((7,)),
            pltpu.SemaphoreType.DMA((copies,)),
            pltpu.SemaphoreType.DMA((copies,)),
        ],
        compiler_params=pltpu.CompilerParams(
            collective_id=1, has_side_effects=True, vmem_limit_bytes=VMEM_LIMIT
        ),
        cost_estimate=cost(45),
        name="import_all",
    )(tokens, w_value, small, vec)


def conv_window(raw_ref, start, size):
    window = raw_ref[HALO + start - 8 : HALO + start + size, :]
    return [pltpu.roll(window, 3 - k, 0)[8:, :] for k in range(3)] + [window[8:, :]]


def conv_rows(moved, taps):
    total = taps[4:5, :] + taps[0:1, :] * moved[0]
    for k in range(1, 4):
        total = total + taps[k : k + 1, :] * moved[k]
    return total


def normalize(tok_ref, gain_ref, normed_ref, inv_ref):
    tokens = tok_ref.shape[0] - HALO
    for at in [0] + list(range(HALO, HALO + tokens, Q)):
        size = HALO if at == 0 else Q
        values = tok_ref[at : at + size, :].astype(F32)
        inv = lax.rsqrt(jnp.mean(values * values, axis=-1, keepdims=True) + EPSILON)
        normed_ref[at : at + size, :] = (values * inv * gain_ref[0:1, :]).astype(BF)
        inv_ref[at : at + size, :] = jnp.broadcast_to(inv, (size, 128))


def project_steps(
    small_ref, pick_ref, head_ref, normed_ref, raw_ref, stepin_ref, step_ref, cum_ref, grow_ref, offs_ref,
    picked_ref,
):
    tokens = step_ref.shape[0]
    picked = mm(small_ref[...], pick_ref[...]).astype(BF)
    picked_ref[...] = picked
    raw_ref[...] = mm(normed_ref[...], picked[:, :TILE])
    step_in = mm(normed_ref[HALO:, :], picked[:, TILE:]) + head_ref[0:1, :]
    small = jnp.exp(-jnp.abs(step_in))
    plus = 1.0 + small
    safe = jnp.where(plus == 1.0, 1.0, plus - 1.0)
    log_part = jnp.where(plus == 1.0, small, jnp.log(plus) * (small / safe))
    step = jnp.maximum(step_in, 0.0) + log_part
    stepin_ref[...] = step_in
    step_ref[...] = step
    falls = step * head_ref[1:2, :]
    lower = (iota2((Q, Q), 0) >= iota2((Q, Q), 1)).astype(F32)
    before = jnp.zeros((1, 128), F32)
    offs_ref[...] = jnp.zeros_like(offs_ref)
    for b in range(tokens // Q):
        rows = slice(b * Q, b * Q + Q)
        cum = mm_exact(lower, falls[rows, :])
        cum_ref[rows, :] = cum
        high, low = split2(jnp.exp(cum + before))
        grow_ref[rows, 0:128] = high
        grow_ref[rows, 128:256] = low
        before = before + cum[Q - 1 : Q, :]
        offs_ref[b + 1 : b + 2, :] = before


def activate(raw_ref, taps, act_ref, copy_ref):
    tokens = act_ref.shape[0]
    for at in range(0, tokens, ROWS):
        pre = conv_rows(conv_window(raw_ref, at, ROWS), taps)
        act = (pre * sigmoid(pre)).astype(BF)
        act_ref[at : at + ROWS, :] = act
        copy_ref[at : at + ROWS, :] = act


def expand(per_head, spread):
    high, low = split2(per_head)
    return mm(jnp.concatenate([high, low], 1), spread)


def transpose_bf(values):
    return values.astype(F32).T.astype(BF)


def expand_rows(per_head, spread):
    high, low = split2(jnp.concatenate(per_head, 0))
    return mm(jnp.concatenate([high, low], 1), spread)


def eight(row):
    return jnp.broadcast_to(row, (8, row.shape[1]))


def spans(total, size):
    size = min(size, total)
    return [slice(at, at + size) for at in range(0, total, size)]


def state_block(x_ref, b_ref, step_ref, cum_ref, spread_ref, held):
    cum = cum_ref[...]
    end = cum[Q - 1 : Q, :]
    tail = jnp.exp(end - cum) * step_ref[...]
    b_t = transpose_bf(b_ref[...])
    b_t2 = jnp.concatenate([b_t, b_t], 1)
    for lanes in spans(x_ref.shape[1], 1536):
        wide = expand_rows([tail, eight(jnp.exp(end))], spread_ref[:, lanes])
        high, low = split2(wide[:Q] * x_ref[:, lanes].astype(F32))
        fresh = mm(b_t2, jnp.concatenate([high, low], 0))
        held[:, lanes] = held[:, lanes] * wide[Q : Q + 1, :] + fresh


def forward_block(x_ref, b_ref, c_ref, step_ref, cum_ref, spread_ref, state_ref, y_ref):
    b_blk, c_blk = b_ref[...], c_ref[...]
    affinity = mm_nt(c_blk, b_blk)
    causal = iota2((Q, Q), 0) >= iota2((Q, Q), 1)
    first = iota2((Q, 128), 1) < HEAD
    cum = cum_ref[...]
    cum_t = cum.T
    step_t = step_ref[...].T
    growth = jnp.exp(cum)
    c2 = jnp.concatenate([c_blk, c_blk], 1)
    zero = jnp.zeros((Q, 128), BF)
    for lanes in spans(x_ref.shape[1], 1536):
        s_high, s_low = split2(state_ref[0, :, lanes])
        reached = mm(c2, jnp.concatenate([s_high, s_low], 0)) * expand_rows([growth], spread_ref[:, lanes])
        for at in range(lanes.start, lanes.stop, 128):
            x_pair = x_ref[:, at : at + 128]
            x0, x1 = jnp.where(first, x_pair, zero), jnp.where(first, zero, x_pair)
            pieces = []
            for half in range(2):
                h = at // HEAD + half
                spread_h = cum[:, h : h + 1] - cum_t[h : h + 1, :]
                decay = jnp.exp(jnp.where(causal, spread_h, -1e30))
                pieces += split2(affinity * decay * step_t[h : h + 1, :])
            intra = mm(jnp.concatenate(pieces, 1), jnp.concatenate([x0, x0, x1, x1], 0))
            inside = at - lanes.start
            y_ref[:, at : at + 128] = intra + reached[:, inside : inside + 128]


def forward_all_kernel(
    cols, dps,
    tok_ref, gain_ref, w_ref, small_ref, pick_ref, taps_ref, head_ref, spread_ref, cot, wg, wo,
    raw_ref, act_ref, normed_ref, stepin_ref, step_ref, cum_ref, grow_ref, offs_ref, inv_ref, picked_ref,
    states_ref, y_ref, graw_ref, gm_ref, early_ref, cot_out, gf, of,
    act_vm, states_vm, held, early_land, cot_vm, g_tiles, o_tiles, wg_vm, wo_vm, sems, local,
):
    step = pl.program_id(0)
    tokens, channels = states_vm.shape[0] * Q, held.shape[1]
    blocks = states_vm.shape[0]
    tiles = channels // TILE
    scan_at = tiles + 1
    out_at = scan_at + blocks
    gate_at = out_at + blocks
    dp, row, col = here()
    group = cols // 2
    place = lax.rem(col, group)
    half, shard = wg.shape
    count = cot.shape[0]
    others = dps - 1
    piece, piece_out = half // dps, wo.shape[0] // dps
    sibling, mirror = (dp, 1 - row, col), mirror_of(cols)
    peers = [(dp, row, col ^ by) for by in range(1, group)]
    my_rows = pl.ds(row * half, half)
    my_piece = pl.ds(row * half + dp * piece, piece)
    out_piece = pl.ds(shard + dp * piece_out, piece_out)
    my_lanes = lanes_at(row, half)
    own, other = pl.ds(0, shard), pl.ds(shard, shard)
    src_piece, src_out = pl.ds(dp * piece, piece), pl.ds(dp * piece_out, piece_out)
    my_cot = cot_vm.at[pl.ds(place * count, count), :]

    g_cross = lambda: copy_to(wg.at[src_piece, :], gf.at[my_piece, other], sems, 0, mirror)
    o_cross = lambda: copy_to(wo.at[src_out, :], of.at[out_piece, my_lanes], sems, 1, mirror)
    g_own = lambda: copy_to(wg, gf.at[my_rows, own], sems, 2, sibling)
    o_own = lambda: copy_to(wo, of.at[own, my_lanes], sems, 3, sibling)
    g_rest = lambda: copy_to(gf.at[my_rows, other], gf.at[my_rows, other], sems, 4, sibling)
    o_rest = lambda: copy_to(of.at[other, my_lanes], of.at[other, my_lanes], sems, 5, sibling)
    early_moves = lambda: [
        copy_to(held.at[:, own], early_land.at[:, other], sems, 6, mirror),
        copy_to(held.at[:, other], early_land.at[:, own], sems, 7, mirror),
    ]
    cot_moves = lambda: [copy_to(cot, my_cot, sems, 8 + i, peer) for i, peer in enumerate(peers)]
    first = 8 + group - 1

    def g_dp():
        ref = gf.at[my_piece, other]
        return dp_copies(dps, sems, lambda to, i: ref, lambda to, i: ref, first)

    def o_dp():
        ref = of.at[out_piece, my_lanes]
        return dp_copies(dps, sems, lambda to, i: ref, lambda to, i: ref, first + others)

    load_cot = pltpu.make_async_copy(cot, my_cot, local.at[0])
    load_g = pltpu.make_async_copy(wg, wg_vm, local.at[1])
    load_o = pltpu.make_async_copy(wo, wo_vm, local.at[2])
    store_g = pltpu.make_async_copy(wg_vm, gf.at[my_rows, own], local.at[1])
    store_o = pltpu.make_async_copy(wo_vm, of.at[own, my_lanes], local.at[2])
    store_cot = pltpu.make_async_copy(cot_vm, cot_out, local.at[0])

    def g_tile(at):
        return pltpu.make_async_copy(gf.at[:, lanes_at(at, TILE)], g_tiles.at[lax.rem(at, 2)], local.at[3])

    def o_tile(at):
        rows = pl.ds(pl.multiple_of(at * TILE, TILE), TILE)
        return pltpu.make_async_copy(of.at[rows, :], o_tiles.at[lax.rem(at, 2)], local.at[4])

    @at_step(0)
    def _():
        load_cot.start()
        load_g.start()
        load_o.start()
        greet([sibling, mirror] + peers + dp_peers(dps))
        for move in [g_cross(), o_cross(), g_own(), o_own()]:
            move.start()
        normalize(tok_ref, gain_ref, normed_ref, inv_ref)

    @at_step(1)
    def _():
        load_g.wait()
        store_g.start()
        load_o.wait()
        store_o.start()

    @at_step(tiles - 2)
    def _():
        for move in cot_moves():
            move.start()

    @at_step(scan_at + 2)
    def _():
        g_cross().wait_recv()
        for move in g_dp():
            move.start()

    @at_step(out_at)
    def _():
        o_cross().wait_recv()
        for move in o_dp():
            move.start()

    @at_step(out_at + blocks // 2)
    def _():
        for move in g_dp():
            move.wait_recv()
        g_rest().start()

    @at_step(gate_at + tiles // 2)
    def _():
        for move in o_dp():
            move.wait_recv()
        o_rest().start()

    @at_step(out_at)
    def _():
        @pl.when(col < group)
        def _():
            for move in early_moves():
                move.start()

    @pl.when(step < tiles)
    def _():
        raw_ref[...] = mm(normed_ref[...], w_ref[...])

    @pl.when(step == tiles)
    def _():
        project_steps(
            small_ref, pick_ref, head_ref, normed_ref, raw_ref, stepin_ref, step_ref, cum_ref, grow_ref, offs_ref,
            picked_ref,
        )

    @pl.when(step <= tiles)
    def _():
        activate(raw_ref, taps_ref[...], act_ref, act_vm.at[:, lanes_at(step, TILE)])

    def block_refs(at):
        rows = pl.ds(pl.multiple_of(at * Q, Q), Q)
        return (
            act_vm.at[rows, pl.ds(0, channels)], act_vm.at[rows, pl.ds(channels, N)],
            act_vm.at[rows, pl.ds(channels + N, N)], step_ref.at[rows, :], cum_ref.at[rows, :],
        )

    @pl.when(step == scan_at)
    def _():
        held[...] = jnp.zeros_like(held)

    @pl.when((step >= scan_at) & (step < out_at))
    def _():
        x_blk, b_blk, _, step_blk, cum_blk = block_refs(step - scan_at)
        states_ref[0] = held[...]
        states_vm[step - scan_at] = held[...]
        state_block(x_blk, b_blk, step_blk, cum_blk, spread_ref, held)

    @pl.when(step == out_at)
    def _():
        states_ref[0] = held[...]

    @pl.when((step >= out_at) & (step < gate_at))
    def _():
        x_blk, b_blk, c_blk, step_blk, cum_blk = block_refs(step - out_at)
        forward_block(
            x_blk, b_blk, c_blk, step_blk, cum_blk, spread_ref, states_vm.at[pl.ds(step - out_at, 1)], y_ref
        )

    @pl.when(step == gate_at)
    def _():
        for move in [g_own(), g_rest()]:
            move.wait_recv()
        store_g.wait()
        g_tile(0).start()

    @pl.when((step >= gate_at) & (step < gate_at + tiles))
    def _():
        at = step - gate_at
        g_tile(at).wait()

        @pl.when(at < tiles - 1)
        def _():
            g_tile(at + 1).start()

        graw_ref[...] = mm(normed_ref[HALO:, :], g_tiles[lax.rem(at, 2)])

    @pl.when(step == gate_at + tiles)
    def _():
        for move in [o_own(), o_rest()] + cot_moves():
            move.wait_recv()
        store_o.wait()
        load_cot.wait()
        store_cot.start()
        o_tile(0).start()

    @pl.when(step >= gate_at + tiles)
    def _():
        at = step - gate_at - tiles
        o_tile(at).wait()

        @pl.when(at < tiles - 1)
        def _():
            o_tile(at + 1).start()

        gm_ref[...] = mm_nt(cot_vm[...], o_tiles[lax.rem(at, 2)])

    @at_step(pl.num_programs(0) - 1)
    def _():
        store_cot.wait()
        for move in [g_cross(), o_cross(), g_own(), o_own(), g_rest(), o_rest()] + cot_moves() + g_dp() + o_dp():
            move.wait_send()

        @pl.when(col < group)
        def _():
            for move in early_moves():
                move.wait_send()
            early_ref[...] = jnp.zeros_like(early_ref)

        @pl.when(col >= group)
        def _():
            for move in early_moves():
                move.wait_recv()
            early_ref[...] = early_land[...]


def forward_all(cols, dps, group_tokens, gain, weights, small, pick, taps, head_rows, spread, cotangent, w_gate, w_out):
    rows, width = group_tokens.shape
    tokens = rows - HALO
    channels = weights.shape[1]
    total = channels + TILE
    blocks, tiles = tokens // Q, channels // TILE
    half, shard = w_gate.shape
    scan_at = tiles + 1
    out_at = scan_at + blocks
    gate_at = out_at + blocks

    def clamp(first, count):
        return lambda i: jnp.clip(i - first, 0, count - 1)

    lanes = lambda at, count: pl.BlockSpec((count, TILE), lambda i: (0, at(i)))
    both, value_at = clamp(0, tiles + 1), clamp(0, tiles)
    state_at, y_at = clamp(scan_at, blocks + 1), clamp(out_at, blocks)
    raw_tile, gm_tile = clamp(gate_at, tiles), clamp(gate_at + tiles, tiles)
    vmem = pltpu.VMEM
    return pl.pallas_call(
        partial(forward_all_kernel, cols, dps),
        grid=(gate_at + 2 * tiles,),
        in_specs=[
            whole((rows, width)),
            whole((1, width)),
            lanes(value_at, width),
            whole(small.shape),
            whole(pick.shape),
            lanes(both, 8),
            whole((8, 128)),
            whole(spread.shape),
            ANY, ANY, ANY,
        ],
        out_specs=[
            lanes(both, rows),
            lanes(both, tokens),
            whole((rows, width)),
            whole((tokens, 128)),
            whole((tokens, 128)),
            whole((tokens, 128)),
            whole((tokens, 256)),
            whole((16, 128)),
            whole((rows, 128)),
            whole((width, TILE + 128)),
            pl.BlockSpec((1, N, channels), lambda i: (state_at(i), 0, 0)),
            pl.BlockSpec((Q, channels), lambda i: (y_at(i), 0)),
            lanes(raw_tile, tokens),
            lanes(gm_tile, tokens),
            whole((N, channels)),
            ANY, ANY, ANY,
        ],
        out_shape=[
            sds((rows, total)),
            sds((tokens, total), BF),
            sds((rows, width), BF),
            sds((tokens, 128)),
            sds((tokens, 128)),
            sds((tokens, 128)),
            sds((tokens, 256), BF),
            sds((16, 128)),
            sds((rows, 128)),
            sds((width, TILE + 128), BF),
            sds((blocks + 1, N, channels)),
            sds((tokens, channels)),
            sds((tokens, channels)),
            sds((tokens, channels)),
            sds((N, channels)),
            sds((tokens, width), BF),
            sds((width, channels), BF),
            sds((channels, width), BF),
        ],
        scratch_shapes=[
            vmem((tokens, total), BF),
            vmem((blocks, N, channels), F32),
            vmem((N, channels), F32),
            vmem((N, channels), F32),
            vmem((tokens, width), BF),
            vmem((2, width, TILE), BF),
            vmem((2, TILE, width), BF),
            vmem((half, shard), BF),
            vmem((shard, half), BF),
            pltpu.SemaphoreType.DMA((2, 7 + cols // 2 + 2 * (dps - 1))),
            pltpu.SemaphoreType.DMA((5,)),
        ],
        compiler_params=remote_params(4),
        cost_estimate=cost(70),
        name="forward_all",
    )(group_tokens, gain, weights, small, pick, taps, head_rows, spread, cotangent, w_gate, w_out)


def grad_state_block(dy_tiles, c_ref, cum_ref, spread_ref, after_ref, held):
    after_ref[0] = held[...]
    growth = jnp.exp(cum_ref[...])
    c_t = transpose_bf(c_ref[...])
    c_t2 = jnp.concatenate([c_t, c_t], 1)
    wide = expand_rows([growth], spread_ref[...])
    for tile in range(held.shape[1] // TILE):
        lanes = slice(tile * TILE, tile * TILE + TILE)
        high, low = split2(dy_tiles[tile] * wide[:, lanes])
        direct = mm(c_t2, jnp.concatenate([high, low], 0))
        held[:, lanes] = held[:, lanes] * wide[Q - 1 : Q, lanes] + direct


def near_block(
    at_block, here_rows, dy_ref, x_ref, b_ref, c_ref, step_ref, cum_ref, spread_ref, state_ref, early_ref,
    offs_ref, gx_ref, gbc_ref,
):
    b_blk, c_blk = b_ref[...], c_ref[...]
    affinity_t = mm_nt(b_blk, c_blk)
    causal_t = iota2((Q, Q), 1) >= iota2((Q, Q), 0)
    first = iota2((Q, 128), 1) < HEAD
    cum = cum_ref[...]
    cum_t = cum.T
    step = step_ref[...]
    growth = jnp.exp(cum)
    early_fall = eight(jnp.exp(offs_ref[pl.ds(at_block, 1), :]))
    zero = jnp.zeros((Q, 128), BF)
    grad_affinity_t = jnp.zeros((Q, Q), F32)
    grad_c = jnp.zeros((Q, N), F32)
    for lanes in spans(x_ref.shape[1], 768):
        wide = expand_rows([growth, early_fall], spread_ref[:, lanes])
        before = state_ref[0, :, lanes] + wide[Q : Q + 1, :] * early_ref[:, lanes]
        dy_wide = dy_ref[:, lanes]
        s_high, s_low = split2(before)
        g_high, g_low = split2(dy_wide * wide[:Q])
        grad_c = grad_c + mm_nt(
            jnp.concatenate([g_high, g_low, g_high], 1), jnp.concatenate([s_high, s_high, s_low], 1)
        )
        for at in range(lanes.start, lanes.stop, 128):
            d_high, d_low = split2(dy_ref[:, at : at + 128])
            x_pair = x_ref[:, at : at + 128]
            x0, x1 = jnp.where(first, x_pair, zero), jnp.where(first, zero, x_pair)
            grad_mixing = mm_nt(
                jnp.concatenate([jnp.concatenate([x0, x0], 1), jnp.concatenate([x1, x1], 1)], 0),
                jnp.concatenate([d_high, d_low], 1),
            )
            left, right = [], []
            for half in range(2):
                h = at // HEAD + half
                spread_h = cum_t[h : h + 1, :] - cum[:, h : h + 1]
                decay = jnp.exp(jnp.where(causal_t, spread_h, -1e30))
                m_high, m_low = split2(affinity_t * decay)
                grad_affinity_t = grad_affinity_t + (
                    grad_mixing[half * Q : half * Q + Q, :] * decay * step[:, h : h + 1]
                )
                keep = first if half == 0 else jnp.logical_not(first)
                dh, dl = jnp.where(keep, d_high, zero), jnp.where(keep, d_low, zero)
                left += [m_high, m_low, m_high]
                right += [dh, dh, dl]
            gx_ref[here_rows, at : at + 128] = mm(jnp.concatenate(left, 1), jnp.concatenate(right, 0))
    a_high, a_low = split2(grad_affinity_t)
    gbc_ref[here_rows, 0:N] = mm(jnp.concatenate([a_high, a_low], 1), jnp.concatenate([c_blk, c_blk], 0))
    t_high, t_low = split2(grad_affinity_t.T)
    gbc_ref[here_rows, N : 2 * N] = grad_c + mm(
        jnp.concatenate([t_high, t_low], 1), jnp.concatenate([b_blk, b_blk], 0)
    )


def far_block(
    blocks, at_block, here_rows, dy_ref, x_ref, y_ref, gx_ref, b_ref, step_ref, cum_ref, stepin_ref, spread_ref,
    gather_ref, after_ref, late_ref, state_ref, early_ref, offs_ref, head_ref, skip_ref, gbc_ref,
    ga_ref, gstep_ref, gbc_out_ref, sums_ref,
):
    b_blk = b_ref[...]
    b2 = jnp.concatenate([b_blk, b_blk], 1)
    cum, step = cum_ref[...], step_ref[...]
    tail = jnp.exp(cum[Q - 1 : Q, :] - cum)
    offs_after = offs_ref[pl.ds(at_block + 1, 1), :]
    late_fall = eight(jnp.exp(offs_ref[pl.ds(blocks, 1), :] - offs_after))
    early_fall = eight(jnp.exp(offs_after))
    dots = jnp.zeros((2 * Q + 8, 128), F32)
    grad_b = gbc_ref[here_rows, 0:N]
    for lanes in spans(x_ref.shape[1], 512):
        wide = expand_rows([tail, step, late_fall, early_fall], spread_ref[:, lanes])
        tail_wide, step_wide = wide[:Q], wide[Q : 2 * Q]
        x = x_ref[:, lanes].astype(F32)
        dy = dy_ref[:, lanes]
        skip = skip_ref[0:1, lanes]
        d_state = after_ref[0, :, lanes] + wide[2 * Q : 2 * Q + 1, :] * late_ref[:, lanes]
        state = state_ref[0, :, lanes] + wide[2 * Q + 8 : 2 * Q + 9, :] * early_ref[:, lanes]
        touch = eight(jnp.sum(d_state * state, axis=0, keepdims=True))
        s_high, s_low = split2(d_state)
        gx = gx_ref[here_rows, lanes] + tail_wide * mm(b2, jnp.concatenate([s_high, s_low], 0))
        w_high, w_low = split2(tail_wide * step_wide * x)
        grad_b = grad_b + mm_nt(
            jnp.concatenate([w_high, w_low, w_high], 1), jnp.concatenate([s_high, s_high, s_low], 1)
        )
        ga_ref[:, lanes] = step_wide * gx + skip * dy
        high, low = split2(jnp.concatenate([dy * (y_ref[:, lanes] - skip * x), x * gx, touch], 0))
        gather = gather_ref[lanes, :]
        dots = dots + mm(jnp.concatenate([high, low], 1), jnp.concatenate([gather, gather], 0))
    row_dots, col_dots, last_add = dots[:Q], dots[Q : 2 * Q], dots[2 * Q :]
    last_row = iota2((Q, 128), 0) == Q - 1
    grad_cum = row_dots - step * col_dots + jnp.where(last_row, last_add[0:1, :], 0.0)
    upper = (iota2((Q, Q), 1) >= iota2((Q, Q), 0)).astype(F32)
    grad_rate = mm_exact(upper, grad_cum)
    grad_step = col_dots + grad_rate * head_ref[1:2, :]
    grad_raw = grad_step * sigmoid(stepin_ref[...])
    gstep_ref[...] = grad_raw.astype(BF)
    sums_ref[0:1, :] += jnp.sum(grad_rate * step, axis=0, keepdims=True)
    sums_ref[1:2, :] += jnp.sum(grad_raw, axis=0, keepdims=True)
    gbc_out_ref[:, 0:N] = grad_b
    gbc_out_ref[:, N : 2 * N] = gbc_ref[here_rows, N : 2 * N]


WEIGHT_TILE = 384


def mm_tn(a, b):
    return lax.dot_general(a, b, (((0,), (0,)), ((), ())), preferred_element_type=F32)


def backward_kernel(
    cols, dps,
    dy_ref, x_ref, y_ref, b_ref, c_ref, step_ref, cum_ref, stepin_ref, spread_ref, gather_ref, after_ref,
    state_ref, early_ref, offs_ref, head_ref, skip_ref, mixed_ref, of_ref, gg_ref,
    first_grad, mixed_hbm, gg_hbm, cot, normed,
    ga_ref, gstep_ref, gbc_out_ref, sums_ref, o_total_ref, g_own_ref, g_cross_ref, branch_ref, branch_in,
    mixed_sib, gg_sib,
    gx_ref, gbc_ref, late_ref, o_low, o_own, o_land, o_cross, o_cross_land, g_low, g_own, g_land, parts,
    c_own, c_sib, n_own, n_sib, m_tiles, gg_tiles, sems, local,
):
    step_at = pl.program_id(0)
    blocks = gx_ref.shape[0] // Q
    dp, row, col = here()
    group = cols // 2
    place = lax.rem(col, group)
    shard, channels = g_own_ref.shape[1], gx_ref.shape[1]
    half = c_own.shape[1]
    count = branch_ref.shape[0]
    others = dps - 1
    own, other = pl.ds(0, shard), pl.ds(shard, shard)
    sibling, mirror = (dp, 1 - row, col), mirror_of(cols)
    peers = [(dp, row, col ^ by) for by in range(1, group)]
    out_steps, o_steps, g_steps = 2 * half // TILE, channels // WEIGHT_TILE, channels // TILE
    o_at = out_steps
    g_at = o_at + o_steps
    near_at = g_at + g_steps
    far_at = near_at + blocks
    last = far_at + blocks - 1

    def o_moves():
        return dp_copies(dps, sems, lambda to, i: o_low.at[:, to], lambda to, i: o_land.at[i])

    def g_moves():
        return dp_copies(dps, sems, lambda to, i: g_low.at[to], lambda to, i: g_land.at[i], others)

    at = 2 * others
    cross_move = lambda: copy_to(o_cross, o_cross_land, sems, at, mirror)
    late_moves = lambda: [
        copy_to(first_grad.at[:, own], late_ref.at[:, other], sems, at + 1, mirror),
        copy_to(first_grad.at[:, other], late_ref.at[:, own], sems, at + 2, mirror),
    ]
    core_moves = lambda: [
        copy_to(cot.at[:, lanes_at(1 - row, half)], c_sib, sems, at + 3, sibling),
        copy_to(mixed_hbm, mixed_sib, sems, at + 4, sibling),
        copy_to(normed.at[:, lanes_at(1 - row, half)], n_sib, sems, at + 5, sibling),
        copy_to(gg_hbm, gg_sib, sems, at + 6, sibling),
    ]
    part_moves = lambda: [
        copy_to(parts.at[i], branch_in.at[i], sems, at + 7 + i, peer) for i, peer in enumerate(peers)
    ]
    load_c = pltpu.make_async_copy(cot.at[:, lanes_at(row, half)], c_own, local.at[0])
    load_n = pltpu.make_async_copy(normed.at[:, lanes_at(row, half)], n_own, local.at[1])

    def m_tile(tile):
        lanes = lanes_at(tile, WEIGHT_TILE)
        return pltpu.make_async_copy(mixed_sib.at[:, lanes], m_tiles.at[lax.rem(tile, 2)], local.at[2])

    def gg_tile(tile):
        lanes = lanes_at(tile, TILE)
        return pltpu.make_async_copy(gg_sib.at[:, lanes], gg_tiles.at[lax.rem(tile, 2)], local.at[3])

    @at_step(0)
    def _():
        load_c.start()
        load_n.start()
        greet([sibling, mirror] + peers + dp_peers(dps))
        for move in core_moves():
            move.start()

        @pl.when(col >= group)
        def _():
            for move in late_moves():
                move.start()
            late_ref[...] = jnp.zeros_like(late_ref)

        sums_ref[...] = jnp.zeros_like(sums_ref)

    @pl.when(step_at < o_at)
    def _():
        rows = lambda index: pl.ds(pl.multiple_of(index * count, 128), count)
        branch_ref[...] = mm(mixed_ref[rows(place), :], of_ref[...])
        for by in range(1, group):
            parts[by - 1, :, lanes_at(step_at, TILE)] = mm(mixed_ref[rows(place ^ by), :], of_ref[...]).astype(BF)

    @pl.when(step_at == o_at)
    def _():
        load_c.wait()
        for move in core_moves()[:2]:
            move.wait_recv()
        m_tile(0).start()

    @pl.when((step_at >= o_at) & (step_at < g_at))
    def _():
        tile = step_at - o_at
        m_tile(tile).wait()

        @pl.when(tile < o_steps - 1)
        def _():
            m_tile(tile + 1).start()

        total = mm_tn(mixed_ref[:, lanes_at(tile, WEIGHT_TILE)], c_own[...])
        total = total + mm_tn(m_tiles[lax.rem(tile, 2)], c_sib[...])
        piece = o_own.shape[1]
        per, each = WEIGHT_TILE // piece, shard // WEIGHT_TILE
        which, inside = lax.div(tile, each), lax.rem(tile, each)
        for p in range(per):
            part = total[p * piece : p * piece + piece, :]
            o_low[which, inside * per + p] = part.astype(BF)

            @pl.when(dp == inside * per + p)
            def _():
                o_own[which] = part

    @pl.when(step_at == g_at)
    def _():
        for move in o_moves():
            move.start()
        load_n.wait()
        for move in core_moves()[2:]:
            move.wait_recv()
        gg_tile(0).start()

    @pl.when((step_at >= g_at) & (step_at < near_at))
    def _():
        tile = step_at - g_at
        gg_tile(tile).wait()

        @pl.when(tile < g_steps - 1)
        def _():
            gg_tile(tile + 1).start()

        lanes = lanes_at(tile, TILE)
        total = mm_tn(n_own[HALO:, :], gg_ref[...]) + mm_tn(n_sib[HALO:, :], gg_tiles[lax.rem(tile, 2)])
        piece = g_own.shape[0]
        for p in range(dps):
            part = total[p * piece : p * piece + piece, :]
            g_low[p, :, lanes] = part.astype(BF)

            @pl.when(dp == p)
            def _():
                g_own[:, lanes] = part

    at_block = lax.rem(jnp.maximum(step_at - near_at, 0), blocks)
    here_rows = pl.ds(pl.multiple_of(at_block * Q, Q), Q)

    @pl.when((step_at >= near_at) & (step_at < far_at))
    def _():
        near_block(
            at_block, here_rows, dy_ref, x_ref, b_ref, c_ref, step_ref, cum_ref, spread_ref, state_ref,
            early_ref, offs_ref, gx_ref, gbc_ref,
        )

    @pl.when(step_at == g_at)
    def _():
        for move in part_moves():
            move.start()

    @pl.when(step_at == near_at + blocks // 2 + 1)
    def _():
        for move in o_moves():
            move.wait_recv()
        for move in g_moves():
            move.start()
        for i in range(others):
            o_own[...] += o_land[i].astype(F32)
        o_cross[...] = o_own[1].astype(BF)
        cross_move().start()

    @pl.when(step_at == far_at)
    def _():
        @pl.when(col < group)
        def _():
            for move in late_moves():
                move.wait_recv()

    @pl.when(step_at >= far_at)
    def _():
        far_block(
            blocks, at_block, here_rows, dy_ref, x_ref, y_ref, gx_ref, b_ref, step_ref, cum_ref, stepin_ref,
            spread_ref, gather_ref, after_ref, late_ref, state_ref, early_ref, offs_ref, head_ref, skip_ref,
            gbc_ref, ga_ref, gstep_ref, gbc_out_ref, sums_ref,
        )

    @at_step(last)
    def _():
        cross_move().wait()
        o_total_ref[...] = o_own[0] + o_cross_land[...].astype(F32)
        for move in g_moves():
            move.wait()
        for i in range(others):
            g_own[...] += g_land[i].astype(F32)
        g_own_ref[...] = g_own[:, :shard]
        g_cross_ref[...] = g_own[:, shard:].astype(BF)
        for move in part_moves():
            move.wait()
        for move in o_moves() + core_moves():
            move.wait_send()

        @pl.when(col >= group)
        def _():
            for move in late_moves():
                move.wait_send()


def scan_backward(
    cols, dps, dy, act, y, step, cum, step_in, spread, gather, after, states, early, offs, head_rows, skip,
    mixed, w_out, gg, first_grad, cot, normed,
):
    tokens, channels = dy.shape
    rows_n, width = normed.shape
    half = width // 2
    blocks, group, shard = tokens // Q, cols // 2, channels // 2
    count = tokens // group
    piece_o, piece_g = shard // dps, half // dps
    out_steps, o_steps, g_steps = width // TILE, channels // WEIGHT_TILE, channels // TILE
    g_at = out_steps + o_steps
    near_at = g_at + g_steps
    far_at = near_at + blocks

    def clamp(first, size):
        return lambda i: jnp.clip(i - first, 0, size - 1)

    block = lambda i: jnp.where(i < near_at, 0, lax.rem(jnp.maximum(i - near_at, 0), blocks))
    second = clamp(far_at, blocks)
    state_at = lambda i: block(i) + jnp.where(i < far_at, 0, 1)
    rows = lambda at, size: pl.BlockSpec((Q, size), lambda i: (at(i), 0))
    lanes = lambda at, size: pl.BlockSpec((size, TILE), lambda i: (0, at(i)))
    once = lambda shape: pl.BlockSpec(shape, lambda *_: (0,) * len(shape), pipeline_mode=pl.Buffered(1))
    vmem = pltpu.VMEM
    dma = pltpu.SemaphoreType.DMA
    return pl.pallas_call(
        partial(backward_kernel, cols, dps),
        grid=(far_at + blocks,),
        in_specs=[
            rows(block, channels),
            rows(block, channels),
            rows(second, channels),
            pl.BlockSpec((Q, N), lambda i: (block(i), channels // N)),
            pl.BlockSpec((Q, N), lambda i: (block(i), channels // N + 1)),
            rows(block, 128),
            rows(block, 128),
            rows(second, 128),
            once(spread.shape),
            once(gather.shape),
            pl.BlockSpec((1, N, channels), lambda i: (second(i), 0, 0)),
            pl.BlockSpec((1, N, channels), lambda i: (state_at(i), 0, 0)),
            once(early.shape),
            once((16, 128)),
            once((8, 128)),
            once((8, channels)),
            once(mixed.shape),
            lanes(clamp(0, out_steps), channels),
            lanes(clamp(g_at, g_steps), tokens),
        ] + [ANY] * 5,
        out_specs=[
            rows(second, channels),
            rows(second, 128),
            rows(second, 2 * N),
            whole((8, 128)),
            whole((piece_o, half)),
            whole((piece_g, shard)),
            whole((piece_g, shard)),
            lanes(clamp(0, out_steps), count),
            ANY, ANY, ANY,
        ],
        out_shape=[
            sds((tokens, channels)),
            sds((tokens, 128), BF),
            sds((tokens, 2 * N)),
            sds((8, 128)),
            sds((piece_o, half)),
            sds((piece_g, shard)),
            sds((piece_g, shard), BF),
            sds((count, width)),
            sds((max(group - 1, 1), count, width), BF),
            sds(mixed.shape, BF),
            sds(gg.shape, BF),
        ],
        scratch_shapes=[
            vmem((tokens, channels), F32), vmem((tokens, 2 * N), F32), vmem((N, channels), F32),
            vmem((2, dps, piece_o, half), BF), vmem((2, piece_o, half), F32),
            vmem((dps - 1, 2, piece_o, half), BF), vmem((piece_o, half), BF), vmem((piece_o, half), BF),
            vmem((dps, piece_g, channels), BF), vmem((piece_g, channels), F32),
            vmem((dps - 1, piece_g, channels), BF),
            vmem((max(group - 1, 1), count, width), BF),
            vmem((tokens, half), BF), vmem((tokens, half), BF),
            vmem((rows_n, half), BF), vmem((rows_n, half), BF),
            vmem((2, tokens, WEIGHT_TILE), BF), vmem((2, tokens, TILE), BF),
            dma((2, 2 * (dps - 1) + 6 + group)),
            dma((4,)),
        ],
        compiler_params=remote_params(3),
        cost_estimate=cost(80),
        name="scan_backward",
    )(
        dy, act, y, act, act, step, cum, step_in, spread, gather, after, states, early, offs, head_rows, skip,
        mixed, w_out, gg, first_grad, mixed, gg, cot, normed,
    )


def gate_kernel(
    cols, inner_channels,
    y0_ref, graw_ref, gm_ref, x_ref, early_ref, c_ref, grow_ref, spread_ref, vec_ref,
    cum_ref, c_block_ref, spread_all_ref,
    y_ref, mixed_ref, gg_ref, dy_ref, sums_ref, after_ref, first_ref,
    y_vm, graw_vm, gm_vm, squares, inners, stats, stats_land, stats_col, held, sems,
):
    step = pl.program_id(0)
    tiles = y_vm.shape[0]
    tokens = y0_ref.shape[0]
    dp, row, col = here()
    group = cols // 2
    peers = [(dp, row, col ^ by) for by in range(1, group)]
    gain = vec_ref[1:2, :]
    nt = (((1,), (1,)), ((), ()))
    moves = lambda: [copy_to(stats, stats_land.at[i], sems, i, peer) for i, peer in enumerate(peers)]

    @at_step(0)
    def _():
        greet(peers)
        squares[...] = jnp.zeros_like(squares)
        inners[...] = jnp.zeros_like(inners)

    @pl.when(step < tiles)
    def _():
        s_high, s_low = split2(early_ref[...])
        s2 = jnp.concatenate([s_high, s_low], 0)
        spread = spread_ref[...]
        skip = vec_ref[0:1, :]
        for at in range(0, tokens, Q):
            rows = slice(at, at + Q)
            c_blk = c_ref[rows, :]
            carried = mm(jnp.concatenate([c_blk, c_blk], 1), s2) * mm(grow_ref[rows, :], spread)
            y = y0_ref[rows, :] + carried + skip * x_ref[rows, :].astype(F32)
            raw, gm = graw_ref[rows, :], gm_ref[rows, :]
            y_ref[rows, :] = y
            y_vm[step, rows, :] = y
            graw_vm[step, rows, :] = raw
            gm_vm[step, rows, :] = gm
            gated = y * raw * sigmoid(raw)
            square = gated * gated
            inner = gm * gain * gated
            squares[rows, :] += square[:, 0:128] + square[:, 128:256]
            inners[rows, :] += inner[:, 0:128] + inner[:, 128:256]

    @at_step(tiles - 1)
    def _():
        ones = jnp.ones((8, 128), F32)
        square_row = lax.dot_general(ones, squares[...], nt, precision=HIGHEST, preferred_element_type=F32)
        inner_row = lax.dot_general(ones, inners[...], nt, precision=HIGHEST, preferred_element_type=F32)
        stats[...] = jnp.where(iota2(square_row.shape, 0) == 0, square_row, inner_row)
        for move in moves():
            move.start()
        for move in moves():
            move.wait_recv()
        total = stats[...]
        for i in range(group - 1):
            total = total + stats_land[i]
        wide = jnp.concatenate([total, jnp.zeros((120, tokens), F32)], 0)
        stats_col[...] = wide.T

    @pl.when((step >= tiles) & (step < 2 * tiles))
    def _():
        tile = step - tiles
        gain_sum = jnp.zeros((1, TILE), F32)
        skip_sum = jnp.zeros((1, TILE), F32)
        for at in range(0, tokens, Q):
            rows = slice(at, at + Q)
            inv = lax.rsqrt(stats_col[rows, 0:1] * (1.0 / inner_channels) + EPSILON)
            pull = inv * inv * inv * (stats_col[rows, 1:2] * (1.0 / inner_channels))
            raw, y, gm = graw_vm[tile, rows, :], y_vm[tile, rows, :], gm_vm[tile, rows, :]
            sig = sigmoid(raw)
            act = raw * sig
            gated = y * act
            unit = gated * inv
            mixed_ref[rows, :] = (unit * gain).astype(BF)
            gain_sum = gain_sum + jnp.sum(gm * unit, axis=0, keepdims=True)
            grad_gated = inv * (gm * gain) - gated * pull
            dy = grad_gated * act
            dy_ref[rows, :] = dy
            y_vm[tile, rows, :] = dy
            gg_ref[rows, :] = (grad_gated * y * (sig * (1.0 + raw * (1.0 - sig)))).astype(BF)
            skip_sum = skip_sum + jnp.sum(dy * x_ref[rows, :].astype(F32), axis=0, keepdims=True)
        sums_ref[...] = jnp.zeros_like(sums_ref)
        sums_ref[0:1, :] = gain_sum
        sums_ref[1:2, :] = skip_sum

    @pl.when(step == 2 * tiles)
    def _():
        for move in moves():
            move.wait_send()
        held[...] = jnp.zeros_like(held)

    @pl.when(step >= 2 * tiles)
    def _():
        at = pl.num_programs(0) - 1 - step
        rows = pl.ds(pl.multiple_of(at * Q, Q), Q)
        grad_state_block(y_vm.at[:, rows, :], c_block_ref, cum_ref, spread_all_ref, after_ref, held)
        first_ref[...] = held[...]


def gate_and_mix(cols, inner_channels, y0, graw, gm, act, early, grow, spread, vectors, cum):
    tokens, channels = y0.shape
    blocks = tokens // Q
    tiles, group = channels // TILE, cols // 2
    first = lambda i: jnp.minimum(i, tiles - 1)
    second = lambda i: jnp.clip(i - tiles, 0, tiles - 1)
    either = lambda i: jnp.where(i < 2 * tiles, lax.rem(i, tiles), tiles - 1)
    third = lambda i: blocks - 1 - jnp.maximum(i - 2 * tiles, 0)
    lanes = lambda at, count: pl.BlockSpec((count, TILE), lambda i: (0, at(i)))
    vmem = pltpu.VMEM
    return pl.pallas_call(
        partial(gate_kernel, cols, inner_channels),
        grid=(2 * tiles + blocks,),
        in_specs=[
            lanes(first, tokens), lanes(first, tokens), lanes(first, tokens), lanes(either, tokens),
            lanes(first, N),
            pl.BlockSpec((tokens, N), lambda i: (0, channels // N + 1)),
            whole((tokens, 256)),
            lanes(first, 256),
            lanes(either, 8),
            pl.BlockSpec((Q, 128), lambda i: (third(i), 0)),
            pl.BlockSpec((Q, N), lambda i: (third(i), channels // N + 1)),
            whole((256, channels)),
        ],
        out_specs=[
            lanes(first, tokens), lanes(second, tokens), lanes(second, tokens), lanes(second, tokens),
            lanes(second, 8),
            pl.BlockSpec((1, N, channels), lambda i: (third(i), 0, 0)),
            whole((N, channels)),
        ],
        out_shape=[
            sds((tokens, channels)), sds((tokens, channels), BF), sds((tokens, channels), BF),
            sds((tokens, channels)), sds((8, channels)), sds((blocks, N, channels)), sds((N, channels)),
        ],
        scratch_shapes=[
            vmem((tiles, tokens, TILE), F32), vmem((tiles, tokens, TILE), F32), vmem((tiles, tokens, TILE), F32),
            vmem((tokens, 128), F32), vmem((tokens, 128), F32),
            vmem((8, tokens), F32), vmem((max(group - 1, 1), 8, tokens), F32), vmem((tokens, 128), F32),
            vmem((N, channels), F32),
            pltpu.SemaphoreType.DMA((2, max(group - 1, 1))),
        ],
        compiler_params=remote_params(6),
        cost_estimate=cost(40),
        name="gate_and_mix",
    )(y0, graw, gm, act, early, act, grow, spread, vectors, cum, act, spread)


def conv_back_tile(ga_ref, raw_ref, taps_ref, gv_ref, sums_ref, g_pad):
    tokens, width = ga_ref.shape
    taps = taps_ref[...]
    g_pad[0:HALO, :] = jnp.zeros((HALO, width), F32)
    g_pad[HALO + tokens :, :] = jnp.zeros((HALO, width), F32)
    sums = [jnp.zeros((8, width), F32)] * 5
    by_eight = lambda values: jnp.sum(values.reshape(ROWS // 8, 8, width), axis=0)
    for row in range(0, tokens, ROWS):
        moved = conv_window(raw_ref, row, ROWS)
        pre = conv_rows(moved, taps)
        sig = sigmoid(pre)
        g = ga_ref[row : row + ROWS, :] * (sig * (1.0 + pre * (1.0 - sig)))
        g_pad[HALO + row : HALO + row + ROWS, :] = g
        for k in range(4):
            sums[k] = sums[k] + by_eight(g * moved[k])
        sums[4] = sums[4] + by_eight(g)
    for row in list(range(HALO, HALO + tokens, ROWS)) + [0]:
        size = HALO if row == 0 else ROWS
        window = g_pad[row : row + size + 8, :]
        total = taps[3:4, :] * window[:size, :]
        for k in range(3):
            total = total + taps[k : k + 1, :] * pltpu.roll(window, size + 5 + k, 0)[:size, :]
        gv_ref[row : row + size, :] = total.astype(BF)
    for k in range(5):
        sums_ref[k : k + 1, :] = jnp.sum(sums[k], axis=0, keepdims=True)


SMALL_ROWS = 16
A_TAKEN = 4
EARLY_TILES = 3


def finish_kernel(
    cols, dps, heads, part, whole_state,
    ga_ref, raw_ref, taps_ref, gg_ref, gt_ref, v_ref, g_ref, pick_v_ref, tok_ref, inv_ref, g_own_ref,
    mix_ref, headsum_ref, gain_ref, o_total, g_cross, gbc, normed, gt_hbm, tok, cot,
    tg_out, o_out, g_out, v_out, ext_out, sm_out,
    gv_vm, gv_sib, gs_vm, gs_sib, gt_sib, bc_own, bc_land, g_pad, raw_part, taps_part, g_pad_part,
    n_own, n_sib, o_vm, g_vm, g_land, gn_tile, gn_own, gn_parts, gn_land, gn_halo, halo_land,
    joint_low, rec, tot, z_send, z_land, state_land, ext, small, small_land, tok_vm, cot_vm, sems, local,
):
    step = pl.program_id(0)
    channels, half = gv_vm.shape[1], n_own.shape[1]
    shard, piece, span = channels // 2, tot.shape[0], gs_vm.shape[1]
    count, width = gn_own.shape
    tokens = bc_own.shape[0]
    tiles, weight_steps, input_steps = channels // TILE, 2, width // TILE
    weight_at = tiles + 1
    input_at = weight_at + weight_steps
    last = input_at + input_steps
    dp, row, col = here()
    group = cols // 2
    place = lax.rem(col, group)
    sibling, mirror = (dp, 1 - row, col), mirror_of(cols)
    col_peer = lambda by: (dp, row, col ^ by)
    peers = [col_peer(by) for by in range(1, group)]
    others = dps - 1
    o_rows = pl.ds(dp * piece_of(o_vm), piece_of(o_vm))
    g_rows = pl.ds(dp * piece, piece)
    cols_a, cols_b = pl.ds(shard, tot.shape[1] - shard), pl.ds(0, shard)
    used = [0]

    def take(size):
        used[0] += size
        return used[0] - size

    def part_at(at):
        return pl.ds(0, span) if whole_state else lanes_at(at, span)

    def to_dp(src_of, dst_of):
        first = take(others)
        return lambda: dp_copies(dps, sems, src_of, dst_of, first)

    def to_all_dp(src, out):
        first = take(max(others, 4))
        return (lambda: hand_out(dps, sems, first, src, out)[0]), (lambda: hand_out(dps, sems, first, src, out)[1])

    def one(src, dst, device):
        at = take(1)
        return lambda: [copy_to(src, dst, sems, at, device)]

    def to_peers(src_of, dst_of):
        first = take(group - 1)
        return lambda: [
            copy_to(src_of(by), dst_of(by), sems, first + by - 1, col_peer(by)) for by in range(1, group)
        ]

    def to_cols(src, dst):
        first = take(cols - 1)
        return lambda: [copy_to(src, dst, sems, first + by - 1, col_peer(by)) for by in range(1, cols)]

    o_moves, o_passed = to_all_dp(o_total, o_out)
    g_moves, g_passed = to_all_dp(g_vm, g_out)
    a_moves = to_dp(lambda to, i: joint_low.at[to, :, cols_a], lambda to, i: rec.at[i, :, cols_a])
    b_moves = to_dp(lambda to, i: joint_low.at[to, :, cols_b], lambda to, i: rec.at[i, :, cols_b])
    v_moves, v_passed = to_all_dp(tot.at[:, cols_b], v_out)
    e_moves, e_passed = to_all_dp(ext, ext_out)
    g_move = one(g_cross, g_land, mirror)
    n_move = one(normed.at[:, lanes_at(1 - row, half)], n_sib, sibling)
    t_move = one(gt_hbm, gt_sib, sibling)
    s_move = one(gs_vm, gs_sib, sibling)
    z_move = one(z_send, z_land, mirror)
    state_moves = to_cols(tot.at[:, pl.ds(channels, span)], state_land.at[col])

    def state_each(sending, act):
        for by, move in enumerate(state_moves(), 1):
            if whole_state:
                act(move)
            else:
                there = col ^ by
                needed = lax.div(there, 2) == place if sending else lax.rem(there, group) == lax.div(col, 2)
                pl.when(needed)(partial(act, move))

    bc_moves = to_peers(lambda by: gbc.at[:, part_at(place ^ by)], lambda by: bc_land.at[by - 1])
    early_lanes = pl.ds(0, EARLY_TILES * TILE)
    late_lanes = pl.ds(EARLY_TILES * TILE, width - EARLY_TILES * TILE)
    gn_early = to_peers(lambda by: gn_parts.at[by - 1, :, early_lanes], lambda by: gn_land.at[by - 1, :, early_lanes])
    gn_late = to_peers(lambda by: gn_parts.at[by - 1, :, late_lanes], lambda by: gn_land.at[by - 1, :, late_lanes])
    gn_moves = lambda: gn_early() + gn_late()
    tile_first = take(tiles)

    def v_tile(tile):
        lanes = lanes_at(tile, TILE)
        return copy_to(gv_vm.at[:, lanes], gv_sib.at[:, lanes], sems, tile_first + tile, sibling)

    halo_first = take(group)
    halos = lambda: [
        copy_to(gn_halo, halo_land.at[j], sems, halo_first + j, (dp, row, group - 1)) for j in range(group)
    ]
    small_steps = [sibling]
    by = 1
    while by < dps:
        small_steps.append((dp ^ by, row, col))
        by *= 2
    small_first = take(len(small_steps))
    small_move = lambda i: copy_to(small, small_land.at[i], sems, small_first + i, small_steps[i])
    small_cols = to_cols(small, sm_out.at[col])

    def small_next(i):
        move = small_move(i)
        move.wait()
        small[...] += small_land[i]
        if i + 1 < len(small_steps):
            small_move(i + 1).start()

    def start(moves):
        for move in moves:
            move.start()

    def arrive(moves):
        for move in moves:
            move.wait_recv()

    def sent(moves):
        for move in moves:
            move.wait_send()

    load_bc = pltpu.make_async_copy(gbc.at[:, part_at(place)], bc_own, local.at[0])
    load_n = pltpu.make_async_copy(normed.at[:, lanes_at(row, half)], n_own, local.at[1])
    load_o = pltpu.make_async_copy(o_total, o_vm, local.at[2])
    load_tok = pltpu.make_async_copy(tok, tok_vm, local.at[3])
    load_cot = pltpu.make_async_copy(cot, cot_vm, local.at[4])
    store_o = pltpu.make_async_copy(o_vm, o_out.at[o_rows, :], local.at[2])
    store_g = pltpu.make_async_copy(g_vm, g_out.at[g_rows, :], local.at[0])
    store_v = pltpu.make_async_copy(tot.at[:, cols_b], v_out.at[g_rows, :], local.at[1])
    store_e = pltpu.make_async_copy(ext, ext_out.at[g_rows, :], local.at[5])
    store_tg = pltpu.make_async_copy(gn_own, tg_out, local.at[3])
    store_small = pltpu.make_async_copy(small, sm_out.at[col], local.at[6])

    @at_step(0)
    def _():
        load_o.start()
        load_bc.start()
        load_n.start()
        load_tok.start()
        load_cot.start()
        greet([sibling] + [col_peer(by) for by in range(1, cols)] + dp_peers(dps))
        start(bc_moves() + o_moves() + t_move() + n_move() + g_move())
        small[...] = jnp.zeros_like(small)
        small[5:7, 0:channels] = mix_ref[0:2, :]
        small[7:9, 0:128] = headsum_ref[0:2, :]
        load_o.wait()
        store_o.start()

    @pl.when(step < tiles)
    def _():
        lanes = lanes_at(step, TILE)
        conv_back_tile(ga_ref, raw_ref, taps_ref, gv_vm.at[:, lanes], small.at[0:5, lanes], g_pad)
        v_tile(step).start()

    @pl.when(step == tiles - 1)
    def _():
        arrive(o_moves())
        start(o_passed())

    @pl.when(step == tiles)
    def _():
        load_bc.wait()
        arrive(bc_moves())
        for i in range(group - 1):
            bc_own[...] += bc_land[i]
        if whole_state:
            lane = iota2(bc_own.shape, 1)
            mine = (lane >= place * part) & (lane < place * part + part)
            bc_own[...] = jnp.where(mine, bc_own[...], 0.0)
        lanes = part_at(place)
        raw_part[...] = raw_ref[:, lanes]
        taps_part[...] = taps_ref[:, lanes]
        conv_back_tile(bc_own, raw_part, taps_part, gs_vm, small.at[10:15, 0:span], g_pad_part)
        start(s_move())
        arrive(g_move())
        g_vm[...] = g_own_ref[...] + g_land[...].astype(F32)
        start(g_moves())
        store_g.start()

    @pl.when(step == weight_at)
    def _():
        load_n.wait()
        arrive(n_move() + t_move() + s_move() + [v_tile(tile) for tile in range(tiles)])

    def keep(first, size, total):
        for p in range(dps):
            rows = total[p * piece : p * piece + piece, :]
            joint_low[p, :, first : first + size] = rows.astype(BF)

            @pl.when(dp == p)
            def _():
                tot[:, first : first + size] = rows

    @pl.when(step == weight_at)
    def _():
        keep(shard, shard, mm_tn(n_own[...], gv_vm[:, shard:]) + mm_tn(n_sib[...], gv_sib[:, shard:]))
        keep(channels, span, mm_tn(n_own[...], gs_vm[...]) + mm_tn(n_sib[...], gs_sib[...]))
        keep(channels + span, 128, mm_tn(n_own[HALO:, :], gt_ref[...]) + mm_tn(n_sib[HALO:, :], gt_sib[...]))
        start(a_moves())

    @pl.when(step == weight_at + 1)
    def _():
        keep(0, shard, mm_tn(n_own[...], gv_vm[:, :shard]) + mm_tn(n_sib[...], gv_sib[:, :shard]))

    @pl.when(step == input_at)
    def _():
        arrive(g_moves())
        start(g_passed())

    @pl.when(step == input_at + EARLY_TILES)
    def _():
        start(gn_early())

    @pl.when(step == input_at + A_TAKEN)
    def _():
        arrive(a_moves())
        start(b_moves())
        for i in range(others):
            tot[:, cols_a] += rec[i, :, cols_a].astype(F32)
        z_send[:, 0:shard] = tot[:, shard:channels].astype(BF)
        z_send[:, shard:] = tot[:, channels + span :].astype(BF)
        start(z_move())
        state_each(True, lambda move: move.start())
        state_land[col] = tot[:, channels : channels + span]

    @pl.when((step >= input_at) & (step < last))
    def _():
        at = step - input_at
        lanes = lanes_at(at, TILE)
        gn_tile[...] = mm_nt(gv_vm[...], v_ref[...]) + mm_nt(gs_vm[...], pick_v_ref[:, part_at(place)])
        gn_tile[HALO:, :] += mm_nt(gg_ref[...], g_ref[...]) + mm_nt(gt_ref[...], pick_v_ref[:, TILE:])
        rows = lambda index: pl.ds(pl.multiple_of(HALO + index * count, HALO), count)
        gn_own[:, lanes] = gn_tile[rows(place), :]
        for by in range(1, group):
            gn_parts[by - 1, :, lanes] = gn_tile[rows(place ^ by), :].astype(BF)
        gn_halo[:, lanes] = gn_tile[0:HALO, :].astype(BF)
        sums = jnp.zeros((1, TILE), F32)
        for first in [0] + list(range(HALO, HALO + tokens, Q)):
            size = HALO if first == 0 else Q
            unit = tok_ref[first : first + size, :].astype(F32) * inv_ref[first : first + size, 0:1]
            sums = sums + jnp.sum(gn_tile[first : first + size, :] * unit, axis=0, keepdims=True)
        small[9:10, lanes] = sums

    @pl.when(step == last)
    def _():
        for j in range(group):
            pl.when(col == group + j)(halos()[j].start)
        small_move(0).start()
        small_next(0)
        arrive(b_moves())
        for i in range(others):
            tot[:, cols_b] += rec[i, :, cols_b].astype(F32)
        arrive(z_move())
        start(gn_late())
        tot[:, cols_b] += z_land[:, 0:shard].astype(F32)
        start(v_moves())
        store_v.start()
        steps = tot[:, channels + span :] + pltpu.roll(z_land[:, shard:].astype(F32), 128 - heads, 1)
        state_each(False, lambda move: move.wait_recv())
        if whole_state:
            ext[:, 0:128] = steps
            ext[:, 128:] = sum(state_land[i] for i in range(cols))
        else:
            states = state_land[lax.div(col, 2)] + state_land[lax.div(col, 2) + group]
            moved = jnp.where(lax.rem(col, 2) == 1, states, pltpu.roll(states, 64, 1))
            ext[...] = jnp.where(iota2(steps.shape, 1) < 64, steps, moved)
        start(e_moves())
        store_e.start()
        for i in range(1, len(small_steps)):
            small_next(i)
        start(small_cols())
        store_small.start()
        arrive(v_moves())
        start(v_passed())
        arrive(e_moves())
        start(e_passed())
        load_tok.wait()
        load_cot.wait()
        arrive(gn_moves())
        for i in range(group - 1):
            gn_own[...] += gn_land[i].astype(F32)

        @pl.when(col == group - 1)
        def _():
            arrive(halos())
            for j in range(group):
                gn_own[count - HALO :, :] += halo_land[j].astype(F32)

        for j in range(group):
            pl.when(col == group + j)(halos()[j].wait_send)
        for first in range(0, count, ROWS):
            rows = slice(first, first + ROWS)
            values = tok_vm[rows, :].astype(F32)
            inv = lax.rsqrt(jnp.mean(values * values, axis=-1, keepdims=True) + EPSILON)
            unit = values * inv
            pulled = gn_own[rows, :] * gain_ref[0:1, :]
            mean = jnp.mean(pulled * unit, axis=-1, keepdims=True)
            gn_own[rows, :] = cot_vm[rows, :].astype(F32) + inv * (pulled - unit * mean)
        store_tg.start()
        store_o.wait()
        store_g.wait()
        store_small.wait()
        store_v.wait()
        store_e.wait()
        arrive(o_passed() + g_passed() + v_passed() + e_passed() + small_cols())
        sent(o_passed() + g_passed() + v_passed() + e_passed())
        sent(bc_moves() + o_moves() + t_move() + n_move() + g_move() + s_move() + a_moves() + b_moves())
        sent([v_tile(tile) for tile in range(tiles)])
        state_each(True, lambda move: move.wait_send())
        sent(gn_moves() + z_move() + g_moves() + v_moves() + e_moves() + small_cols())
        store_tg.wait()


def piece_of(ref):
    return ref.shape[0]


def finish(
    cols, dps, heads, part, ga, raw, taps, gg, gt, w_value, w_gate, picked, tokens_in, inv_rms, g_own, mix_sums,
    head_sums, gain, o_total, g_cross, gbc, normed, tokens_own, cotangent,
):
    tokens, channels = ga.shape
    rows, width = normed.shape
    half, shard = width // 2, channels // 2
    whole_state = part % 128 != 0
    span = 2 * N if whole_state else part
    extra = 128 + span if whole_state else 128
    group = cols // 2
    tiles, weight_steps, input_steps = channels // TILE, 2, width // TILE
    piece, wide = g_own.shape[0], channels + span + 128
    count = tokens_own.shape[0]
    input_at = tiles + 1 + weight_steps
    small_steps = dps.bit_length()

    def clamp(first, size):
        return lambda i: jnp.clip(i - first, 0, size - 1)

    conv, both, input_tile = clamp(0, tiles), clamp(0, tiles + 1), clamp(input_at, input_steps)
    lanes = lambda at, size: pl.BlockSpec((size, TILE), lambda i: (0, at(i)))
    slab = lambda at, size: pl.BlockSpec((TILE, size), lambda i: (at(i), 0))
    once = lambda values: pl.BlockSpec(
        values.shape, lambda *_: (0,) * len(values.shape), pipeline_mode=pl.Buffered(1)
    )
    vmem = pltpu.VMEM
    dma = pltpu.SemaphoreType.DMA
    more = max(group - 1, 1)
    copies = 2 * (dps - 1) + 4 * max(dps - 1, 4) + 6 + 2 * (cols - 1) + 3 * (group - 1) + tiles + group + small_steps
    return pl.pallas_call(
        partial(finish_kernel, cols, dps, heads, part, whole_state),
        grid=(input_at + input_steps + 1,),
        in_specs=[
            lanes(conv, tokens),
            lanes(both, rows),
            lanes(both, 8),
            once(gg),
            once(gt),
            slab(input_tile, channels),
            slab(input_tile, channels),
            slab(input_tile, TILE + 128),
            lanes(input_tile, rows),
            once(inv_rms),
            once(g_own),
            once(mix_sums),
            once(head_sums),
            once(gain),
        ] + [ANY] * 7,
        out_specs=[ANY] * 6,
        out_shape=[
            sds((count, width)), sds((dps * o_total.shape[0], o_total.shape[1])), sds((half, shard)),
            sds((half, shard)), sds((half, extra)), sds((cols, SMALL_ROWS, width)),
        ],
        scratch_shapes=[
            vmem((rows, channels), BF), vmem((rows, channels), BF), vmem((rows, span), BF), vmem((rows, span), BF),
            vmem((tokens, 128), BF), vmem((tokens, span), F32), vmem((more, tokens, span), F32),
            vmem((tokens + 2 * HALO, TILE), F32), vmem((rows, span), F32), vmem((8, span), F32),
            vmem((tokens + 2 * HALO, span), F32),
            vmem((rows, half), BF), vmem((rows, half), BF),
            vmem(o_total.shape, F32), vmem(g_own.shape, F32), vmem(g_own.shape, BF),
            vmem((rows, TILE), F32),
            vmem((count, width), F32), vmem((more, count, width), BF), vmem((more, count, width), BF),
            vmem((HALO, width), BF), vmem((group, HALO, width), BF),
            vmem((dps, piece, wide), BF), vmem((dps - 1, piece, wide), BF), vmem((piece, wide), F32),
            vmem((piece, shard + 128), BF), vmem((piece, shard + 128), BF),
            vmem((cols, piece, span), F32), vmem((piece, extra), F32),
            vmem((SMALL_ROWS, width), F32), vmem((small_steps, SMALL_ROWS, width), F32),
            vmem((count, width), BF), vmem((count, width), BF),
            dma((2, copies)),
            dma((7,)),
        ],
        compiler_params=remote_params(5),
        cost_estimate=cost(110),
        name="finish",
    )(
        ga, raw, taps, gg, gt, w_value, w_gate, picked, tokens_in, inv_rms, g_own, mix_sums, head_sums, gain,
        o_total, g_cross, gbc, normed, gt, tokens_own, cotangent,
    )


def collect_kernel(tok_ref, branch_ref, in_ref, *refs):
    half = (len(refs) - 1) // 2
    refs[half][...] = (
        tok_ref[...].astype(F32) + branch_ref[...] + jnp.sum(in_ref[...].astype(F32), axis=0)
    ).astype(BF)
    for source, target in zip(refs[:half], refs[half + 1 :]):
        target[...] = source[...]


def collect(tokens, branch, branch_in, results):
    steps = 4
    slab = lambda v: pl.BlockSpec((v.shape[0] // steps, v.shape[1]), lambda i: (i, 0))
    more, count, width = branch_in.shape
    return pl.pallas_call(
        collect_kernel,
        grid=(steps,),
        in_specs=[
            slab(tokens), slab(branch), pl.BlockSpec((more, count // steps, width), lambda i: (0, i, 0)),
        ] + [slab(v) for v in results],
        out_specs=[slab(tokens)] + [slab(v) for v in results],
        out_shape=[sds(tokens.shape, BF)] + [sds(v.shape) for v in results],
        compiler_params=params(),
        cost_estimate=cost(8),
        name="collect",
    )(tokens, branch, branch_in, *results)


def flips(size, by):
    return [(i, i ^ by) for i in range(size)]


def butterfly(values, axis):
    size = lax.axis_size(axis)
    by = 1
    while by < size:
        values = values + lax.ppermute(values, axis, flips(size, by))
        by *= 2
    return values


def at_rows(values, index, size):
    return lax.dynamic_slice_in_dim(values, index * size, size, axis=0)


def collect_dp(piece, dp):
    size = lax.axis_size("dp")
    rows = piece.shape[0]
    out = jnp.zeros((size * rows,) + piece.shape[1:], piece.dtype)
    out = lax.dynamic_update_slice_in_dim(out, piece, dp * rows, 0)
    for by in range(1, size):
        other = lax.ppermute(piece, "dp", flips(size, by))
        out = lax.dynamic_update_slice_in_dim(out, other, (dp ^ by) * rows, 0)
    return out


def swap_core(values):
    return lax.ppermute(values, "row", [(0, 1), (1, 0)])


def per_device(
    tokens, norm_gain, w_gate, w_value, w_state, w_step, conv_value, bias_value, conv_state,
    bias_state, a_log, d_skip, dt_bias, mix_gain, w_out, cotangent,
):
    cols, rows_n, dps = lax.axis_size("col"), lax.axis_size("row"), lax.axis_size("dp")
    col, row, dp = lax.axis_index("col"), lax.axis_index("row"), lax.axis_index("dp")
    group = cols // 2
    place = lax.rem(col, group)
    local, width = tokens.shape
    span = local * group
    half_width = width // 2
    shard = w_value.shape[1]
    channels = 2 * shard
    heads = a_log.shape[0]
    inner_channels = shard * cols
    state_all = w_state.shape[1] * cols
    mirror = [(i, cols - 1 - i) for i in range(cols)]
    forth = [(i, cols - 1 - i) for i in range(group)]
    back = [(cols - 1 - i, i) for i in range(group)]

    def ring(by):
        return [(i, (i // group) * group + (i % group + by) % group) for i in range(cols)]

    state_width = w_state.shape[1]
    small = jnp.pad(
        jnp.concatenate([w_state, w_step], axis=1), ((0, 0), (0, 128 - state_width - heads))
    )
    heads_row = jnp.pad(
        jnp.concatenate([d_skip, a_log, dt_bias]), (0, shard - 3 * heads)
    )[None]
    state_rows = jnp.concatenate([conv_state.T, bias_state[None]], axis=0)
    vec = jnp.concatenate(
        [
            conv_value.T, bias_value[None], mix_gain[None], heads_row, jnp.zeros((1, shard), BF),
            jnp.pad(state_rows, ((0, 3), (0, shard - state_width))),
        ],
        axis=0,
    )
    group_tokens, value_full, small_full, vecs = import_all(cols, dps, tokens, w_value, small, vec)
    from_col = lax.broadcasted_iota(jnp.int32, (cols * 128, TILE + 128), 0) // 128
    from_lane = lax.broadcasted_iota(jnp.int32, (cols * 128, TILE + 128), 0) % 128
    to = lax.broadcasted_iota(jnp.int32, (cols * 128, TILE + 128), 1)
    head_to = to - TILE
    is_state = (to < TILE) & (from_lane < state_width) & (from_col * state_width + from_lane == to)
    is_own = (from_col == col) & (head_to < heads) & (from_lane == state_width + head_to)
    is_mirror = (from_col == cols - 1 - col) & (head_to >= heads) & (head_to < 2 * heads)
    is_mirror = is_mirror & (from_lane == state_width + head_to - heads)
    pick = (is_state | ((head_to >= 0) & (is_own | is_mirror))).astype(BF)

    vecs = vecs.astype(F32)
    both = jnp.concatenate(
        [
            lax.dynamic_index_in_dim(vecs, col, 0, keepdims=False),
            lax.dynamic_index_in_dim(vecs, cols - 1 - col, 0, keepdims=False),
        ],
        axis=1,
    )
    state_vecs = jnp.transpose(vecs[:, 8:16, :state_width], (1, 0, 2)).reshape(8, state_all)
    taps = jnp.concatenate([both[0:8], state_vecs], axis=1)

    def both_heads(at):
        return jnp.concatenate(
            [both[6, at * heads : (at + 1) * heads], both[6, shard + at * heads : shard + (at + 1) * heads]]
        )

    skip_both, a_both, dt_both = both_heads(0), both_heads(1), both_heads(2)
    vectors = jnp.concatenate(
        [jnp.repeat(skip_both, HEAD)[None], both[5:6], jnp.zeros((6, channels), F32)], axis=0
    )
    rate = -jnp.exp(a_both)
    head_rows = jnp.pad(jnp.stack([dt_both, rate]), ((0, 6), (0, 128 - 2 * heads)))
    head_of = np.arange(channels) // HEAD
    one_hot = (np.arange(128)[:, None] == head_of[None, :]).astype(np.float32)
    spread = jnp.asarray(np.concatenate([one_hot, one_hot], axis=0), BF)
    gather = jnp.asarray(one_hot.T, BF)

    gain = norm_gain.astype(F32)
    (
        raw, act, normed, step_in, step, cum, grow, offs, inv_rms, picked, states, y0, graw, gm, early,
        group_cot, gate_full, out_full,
    ) = forward_all(
        cols, dps, group_tokens, gain[None], value_full, small_full, pick, taps, head_rows, spread, cotangent,
        w_gate, w_out,
    )
    y, mixed, grad_gate, dy, mix_sums, after, first_grad = gate_and_mix(
        cols, inner_channels, y0, graw, gm, act, early, grow, spread, vectors, cum
    )
    (
        ga, grad_step, gbc, head_sums, out_total, gate_own, gate_cross, branch, branch_in, _, _,
    ) = scan_backward(
        cols, dps, dy, act, y, step, cum, step_in, spread, gather, after, states, early, offs, head_rows, vectors,
        mixed, out_full, grad_gate, first_grad, group_cot, normed,
    )
    state_part = state_all // group

    tokens_grad, sum_out, sum_gate, sum_value, extra, small_sums = finish(
        cols, dps, heads, state_part, ga, raw, taps, grad_gate, grad_step, value_full, gate_full, picked,
        group_tokens, inv_rms, gate_own, mix_sums, head_sums, gain[None], out_total, gate_cross, gbc, normed,
        tokens, cotangent,
    )
    block_out, tokens_grad, sum_out, sum_gate, sum_value = collect(
        tokens, branch, branch_in, [tokens_grad, sum_out, sum_gate, sum_value]
    )
    sum_step = extra[:, :heads]
    whole_state = state_part % 128 != 0
    if whole_state:
        sum_state = lax.dynamic_slice_in_dim(extra, 128 + col * state_width, state_width, axis=1)
    else:
        sum_state = extra[:, 64:]
    own_sums = lax.dynamic_index_in_dim(small_sums, col, 0, keepdims=False)
    mirror_sums = lax.dynamic_index_in_dim(small_sums, cols - 1 - col, 0, keepdims=False)
    wide = own_sums[0:7, :shard] + mirror_sums[0:7, shard:channels]
    head_own = own_sums[7:9, :heads] + mirror_sums[7:9, heads : 2 * heads]
    skip_own = jnp.sum(wide[6].reshape(heads, HEAD), axis=1)
    norm_total = small_sums[0, 9]
    for i in range(1, cols):
        norm_total = norm_total + small_sums[i, 9]
    if whole_state:
        state_sums = jnp.sum(small_sums[:, 10:15, :state_all], axis=0)
        state_first = col * state_width
    else:
        half_at = col * state_width // state_part
        state_sums = lax.dynamic_index_in_dim(small_sums, half_at, 0, keepdims=False)[10:15, :state_part]
        state_sums = state_sums + lax.dynamic_index_in_dim(
            small_sums, half_at + group, 0, keepdims=False
        )[10:15, :state_part]
        state_first = lax.rem(col * state_width, state_part)
    state_own = lax.dynamic_slice_in_dim(state_sums, state_first, state_width, axis=1)

    return (
        block_out,
        tokens_grad,
        norm_total,
        sum_gate,
        sum_value,
        sum_state,
        sum_step,
        wide[:4].T,
        wide[4],
        state_own[:4].T,
        state_own[4],
        head_own[0] * rate[:heads],
        skip_own,
        head_own[1],
        wide[5],
        sum_out,
    )


def solution(mesh):
    rows = P(("dp", "row", "col"), None)
    grid = P("row", "col")
    vec = P("col")
    taps = P("col", None)
    return jax.shard_map(
        per_device,
        mesh=mesh,
        in_specs=(
            rows, P(), grid, grid, grid, grid, taps, vec, taps, vec, vec, vec, vec, vec,
            P("col", "row"), rows,
        ),
        out_specs=(
            rows, rows, P(), grid, grid, grid, grid, taps, vec, taps, vec, vec, vec, vec, vec,
            P("col", "row"),
        ),
        check_vma=False,
    )
```
